32 devices in a mesh: dp: 4 (over z), fsdp: 8 (over y, x, core).
Axes of the slice: x: 2, y: 2, z: 4, core: 2. Of those that a mesh axis runs over, the one named last changes fastest.
Arguments:
- images: bfloat16 [512, 16, 16, 256], P(('dp', 'fsdp')), may hold values from -6 to 6
- timesteps: int32 [512], P(('dp', 'fsdp')), may hold values from 0 to 999
- counts: int32 [32], P(('dp', 'fsdp')), may hold values from 1 to 16
- cotangent: bfloat16 [512, 16, 16, 256], P(('dp', 'fsdp')), may hold values from -6 to 6
- conv_master: float32 [1, 2, 9, 256, 256], P(None, None, None, 'dp', 'fsdp'), may hold values from -0.125 to 0.125
- conv_moment: float32 [1, 2, 9, 256, 256], P(None, None, None, 'dp', 'fsdp'), may hold values from -1 to 1
- conv_square: float32 [1, 2, 9, 256, 256], P(None, None, None, 'dp', 'fsdp'), may hold values from 0 to 1
- embed_master: float32 [1, 512, 256], P(None, 'dp', 'fsdp'), may hold values from -0.5 to 0.5
- embed_moment: float32 [1, 512, 256], P(None, 'dp', 'fsdp'), may hold values from -1 to 1
- embed_square: float32 [1, 512, 256], P(None, 'dp', 'fsdp'), may hold values from 0 to 1
- attend_master: float32 [1, 256, 768], P(None, 'dp', 'fsdp'), may hold values from -0.375 to 0.375
- attend_moment: float32 [1, 256, 768], P(None, 'dp', 'fsdp'), may hold values from -1 to 1
- attend_square: float32 [1, 256, 768], P(None, 'dp', 'fsdp'), may hold values from 0 to 1
- output_master: float32 [1, 256, 256], P(None, 'dp', 'fsdp'), may hold values from -1 to 1
- output_moment: float32 [1, 256, 256], P(None, 'dp', 'fsdp'), may hold values from -1 to 1
- output_square: float32 [1, 256, 256], P(None, 'dp', 'fsdp'), may hold values from 0 to 1
- vector_master: float32 [1, 3072], P(None, ('dp', 'fsdp')), may hold values from -3 to 3
- vector_moment: float32 [1, 3072], P(None, ('dp', 'fsdp')), may hold values from -1 to 1
- vector_square: float32 [1, 3072], P(None, ('dp', 'fsdp')), may hold values from 0 to 1
Outputs:
- block_output: float32 [512, 16, 16, 256], P(('dp', 'fsdp'))
- input_grad: float32 [512, 16, 16, 256], P(('dp', 'fsdp'))
- conv_first: float32 [1, 2, 9, 256, 256], P(None, None, None, 'dp', 'fsdp')
- conv_second: float32 [1, 2, 9, 256, 256], P(None, None, None, 'dp', 'fsdp')
- conv_updated: float32 [1, 2, 9, 256, 256], P(None, None, None, 'dp', 'fsdp')
- embed_first: float32 [1, 512, 256], P(None, 'dp', 'fsdp')
- embed_second: float32 [1, 512, 256], P(None, 'dp', 'fsdp')
- embed_updated: float32 [1, 512, 256], P(None, 'dp', 'fsdp')
- attend_first: float32 [1, 256, 768], P(None, 'dp', 'fsdp')
- attend_second: float32 [1, 256, 768], P(None, 'dp', 'fsdp')
- attend_updated: float32 [1, 256, 768], P(None, 'dp', 'fsdp')
- output_first: float32 [1, 256, 256], P(None, 'dp', 'fsdp')
- output_second: float32 [1, 256, 256], P(None, 'dp', 'fsdp')
- output_updated: float32 [1, 256, 256], P(None, 'dp', 'fsdp')
- vector_first: float32 [1, 3072], P(None, ('dp', 'fsdp'))
- vector_second: float32 [1, 3072], P(None, ('dp', 'fsdp'))
- vector_updated: float32 [1, 3072], P(None, ('dp', 'fsdp'))
- grad_norm: float32 [], replicated
The draws below stay inside these ranges and needn't reach their ends.
Inputs may be any that keep to these rules, and one draw needn't show every extreme that they name: `counts`: a device's live images are its first slots in order.
All inputs are finite; a program needn't handle non-finite values.
Results may differ from the reference program's by a relative error of at most 0.018.
The reference program's roundings to bfloat16 on the way count: a program that leaves them out, or rounds other values in their place, can miss the bound.
Values may be sent and summed in bfloat16 or wider, within the bound.
No kernel may reach another device: no remote copies, remote signals or barrier semaphores. Data moves between devices by JAX's collectives and lax.ppermute only.
A program may use at most 192 MiB of HBM per device.

```python
import math
import jax
import jax.numpy as jnp
from jax import lax

C = 256
E = 512
GROUPS = 32
H = 16
L = 1
IMG_DEV = 16
STEP = 10
IMAGES = 512
PARAMS = 1575936
N_DP = 4
N_FSDP = 8


def channel_rise(channels):
    top_factor = 3.0
    return jnp.exp(0.5 * math.log(top_factor) * jnp.arange(channels, dtype=jnp.float32) / (channels - 1))


def draw_cotangent(key, part):
    key = jax.random.fold_in(key, 101)
    shape_all = (IMAGES, H, H, C)
    base_values = 0.8 * jnp.clip(jax.random.normal(key, shape_all), -4.0, 4.0)
    return (base_values * channel_rise(C)).astype(jnp.bfloat16)


def draw_vector_master(key, part):
    key = jax.random.fold_in(key, 103)
    key_spread, key_factor = jax.random.split(key)
    spread_values = 0.3 * jnp.clip(jax.random.normal(key_spread, (L, 12, C)), -5.0, 5.0)
    factors = jax.random.uniform(key_factor, (L, 12, C), minval=0.8, maxval=1.25)
    row_index = jnp.arange(12)
    gain_rows = (row_index == 0) | (row_index == 4) | (row_index == 7)
    gains = channel_rise(C)[None, None, :] * factors
    return jnp.where(gain_rows[:, None], gains, spread_values).reshape(L, 12 * C)


def moment_first(key, shape_all, factor, salt):
    key = jax.random.fold_in(key, salt)
    unit_size = factor / math.sqrt(PARAMS)
    return 0.11 * unit_size * jnp.clip(jax.random.normal(key, shape_all), -5.0, 5.0)


def moment_second(key, shape_all, factor, salt):
    key = jax.random.fold_in(key, salt)
    unit_size = factor * factor / PARAMS
    exponent = jax.random.uniform(key, shape_all, minval=0.0, maxval=math.log(4.0))
    return 0.001 * unit_size * jnp.exp(exponent)


def draw_conv_moment(key, part):
    return moment_first(key, (L, 2, 9, C, C), 1.0, 11)


def draw_conv_square(key, part):
    return moment_second(key, (L, 2, 9, C, C), 1.0, 12)


def draw_embed_moment(key, part):
    return moment_first(key, (L, E, C), 1.0, 21)


def draw_embed_square(key, part):
    return moment_second(key, (L, E, C), 1.0, 22)


def draw_attend_moment(key, part):
    return moment_first(key, (L, C, 3 * C), 0.7, 31)


def draw_attend_square(key, part):
    return moment_second(key, (L, C, 3 * C), 0.7, 32)


def draw_output_moment(key, part):
    return moment_first(key, (L, C, C), 1.0, 41)


def draw_output_square(key, part):
    return moment_second(key, (L, C, C), 1.0, 42)


def draw_vector_moment(key, part):
    return moment_first(key, (L, 12 * C), 3.0, 51)


def draw_vector_square(key, part):
    return moment_second(key, (L, 12 * C), 3.0, 52)


def set_ends(entries, own_key, low, high):
    dims = entries.shape
    spot = [jax.random.randint(jax.random.fold_in(own_key, axis), (), 0, dims[axis]) for axis in range(len(dims))]
    entries = entries.at[tuple(spot)].set(low)
    longest = dims.index(max(dims))
    spot[longest] = (spot[longest] + 1) % dims[longest]
    return entries.at[tuple(spot)].set(high)


def levels(stream_key, shape, cuts, smallest, high):
    def one(position, parts):
        steps = jax.random.uniform(jax.random.fold_in(jax.random.fold_in(stream_key, 6), position), (parts,), jnp.float32, smallest / len(cuts), high / len(cuts))
        return jnp.repeat(jnp.exp(steps), shape[position] // parts).reshape((-1,) + (1,) * (len(shape) - position - 1))

    level = one(*cuts[0])
    for cut in cuts[1:]:
        level = level * one(*cut)
    return level


def scatter_about(stream_key, shape, scale, most, cuts=(), held_as=jnp.bfloat16):
    values = jax.random.normal(stream_key, shape, jnp.float32) * scale
    if len(cuts) > 0:
        values = levels(stream_key, shape, cuts, -0.22, 0.18) * values
    return jnp.clip(values, min=-most, max=most).astype(held_as)


def setup_inputs(seed: int = 0) -> dict:
    key_of = jax.random.split(jax.random.key(seed), 20)
    images = scatter_about(key_of[0], (IMAGES, H, H, C), 1.0, 6.0, ((0, 32),))
    timesteps = set_ends(jax.random.randint(key_of[1], (IMAGES,), 0, 1000), jax.random.fold_in(key_of[1], 1), 0, 999).astype(jnp.int32)
    counts = set_ends(jax.random.randint(key_of[2], (N_DP * N_FSDP,), 1, IMG_DEV + 1), jax.random.fold_in(key_of[2], 1), 1, IMG_DEV).astype(jnp.int32)
    cotangent = draw_cotangent(jax.random.fold_in(key_of[19], 71), 0)
    conv_master = scatter_about(key_of[4], (L, 2, 9, C, C), (9 * C) ** -0.5, 0.125, ((3, 4), (4, 8)), jnp.float32)
    conv_moment = draw_conv_moment(jax.random.fold_in(key_of[19], 71), 0)
    conv_square = draw_conv_square(jax.random.fold_in(key_of[19], 71), 0)
    embed_master = scatter_about(key_of[7], (L, E, C), (E // 4) ** -0.5, 0.5, ((1, 4), (2, 8)), jnp.float32)
    embed_moment = draw_embed_moment(jax.random.fold_in(key_of[19], 71), 0)
    embed_square = draw_embed_square(jax.random.fold_in(key_of[19], 71), 0)
    attend_master = scatter_about(key_of[10], (L, C, 3 * C), C ** -0.5, 0.375, ((1, 4), (2, 8)), jnp.float32)
    attend_moment = draw_attend_moment(jax.random.fold_in(key_of[19], 71), 0)
    attend_square = draw_attend_square(jax.random.fold_in(key_of[19], 71), 0)
    output_master = scatter_about(key_of[13], (L, C, C), (C // 8) ** -0.5, 1.0, ((1, 4), (2, 8)), jnp.float32)
    output_moment = draw_output_moment(jax.random.fold_in(key_of[19], 71), 0)
    output_square = draw_output_square(jax.random.fold_in(key_of[19], 71), 0)
    vector_master = draw_vector_master(jax.random.fold_in(key_of[19], 71), 0)
    vector_moment = draw_vector_moment(jax.random.fold_in(key_of[19], 71), 0)
    vector_square = draw_vector_square(jax.random.fold_in(key_of[19], 71), 0)
    return {"images": images, "timesteps": timesteps, "counts": counts, "cotangent": cotangent, "conv_master": conv_master, "conv_moment": conv_moment, "conv_square": conv_square, "embed_master": embed_master, "embed_moment": embed_moment, "embed_square": embed_square, "attend_master": attend_master, "attend_moment": attend_moment, "attend_square": attend_square, "output_master": output_master, "output_moment": output_moment, "output_square": output_square, "vector_master": vector_master, "vector_moment": vector_moment, "vector_square": vector_square}


@jax.custom_vjp
def low(v):
    return lax.optimization_barrier(v.astype(jnp.bfloat16)).astype(jnp.float32)

@jax.custom_vjp
def low_back(v):
    return v

def low_keep(v):
    return (low(v), None)

def low_pass(kept, grad):
    return (grad,)

def back_keep(v):
    return (v, None)

def back_low(kept, grad):
    return (low(grad),)
low.defvjp(low_keep, low_pass)
low_back.defvjp(back_keep, back_low)
highest = lax.Precision.HIGHEST
norm_eps = 1e-06
beta_first = 0.9
beta_second = 0.999
adam_eps = 1e-08
clip_norm = 1.0
rates_kind = (0.01, 0.03, 0.02, 0.05, 0.3)
decays_kind = (0.1, 0.1, 0.1, 0.1, 0.0)

def sinus_embed(steps_in):
    half_width = E // 2
    frequency = jnp.exp(-math.log(10000.0) * jnp.arange(half_width, dtype=jnp.float32) / (half_width - 1))
    angles = steps_in.astype(jnp.float32)[:, None] * frequency[None, :]
    return jnp.concatenate([jnp.sin(angles), jnp.cos(angles)], axis=1)

def norm_act(source_map, gain_row, bias_row):
    num_img = source_map.shape[0]
    channels = source_map.shape[3]
    grouped = source_map.reshape(num_img, -1, GROUPS, channels // GROUPS)
    group_mean = lax.optimization_barrier(jnp.mean(grouped, axis=(1, 3), keepdims=True))
    centered = grouped - group_mean
    group_var = lax.optimization_barrier(jnp.mean(centered * centered, axis=(1, 3), keepdims=True))
    normed = (centered * lax.rsqrt(group_var + norm_eps)).reshape(source_map.shape)
    return normed * gain_row + bias_row

def shifted(source_map):
    height = source_map.shape[1]
    padded = jnp.pad(source_map, ((0, 0), (1, 1), (1, 1), (0, 0)))
    return jnp.stack([padded[:, row_at:row_at + height, col_at:col_at + height, :] for row_at in range(3) for col_at in range(3)])

def conv_ref(source_map, kernel):
    return jnp.einsum('tnhwc,tcd->nhwd', shifted(source_map), kernel, precision=highest)

def layer_apply(stream, embed_act, conv_kernels, embed_weight, attend_weight, output_weight, vectors):
    num_img = stream.shape[0]
    channels = stream.shape[3]
    active_one = low(jax.nn.silu(norm_act(stream, vectors[0], vectors[1])))
    shift_emb = low_back(jnp.dot(embed_act, embed_weight, precision=highest)) + vectors[3]
    hidden = low_back(conv_ref(active_one, conv_kernels[0])) + vectors[2] + shift_emb[:, None, None, :]
    active_two = low(jax.nn.silu(norm_act(hidden, vectors[4], vectors[5])))
    middle = stream + low_back(conv_ref(active_two, conv_kernels[1])) + vectors[6]
    active_three = low(norm_act(middle, vectors[7], vectors[8]))
    flat_three = active_three.reshape(num_img, -1, channels)
    bias_cat = jnp.concatenate([vectors[9], jnp.zeros_like(vectors[9]), vectors[10]])
    mixed_rows = low(low_back(jnp.einsum('npc,cd->npd', flat_three, attend_weight, precision=highest) + bias_cat))
    query_part = mixed_rows[..., :channels]
    key_part = mixed_rows[..., channels:2 * channels]
    value_part = mixed_rows[..., 2 * channels:]
    scores = low_back(jnp.einsum('npc,nqc->npq', query_part, key_part, precision=highest) * channels ** (-0.5))
    prob_low = low(jax.nn.softmax(scores, axis=-1))
    attended = low(low_back(jnp.einsum('npq,nqc->npc', prob_low, value_part, precision=highest)))
    projected = low_back(jnp.einsum('npc,cd->npd', attended, output_weight, precision=highest)) + vectors[11]
    return middle + projected.reshape(stream.shape)

def forward(masters, stream, embed_act):
    lowered = [low(member) for member in masters]
    for layer_at in range(L):
        stream = layer_apply(stream, embed_act, lowered[0][layer_at], lowered[1][layer_at], lowered[2][layer_at], lowered[3][layer_at], lowered[4][layer_at].reshape(12, C))
    return stream

def reference(images, timesteps, counts, cotangent, conv_master, conv_moment, conv_square, embed_master, embed_moment, embed_square, attend_master, attend_moment, attend_square, output_master, output_moment, output_square, vector_master, vector_moment, vector_square):
    masters = (conv_master, embed_master, attend_master, output_master, vector_master)
    moments = (conv_moment, embed_moment, attend_moment, output_moment, vector_moment)
    squares = (conv_square, embed_square, attend_square, output_square, vector_square)
    devices = counts.shape[0]
    fields = images.astype(jnp.float32).reshape(devices, IMG_DEV, H, H, C)
    cot_fields = cotangent.astype(jnp.float32).reshape(devices, IMG_DEV, H, H, C)
    embeds = low(jax.nn.silu(sinus_embed(timesteps))).reshape(devices, IMG_DEV, E)
    alive_mask = (jnp.arange(IMG_DEV)[None, :] < counts[:, None]).astype(jnp.float32)

    def one_device(totals, pieces):
        stream, embed_act, cot_field, alive_row = pieces
        mask_row = alive_row[:, None, None, None]
        result, pull_back = jax.vjp(lambda params, inputs: forward(params, inputs, embed_act), masters, stream)
        grad_list, input_grad = pull_back(cot_field * mask_row)
        totals = tuple((total_item + grad_item for total_item, grad_item in zip(totals, grad_list)))
        return (totals, (result * mask_row, input_grad * mask_row))
    start_sums = tuple((jnp.zeros_like(member) for member in masters))
    totals, (outputs, input_grads) = lax.scan(one_device, start_sums, (fields, embeds, cot_fields, alive_mask))
    square_sum = sum((jnp.sum(member * member) for member in totals))
    grad_norm = jnp.sqrt(square_sum)
    factor = clip_norm / jnp.maximum(grad_norm, clip_norm)
    results = []
    for index_at in range(5):
        clipped = totals[index_at] * factor
        first_new = beta_first * moments[index_at] + (1.0 - beta_first) * clipped
        second_new = beta_second * squares[index_at] + (1.0 - beta_second) * clipped * clipped
        first_hat = first_new / (1.0 - beta_first ** STEP)
        second_hat = second_new / (1.0 - beta_second ** STEP)
        update_new = masters[index_at] - rates_kind[index_at] * (first_hat / (jnp.sqrt(second_hat) + adam_eps) + decays_kind[index_at] * masters[index_at])
        results += [first_new, second_new, update_new]
    return (outputs.reshape(images.shape), input_grads.reshape(images.shape), results[0], results[1], results[2], results[3], results[4], results[5], results[6], results[7], results[8], results[9], results[10], results[11], results[12], results[13], results[14], grad_norm)
```

```python
from functools import partial
import functools
import math

import jax, jax.numpy as jnp
from jax import lax
from jax.sharding import PartitionSpec as P
from jax.experimental import pallas as pl
from jax.experimental.pallas import tpu as pltpu

BF=jnp.bfloat16; F32=jnp.float32
EPS=1e-6
def dot(a,b): return lax.dot_general(a,b,(((1,),(0,)),((),())),preferred_element_type=F32)
def dot_nt(a,b): return lax.dot_general(a,b,(((1,),(1,)),((),())),preferred_element_type=F32)
def dot_tn(a,b): return lax.dot_general(a,b,(((0,),(0,)),((),())),preferred_element_type=F32)

def gsum(s):
    n=s.shape[0]
    c=jnp.concatenate([s[:,:128],s[:,128:]],axis=0)
    lane=lax.broadcasted_iota(jnp.int32,c.shape,1)
    for k in (1,2,4):
        up=pltpu.roll(c,128-k,1); dn=pltpu.roll(c,k,1)
        c=c+jnp.where((lane & k)==0,up,dn)
    return jnp.concatenate([c[:n],c[n:]],axis=1)

def csum(v):
    return jnp.sum(v.reshape(-1,8,v.shape[-1]),axis=0)
def fsum(v8):
    return jnp.sum(v8,axis=0,keepdims=True)

def stats(load, npos, extra):
    p=load(0)[0:1]
    pb=p+extra
    q=gsum(jnp.concatenate([pb,pb],axis=0))[0:1]*0.125
    s1=None
    for r in range(0,256,CH):
        v=load(r)-p
        a=csum(v); b=csum(v*v)
        s1=a if s1 is None else s1+a
        s2=b if r==0 else s2+b
    S1=fsum(s1); S2=fsum(s2)
    d=pb-q
    t1=S1+256.0*d
    t2=S2+2.0*d*S1+256.0*d*d
    g=gsum(jnp.concatenate([t1,t2],axis=0))*(1.0/2048.0)
    dm=g[0:1]
    m=q+dm
    var=g[1:2]-dm*dm
    rs=lax.rsqrt(var+EPS)
    return m,rs
CH=32

def shift3(a, rev):
    R=a.shape[0]
    row=lax.broadcasted_iota(jnp.int32,a.shape,0) & 15
    prev=jnp.where(row==0,0.0,pltpu.roll(a,1,0))
    nxt=jnp.where(row==15,0.0,pltpu.roll(a,R-1,0))
    lo,hi=(nxt,prev) if rev else (prev,nxt)
    return lo.astype(BF),a.astype(BF),hi.astype(BF)

def zero_pads(pref,NB):
    z=jnp.zeros((16,768),BF)
    for n in range(NB):
        pref[n,0:16,:]=z
        pref[n,272:288,:]=z

def put3(pref,n,r,a,rev=False):
    lo,mid,hi=shift3(a,rev)
    R=a.shape[0]
    pref[n,16+r:16+r+R,0:256]=lo
    pref[n,16+r:16+r+R,256:512]=mid
    pref[n,16+r:16+r+R,512:768]=hi
    return mid

def conv3(pref,wref,NB,rev=False):
    acc=None
    for i in range(3):
        o=16*(2-i) if rev else 16*i
        l=pref[:,o:o+256,:].reshape(NB*256,768)
        d=dot(l,wref[768*i:768*i+768,:])
        acc=d if acc is None else acc+d
    return acc

def k1_body(NB, cnt_ref, x_ref, vec_ref, wa_ref, h0_ref, cf_ref, pa):
    i=pl.program_id(0)
    @pl.when(i==0)
    def _(): zero_pads(pa,NB)
    @pl.when(i*NB<cnt_ref[0])
    def _():
        g1=vec_ref[0:1,:]; b1=vec_ref[1:2,:]
        for n in range(NB):
            load=lambda r: x_ref[n,r:r+CH,:].astype(F32)
            m,rs=stats(load,256,0.0)
            sc=0.5*rs*g1; sh=0.5*b1-m*sc
            for r in range(0,256,CH):
                h=load(r)*sc+sh
                a=h+h*jnp.tanh(h)
                put3(pa,n,r,a)
            cf_ref[n]=jnp.concatenate([m,rs,sc,sh,m,rs,sc,sh],axis=0)
        o=conv3(pa,wa_ref,NB)
        h0_ref[...]=o.reshape(NB,256,256)

def k1(cnt,x,vec,wa,NB,n_img=16):
    grid=(n_img//NB,)
    cl=lambda i,c: jnp.minimum(i,(c[0]-1)//NB)
    return pl.pallas_call(
        functools.partial(k1_body,NB),
        grid_spec=pltpu.PrefetchScalarGridSpec(num_scalar_prefetch=1,grid=grid,
            in_specs=[pl.BlockSpec((NB,256,256),lambda i,c:(cl(i,c),0,0)),
                pl.BlockSpec((16,256),lambda i,c:(0,0)),
                pl.BlockSpec((2304,256),lambda i,c:(0,0))],
            out_specs=[pl.BlockSpec((NB,256,256),lambda i,c:(i,0,0)),pl.BlockSpec((NB,8,256),lambda i,c:(i,0,0))],
            scratch_shapes=[pltpu.VMEM((NB,288,768),BF)]),
        out_shape=[jax.ShapeDtypeStruct((n_img,256,256),F32),jax.ShapeDtypeStruct((n_img,8,256),F32)],
        compiler_params=pltpu.CompilerParams(vmem_limit_bytes=60*2**20),
        name="conv_one_forward",
    )(cnt,x,vec,wa)

def k2_body(NB, NS, cnt_ref, x_ref, h0_ref, cot_ref, emb_ref, vec_ref, wt_ref, wb_ref, wbt_ref, wq_ref, wqt_ref, wo_ref, wot_ref,
            out_ref, ga_ref, dm_ref, dwb_ref, dwq_ref, dwo_ref, dvec_ref, dsh_ref,
            pa, pg, at2, mid, a3, mx, attb, dmx, dz, she):
    i=pl.program_id(0)
    cnt=cnt_ref[0]
    @pl.when(i==0)
    def _():
        zero_pads(pa,NB); zero_pads(pg,NB)
        dwb_ref[...]=jnp.zeros_like(dwb_ref); dwq_ref[...]=jnp.zeros_like(dwq_ref); dwo_ref[...]=jnp.zeros_like(dwo_ref)
        dvec_ref[...]=jnp.zeros_like(dvec_ref)
        she[...]=dot(emb_ref[...],wt_ref[...])+(vec_ref[2:3,:]+vec_ref[3:4,:])
    live=i*NB<cnt
    @pl.when(jnp.logical_not(live))
    def _():
        out_ref[...]=jnp.zeros_like(out_ref); ga_ref[...]=jnp.zeros_like(ga_ref); dm_ref[...]=jnp.zeros_like(dm_ref)
        dsh_ref[...]=jnp.zeros_like(dsh_ref)
    @pl.when(live)
    def _():
        V=lambda j: vec_ref[j:j+1,:]
        g2,b2,c2,g3,b3,qb,vb,ob=[V(j) for j in range(4,12)]
        coef=[]
        for n in range(NB):
            br=she[pl.ds(i*NB+n,1),:]
            load=lambda r: h0_ref[n,r:r+CH,:]
            m,rs=stats(load,256,br)
            sc=0.5*rs*g2; sh=0.5*b2+(br-m)*sc
            coef.append((br-m,rs,sc,sh))
            for r in range(0,256,CH):
                h=load(r)*sc+sh
                a=h+h*jnp.tanh(h)
                ab=put3(pa,n,r,a)
            at2[:,n*256:(n+1)*256]=pa[n,16:272,256:512].T
        o=conv3(pa,wb_ref,NB)
        coef3=[]
        for n in range(NB):
            for r in range(0,256,CH):
                mid[n,r:r+CH,:]=o[n*256+r:n*256+r+CH]+(x_ref[n,r:r+CH,:].astype(F32)+c2)
            load=lambda r: mid[n,r:r+CH,:]
            m,rs=stats(load,256,0.0)
            sc=rs*g3; sh=b3-m*sc
            coef3.append((m,rs))
            for r in range(0,256,CH):
                a3[n*256+r:n*256+r+CH,:]=(load(r)*sc+sh).astype(BF)
        bc=jnp.concatenate([qb,jnp.zeros_like(qb),vb],axis=1)
        mx[...]=(dot(a3[...],wq_ref[...])+bc).astype(BF)
        dob=jnp.zeros((8,256),F32); dqb=jnp.zeros((8,256),F32); dvb=jnp.zeros((8,256),F32)
        datts=[]
        for n in range(NB):
            mask=(i*NB+n<cnt).astype(F32)
            lo=n*256
            q=mx[lo:lo+256,0:256]; k=mx[lo:lo+256,256:512]; v=mx[lo:lo+256,512:768]
            st=dot_nt(k,q)*0.0625
            mxx=jnp.max(st,axis=0,keepdims=True)
            e=jnp.exp(st-mxx)
            inv=1.0/jnp.sum(e,axis=0,keepdims=True)
            pt=e*inv
            ptb=pt.astype(BF)
            att=dot_tn(ptb,v).astype(BF)
            attb[lo:lo+256,:]=att
            go=(cot_ref[n].astype(F32)*mask)
            dob=dob+csum(go)
            gob=go.astype(BF)
            out_ref[n]=(mid[n]+(dot(att,wo_ref[...])+ob))*mask
            dwo_ref[...]+=dot_tn(att,gob)
            datt=dot(gob,wot_ref[...]).astype(BF)
            dpt=dot_nt(v,datt)
            dv=dot(ptb,datt)
            t=dpt*pt
            dst=(t-pt*jnp.sum(t,axis=0,keepdims=True)).astype(BF)
            dq=(dot_tn(dst,k)*0.0625).astype(BF)
            dk=(dot(dst,q)*0.0625).astype(BF)
            dvl=dv.astype(BF)
            dmx[lo:lo+256,0:256]=dq
            dmx[lo:lo+256,256:512]=dk
            dmx[lo:lo+256,512:768]=dvl
            dqb=dqb+csum(dq.astype(F32)); dvb=dvb+csum(dvl.astype(F32))
        dwq_ref[...]+=dot_tn(a3[...],dmx[...])
        d3=dot(dmx[...],wqt_ref[...])
        dz[...]=d3
        rows=[]
        dc2=jnp.zeros((8,256),F32); dg3=0.0; db3=0.0
        for n in range(NB):
            mask=(i*NB+n<cnt).astype(F32)
            m,rs=coef3[n]
            A=jnp.zeros((8,256),F32); B=jnp.zeros((8,256),F32)
            for r in range(0,256,CH):
                dy=dz[n*256+r:n*256+r+CH,:]
                A=A+csum(dy); B=B+csum(dy*(mid[n,r:r+CH,:]-m))
            A=fsum(A); B=fsum(B)*rs
            db3=db3+A; dg3=dg3+B
            g=gsum(jnp.concatenate([A*g3,B*g3],axis=0))*(1.0/2048.0)
            al=rs*g3; be=-rs*rs*g[1:2]; ga=-rs*g[0:1]-m*be
            for r in range(0,256,CH):
                dm=cot_ref[n,r:r+CH,:].astype(F32)*mask+(dz[n*256+r:n*256+r+CH,:]*al+(mid[n,r:r+CH,:]*be+ga))
                dm_ref[n,r:r+CH,:]=dm
                dc2=dc2+csum(dm)
                put3(pg,n,r,dm,True)
        at=at2[...]
        for t in range(3):
            l=pg[:,16*(2-t):16*(2-t)+256,:].reshape(NB*256,768)
            dwb_ref[256*t:256*t+256,:]+=dot(at,l)
        o=conv3(pg,wbt_ref,NB,True)
        dg2=0.0; db2=0.0; dsr=[]
        for n in range(NB):
            hm,rs,sc,sh=coef[n]
            A=jnp.zeros((8,256),F32); B=jnp.zeros((8,256),F32)
            for r in range(0,256,CH):
                h0=h0_ref[n,r:r+CH,:]
                h=h0*sc+sh
                t=jnp.tanh(h)
                dzz=o[n*256+r:n*256+r+CH]*((1.0+t)*(1.0+(h-h*t)))
                dz[n*256+r:n*256+r+CH,:]=dzz
                A=A+csum(dzz); B=B+csum(dzz*(h0+hm))
            A=fsum(A)*0.5; B=fsum(B)*(rs*0.5)
            db2=db2+A; dg2=dg2+B
            g=gsum(jnp.concatenate([A*g2,B*g2],axis=0))*(1.0/2048.0)
            al=0.5*rs*g2; be=-rs*rs*g[1:2]; ga=-rs*g[0:1]+hm*be
            ds=jnp.zeros((8,256),F32)
            for r in range(0,256,CH):
                dh=dz[n*256+r:n*256+r+CH,:]*al+(h0_ref[n,r:r+CH,:]*be+ga)
                ga_ref[n,r:r+CH,:]=dh.astype(BF)
                ds=ds+csum(dh)
            dsr.append(fsum(ds))
        for n in range(NB):
            dsh_ref[n]=jnp.concatenate([dsr[n]]*8,axis=0)
        z=jnp.zeros((1,256),F32)
        dvec_ref[...]+=jnp.concatenate([z,z,z,z,dg2,db2,fsum(dc2),dg3,db3,fsum(dqb),fsum(dvb),fsum(dob),z,z,z,z],axis=0)

def k2(cnt,x,h0,cot,emb,vec,wt,wb,wbt,wq,wqt,wo,wot,NB,n_img=16):
    grid=(n_img//NB,)
    cl=lambda i,c: jnp.minimum(i,(c[0]-1)//NB)
    blk=pl.BlockSpec((NB,256,256),lambda i,c:(cl(i,c),0,0))
    oblk=pl.BlockSpec((NB,256,256),lambda i,c:(i,0,0))
    full=lambda s: pl.BlockSpec(s,lambda i,c:(0,)*len(s))
    sd=jax.ShapeDtypeStruct
    return pl.pallas_call(
        functools.partial(k2_body,NB,n_img//NB),
        grid_spec=pltpu.PrefetchScalarGridSpec(num_scalar_prefetch=1,grid=grid,
            in_specs=[blk,blk,blk,full(emb.shape),full((16,256)),full(wt.shape)]+[full(w.shape) for w in (wb,wbt,wq,wqt,wo,wot)],
            out_specs=[oblk,oblk,oblk,full((768,768)),full((256,768)),full((256,256)),full((16,256)),pl.BlockSpec((NB,8,256),lambda i,c:(i,0,0))],
            scratch_shapes=[pltpu.VMEM((NB,288,768),BF),pltpu.VMEM((NB,288,768),BF),pltpu.VMEM((256,NB*256),BF),
                pltpu.VMEM((NB,256,256),F32),pltpu.VMEM((NB*256,256),BF),pltpu.VMEM((NB*256,768),BF),pltpu.VMEM((NB*256,256),BF),
                pltpu.VMEM((NB*256,768),BF),pltpu.VMEM((NB*256,256),F32),pltpu.VMEM((n_img,256),F32)]),
        out_shape=[sd((n_img,256,256),F32),sd((n_img,256,256),BF),sd((n_img,256,256),F32),sd((768,768),F32),sd((256,768),F32),sd((256,256),F32),sd((16,256),F32),sd((n_img,8,256),F32)],
        compiler_params=pltpu.CompilerParams(vmem_limit_bytes=60*2**20),
        name="layer_middle",
    )(cnt,x,h0,cot,emb,vec,wt,wb,wbt,wq,wqt,wo,wot)

def k3_body(NB, cnt_ref, x_ref, ga_ref, dm_ref, cf_ref, vec_ref, wat_ref, ig_ref, dwa_ref, dvec_ref, pg, at1, dz):
    i=pl.program_id(0)
    cnt=cnt_ref[0]
    @pl.when(i==0)
    def _():
        zero_pads(pg,NB)
        dwa_ref[...]=jnp.zeros_like(dwa_ref); dvec_ref[...]=jnp.zeros_like(dvec_ref)
    live=i*NB<cnt
    @pl.when(jnp.logical_not(live))
    def _():
        ig_ref[...]=jnp.zeros_like(ig_ref)
    @pl.when(live)
    def _():
        g1=vec_ref[0:1,:]
        for n in range(NB):
            sc=cf_ref[n,2:3,:]; sh=cf_ref[n,3:4,:]
            tmp=[]
            for r in range(0,256,CH):
                h=x_ref[n,r:r+CH,:].astype(F32)*sc+sh
                tmp.append((h+h*jnp.tanh(h)).astype(BF))
                put3(pg,n,r,ga_ref[n,r:r+CH,:].astype(F32),True)
            at1[:,n*256:(n+1)*256]=jnp.concatenate(tmp,axis=0).T
        at=at1[...]
        for t in range(3):
            l=pg[:,16*(2-t):16*(2-t)+256,:].reshape(NB*256,768)
            dwa_ref[256*t:256*t+256,:]+=dot(at,l)
        o=conv3(pg,wat_ref,NB,True)
        dg=0.0; db=0.0
        for n in range(NB):
            m=cf_ref[n,0:1,:]; rs=cf_ref[n,1:2,:]; sc=cf_ref[n,2:3,:]; sh=cf_ref[n,3:4,:]
            A=jnp.zeros((8,256),F32); B=jnp.zeros((8,256),F32)
            for r in range(0,256,CH):
                x=x_ref[n,r:r+CH,:].astype(F32)
                h=x*sc+sh
                t=jnp.tanh(h)
                dzz=o[n*256+r:n*256+r+CH]*((1.0+t)*(1.0+(h-h*t)))
                dz[n*256+r:n*256+r+CH,:]=dzz
                A=A+csum(dzz); B=B+csum(dzz*(x-m))
            A=fsum(A)*0.5; B=fsum(B)*(rs*0.5)
            db=db+A; dg=dg+B
            g=gsum(jnp.concatenate([A*g1,B*g1],axis=0))*(1.0/2048.0)
            al=0.5*rs*g1; be=-rs*rs*g[1:2]; ga=-rs*g[0:1]-m*be
            for r in range(0,256,CH):
                ig_ref[n,r:r+CH,:]=dm_ref[n,r:r+CH,:]+(dz[n*256+r:n*256+r+CH,:]*al+(x_ref[n,r:r+CH,:].astype(F32)*be+ga))
        z=jnp.zeros((1,256),F32)
        dvec_ref[...]+=jnp.concatenate([dg,db,z,z,z,z,z,z],axis=0)

def k3(cnt,x,ga,dm,cf,vec,wat,NB,n_img=16):
    grid=(n_img//NB,)
    cl=lambda i,c: jnp.minimum(i,(c[0]-1)//NB)
    blk=pl.BlockSpec((NB,256,256),lambda i,c:(cl(i,c),0,0))
    oblk=pl.BlockSpec((NB,256,256),lambda i,c:(i,0,0))
    full=lambda s: pl.BlockSpec(s,lambda i,c:(0,)*len(s))
    sd=jax.ShapeDtypeStruct
    return pl.pallas_call(
        functools.partial(k3_body,NB),
        grid_spec=pltpu.PrefetchScalarGridSpec(num_scalar_prefetch=1,grid=grid,
            in_specs=[blk,blk,blk,pl.BlockSpec((NB,8,256),lambda i,c:(cl(i,c),0,0)),full((16,256)),full(wat.shape)],
            out_specs=[oblk,full((768,768)),full((8,256))],
            scratch_shapes=[pltpu.VMEM((NB,288,768),BF),pltpu.VMEM((256,NB*256),BF),pltpu.VMEM((NB*256,256),F32)]),
        out_shape=[sd((n_img,256,256),F32),sd((768,768),F32),sd((8,256),F32)],
        compiler_params=pltpu.CompilerParams(vmem_limit_bytes=60*2**20),
        name="conv_one_backward",
    )(cnt,x,ga,dm,cf,vec,wat)

STEP = 10
clip_norm = 1.0
beta_first = 0.9
beta_second = 0.999
adam_eps = 1e-08
rates_kind = (0.01, 0.03, 0.02, 0.05, 0.3)
decays_kind = (0.1, 0.1, 0.1, 0.1, 0.0)
E = 512
NB = 2


def sinus_embed(steps_in):
    half_width = E // 2
    frequency = jnp.exp(
        -math.log(10000.0) * jnp.arange(half_width, dtype=jnp.float32) / (half_width - 1)
    )
    angles = steps_in.astype(jnp.float32)[:, None] * frequency[None, :]
    return jnp.concatenate([jnp.sin(angles), jnp.cos(angles)], axis=1)


def gather_flat(masters, dp, fs):
    sizes = [m.size for m in masters]
    total = sum(sizes)
    full = -(-total // 2048) * 2048
    flat = jnp.concatenate([m.reshape(-1).astype(BF) for m in masters] + [jnp.zeros((full - total,), BF)])
    flat = flat.reshape(-1, 128)
    g = lax.all_gather(lax.all_gather(flat, "dp"), "fsdp").reshape(fs, dp, full)
    out = []
    at = 0
    for n in sizes:
        out.append(g[:, :, at : at + n])
        at += n
    conv = out[0].reshape((fs, dp) + masters[0].shape[1:]).transpose(2, 3, 1, 4, 0, 5)
    conv = conv.reshape(2, 9, 256, 256)
    mats = []
    for p, m in zip(out[1:4], masters[1:4]):
        r, c = m.shape[1:]
        mats.append(p.reshape(fs, dp, r, c).transpose(1, 2, 0, 3).reshape(dp * r, fs * c))
    vec = out[4].transpose(1, 0, 2).reshape(12, 256).astype(F32)
    return conv, mats[0], mats[1], mats[2], vec


def reduce_flat(grads, dp, fs):
    conv, embed, attend, output, vec = grads
    pieces = [conv.reshape(18, dp, 256 // dp, fs, 256 // fs).transpose(3, 1, 0, 2, 4).reshape(fs, dp, -1)]
    for g in (embed, attend, output):
        r, c = g.shape
        pieces.append(g.reshape(dp, r // dp, fs, c // fs).transpose(2, 0, 1, 3).reshape(fs, dp, -1))
    pieces.append(vec.reshape(dp, fs, -1).transpose(1, 0, 2))
    sizes = [p.shape[2] for p in pieces]
    total = sum(sizes)
    full = -(-total // 2048) * 2048
    pieces.append(jnp.zeros((fs, dp, full - total), F32))
    flat = jnp.concatenate(pieces, axis=2).reshape(fs, dp, -1, 128)
    part = lax.psum_scatter(flat, "fsdp", scatter_dimension=0, tiled=False)
    part = lax.psum_scatter(part, "dp", scatter_dimension=0, tiled=False).reshape(-1)
    out = []
    at = 0
    for n in sizes:
        out.append(part[at : at + n])
        at += n
    return out


def per_device(images, timesteps, counts, cotangent, *state):
    masters = state[0::3]
    moments = state[1::3]
    squares = state[2::3]
    dp = lax.axis_size("dp")
    fs = lax.axis_size("fsdp")
    n_img = images.shape[0]
    emb = jax.nn.silu(sinus_embed(timesteps)).astype(BF)
    x = images.reshape(n_img, 256, 256)
    cot = cotangent.reshape(n_img, 256, 256)
    conv, wt, wq, wo, vec = gather_flat(masters, dp, fs)
    vp = jnp.pad(vec, ((0, 4), (0, 0)))
    wa = conv[0].reshape(2304, 256)
    wb = conv[1].reshape(2304, 256)
    wat = jnp.swapaxes(conv[0], 1, 2).reshape(2304, 256)
    wbt = jnp.swapaxes(conv[1], 1, 2).reshape(2304, 256)
    h0, cf = k1(counts, x, vp, wa, NB, n_img)
    out, ga, dm, dwb, dwq, dwo, dv, dsh = k2(counts, x, h0, cot, emb, vp, wt, wb, wbt, wq, wq.T, wo, wo.T, NB, n_img)
    ig, dwa, dv1 = k3(counts, x, ga, dm, cf, vp, wat, NB, n_img)
    un = lambda w: w.reshape(3, 256, 3, 256).transpose(0, 2, 1, 3).reshape(9, 256, 256)
    ds = dsh[:, 0]
    demb = dot_tn(emb, ds.astype(BF))
    dst = jnp.sum(ds, axis=0)
    dvec = jnp.concatenate([dv1[:2], dst[None], dst[None], dv[4:12]], axis=0)
    shares = reduce_flat((jnp.stack([un(dwa), un(dwb)]), demb, dwq, dwo, dvec), dp, fs)
    local = sum(jnp.sum(s * s) for s in shares)
    norm = jnp.sqrt(lax.psum(lax.psum(local, "fsdp"), "dp"))
    factor = clip_norm / jnp.maximum(norm, clip_norm)
    results = []
    for kind in range(5):
        clipped = shares[kind].reshape(masters[kind].shape) * factor
        first_new = beta_first * moments[kind] + (1.0 - beta_first) * clipped
        second_new = beta_second * squares[kind] + (1.0 - beta_second) * clipped * clipped
        first_hat = first_new / (1.0 - beta_first**STEP)
        second_hat = second_new / (1.0 - beta_second**STEP)
        update_new = masters[kind] - rates_kind[kind] * (
            first_hat / (jnp.sqrt(second_hat) + adam_eps) + decays_kind[kind] * masters[kind]
        )
        results += [first_new, second_new, update_new]
    return (out.reshape(images.shape), ig.reshape(images.shape), *results, norm)


def solution(mesh):
    both = P(("dp", "fsdp"), None, None, None)
    one = P(("dp", "fsdp"))
    conv = P(None, None, None, "dp", "fsdp")
    mat = P(None, "dp", "fsdp")
    vec = P(None, ("dp", "fsdp"))
    trios = (conv,) * 3 + (mat,) * 9 + (vec,) * 3
    return jax.shard_map(
        per_device,
        mesh=mesh,
        in_specs=(both, one, one, both) + trios,
        out_specs=(both, both) + trios + (P(),),
        check_vma=False,
    )
```

```python
from functools import partial
import math

import functools
import jax, jax.numpy as jnp
from jax import lax
from jax.sharding import PartitionSpec as P
from jax.experimental import pallas as pl
from jax.experimental.pallas import tpu as pltpu

BF=jnp.bfloat16; F32=jnp.float32
EPS=1e-6
def dot(a,b): return lax.dot_general(a,b,(((1,),(0,)),((),())),preferred_element_type=F32)
def dot_nt(a,b): return lax.dot_general(a,b,(((1,),(1,)),((),())),preferred_element_type=F32)
def dot_tn(a,b): return lax.dot_general(a,b,(((0,),(0,)),((),())),preferred_element_type=F32)

def gsum(s):
    n=s.shape[0]
    c=jnp.concatenate([s[:,:128],s[:,128:]],axis=0)
    lane=lax.broadcasted_iota(jnp.int32,c.shape,1)
    for k in (1,2,4):
        up=pltpu.roll(c,128-k,1); dn=pltpu.roll(c,k,1)
        c=c+jnp.where((lane & k)==0,up,dn)
    return jnp.concatenate([c[:n],c[n:]],axis=1)

def csum(v):
    return jnp.sum(v.reshape(-1,8,v.shape[-1]),axis=0)
def fsum(v8):
    return jnp.sum(v8,axis=0,keepdims=True)

def stats(load, npos, extra):
    p=load(0)[0:1]
    pb=p+extra
    q=gsum(jnp.concatenate([pb,pb],axis=0))[0:1]*0.125
    s1=None
    for r in range(0,256,CH):
        v=load(r)-p
        a=csum(v); b=csum(v*v)
        s1=a if s1 is None else s1+a
        s2=b if r==0 else s2+b
    S1=fsum(s1); S2=fsum(s2)
    d=pb-q
    t1=S1+256.0*d
    t2=S2+2.0*d*S1+256.0*d*d
    g=gsum(jnp.concatenate([t1,t2],axis=0))*(1.0/2048.0)
    dm=g[0:1]
    m=q+dm
    var=g[1:2]-dm*dm
    rs=lax.rsqrt(var+EPS)
    return m,rs
CH=32

def shift3(a, rev):
    R=a.shape[0]
    row=lax.broadcasted_iota(jnp.int32,a.shape,0) & 15
    prev=jnp.where(row==0,0.0,pltpu.roll(a,1,0))
    nxt=jnp.where(row==15,0.0,pltpu.roll(a,R-1,0))
    lo,hi=(nxt,prev) if rev else (prev,nxt)
    return lo.astype(BF),a.astype(BF),hi.astype(BF)

def zero_pads(pref,NB):
    z=jnp.zeros((16,768),BF)
    for n in range(NB):
        pref[n,0:16,:]=z
        pref[n,272:288,:]=z

def put3(pref,n,r,a,rev=False):
    lo,mid,hi=shift3(a,rev)
    R=a.shape[0]
    pref[n,16+r:16+r+R,0:256]=lo
    pref[n,16+r:16+r+R,256:512]=mid
    pref[n,16+r:16+r+R,512:768]=hi
    return mid

def conv3(pref,wref,NB,rev=False):
    acc=None
    for i in range(3):
        o=16*(2-i) if rev else 16*i
        l=pref[:,o:o+256,:].reshape(NB*256,768)
        d=dot(l,wref[768*i:768*i+768,:])
        acc=d if acc is None else acc+d
    return acc

def k1_body(NB, cnt_ref, x_ref, vec_ref, wa_ref, h0_ref, cf_ref, pa):
    i=pl.program_id(0)
    @pl.when(i==0)
    def _(): zero_pads(pa,NB)
    @pl.when(i*NB<cnt_ref[0])
    def _():
        g1=vec_ref[0:1,:]; b1=vec_ref[1:2,:]
        for n in range(NB):
            load=lambda r: x_ref[n,r:r+CH,:].astype(F32)
            m,rs=stats(load,256,0.0)
            sc=0.5*rs*g1; sh=0.5*b1-m*sc
            for r in range(0,256,CH):
                h=load(r)*sc+sh
                a=h+h*jnp.tanh(h)
                put3(pa,n,r,a)
            cf_ref[n]=jnp.concatenate([m,rs,sc,sh,m,rs,sc,sh],axis=0)
        o=conv3(pa,wa_ref,NB)
        h0_ref[...]=o.reshape(NB,256,256)

def k1(cnt,x,vec,wa,NB,n_img=16):
    grid=(n_img//NB,)
    cl=lambda i,c: jnp.minimum(i,(c[0]-1)//NB)
    return pl.pallas_call(
        functools.partial(k1_body,NB),
        grid_spec=pltpu.PrefetchScalarGridSpec(num_scalar_prefetch=1,grid=grid,
            in_specs=[pl.BlockSpec((NB,256,256),lambda i,c:(cl(i,c),0,0)),
                pl.BlockSpec((16,256),lambda i,c:(0,0)),
                pl.BlockSpec((2304,256),lambda i,c:(0,0))],
            out_specs=[pl.BlockSpec((NB,256,256),lambda i,c:(i,0,0)),pl.BlockSpec((NB,8,256),lambda i,c:(i,0,0))],
            scratch_shapes=[pltpu.VMEM((NB,288,768),BF)]),
        out_shape=[jax.ShapeDtypeStruct((n_img,256,256),F32),jax.ShapeDtypeStruct((n_img,8,256),F32)],
        compiler_params=pltpu.CompilerParams(vmem_limit_bytes=60*2**20),
        name="conv_one_forward",
    )(cnt,x,vec,wa)

def k2_body(NB, NS, cnt_ref, x_ref, h0_ref, cot_ref, emb_ref, vec_ref, wt_ref, wb_ref, wbt_ref, wq_ref, wqt_ref, wo_ref, wot_ref,
            out_ref, ga_ref, dm_ref, dwb_ref, dwq_ref, dwo_ref, dvec_ref, dsh_ref,
            pa, pg, at2, mid, a3, mx, attb, dmx, dz, she):
    i=pl.program_id(0)
    cnt=cnt_ref[0]
    @pl.when(i==0)
    def _():
        zero_pads(pa,NB); zero_pads(pg,NB)
        dwb_ref[...]=jnp.zeros_like(dwb_ref); dwq_ref[...]=jnp.zeros_like(dwq_ref); dwo_ref[...]=jnp.zeros_like(dwo_ref)
        dvec_ref[...]=jnp.zeros_like(dvec_ref)
        she[...]=dot_nt(emb_ref[...],wt_ref[...])+(vec_ref[2:3,:]+vec_ref[3:4,:])
    live=i*NB<cnt
    @pl.when(jnp.logical_not(live))
    def _():
        out_ref[...]=jnp.zeros_like(out_ref); ga_ref[...]=jnp.zeros_like(ga_ref); dm_ref[...]=jnp.zeros_like(dm_ref)
        dsh_ref[...]=jnp.zeros_like(dsh_ref)
    @pl.when(live)
    def _():
        V=lambda j: vec_ref[j:j+1,:]
        g2,b2,c2,g3,b3,qb,vb,ob=[V(j) for j in range(4,12)]
        coef=[]
        for n in range(NB):
            br=she[pl.ds(i*NB+n,1),:]
            load=lambda r: h0_ref[n,r:r+CH,:]
            m,rs=stats(load,256,br)
            sc=0.5*rs*g2; sh=0.5*b2+(br-m)*sc
            coef.append((br-m,rs,sc,sh))
            for r in range(0,256,CH):
                h=load(r)*sc+sh
                a=h+h*jnp.tanh(h)
                ab=put3(pa,n,r,a)
            at2[:,n*256:(n+1)*256]=pa[n,16:272,256:512].T
        o=conv3(pa,wb_ref,NB)
        coef3=[]
        for n in range(NB):
            for r in range(0,256,CH):
                mid[n,r:r+CH,:]=o[n*256+r:n*256+r+CH]+(x_ref[n,r:r+CH,:].astype(F32)+c2)
            load=lambda r: mid[n,r:r+CH,:]
            m,rs=stats(load,256,0.0)
            sc=rs*g3; sh=b3-m*sc
            coef3.append((m,rs))
            for r in range(0,256,CH):
                a3[n*256+r:n*256+r+CH,:]=(load(r)*sc+sh).astype(BF)
        bc=jnp.concatenate([qb,jnp.zeros_like(qb),vb],axis=1)
        mx[...]=(dot(a3[...],wq_ref[...])+bc).astype(BF)
        dob=jnp.zeros((8,256),F32); dqb=jnp.zeros((8,256),F32); dvb=jnp.zeros((8,256),F32)
        datts=[]
        for n in range(NB):
            mask=(i*NB+n<cnt).astype(F32)
            lo=n*256
            q=mx[lo:lo+256,0:256]; k=mx[lo:lo+256,256:512]; v=mx[lo:lo+256,512:768]
            st=dot_nt(k,q)*0.0625
            mxx=jnp.max(st,axis=0,keepdims=True)
            e=jnp.exp(st-mxx)
            inv=1.0/jnp.sum(e,axis=0,keepdims=True)
            pt=e*inv
            ptb=pt.astype(BF)
            att=dot_tn(ptb,v).astype(BF)
            attb[lo:lo+256,:]=att
            go=(cot_ref[n].astype(F32)*mask)
            dob=dob+csum(go)
            gob=go.astype(BF)
            out_ref[n]=(mid[n]+(dot(att,wo_ref[...])+ob))*mask
            dwo_ref[...]+=dot_tn(att,gob)
            datt=dot(gob,wot_ref[...]).astype(BF)
            dpt=dot_nt(v,datt)
            dv=dot(ptb,datt)
            t=dpt*pt
            dst=(t-pt*jnp.sum(t,axis=0,keepdims=True)).astype(BF)
            dq=(dot_tn(dst,k)*0.0625).astype(BF)
            dk=(dot(dst,q)*0.0625).astype(BF)
            dvl=dv.astype(BF)
            dmx[lo:lo+256,0:256]=dq
            dmx[lo:lo+256,256:512]=dk
            dmx[lo:lo+256,512:768]=dvl
            dqb=dqb+csum(dq.astype(F32)); dvb=dvb+csum(dvl.astype(F32))
        dwq_ref[...]+=dot_tn(a3[...],dmx[...])
        d3=dot(dmx[...],wqt_ref[...])
        dz[...]=d3
        rows=[]
        dc2=jnp.zeros((8,256),F32); dg3=0.0; db3=0.0
        for n in range(NB):
            mask=(i*NB+n<cnt).astype(F32)
            m,rs=coef3[n]
            A=jnp.zeros((8,256),F32); B=jnp.zeros((8,256),F32)
            for r in range(0,256,CH):
                dy=dz[n*256+r:n*256+r+CH,:]
                A=A+csum(dy); B=B+csum(dy*(mid[n,r:r+CH,:]-m))
            A=fsum(A); B=fsum(B)*rs
            db3=db3+A; dg3=dg3+B
            g=gsum(jnp.concatenate([A*g3,B*g3],axis=0))*(1.0/2048.0)
            al=rs*g3; be=-rs*rs*g[1:2]; ga=-rs*g[0:1]-m*be
            for r in range(0,256,CH):
                dm=cot_ref[n,r:r+CH,:].astype(F32)*mask+(dz[n*256+r:n*256+r+CH,:]*al+(mid[n,r:r+CH,:]*be+ga))
                dm_ref[n,r:r+CH,:]=dm
                dc2=dc2+csum(dm)
                put3(pg,n,r,dm,True)
        at=at2[...]
        for t in range(3):
            l=pg[:,16*(2-t):16*(2-t)+256,:].reshape(NB*256,768)
            dwb_ref[256*t:256*t+256,:]+=dot(at,l)
        o=conv3(pg,wbt_ref,NB,True)
        dg2=0.0; db2=0.0; dsr=[]
        for n in range(NB):
            hm,rs,sc,sh=coef[n]
            A=jnp.zeros((8,256),F32); B=jnp.zeros((8,256),F32)
            for r in range(0,256,CH):
                h0=h0_ref[n,r:r+CH,:]
                h=h0*sc+sh
                t=jnp.tanh(h)
                dzz=o[n*256+r:n*256+r+CH]*((1.0+t)*(1.0+(h-h*t)))
                dz[n*256+r:n*256+r+CH,:]=dzz
                A=A+csum(dzz); B=B+csum(dzz*(h0+hm))
            A=fsum(A)*0.5; B=fsum(B)*(rs*0.5)
            db2=db2+A; dg2=dg2+B
            g=gsum(jnp.concatenate([A*g2,B*g2],axis=0))*(1.0/2048.0)
            al=0.5*rs*g2; be=-rs*rs*g[1:2]; ga=-rs*g[0:1]+hm*be
            ds=jnp.zeros((8,256),F32)
            for r in range(0,256,CH):
                dh=dz[n*256+r:n*256+r+CH,:]*al+(h0_ref[n,r:r+CH,:]*be+ga)
                ga_ref[n,r:r+CH,:]=dh.astype(BF)
                ds=ds+csum(dh)
            dsr.append(fsum(ds))
        for n in range(NB):
            dsh_ref[n]=jnp.concatenate([dsr[n]]*8,axis=0)
        z=jnp.zeros((1,256),F32)
        dvec_ref[...]+=jnp.concatenate([z,z,z,z,dg2,db2,fsum(dc2),dg3,db3,fsum(dqb),fsum(dvb),fsum(dob),z,z,z,z],axis=0)

def k2(cnt,x,h0,cot,emb,vec,wt,wb,wbt,wq,wqt,wo,wot,NB,n_img=16):
    grid=(n_img//NB,)
    cl=lambda i,c: jnp.minimum(i,(c[0]-1)//NB)
    blk=pl.BlockSpec((NB,256,256),lambda i,c:(cl(i,c),0,0))
    oblk=pl.BlockSpec((NB,256,256),lambda i,c:(i,0,0))
    full=lambda s: pl.BlockSpec(s,lambda i,c:(0,)*len(s))
    sd=jax.ShapeDtypeStruct
    return pl.pallas_call(
        functools.partial(k2_body,NB,n_img//NB),
        grid_spec=pltpu.PrefetchScalarGridSpec(num_scalar_prefetch=1,grid=grid,
            in_specs=[blk,blk,blk,full(emb.shape),full((16,256)),full(wt.shape)]+[full(w.shape) for w in (wb,wbt,wq,wqt,wo,wot)],
            out_specs=[oblk,oblk,oblk,full((768,768)),full((256,768)),full((256,256)),full((16,256)),pl.BlockSpec((NB,8,256),lambda i,c:(i,0,0))],
            scratch_shapes=[pltpu.VMEM((NB,288,768),BF),pltpu.VMEM((NB,288,768),BF),pltpu.VMEM((256,NB*256),BF),
                pltpu.VMEM((NB,256,256),F32),pltpu.VMEM((NB*256,256),BF),pltpu.VMEM((NB*256,768),BF),pltpu.VMEM((NB*256,256),BF),
                pltpu.VMEM((NB*256,768),BF),pltpu.VMEM((NB*256,256),F32),pltpu.VMEM((n_img,256),F32)]),
        out_shape=[sd((n_img,256,256),F32),sd((n_img,256,256),BF),sd((n_img,256,256),F32),sd((768,768),F32),sd((256,768),F32),sd((256,256),F32),sd((16,256),F32),sd((n_img,8,256),F32)],
        compiler_params=pltpu.CompilerParams(vmem_limit_bytes=60*2**20),
        name="layer_middle",
    )(cnt,x,h0,cot,emb,vec,wt,wb,wbt,wq,wqt,wo,wot)

def k3_body(NB, cnt_ref, x_ref, ga_ref, dm_ref, cf_ref, vec_ref, wat_ref, ig_ref, dwa_ref, dvec_ref, pg, at1, dz):
    i=pl.program_id(0)
    cnt=cnt_ref[0]
    @pl.when(i==0)
    def _():
        zero_pads(pg,NB)
        dwa_ref[...]=jnp.zeros_like(dwa_ref); dvec_ref[...]=jnp.zeros_like(dvec_ref)
    live=i*NB<cnt
    @pl.when(jnp.logical_not(live))
    def _():
        ig_ref[...]=jnp.zeros_like(ig_ref)
    @pl.when(live)
    def _():
        g1=vec_ref[0:1,:]
        for n in range(NB):
            sc=cf_ref[n,2:3,:]; sh=cf_ref[n,3:4,:]
            tmp=[]
            for r in range(0,256,CH):
                h=x_ref[n,r:r+CH,:].astype(F32)*sc+sh
                tmp.append((h+h*jnp.tanh(h)).astype(BF))
                put3(pg,n,r,ga_ref[n,r:r+CH,:].astype(F32),True)
            at1[:,n*256:(n+1)*256]=jnp.concatenate(tmp,axis=0).T
        at=at1[...]
        for t in range(3):
            l=pg[:,16*(2-t):16*(2-t)+256,:].reshape(NB*256,768)
            dwa_ref[256*t:256*t+256,:]+=dot(at,l)
        o=conv3(pg,wat_ref,NB,True)
        dg=0.0; db=0.0
        for n in range(NB):
            m=cf_ref[n,0:1,:]; rs=cf_ref[n,1:2,:]; sc=cf_ref[n,2:3,:]; sh=cf_ref[n,3:4,:]
            A=jnp.zeros((8,256),F32); B=jnp.zeros((8,256),F32)
            for r in range(0,256,CH):
                x=x_ref[n,r:r+CH,:].astype(F32)
                h=x*sc+sh
                t=jnp.tanh(h)
                dzz=o[n*256+r:n*256+r+CH]*((1.0+t)*(1.0+(h-h*t)))
                dz[n*256+r:n*256+r+CH,:]=dzz
                A=A+csum(dzz); B=B+csum(dzz*(x-m))
            A=fsum(A)*0.5; B=fsum(B)*(rs*0.5)
            db=db+A; dg=dg+B
            g=gsum(jnp.concatenate([A*g1,B*g1],axis=0))*(1.0/2048.0)
            al=0.5*rs*g1; be=-rs*rs*g[1:2]; ga=-rs*g[0:1]-m*be
            for r in range(0,256,CH):
                ig_ref[n,r:r+CH,:]=dm_ref[n,r:r+CH,:]+(dz[n*256+r:n*256+r+CH,:]*al+(x_ref[n,r:r+CH,:].astype(F32)*be+ga))
        z=jnp.zeros((1,256),F32)
        dvec_ref[...]+=jnp.concatenate([dg,db,z,z,z,z,z,z],axis=0)

def k3(cnt,x,ga,dm,cf,vec,wat,NB,n_img=16):
    grid=(n_img//NB,)
    cl=lambda i,c: jnp.minimum(i,(c[0]-1)//NB)
    blk=pl.BlockSpec((NB,256,256),lambda i,c:(cl(i,c),0,0))
    oblk=pl.BlockSpec((NB,256,256),lambda i,c:(i,0,0))
    full=lambda s: pl.BlockSpec(s,lambda i,c:(0,)*len(s))
    sd=jax.ShapeDtypeStruct
    return pl.pallas_call(
        functools.partial(k3_body,NB),
        grid_spec=pltpu.PrefetchScalarGridSpec(num_scalar_prefetch=1,grid=grid,
            in_specs=[blk,blk,blk,pl.BlockSpec((NB,8,256),lambda i,c:(cl(i,c),0,0)),full((16,256)),full(wat.shape)],
            out_specs=[oblk,full((768,768)),full((8,256))],
            scratch_shapes=[pltpu.VMEM((NB,288,768),BF),pltpu.VMEM((256,NB*256),BF),pltpu.VMEM((NB*256,256),F32)]),
        out_shape=[sd((n_img,256,256),F32),sd((768,768),F32),sd((8,256),F32)],
        compiler_params=pltpu.CompilerParams(vmem_limit_bytes=60*2**20),
        name="conv_one_backward",
    )(cnt,x,ga,dm,cf,vec,wat)


STEP = 10
clip_norm = 1.0
beta_first = 0.9
beta_second = 0.999
adam_eps = 1e-08
rates_kind = (0.01, 0.03, 0.02, 0.05, 0.3)
decays_kind = (0.1, 0.1, 0.1, 0.1, 0.0)
E = 512
NB = 2
AXES = ("dp", "fsdp")
VMEM = pltpu.CompilerParams(vmem_limit_bytes=60 * 2**20)
RA = 160
RB = 240
GB = 208
GA = 192


def sinus_embed(steps_in):
    half_width = E // 2
    frequency = jnp.exp(
        -math.log(10000.0) * jnp.arange(half_width, dtype=jnp.float32) / (half_width - 1)
    )
    angles = steps_in.astype(jnp.float32)[:, None] * frequency[None, :]
    return jnp.concatenate([jnp.sin(angles), jnp.cos(angles)], axis=1)


def halves(s0, s1):
    first = jnp.concatenate([s0[:, :64], s1[:, :64]], axis=1)
    second = jnp.concatenate([s0[:, 64:], s1[:, 64:]], axis=1)
    return first, second


def pack_body(conv, embed, attend, output, vec, a_ref, b_ref):
    for side, ref, base in ((0, a_ref, 0), (1, b_ref, 32)):
        for k in range(9):
            w = conv[9 * side + k]
            ref[base + 16 * k : base + 16 * k + 16, :] = jnp.concatenate([w[:16], w[16:]], axis=1).astype(BF)
    row = jnp.concatenate([vec[...], jnp.zeros((1, 32), F32)], axis=1)
    a_ref[144:160, :] = jnp.broadcast_to(row, (16, 128)).astype(BF)
    b_ref[0:32, :] = embed[...].astype(BF)
    at = jnp.concatenate([attend[...], jnp.zeros((64, 32), F32)], axis=1).T
    b_ref[176:224, :] = jnp.concatenate([at[:48], at[48:96]], axis=1).astype(BF)
    o = output[...]
    b_ref[224:240, :] = jnp.concatenate([o[:16], o[16:]], axis=1).astype(BF)


def pack(trans):
    return pl.pallas_call(
        pack_body,
        out_shape=[jax.ShapeDtypeStruct((RA, 128), BF), jax.ShapeDtypeStruct((RB, 128), BF)],
        compiler_params=VMEM,
        name="pack_shards",
    )(*trans)


def swap(x, bits):
    return lax.ppermute(x, AXES, [(i, i ^ bits) for i in range(32)])


def spread(s):
    line = jnp.stack([s, swap(s, 8), swap(s, 16), swap(s, 24)])
    plane = [line, swap(line, 2), swap(line, 4), swap(line, 6)]
    out = []
    for p in plane:
        out += [p, swap(p, 1)]
    return out


def pairs(g, z, lo, rows, h):
    s0 = g[z ^ (2 * h), lo : lo + rows, :]
    s1 = g[z ^ (2 * h + 1), lo : lo + rows, :]
    return halves(s0, s1)


def unpack_a_body(me, *refs):
    gs = refs[:8]
    wt_ref, w_ref, vec_ref, vrows = refs[8:]
    z = me[0]
    f = me[1]
    for rf in range(8):
        d0 = (f ^ rf) * 32
        for h in range(2):
            for k in range(9):
                j0, j1 = pairs(gs[rf], z, 16 * k, 16, h)
                at = pl.multiple_of(256 * k + d0, 32)
                wt_ref[pl.ds(at, 16), 128 * h : 128 * h + 128] = j0
                wt_ref[pl.ds(at + 16, 16), 128 * h : 128 * h + 128] = j1
        for rz in range(4):
            vrows[pl.ds((z ^ rz) * 8 + (f ^ rf), 1), :] = gs[rf][rz, 144:160, :].astype(F32)[0:1]
    for k in range(9):
        w_ref[256 * k : 256 * k + 256, :] = wt_ref[256 * k : 256 * k + 256, :].T
    v = vrows[...]
    v3 = jnp.concatenate([v, pltpu.roll(v, 96, 1), pltpu.roll(v, 64, 1)], axis=0).astype(BF)
    col = lax.broadcasted_iota(jnp.int32, (16, 96), 1)
    row = lax.broadcasted_iota(jnp.int32, (16, 96), 0)
    unit = 3 * (col & 31) + (col >> 5)
    lane = lax.broadcasted_iota(jnp.int32, (16, 128), 1)
    for half in range(2):
        acc = jnp.zeros((16, 128), F32)
        for t in range(4):
            sel = jnp.where(unit == 8 * row + 4 * half + t, 1.0, 0.0).astype(BF)
            piece = dot(sel, v3)
            if t:
                piece = pltpu.roll(piece, 32 * t, 1)
            acc = jnp.where((lane >> 5) == t, piece, acc)
        vec_ref[:, 128 * half : 128 * half + 128] = acc


def unpack_a(me, gs):
    sd = jax.ShapeDtypeStruct
    vm = pl.BlockSpec(memory_space=pltpu.VMEM)
    return pl.pallas_call(
        unpack_a_body,
        in_specs=[pl.BlockSpec(memory_space=pltpu.SMEM)] + [vm] * 8,
        out_specs=[vm] * 3,
        out_shape=[sd((2304, 256), BF), sd((2304, 256), BF), sd((16, 256), F32)],
        scratch_shapes=[pltpu.VMEM((32, 128), F32)],
        compiler_params=VMEM,
        name="unpack_first",
    )(me, *gs)


def unpack_b_body(me, *refs):
    gs = refs[:8]
    wet_ref, wbt_ref, wb_ref, wqt_ref, wq_ref, wot_ref, wo_ref = refs[8:]
    z = me[0]
    f = me[1]
    for rf in range(8):
        own = f ^ rf
        d0 = own * 32
        q0 = own * 96
        g = gs[rf]
        for dpi in range(4):
            wet_ref[pl.ds(pl.multiple_of(d0, 32), 32), 128 * dpi : 128 * dpi + 128] = g[z ^ dpi, 0:32, :]
        for h in range(2):
            lanes = slice(128 * h, 128 * h + 128)
            for k in range(9):
                j0, j1 = pairs(g, z, 32 + 16 * k, 16, h)
                at = pl.multiple_of(256 * k + d0, 32)
                wbt_ref[pl.ds(at, 16), lanes] = j0
                wbt_ref[pl.ds(at + 16, 16), lanes] = j1
            j0, j1 = pairs(g, z, 176, 48, h)
            at = pl.multiple_of(q0, 32)
            wqt_ref[pl.ds(at, 48), lanes] = j0
            wqt_ref[pl.ds(at + 48, 48), lanes] = j1
            j0, j1 = pairs(g, z, 224, 16, h)
            at = pl.multiple_of(d0, 32)
            wot_ref[pl.ds(at, 16), lanes] = j0
            wot_ref[pl.ds(at + 16, 16), lanes] = j1
    for k in range(9):
        wb_ref[256 * k : 256 * k + 256, :] = wbt_ref[256 * k : 256 * k + 256, :].T
    for k in range(3):
        wq_ref[:, 256 * k : 256 * k + 256] = wqt_ref[256 * k : 256 * k + 256, :].T
    wo_ref[...] = wot_ref[...].T


def unpack_b(me, gs):
    sd = jax.ShapeDtypeStruct
    vm = pl.BlockSpec(memory_space=pltpu.VMEM)
    return pl.pallas_call(
        unpack_b_body,
        in_specs=[pl.BlockSpec(memory_space=pltpu.SMEM)] + [vm] * 8,
        out_specs=[vm] * 7,
        out_shape=[
            sd((256, 512), BF),
            sd((2304, 256), BF),
            sd((2304, 256), BF),
            sd((768, 256), BF),
            sd((256, 768), BF),
            sd((256, 256), BF),
            sd((256, 256), BF),
        ],
        compiler_params=VMEM,
        name="unpack_second",
    )(me, *gs)


def place(outs, me, turned, base, lo, rows, step):
    z = me[0]
    f = me[1]
    for rf in range(8):
        at = pl.multiple_of(base + (f ^ rf) * step, 32)
        for h in range(2):
            lanes = slice(128 * h, 128 * h + 128)
            s0 = turned[pl.ds(at, rows), lanes]
            s1 = turned[pl.ds(at + rows, rows), lanes]
            e0, e1 = halves(s0, s1)
            ref = outs[rf & 1]
            ref[rf >> 1, z ^ (2 * h), lo : lo + rows, :] = e0
            ref[rf >> 1, z ^ (2 * h + 1), lo : lo + rows, :] = e1


def grads_b_body(me, dwb, dwq, dwo, keep, send, turn):
    outs = (keep, send)
    for k in range(9):
        block = dwb[256 * (k // 3) : 256 * (k // 3) + 256, 256 * (k % 3) : 256 * (k % 3) + 256]
        turn[256 * k : 256 * k + 256, :] = block.astype(BF).T
        place(outs, me, turn, 256 * k, 16 * k, 16, 32)
    for k in range(3):
        turn[2304 + 256 * k : 2560 + 256 * k, :] = dwq[:, 256 * k : 256 * k + 256].astype(BF).T
    place(outs, me, turn, 2304, 144, 48, 96)
    turn[3072:3328, :] = dwo[...].astype(BF).T
    place(outs, me, turn, 3072, 192, 16, 32)


def grads_b(me, dwb, dwq, dwo):
    sd = jax.ShapeDtypeStruct
    vm = pl.BlockSpec(memory_space=pltpu.VMEM)
    return pl.pallas_call(
        grads_b_body,
        in_specs=[pl.BlockSpec(memory_space=pltpu.SMEM)] + [vm] * 3,
        out_specs=[vm] * 2,
        out_shape=[sd((4, 4, GB, 128), BF)] * 2,
        scratch_shapes=[pltpu.VMEM((3328, 256), BF)],
        compiler_params=VMEM,
        name="pack_grads_first",
    )(me, dwb, dwq, dwo)


def grads_a_body(me, dwa, emb, dsh, dva, dvb, keep, send, turn, wide):
    outs = (keep, send)
    z = me[0]
    f = me[1]
    for k in range(9):
        block = dwa[256 * (k // 3) : 256 * (k // 3) + 256, 256 * (k % 3) : 256 * (k % 3) + 256]
        turn[256 * k : 256 * k + 256, :] = block.astype(BF).T
        place(outs, me, turn, 256 * k, 16 * k, 16, 32)
    ds = dsh[:, 0, :]
    total = jnp.sum(ds, axis=0, keepdims=True)
    wide[...] = dot_tn(ds.astype(BF), emb[...]).astype(BF)
    for dpi in range(4):
        for rf in range(8):
            at = pl.multiple_of((f ^ rf) * 32, 32)
            outs[rf & 1][rf >> 1, z ^ dpi, 144:176, :] = wide[pl.ds(at, 32), 128 * dpi : 128 * dpi + 128]
    rows = jnp.concatenate([dva[0:2, :], total, total, dvb[4:16, :]], axis=0)
    a8 = []
    for s in range(8):
        piece = rows[:, 128 * (s // 4) : 128 * (s // 4) + 128]
        a8.append(pltpu.roll(piece, 128 - 32 * (s % 4), 1) if s % 4 else piece)
    a8 = jnp.concatenate(a8, axis=0).astype(BF)
    col = lax.broadcasted_iota(jnp.int32, (32, 128), 1)
    row = lax.broadcasted_iota(jnp.int32, (32, 128), 0)
    owner = ((row & 3) ^ z) * 8 + ((row >> 2) ^ f)
    lane = lax.broadcasted_iota(jnp.int32, (32, 128), 1)
    acc = jnp.zeros((32, 128), F32)
    unit = 8 * (col & 15) + (col >> 4)
    for u in range(3):
        sel = jnp.where(unit == 3 * owner + u, 1.0, 0.0).astype(BF)
        piece = dot(sel, a8)
        if u:
            piece = pltpu.roll(piece, 32 * u, 1)
        acc = jnp.where((lane >> 5) == u, piece, acc)
    for rf in range(8):
        for rz in range(4):
            r = 4 * rf + rz
            outs[rf & 1][rf >> 1, rz, 176:192, :] = jnp.broadcast_to(acc[r : r + 1], (16, 128)).astype(BF)


def grads_a(me, dwa, emb, dsh, dva, dvb):
    sd = jax.ShapeDtypeStruct
    vm = pl.BlockSpec(memory_space=pltpu.VMEM)
    return pl.pallas_call(
        grads_a_body,
        in_specs=[pl.BlockSpec(memory_space=pltpu.SMEM)] + [vm] * 5,
        out_specs=[vm] * 2,
        out_shape=[sd((4, 4, GA, 128), BF)] * 2,
        scratch_shapes=[pltpu.VMEM((2304, 256), BF), pltpu.VMEM((256, 512), BF)],
        compiler_params=VMEM,
        name="pack_grads_second",
    )(me, dwa, emb, dsh, dva, dvb)


def collect(keep, send):
    got = swap(send, 1)
    parts = [(keep[j].astype(F32) + got[j].astype(F32)).astype(BF) for j in range(4)]
    got = [swap(parts[1], 2), swap(parts[2], 4), swap(parts[3], 6)]
    line = [sum((g[rz].astype(F32) for g in got), parts[0][rz].astype(F32)) for rz in range(4)]
    got = [swap(line[rz].astype(BF), 8 * rz) for rz in range(1, 4)]
    return sum((g.astype(F32) for g in got), line[0])


def total_over(s):
    s = s + swap(s, 1)
    s = (s + swap(s, 2)) + (swap(s, 4) + swap(s, 6))
    return (s + swap(s, 8)) + (swap(s, 16) + swap(s, 24))


def square_body(gb, ga, out):
    row = lax.broadcasted_iota(jnp.int32, (16, 128), 0)
    v = jnp.where(row == 0, ga[176:192, :], 0.0)
    t = csum2(gb[...] * gb[...]) + csum2(ga[0:176, :] * ga[0:176, :]) + csum2(v * v)
    t = jnp.sum(t, axis=0, keepdims=True)
    out[...] = jnp.broadcast_to(jnp.sum(t, axis=1, keepdims=True), (8, 128))


def csum2(v):
    return jnp.sum(v.reshape(-1, 8, 128), axis=0)


def squares_of(gb, ga):
    return pl.pallas_call(
        square_body, out_shape=jax.ShapeDtypeStruct((8, 128), F32), compiler_params=VMEM, name="squares"
    )(gb, ga)


def adam_body(*refs):
    total, gb, ga = refs[:3]
    state = refs[3:18]
    outs = refs[18:]
    norm = jnp.sqrt(total[0:1, 0:1])
    factor = clip_norm / jnp.maximum(norm, clip_norm)

    def put(kind, at, grad):
        clipped = grad * factor
        mas, mom, squ = (r[at] for r in state[3 * kind : 3 * kind + 3])
        first_new = beta_first * mom + (1.0 - beta_first) * clipped
        second_new = beta_second * squ + (1.0 - beta_second) * clipped * clipped
        first_hat = first_new / (1.0 - beta_first**STEP)
        second_hat = second_new / (1.0 - beta_second**STEP)
        update = mas - rates_kind[kind] * (
            first_hat / (jnp.sqrt(second_hat) + adam_eps) + decays_kind[kind] * mas
        )
        outs[3 * kind][at] = first_new
        outs[3 * kind + 1][at] = second_new
        outs[3 * kind + 2][at] = update

    for side, ref in ((0, ga), (1, gb)):
        for k in range(9):
            g = ref[16 * k : 16 * k + 16, :]
            put(0, (9 * side + k,), jnp.concatenate([g[:, :64], g[:, 64:]], axis=0))
    put(1, (Ellipsis,), ga[144:176, :])
    g = gb[144:192, :]
    g = jnp.concatenate([jnp.concatenate([g[:, :64], g[:, 64:]], axis=0), jnp.zeros((96, 64), F32)], axis=1)
    g = jnp.concatenate([g, jnp.zeros((32, 128), F32)], axis=0).T
    put(2, (Ellipsis,), g[:64, :96])
    g = gb[192:208, :]
    put(3, (Ellipsis,), jnp.concatenate([g[:, :64], g[:, 64:]], axis=0))
    put(4, (Ellipsis,), ga[176:177, :96])
    outs[15][...] = jnp.broadcast_to(norm, (8, 128))


def adam(total, gb, ga, state):
    sd = jax.ShapeDtypeStruct
    return pl.pallas_call(
        adam_body,
        out_shape=[sd(s.shape, F32) for s in state] + [sd((8, 128), F32)],
        compiler_params=VMEM,
        name="clipped_adamw",
    )(total, gb, ga, *state)


def turned_state(state):
    out = []
    for kind in range(5):
        for a in state[3 * kind : 3 * kind + 3]:
            if kind == 0:
                a = jnp.swapaxes(a, 3, 4).reshape(18, 32, 64)
            elif kind == 2:
                a = a[0]
            elif kind < 4:
                a = jnp.swapaxes(a, 1, 2)[0]
            out.append(a)
    return out


def turned_back(results):
    out = []
    for kind in range(5):
        for a in results[3 * kind : 3 * kind + 3]:
            if kind == 0:
                a = jnp.swapaxes(a.reshape(1, 2, 9, 32, 64), 3, 4)
            elif kind == 2:
                a = a[None]
            elif kind < 4:
                a = jnp.swapaxes(a[None], 1, 2)
            out.append(a)
    return out


def per_device_here(images, timesteps, counts, cotangent, *state):
    n_img = images.shape[0]
    state = turned_state(state)
    me = jnp.stack([lax.axis_index("dp"), lax.axis_index("fsdp")]).astype(jnp.int32)
    sa, sb = pack(state[0::3])
    ga = spread(sa)
    gb = spread(sb)
    emb = jax.nn.silu(sinus_embed(timesteps)).astype(BF)
    x = images.reshape(n_img, 256, 256)
    cot = cotangent.reshape(n_img, 256, 256)
    wat, wa, vp = unpack_a(me, ga)
    h0, cf = k1(counts, x, vp, wa, NB, n_img)
    wet, wbt, wb, wqt, wq, wot, wo = unpack_b(me, gb)
    out, gh, dm, dwb, dwq, dwo, dvb, dsh = k2(counts, x, h0, cot, emb, vp, wet, wb, wbt, wq, wqt, wo, wot, NB, n_img)
    share_b = collect(*grads_b(me, dwb, dwq, dwo))
    ig, dwa, dva = k3(counts, x, gh, dm, cf, vp, wat, NB, n_img)
    share_a = collect(*grads_a(me, dwa, emb, dsh, dva, dvb))
    total = total_over(squares_of(share_b, share_a))
    results = adam(total, share_b, share_a, state)
    return (out.reshape(images.shape), ig.reshape(images.shape), *turned_back(results[:15]), results[15][0, 0])


def gather_flat(masters, dp, fs):
    sizes = [m.size for m in masters]
    total = sum(sizes)
    full = -(-total // 2048) * 2048
    flat = jnp.concatenate([m.reshape(-1).astype(BF) for m in masters] + [jnp.zeros((full - total,), BF)])
    flat = flat.reshape(-1, 128)
    g = lax.all_gather(lax.all_gather(flat, "dp"), "fsdp").reshape(fs, dp, full)
    out = []
    at = 0
    for n in sizes:
        out.append(g[:, :, at : at + n])
        at += n
    conv = out[0].reshape((fs, dp) + masters[0].shape[1:]).transpose(2, 3, 1, 4, 0, 5)
    conv = conv.reshape(2, 9, 256, 256)
    mats = []
    for p, m in zip(out[1:4], masters[1:4]):
        r, c = m.shape[1:]
        mats.append(p.reshape(fs, dp, r, c).transpose(1, 2, 0, 3).reshape(dp * r, fs * c))
    vec = out[4].transpose(1, 0, 2).reshape(12, 256).astype(F32)
    return conv, mats[0], mats[1], mats[2], vec


def reduce_flat(grads, dp, fs):
    conv, embed, attend, output, vec = grads
    pieces = [conv.reshape(18, dp, 256 // dp, fs, 256 // fs).transpose(3, 1, 0, 2, 4).reshape(fs, dp, -1)]
    for g in (embed, attend, output):
        r, c = g.shape
        pieces.append(g.reshape(dp, r // dp, fs, c // fs).transpose(2, 0, 1, 3).reshape(fs, dp, -1))
    pieces.append(vec.reshape(dp, fs, -1).transpose(1, 0, 2))
    sizes = [p.shape[2] for p in pieces]
    total = sum(sizes)
    full = -(-total // 2048) * 2048
    pieces.append(jnp.zeros((fs, dp, full - total), F32))
    flat = jnp.concatenate(pieces, axis=2).reshape(fs, dp, -1, 128)
    part = lax.psum_scatter(flat, "fsdp", scatter_dimension=0, tiled=False)
    part = lax.psum_scatter(part, "dp", scatter_dimension=0, tiled=False).reshape(-1)
    out = []
    at = 0
    for n in sizes:
        out.append(part[at : at + n])
        at += n
    return out


def per_device_any(images, timesteps, counts, cotangent, *state):
    masters = state[0::3]
    moments = state[1::3]
    squares = state[2::3]
    dp = lax.axis_size("dp")
    fs = lax.axis_size("fsdp")
    n_img = images.shape[0]
    emb = jax.nn.silu(sinus_embed(timesteps)).astype(BF)
    x = images.reshape(n_img, 256, 256)
    cot = cotangent.reshape(n_img, 256, 256)
    conv, wt, wq, wo, vec = gather_flat(masters, dp, fs)
    vp = jnp.pad(vec, ((0, 4), (0, 0)))
    wa = conv[0].reshape(2304, 256)
    wb = conv[1].reshape(2304, 256)
    wat = jnp.swapaxes(conv[0], 1, 2).reshape(2304, 256)
    wbt = jnp.swapaxes(conv[1], 1, 2).reshape(2304, 256)
    h0, cf = k1(counts, x, vp, wa, NB, n_img)
    out, ga, dm, dwb, dwq, dwo, dv, dsh = k2(counts, x, h0, cot, emb, vp, wt.T, wb, wbt, wq, wq.T, wo, wo.T, NB, n_img)
    ig, dwa, dv1 = k3(counts, x, ga, dm, cf, vp, wat, NB, n_img)
    un = lambda w: w.reshape(3, 256, 3, 256).transpose(0, 2, 1, 3).reshape(9, 256, 256)
    ds = dsh[:, 0]
    demb = dot_tn(emb, ds.astype(BF))
    dst = jnp.sum(ds, axis=0)
    dvec = jnp.concatenate([dv1[:2], dst[None], dst[None], dv[4:12]], axis=0)
    shares = reduce_flat((jnp.stack([un(dwa), un(dwb)]), demb, dwq, dwo, dvec), dp, fs)
    local = sum(jnp.sum(s * s) for s in shares)
    norm = jnp.sqrt(lax.psum(lax.psum(local, "fsdp"), "dp"))
    factor = clip_norm / jnp.maximum(norm, clip_norm)
    results = []
    for kind in range(5):
        clipped = shares[kind].reshape(masters[kind].shape) * factor
        first_new = beta_first * moments[kind] + (1.0 - beta_first) * clipped
        second_new = beta_second * squares[kind] + (1.0 - beta_second) * clipped * clipped
        first_hat = first_new / (1.0 - beta_first**STEP)
        second_hat = second_new / (1.0 - beta_second**STEP)
        update_new = masters[kind] - rates_kind[kind] * (
            first_hat / (jnp.sqrt(second_hat) + adam_eps) + decays_kind[kind] * masters[kind]
        )
        results += [first_new, second_new, update_new]
    return (out.reshape(images.shape), ig.reshape(images.shape), *results, norm)


def solution(mesh):
    both = P(("dp", "fsdp"), None, None, None)
    one = P(("dp", "fsdp"))
    conv = P(None, None, None, "dp", "fsdp")
    mat = P(None, "dp", "fsdp")
    vec = P(None, ("dp", "fsdp"))
    trios = (conv,) * 3 + (mat,) * 9 + (vec,) * 3
    here = mesh.shape["dp"] == 4 and mesh.shape["fsdp"] == 8
    return jax.shard_map(
        per_device_here if here else per_device_any,
        mesh=mesh,
        in_specs=(both, one, one, both) + trios,
        out_specs=(both, both) + trios + (P(),),
        check_vma=False,
    )
```

```python
import math

import jax
import jax.numpy as jnp
from jax import lax
from jax.experimental import pallas as pl
from jax.experimental.pallas import tpu as pltpu
from jax.sharding import PartitionSpec as P

BF = jnp.bfloat16
F32 = jnp.float32
EPS = 1e-6
E = 512
STEP = 10
clip_norm = 1.0
beta_first = 0.9
beta_second = 0.999
adam_eps = 1e-08
rates_kind = (0.01, 0.03, 0.02, 0.05, 0.3)
decays_kind = (0.1, 0.1, 0.1, 0.1, 0.0)
AXES = ("dp", "fsdp")
VMEM = pltpu.CompilerParams(vmem_limit_bytes=60 * 2**20)
NB = 4
HB = 2
CH = 32
R = range(0, 256, CH)
RA = 160
RB = 240
GB = 256
GA = 144

sd = jax.ShapeDtypeStruct


def dot(a, b):
    return lax.dot_general(a, b, (((1,), (0,)), ((), ())), preferred_element_type=F32)


def dot_nt(a, b):
    return lax.dot_general(a, b, (((1,), (1,)), ((), ())), preferred_element_type=F32)


def dot_tn(a, b):
    return lax.dot_general(a, b, (((0,), (0,)), ((), ())), preferred_element_type=F32)


def gsum(s):
    n = s.shape[0]
    c = jnp.concatenate([s[:, :128], s[:, 128:]], axis=0)
    lane = lax.broadcasted_iota(jnp.int32, c.shape, 1)
    for k in (1, 2, 4):
        up = pltpu.roll(c, 128 - k, 1)
        down = pltpu.roll(c, k, 1)
        c = c + jnp.where((lane & k) == 0, up, down)
    return jnp.concatenate([c[:n], c[n:]], axis=1)


def csum(v):
    return jnp.sum(v.reshape(-1, 8, v.shape[-1]), axis=0)


def fsum(v):
    return jnp.sum(v, axis=0, keepdims=True)


def row_sums(load, base):
    s1 = s2 = None
    for r in R:
        v = load(r) - base
        a = csum(v)
        b = csum(v * v)
        s1 = a if s1 is None else s1 + a
        s2 = b if s2 is None else s2 + b
    return fsum(s1), fsum(s2)


def stats(loads, extras=None):
    firsts = [load(0)[0:1] for load in loads]
    p = jnp.concatenate(firsts, axis=0)
    if extras is not None:
        p = p + jnp.concatenate(extras, axis=0)
    q = gsum(p) * 0.125
    sums = [row_sums(load, first) for load, first in zip(loads, firsts)]
    s1 = jnp.concatenate([t[0] for t in sums], axis=0)
    s2 = jnp.concatenate([t[1] for t in sums], axis=0)
    d = p - q
    g = gsum(jnp.concatenate([s1 + 256.0 * d, s2 + d * (2.0 * s1 + 256.0 * d)], axis=0)) * (1.0 / 2048.0)
    n = len(loads)
    dm = g[:n]
    return q + dm, lax.rsqrt(g[n:] - dm * dm + EPS)


def back_coefs(sum_dy, sum_dyn, gain, rs, m):
    n = sum_dy.shape[0]
    g = gsum(jnp.concatenate([sum_dy * gain, sum_dyn * gain], axis=0)) * (1.0 / 2048.0)
    be = -rs * rs * g[n:]
    return rs * gain, be, -rs * g[:n] - m * be


def put3(pref, n, r, a, rev=False):
    rows = a.shape[0]
    col = lax.broadcasted_iota(jnp.int32, a.shape, 0) & 15
    prev = jnp.where(col == 0, 0.0, pltpu.roll(a, 1, 0))
    post = jnp.where(col == 15, 0.0, pltpu.roll(a, rows - 1, 0))
    lo, hi = (post, prev) if rev else (prev, post)
    pref[n, 16 + r : 16 + r + rows, 0:256] = lo.astype(BF)
    pref[n, 16 + r : 16 + r + rows, 256:512] = a.astype(BF)
    pref[n, 16 + r : 16 + r + rows, 512:768] = hi.astype(BF)


def zero_pads(pref):
    z = jnp.zeros((16, 768), BF)
    for n in range(NB):
        pref[n, 0:16, :] = z
        pref[n, 272:288, :] = z


def conv_forward(pref, wt_ref, N):
    acc = None
    for i in range(3):
        for j in range(3):
            rows = pref[N.start : N.stop, 16 * i : 16 * i + 256, 256 * j : 256 * j + 256]
            k = 3 * i + j
            d = dot_nt(rows.reshape(len(N) * 256, 256), wt_ref[256 * k : 256 * k + 256, :])
            acc = d if acc is None else acc + d
    return acc


def conv_turned(pref, wt_ref, N):
    acc = None
    for i in range(3):
        o = 16 * (2 - i)
        rows = pref[N.start : N.stop, o : o + 256, :].reshape(len(N) * 256, 768)
        d = dot(rows, wt_ref[768 * i : 768 * i + 768, :])
        acc = d if acc is None else acc + d
    return acc


def add_taps(acc_ref, gt, pref, N):
    for i in range(3):
        rows = pref[N.start : N.stop, 16 * i : 16 * i + 256, :].reshape(len(N) * 256, 768)
        acc_ref[256 * i : 256 * i + 256, :] += dot(gt, rows)


def interleave(gens):
    gens = list(gens)
    done = [False] * len(gens)
    at = 0
    while not all(done):
        for j, g in enumerate(gens):
            if not done[j] and at >= j:
                try:
                    next(g)
                except StopIteration:
                    done[j] = True
        at += 1


def parts():
    return [range(j, j + HB) for j in range(0, NB, HB)]


def row(ref, j):
    return ref[j : j + 1, :]


def whole(shape):
    return pl.BlockSpec(shape, lambda i, c: (0,) * len(shape))


def clamped(i, c):
    return jnp.minimum(i, (c[0] - 1) // NB)


def blocks(*tail):
    return pl.BlockSpec((NB,) + tail, lambda i, c: (clamped(i, c),) + (0,) * len(tail))


def out_blocks(*tail):
    return pl.BlockSpec((NB,) + tail, lambda i, c: (i,) + (0,) * len(tail))


def image_call(body, name, n_img, cost, in_specs, out_specs, out_shape, scratch, args):
    products, passes = cost
    return pl.pallas_call(
        body,
        grid_spec=pltpu.PrefetchScalarGridSpec(
            num_scalar_prefetch=1,
            grid=(n_img // NB,),
            in_specs=in_specs,
            out_specs=out_specs,
            scratch_shapes=scratch,
        ),
        out_shape=out_shape,
        cost_estimate=pl.CostEstimate(
            flops=n_img * products * 2 * 256**3,
            transcendentals=n_img * passes * 256**2,
            bytes_accessed=n_img * passes * 4 * 256**2,
        ),
        compiler_params=VMEM,
        name=name,
    )(*args)


def figures_body(cnt_ref, x_ref, cf_ref):
    @pl.when(pl.program_id(0) * NB < cnt_ref[0])
    def _():
        m, rs = stats([lambda r, n=n: x_ref[n, r : r + CH, :].astype(F32) for n in range(NB)])
        for n in range(NB):
            cf_ref[n] = jnp.concatenate([m[n : n + 1], rs[n : n + 1], jnp.zeros((6, 256), F32)], axis=0)


def figures(cnt, x):
    n = x.shape[0]
    return image_call(
        figures_body, "figures", n, (1, 2), [blocks(256, 256)], out_blocks(8, 256), sd((n, 8, 256), F32), [], (cnt, x)
    )


def conv_one_body(cnt_ref, x_ref, cf_ref, vec_ref, wat_ref, h0_ref, pa_ref):
    zero_pads(pa_ref)

    @pl.when(pl.program_id(0) * NB < cnt_ref[0])
    def _():
        def part(N):
            for n in N:
                sc = 0.5 * cf_ref[n, 1:2, :] * row(vec_ref, 0)
                sh = 0.5 * row(vec_ref, 1) - cf_ref[n, 0:1, :] * sc
                for r in R:
                    h = x_ref[n, r : r + CH, :].astype(F32) * sc + sh
                    put3(pa_ref, n, r, h + h * jnp.tanh(h))
            yield
            h0_ref[N.start : N.stop] = conv_forward(pa_ref, wat_ref, N).reshape(len(N), 256, 256)
            yield

        interleave([part(N) for N in parts()])


def conv_one(cnt, x, cf, vec, wat):
    n = x.shape[0]
    return image_call(
        conv_one_body,
        "conv_one",
        n,
        (18, 10),
        [blocks(256, 256), blocks(8, 256), whole((16, 256)), whole((2304, 256))],
        [out_blocks(256, 256), out_blocks(288, 768)],
        [sd((n, 256, 256), F32), sd((n, 288, 768), BF)],
        [],
        (cnt, x, cf, vec, wat),
    )


def middle_body(finish, n_out, *refs):
    (cnt_ref, x_ref, h0_ref, cot_ref, emb_ref, vec_ref, me_ref, wet_ref, wbt_ref, wqt_ref, wot_ref) = refs[:11]
    out_ref, ga_ref, dm_ref = refs[11:14]
    ends = refs[14 : 14 + n_out]
    (pa, pg, gt, mid, a3, mx, dmx, dz, she, dsr, dwb, dwq, dwo, dvec, turn) = refs[14 + n_out :]
    i = pl.program_id(0)
    cnt = cnt_ref[0]

    @pl.when(i == 0)
    def _():
        zero_pads(pa)
        zero_pads(pg)
        for ref in (dwb, dwq, dwo, dvec, dsr):
            ref[...] = jnp.zeros_like(ref)
        she[...] = dot_nt(emb_ref[...], wet_ref[...]) + (row(vec_ref, 2) + row(vec_ref, 3))

    live = i * NB < cnt

    @pl.when(jnp.logical_not(live))
    def _():
        for ref in (out_ref, ga_ref, dm_ref):
            ref[...] = jnp.zeros_like(ref)

    @pl.when(live)
    def _():
        g2, b2, c2, g3, b3, qb, vb, ob = (row(vec_ref, j) for j in range(4, 12))
        tot = {}

        def add(key, v):
            tot[key] = v if key not in tot else tot[key] + v

        def part(N):
            lo = N.start * 256
            hi = N.stop * 256
            W = range(len(N))
            L = lambda j: slice(j * 256, j * 256 + 256)
            masks = [(i * NB + n < cnt).astype(F32) for n in N]
            shifts = [she[pl.ds(i * NB + n, 1), :] for n in N]
            br = jnp.concatenate(shifts, axis=0)
            hload = [lambda r, n=n: h0_ref[n, r : r + CH, :] for n in N]
            m2, rs2 = stats(hload, shifts)
            sc2 = 0.5 * rs2 * g2
            sh2 = 0.5 * b2 + (br - m2) * sc2
            hm2 = br - m2
            for j, n in enumerate(N):
                for r in R:
                    h = hload[j](r) * sc2[j : j + 1] + sh2[j : j + 1]
                    put3(pa, n, r, h + h * jnp.tanh(h))
            yield
            o = conv_forward(pa, wbt_ref, N)
            yield
            for j, n in enumerate(N):
                for r in R:
                    mid[n, r : r + CH, :] = o[j * 256 + r : j * 256 + r + CH] + (x_ref[n, r : r + CH, :].astype(F32) + c2)
            mload = [lambda r, n=n: mid[n, r : r + CH, :] for n in N]
            m3, rs3 = stats(mload)
            sc3 = rs3 * g3
            sh3 = b3 - m3 * sc3
            for j, n in enumerate(N):
                for r in R:
                    a3[n * 256 + r : n * 256 + r + CH, :] = (mload[j](r) * sc3[j : j + 1] + sh3[j : j + 1]).astype(BF)
            gob = []
            for j, n in enumerate(N):
                go = cot_ref[n].astype(F32) * masks[j]
                add("ob", csum(go))
                gob.append(go.astype(BF))
            gall = jnp.concatenate(gob, axis=0)
            yield
            bc = jnp.concatenate([qb, jnp.zeros_like(qb), vb], axis=1)
            mx[lo:hi] = (dot_nt(a3[lo:hi], wqt_ref[...]) + bc).astype(BF)
            M = lambda j, p: mx[lo + j * 256 : lo + j * 256 + 256, 256 * p : 256 * p + 256]
            datt = dot(gall, wot_ref[...]).astype(BF)
            yield
            st = [dot_nt(M(j, 1), M(j, 0)) for j in W]
            dpt = [dot_nt(M(j, 2), datt[L(j)]) for j in W]
            yield
            pts = []
            ptb = []
            for j in W:
                s = st[j] * 0.0625
                e = jnp.exp(s - jnp.max(s, axis=0, keepdims=True))
                p = e * (1.0 / jnp.sum(e, axis=0, keepdims=True))
                pts.append(p)
                ptb.append(p.astype(BF))
            yield
            att = [dot_tn(ptb[j], M(j, 2)).astype(BF) for j in W]
            dv = [dot(ptb[j], datt[L(j)]).astype(BF) for j in W]
            yield
            dst = []
            for j in W:
                t = dpt[j] * pts[j]
                dst.append((t - pts[j] * jnp.sum(t, axis=0, keepdims=True)).astype(BF))
            yield
            attall = jnp.concatenate(att, axis=0)
            proj = dot_nt(attall, wot_ref[...])
            dwo[...] += dot_tn(gall, attall)
            dq = [(dot_tn(dst[j], M(j, 1)) * 0.0625).astype(BF) for j in W]
            dk = [(dot(dst[j], M(j, 0)) * 0.0625).astype(BF) for j in W]
            yield
            for j, n in enumerate(N):
                out_ref[n] = (mid[n] + (proj[L(j)] + ob)) * masks[j]
                s = slice(n * 256, n * 256 + 256)
                dmx[s, 0:256] = dq[j]
                dmx[s, 256:512] = dk[j]
                dmx[s, 512:768] = dv[j]
                add("qb", csum(dq[j].astype(F32)))
                add("vb", csum(dv[j].astype(F32)))
            yield
            d3 = dot(dmx[lo:hi], wqt_ref[...])
            dwq[...] += dot_tn(a3[lo:hi], dmx[lo:hi])
            yield
            As = []
            Bs = []
            for j, n in enumerate(N):
                A = B = jnp.zeros((8, 256), F32)
                for r in R:
                    dy = d3[j * 256 + r : j * 256 + r + CH]
                    A = A + csum(dy)
                    B = B + csum(dy * (mid[n, r : r + CH, :] - m3[j : j + 1]))
                As.append(fsum(A))
                Bs.append(fsum(B))
            A3 = jnp.concatenate(As, axis=0)
            B3 = jnp.concatenate(Bs, axis=0) * rs3
            add("b3", fsum(A3))
            add("g3", fsum(B3))
            al, be, ga = back_coefs(A3, B3, g3, rs3, m3)
            for j, n in enumerate(N):
                for r in R:
                    dm = cot_ref[n, r : r + CH, :].astype(F32) * masks[j] + (
                        d3[j * 256 + r : j * 256 + r + CH] * al[j : j + 1]
                        + (mid[n, r : r + CH, :] * be[j : j + 1] + ga[j : j + 1])
                    )
                    dm_ref[n, r : r + CH, :] = dm
                    add("c2", csum(dm))
                    put3(pg, n, r, dm, True)
                gt[:, n * 256 : n * 256 + 256] = pg[n, 16:272, 256:512].T
            yield
            o = conv_turned(pg, wbt_ref, N)
            add_taps(dwb, gt[:, lo:hi], pa, N)
            yield
            As = []
            Bs = []
            for j, n in enumerate(N):
                A = B = jnp.zeros((8, 256), F32)
                for r in R:
                    h0 = hload[j](r)
                    h = h0 * sc2[j : j + 1] + sh2[j : j + 1]
                    t = jnp.tanh(h)
                    dzz = o[j * 256 + r : j * 256 + r + CH] * ((1.0 + t) * (1.0 + (h - h * t)))
                    dz[n * 256 + r : n * 256 + r + CH, :] = dzz
                    A = A + csum(dzz)
                    B = B + csum(dzz * (h0 + hm2[j : j + 1]))
                As.append(fsum(A))
                Bs.append(fsum(B))
            A2 = jnp.concatenate(As, axis=0) * 0.5
            B2 = jnp.concatenate(Bs, axis=0) * (rs2 * 0.5)
            add("b2", fsum(A2))
            add("g2", fsum(B2))
            al, be, ga = back_coefs(A2, B2, g2, rs2, -hm2)
            al = al * 0.5
            for j, n in enumerate(N):
                ds = jnp.zeros((8, 256), F32)
                for r in R:
                    dh = dz[n * 256 + r : n * 256 + r + CH, :] * al[j : j + 1] + (
                        hload[j](r) * be[j : j + 1] + ga[j : j + 1]
                    )
                    ga_ref[n, r : r + CH, :] = dh.astype(BF)
                    ds = ds + csum(dh)
                dsr[pl.ds(i * NB + n, 1), :] = fsum(ds)
            yield

        interleave([part(N) for N in parts()])
        z = jnp.zeros((4, 256), F32)
        rows = [tot["g2"], tot["b2"], fsum(tot["c2"]), tot["g3"], tot["b3"]]
        rows += [fsum(tot[k]) for k in ("qb", "vb", "ob")]
        dvec[...] += jnp.concatenate([z] + rows + [z], axis=0)

    @pl.when(i == pl.num_programs(0) - 1)
    def _():
        ds = dsr[...]
        total = fsum(ds)
        rows = jnp.concatenate([jnp.zeros((2, 256), F32), total, total, dvec[4:16, :]], axis=0)
        finish(ends, me_ref, dwb, dwq, dwo, dot_tn(ds.astype(BF), emb_ref[...]), rows, turn)


def middle(cnt, x, h0, cot, emb, vec, me, wet, wbt, wqt, wot, finish, ends):
    n = x.shape[0]
    V = pltpu.VMEM
    return image_call(
        lambda *refs: middle_body(finish, len(ends), *refs),
        "middle",
        n,
        (90, 40),
        [blocks(256, 256)] * 3
        + [whole(emb.shape), whole((16, 256)), pl.BlockSpec(memory_space=pltpu.SMEM)]
        + [whole(w.shape) for w in (wet, wbt, wqt, wot)],
        [out_blocks(256, 256)] * 3 + [whole(e.shape) for e in ends],
        [sd((n, 256, 256), F32), sd((n, 256, 256), BF), sd((n, 256, 256), F32)] + list(ends),
        [
            V((NB, 288, 768), BF),
            V((NB, 288, 768), BF),
            V((256, NB * 256), BF),
            V((NB, 256, 256), F32),
            V((NB * 256, 256), BF),
            V((NB * 256, 768), BF),
            V((NB * 256, 768), BF),
            V((NB * 256, 256), F32),
            V((n, 256), F32),
            V((n, 256), F32),
            V((768, 768), F32),
            V((256, 768), F32),
            V((256, 256), F32),
            V((16, 256), F32),
            V((1280, 512), F32),
        ],
        (cnt, x, h0, cot, emb, vec, me, wet, wbt, wqt, wot),
    )


def conv_one_grad_body(finish, n_out, *refs):
    cnt_ref, ga_ref, pa_ref, me_ref = refs[:4]
    ends = refs[4 : 4 + n_out]
    gt, dwa = refs[4 + n_out :]
    i = pl.program_id(0)

    @pl.when(i == 0)
    def _():
        dwa[...] = jnp.zeros_like(dwa)

    @pl.when(i * NB < cnt_ref[0])
    def _():
        for n in range(NB):
            gt[:, n * 256 : n * 256 + 256] = ga_ref[n].T
        add_taps(dwa, gt[...], pa_ref, range(NB))

    @pl.when(i == pl.num_programs(0) - 1)
    def _():
        finish(ends, me_ref, dwa)


def conv_one_grad(cnt, ga, pa, me, finish, ends):
    n = ga.shape[0]
    return image_call(
        lambda *refs: conv_one_grad_body(finish, len(ends), *refs),
        "conv_one_grad",
        n,
        (18, 10),
        [blocks(256, 256), blocks(288, 768), pl.BlockSpec(memory_space=pltpu.SMEM)],
        [whole(e.shape) for e in ends],
        list(ends),
        [pltpu.VMEM((256, NB * 256), BF), pltpu.VMEM((768, 768), F32)],
        (cnt, ga, pa, me),
    )


def input_grad_body(finish, n_out, *refs):
    cnt_ref, x_ref, ga_ref, dm_ref, cf_ref, vec_ref, me_ref, wat_ref = refs[:8]
    ig_ref = refs[8]
    ends = refs[9 : 9 + n_out]
    pg, dz, dvec = refs[9 + n_out :]
    i = pl.program_id(0)

    @pl.when(i == 0)
    def _():
        zero_pads(pg)
        dvec[...] = jnp.zeros_like(dvec)

    live = i * NB < cnt_ref[0]

    @pl.when(jnp.logical_not(live))
    def _():
        ig_ref[...] = jnp.zeros_like(ig_ref)

    @pl.when(live)
    def _():
        g1 = row(vec_ref, 0)
        tot = {}

        def add(key, v):
            tot[key] = v if key not in tot else tot[key] + v

        def part(N):
            for n in N:
                for r in R:
                    put3(pg, n, r, ga_ref[n, r : r + CH, :].astype(F32), True)
            yield
            o = conv_turned(pg, wat_ref, N)
            yield
            As = []
            Bs = []
            ms = jnp.concatenate([cf_ref[n, 0:1, :] for n in N], axis=0)
            rss = jnp.concatenate([cf_ref[n, 1:2, :] for n in N], axis=0)
            for j, n in enumerate(N):
                m = cf_ref[n, 0:1, :]
                sc = 0.5 * cf_ref[n, 1:2, :] * g1
                sh = 0.5 * row(vec_ref, 1) - m * sc
                A = B = jnp.zeros((8, 256), F32)
                for r in R:
                    x = x_ref[n, r : r + CH, :].astype(F32)
                    h = x * sc + sh
                    t = jnp.tanh(h)
                    dzz = o[j * 256 + r : j * 256 + r + CH] * ((1.0 + t) * (1.0 + (h - h * t)))
                    dz[n * 256 + r : n * 256 + r + CH, :] = dzz
                    A = A + csum(dzz)
                    B = B + csum(dzz * (x - m))
                As.append(fsum(A))
                Bs.append(fsum(B))
            A1 = jnp.concatenate(As, axis=0) * 0.5
            B1 = jnp.concatenate(Bs, axis=0) * (rss * 0.5)
            add("b1", fsum(A1))
            add("g1", fsum(B1))
            al, be, ga = back_coefs(A1, B1, g1, rss, ms)
            al = al * 0.5
            for j, n in enumerate(N):
                for r in R:
                    ig_ref[n, r : r + CH, :] = dm_ref[n, r : r + CH, :] + (
                        dz[n * 256 + r : n * 256 + r + CH, :] * al[j : j + 1]
                        + (x_ref[n, r : r + CH, :].astype(F32) * be[j : j + 1] + ga[j : j + 1])
                    )
            yield

        interleave([part(N) for N in parts()])
        dvec[...] += jnp.concatenate([tot["g1"], tot["b1"], jnp.zeros((14, 256), F32)], axis=0)

    @pl.when(i == pl.num_programs(0) - 1)
    def _():
        finish(ends, me_ref, dvec[...])


def input_grad(cnt, x, ga, dm, cf, vec, me, wat, finish, ends):
    n = x.shape[0]
    return image_call(
        lambda *refs: input_grad_body(finish, len(ends), *refs),
        "input_grad",
        n,
        (24, 14),
        [blocks(256, 256)] * 3
        + [blocks(8, 256), whole((16, 256)), pl.BlockSpec(memory_space=pltpu.SMEM), whole(wat.shape)],
        [out_blocks(256, 256)] + [whole(e.shape) for e in ends],
        [sd((n, 256, 256), F32)] + list(ends),
        [pltpu.VMEM((NB, 288, 768), BF), pltpu.VMEM((NB * 256, 256), F32), pltpu.VMEM((16, 256), F32)],
        (cnt, x, ga, dm, cf, vec, me, wat),
    )


def sinus_embed(steps_in):
    half_width = E // 2
    frequency = jnp.exp(
        -math.log(10000.0) * jnp.arange(half_width, dtype=jnp.float32) / (half_width - 1)
    )
    angles = steps_in.astype(jnp.float32)[:, None] * frequency[None, :]
    return jnp.concatenate([jnp.sin(angles), jnp.cos(angles)], axis=1)


def halves(s0, s1):
    first = jnp.concatenate([s0[:, :64], s1[:, :64]], axis=1)
    second = jnp.concatenate([s0[:, 64:], s1[:, 64:]], axis=1)
    return first, second


def pack_body(conv, embed, attend, output, vec, a_ref, b_ref):
    for side, ref, base in ((0, a_ref, 0), (1, b_ref, 32)):
        for k in range(9):
            w = conv[9 * side + k]
            ref[base + 16 * k : base + 16 * k + 16, :] = jnp.concatenate([w[:16], w[16:]], axis=1).astype(BF)
    line = jnp.concatenate([vec[...], jnp.zeros((1, 32), F32)], axis=1)
    a_ref[144:160, :] = jnp.broadcast_to(line, (16, 128)).astype(BF)
    b_ref[0:32, :] = embed[...].astype(BF)
    at = jnp.concatenate([attend[...], jnp.zeros((64, 32), F32)], axis=1).T
    b_ref[176:224, :] = jnp.concatenate([at[:48], at[48:96]], axis=1).astype(BF)
    o = output[...]
    b_ref[224:240, :] = jnp.concatenate([o[:16], o[16:]], axis=1).astype(BF)


def pack(masters):
    return pl.pallas_call(
        pack_body, out_shape=[sd((RA, 128), BF), sd((RB, 128), BF)], compiler_params=VMEM, name="pack_shards"
    )(*masters)


def swap(x, bits):
    return lax.ppermute(x, AXES, [(i, i ^ bits) for i in range(32)])


def pairs(g, z, lo, rows, h):
    s0 = g[z ^ (2 * h), lo : lo + rows, :]
    s1 = g[z ^ (2 * h + 1), lo : lo + rows, :]
    return halves(s0, s1)


def unpack_a_body(me, *refs):
    gs = refs[:8]
    wat_ref, vec_ref, vrows = refs[8:]
    z = me[0]
    f = me[1]
    for rf in range(8):
        d0 = (f ^ rf) * 32
        for h in range(2):
            for k in range(9):
                j0, j1 = pairs(gs[rf], z, 16 * k, 16, h)
                at = pl.multiple_of(256 * k + d0, 32)
                wat_ref[pl.ds(at, 16), 128 * h : 128 * h + 128] = j0
                wat_ref[pl.ds(at + 16, 16), 128 * h : 128 * h + 128] = j1
        for rz in range(4):
            vrows[pl.ds((z ^ rz) * 8 + (f ^ rf), 1), :] = gs[rf][rz, 144:160, :].astype(F32)[0:1]
    v = vrows[...]
    v3 = jnp.concatenate([v, pltpu.roll(v, 96, 1), pltpu.roll(v, 64, 1)], axis=0).astype(BF)
    col = lax.broadcasted_iota(jnp.int32, (16, 96), 1)
    line = lax.broadcasted_iota(jnp.int32, (16, 96), 0)
    unit = 3 * (col & 31) + (col >> 5)
    lane = lax.broadcasted_iota(jnp.int32, (16, 128), 1)
    for half in range(2):
        acc = jnp.zeros((16, 128), F32)
        for t in range(4):
            sel = jnp.where(unit == 8 * line + 4 * half + t, 1.0, 0.0).astype(BF)
            piece = dot(sel, v3)
            if t:
                piece = pltpu.roll(piece, 32 * t, 1)
            acc = jnp.where((lane >> 5) == t, piece, acc)
        vec_ref[:, 128 * half : 128 * half + 128] = acc


def unpack_b_body(me, *refs):
    gs = refs[:8]
    wet_ref, wbt_ref, wqt_ref, wot_ref = refs[8:]
    z = me[0]
    f = me[1]
    for rf in range(8):
        own = f ^ rf
        d0 = own * 32
        g = gs[rf]
        for d in range(4):
            wet_ref[pl.ds(pl.multiple_of(d0, 32), 32), 128 * d : 128 * d + 128] = g[z ^ d, 0:32, :]
        for h in range(2):
            lanes = slice(128 * h, 128 * h + 128)
            for k in range(9):
                j0, j1 = pairs(g, z, 32 + 16 * k, 16, h)
                at = pl.multiple_of(256 * k + d0, 32)
                wbt_ref[pl.ds(at, 16), lanes] = j0
                wbt_ref[pl.ds(at + 16, 16), lanes] = j1
            j0, j1 = pairs(g, z, 176, 48, h)
            at = pl.multiple_of(own * 96, 32)
            wqt_ref[pl.ds(at, 48), lanes] = j0
            wqt_ref[pl.ds(at + 48, 48), lanes] = j1
            j0, j1 = pairs(g, z, 224, 16, h)
            at = pl.multiple_of(d0, 32)
            wot_ref[pl.ds(at, 16), lanes] = j0
            wot_ref[pl.ds(at + 16, 16), lanes] = j1


def unpack(body, name, me, gs, outs, scratch):
    return pl.pallas_call(
        body,
        in_specs=[pl.BlockSpec(memory_space=pltpu.SMEM)] + [pl.BlockSpec(g.shape) for g in gs],
        out_shape=outs,
        scratch_shapes=scratch,
        compiler_params=VMEM,
        name=name,
    )(me, *gs)


def place(outs, me, src, base, lanes, lo, rows, step):
    z = me[0]
    f = me[1]
    for rf in range(8):
        at = pl.multiple_of(base + (f ^ rf) * step, 16)
        ref = outs[rf & 1]
        for h in range(2):
            cut = slice(lanes + 128 * h, lanes + 128 * h + 128)
            e0, e1 = halves(src[pl.ds(at, rows), cut], src[pl.ds(at + rows, rows), cut])
            ref[rf >> 1, z ^ (2 * h), lo : lo + rows, :] = e0.astype(BF)
            ref[rf >> 1, z ^ (2 * h + 1), lo : lo + rows, :] = e1.astype(BF)


def spread_rows(rows, me):
    a8 = []
    for s in range(8):
        piece = rows[:, 128 * (s // 4) : 128 * (s // 4) + 128]
        a8.append(pltpu.roll(piece, 128 - 32 * (s % 4), 1) if s % 4 else piece)
    a8 = jnp.concatenate(a8, axis=0)
    top = a8.astype(BF)
    rest = (a8 - top.astype(F32)).astype(BF)
    col = lax.broadcasted_iota(jnp.int32, (32, 128), 1)
    line = lax.broadcasted_iota(jnp.int32, (32, 128), 0)
    owner = ((line & 3) ^ me[0]) * 8 + ((line >> 2) ^ me[1])
    acc = jnp.zeros((32, 128), F32)
    unit = 8 * (col & 15) + (col >> 4)
    for u in range(3):
        sel = jnp.where(unit == 3 * owner + u, 1.0, 0.0).astype(BF)
        piece = dot(sel, top) + dot(sel, rest)
        if u:
            piece = pltpu.roll(piece, 32 * u, 1)
        acc = jnp.where((col >> 5) == u, piece, acc)
    return acc


def finish_b(outs, me, dwb, dwq, dwo, de, rows, turn):
    for k in range(9):
        place(outs, me, dwb, 256 * (k // 3), 256 * (k % 3), 16 * k, 16, 32)
    for k in range(3):
        turn[256 * k : 256 * k + 256, 0:256] = dwq[:, 256 * k : 256 * k + 256].T
    place(outs, me, turn, 0, 0, 144, 48, 96)
    place(outs, me, dwo, 0, 0, 192, 16, 32)
    turn[1024:1280, :] = de
    for d in range(4):
        for rf in range(8):
            at = pl.multiple_of(1024 + (me[1] ^ rf) * 32, 32)
            block = turn[pl.ds(at, 32), 128 * d : 128 * d + 128]
            outs[rf & 1][rf >> 1, me[0] ^ d, 208:240, :] = block.astype(BF)
    acc = spread_rows(rows, me)
    for rf in range(8):
        for rz in range(4):
            r = 4 * rf + rz
            outs[rf & 1][rf >> 1, rz, 240:256, :] = jnp.broadcast_to(acc[r : r + 1], (16, 128)).astype(BF)


def finish_a(outs, me, dwa):
    for k in range(9):
        place(outs, me, dwa, 256 * (k // 3), 256 * (k % 3), 16 * k, 16, 32)


def finish_v(outs, me, rows):
    acc = spread_rows(rows, me)
    for rf in range(8):
        outs[rf & 1][rf >> 1] = acc[4 * rf : 4 * rf + 4]


def core_sum_body(keep, got, *outs):
    for j in range(4):
        outs[j][...] = (keep[j].astype(F32) + got[j].astype(F32)).astype(outs[j].dtype)


def over_core(keep, send):
    got = swap(send, 1)
    tail = keep.shape[2:]
    return pl.pallas_call(
        core_sum_body,
        grid=(4,),
        in_specs=[pl.BlockSpec((4, 1) + tail, lambda i: (0, i, 0, 0))] * 2,
        out_specs=[pl.BlockSpec((1,) + tail, lambda i: (i, 0, 0))] * 4,
        out_shape=[pltpu.HBM((4,) + tail, keep.dtype)] * 4,
        compiler_params=VMEM,
        name="core_sum",
    )(keep, got)


def over_core_small(keep, send):
    s = keep + swap(send, 1)
    return [s[j] for j in range(4)]


def to_plane(parts):
    return [swap(parts[1], 2), swap(parts[2], 4), swap(parts[3], 6)]


def plane_sum(own, got):
    line = [sum((g[rz].astype(F32) for g in got), own[rz].astype(F32)) for rz in range(4)]
    return line[0], [v.astype(own.dtype) for v in line[1:]]


def over_line(others):
    return [swap(v, 8 * (rz + 1)) for rz, v in enumerate(others)]


def shares_body(*refs):
    sb, sa, sv = (refs[4 * k][...] + sum(r[...].astype(F32) for r in refs[4 * k + 1 : 4 * k + 4]) for k in range(3))
    gb, ga, out = refs[12:]
    gb[0:240, :] = sb[0:240]
    vec = sb[240:241] + sv[0:1]
    gb[240:256, :] = jnp.broadcast_to(vec, (16, 128))
    ga[...] = sa
    fold = lambda v: jnp.sum((v * v).reshape(-1, 8, 128), axis=0)
    t = fsum(fold(sb[0:240]) + fold(sa)) + vec * vec
    out[...] = jnp.broadcast_to(jnp.sum(t, axis=1, keepdims=True), (8, 128))


def shares(b, a, v):
    args = []
    for own, got in (b, a, v):
        args += [own, *got]
    return pl.pallas_call(
        shares_body,
        out_shape=[sd((GB, 128), F32), sd((GA, 128), F32), sd((8, 128), F32)],
        compiler_params=VMEM,
        name="shares",
    )(*args)


def total_over(s):
    s = s + swap(s, 1)
    s = (s + swap(s, 2)) + (swap(s, 4) + swap(s, 6))
    return s, swap(s, 8), swap(s, 16), swap(s, 24)


def adam_body(*refs):
    t0, t1, t2, t3, gb, ga = refs[:6]
    state = refs[6:21]
    outs = refs[21:]
    norm = jnp.sqrt((t0[...] + t1[...]) + (t2[...] + t3[...]))[0:1]
    factor = clip_norm / jnp.maximum(norm, clip_norm)

    def put(kind, at, grad):
        clipped = grad * factor[:, : grad.shape[1]]
        mas, mom, squ = (r[at] for r in state[3 * kind : 3 * kind + 3])
        first_new = beta_first * mom + (1.0 - beta_first) * clipped
        second_new = beta_second * squ + (1.0 - beta_second) * clipped * clipped
        first_hat = first_new / (1.0 - beta_first**STEP)
        second_hat = second_new / (1.0 - beta_second**STEP)
        update = mas - rates_kind[kind] * (
            first_hat / (jnp.sqrt(second_hat) + adam_eps) + decays_kind[kind] * mas
        )
        outs[3 * kind][at] = first_new
        outs[3 * kind + 1][at] = second_new
        outs[3 * kind + 2][at] = update

    for side, ref in ((0, ga), (1, gb)):
        for k in range(9):
            g = ref[16 * k : 16 * k + 16, :]
            put(0, (9 * side + k,), jnp.concatenate([g[:, :64], g[:, 64:]], axis=0))
    put(1, (Ellipsis,), gb[208:240, :])
    g = gb[144:192, :]
    g = jnp.concatenate([jnp.concatenate([g[:, :64], g[:, 64:]], axis=0), jnp.zeros((96, 64), F32)], axis=1)
    g = jnp.concatenate([g, jnp.zeros((32, 128), F32)], axis=0).T
    put(2, (Ellipsis,), g[:64, :96])
    g = gb[192:208, :]
    put(3, (Ellipsis,), jnp.concatenate([g[:, :64], g[:, 64:]], axis=0))
    put(4, (Ellipsis,), gb[240:241, :96])
    outs[15][0] = norm[0, 0]


def adam(totals, gb, ga, state):
    return pl.pallas_call(
        adam_body,
        out_specs=[pl.BlockSpec(s.shape) for s in state] + [pl.BlockSpec(memory_space=pltpu.SMEM)],
        out_shape=[sd(s.shape, F32) for s in state] + [sd((1,), F32)],
        compiler_params=VMEM,
        name="clipped_adamw",
    )(*totals, gb, ga, *state)


def turned_state(state):
    out = []
    for kind in range(5):
        for a in state[3 * kind : 3 * kind + 3]:
            if kind == 0:
                a = jnp.swapaxes(a, 3, 4).reshape(18, 32, 64)
            elif kind == 2:
                a = a[0]
            elif kind < 4:
                a = jnp.swapaxes(a, 1, 2)[0]
            out.append(a)
    return out


def turned_back(results):
    out = []
    for kind in range(5):
        for a in results[3 * kind : 3 * kind + 3]:
            if kind == 0:
                a = jnp.swapaxes(a.reshape(1, 2, 9, 32, 64), 3, 4)
            elif kind == 2:
                a = a[None]
            elif kind < 4:
                a = jnp.swapaxes(a[None], 1, 2)
            out.append(a)
    return out


def per_device_here(images, timesteps, counts, cotangent, *state):
    n_img = images.shape[0]
    state = turned_state(state)
    me = jnp.stack([lax.axis_index("dp"), lax.axis_index("fsdp")]).astype(jnp.int32)
    sa, sb = pack(state[0::3])
    x = images.reshape(n_img, 256, 256)
    cot = cotangent.reshape(n_img, 256, 256)
    cf = figures(counts, x)
    emb = jax.nn.silu(sinus_embed(timesteps)).astype(BF)

    line_a = jnp.stack([sa] + [swap(sa, 8 * rz) for rz in range(1, 4)])
    rows_b = [sb] + [swap(sb, 8 * rz) for rz in range(1, 4)]
    plane_a = [line_a] + [swap(line_a, bits) for bits in (2, 4, 6)]
    rows_b, plane_a, cf = lax.optimization_barrier((rows_b, plane_a, cf))
    all_a = [p for line in plane_a for p in (line, swap(line, 1))]
    line_b = jnp.stack(rows_b)
    plane_b = [line_b] + [swap(line_b, bits) for bits in (2, 4, 6)]
    wat, vec = unpack(
        unpack_a_body, "unpack_first", me, all_a, [sd((2304, 256), BF), sd((16, 256), F32)], [pltpu.VMEM((32, 128), F32)]
    )
    wat, line_b = lax.optimization_barrier((wat, line_b))
    h0, pa1 = conv_one(counts, x, cf, vec, wat)
    h0, plane_b = lax.optimization_barrier((h0, plane_b))
    all_b = [p for line in plane_b for p in (line, swap(line, 1))]
    wet, wbt, wqt, wot = unpack(
        unpack_b_body,
        "unpack_second",
        me,
        all_b,
        [sd((256, 512), BF), sd((2304, 256), BF), sd((768, 256), BF), sd((256, 256), BF)],
        [],
    )
    out, ga, dm, keep, send = middle(
        counts, x, h0, cot, emb, vec, me, wet, wbt, wqt, wot, finish_b, [sd((4, 4, GB, 128), BF)] * 2
    )
    parts_b = over_core(keep, send)
    ga, parts_b = lax.optimization_barrier((ga, parts_b))
    plane_b = to_plane(parts_b)
    keep, send = conv_one_grad(counts, ga, pa1, me, finish_a, [sd((4, 4, GA, 128), BF)] * 2)
    keep, send, plane_b = lax.optimization_barrier((keep, send, plane_b))
    parts_a = over_core(keep, send)
    own_b, others = plane_sum(parts_b[0], plane_b)
    dm, parts_a, others = lax.optimization_barrier((dm, parts_a, others))
    plane_a = to_plane(parts_a)
    got_b = over_line(others)
    ig, keep, send = input_grad(counts, x, ga, dm, cf, vec, me, wat, finish_v, [sd((4, 4, 128), F32)] * 2)
    keep, send, plane_a, got_b = lax.optimization_barrier((keep, send, plane_a, got_b))
    own_a, others = plane_sum(parts_a[0], plane_a)
    got_a = over_line(others)
    parts_v = over_core_small(keep, send)
    own_v, others = plane_sum(parts_v[0], to_plane(parts_v))
    got_v = over_line(others)
    wide = lambda v: v[None]
    gb, ga, squares = shares(
        (own_b, got_b), (own_a, got_a), (wide(own_v), [wide(g) for g in got_v])
    )
    results = adam(total_over(squares), gb, ga, state)
    return (out.reshape(images.shape), ig.reshape(images.shape), *turned_back(results[:15]), results[15].reshape(()))


def gather_flat(masters, dp, fs):
    sizes = [m.size for m in masters]
    total = sum(sizes)
    full = -(-total // 2048) * 2048
    flat = jnp.concatenate([m.reshape(-1).astype(BF) for m in masters] + [jnp.zeros((full - total,), BF)])
    flat = flat.reshape(-1, 128)
    g = lax.all_gather(lax.all_gather(flat, "dp"), "fsdp").reshape(fs, dp, full)
    out = []
    at = 0
    for n in sizes:
        out.append(g[:, :, at : at + n])
        at += n
    conv = out[0].reshape((fs, dp) + masters[0].shape[1:]).transpose(2, 3, 0, 5, 1, 4)
    conv = conv.reshape(2, 2304, 256)
    mats = []
    for p, m in zip(out[1:4], masters[1:4]):
        r, c = m.shape[1:]
        mats.append(p.reshape(fs, dp, r, c).transpose(0, 3, 1, 2).reshape(fs * c, dp * r))
    vec = out[4].transpose(1, 0, 2).reshape(12, 256).astype(F32)
    return conv, mats, vec


def reduce_flat(grads, dp, fs):
    conv, mats, vec = grads
    pieces = [conv.reshape(18, fs, 256 // fs, dp, 256 // dp).transpose(1, 3, 0, 4, 2).reshape(fs, dp, -1)]
    for g in mats:
        c, r = g.shape
        pieces.append(g.reshape(fs, c // fs, dp, r // dp).transpose(0, 2, 3, 1).reshape(fs, dp, -1))
    pieces.append(vec.reshape(dp, fs, -1).transpose(1, 0, 2))
    sizes = [p.shape[2] for p in pieces]
    total = sum(sizes)
    full = -(-total // 2048) * 2048
    pieces.append(jnp.zeros((fs, dp, full - total), F32))
    flat = jnp.concatenate(pieces, axis=2).reshape(fs, dp, -1, 128)
    part = lax.psum_scatter(flat, "fsdp", scatter_dimension=0, tiled=False)
    part = lax.psum_scatter(part, "dp", scatter_dimension=0, tiled=False).reshape(-1)
    out = []
    at = 0
    for n in sizes:
        out.append(part[at : at + n])
        at += n
    return out


def finish_whole(outs, me, dwb, dwq, dwo, de, rows, turn):
    for out, got in zip(outs, (dwb[...], dwq[...], dwo[...], de, rows)):
        out[...] = got


def finish_one(outs, me, got):
    outs[0][...] = got[...]


def per_device_any(images, timesteps, counts, cotangent, *state):
    masters = state[0::3]
    moments = state[1::3]
    squares = state[2::3]
    dp = lax.axis_size("dp")
    fs = lax.axis_size("fsdp")
    n_img = images.shape[0]
    me = jnp.zeros((2,), jnp.int32)
    emb = jax.nn.silu(sinus_embed(timesteps)).astype(BF)
    x = images.reshape(n_img, 256, 256)
    cot = cotangent.reshape(n_img, 256, 256)
    conv, (wet, wqt, wot), vec = gather_flat(masters, dp, fs)
    vec = jnp.pad(vec, ((0, 4), (0, 0)))
    cf = figures(counts, x)
    h0, pa1 = conv_one(counts, x, cf, vec, conv[0])
    ends = [sd(s, F32) for s in ((768, 768), (256, 768), (256, 256), (256, 512), (16, 256))]
    out, ga, dm, dwb, dwq, dwo, de, rows = middle(
        counts, x, h0, cot, emb, vec, me, wet, conv[1], wqt, wot, finish_whole, ends
    )
    (dwa,) = conv_one_grad(counts, ga, pa1, me, finish_one, [sd((768, 768), F32)])
    ig, first = input_grad(counts, x, ga, dm, cf, vec, me, conv[0], finish_one, [sd((16, 256), F32)])
    apart = lambda w: w.reshape(3, 256, 3, 256).transpose(0, 2, 1, 3).reshape(9, 256, 256)
    shares_here = reduce_flat(
        (jnp.stack([apart(dwa), apart(dwb)]), (de, dwq.T, dwo), (rows + first)[:12]), dp, fs
    )
    local = sum(jnp.sum(s * s) for s in shares_here)
    norm = jnp.sqrt(lax.psum(lax.psum(local, "fsdp"), "dp"))
    factor = clip_norm / jnp.maximum(norm, clip_norm)
    results = []
    for kind in range(5):
        clipped = shares_here[kind].reshape(masters[kind].shape) * factor
        first_new = beta_first * moments[kind] + (1.0 - beta_first) * clipped
        second_new = beta_second * squares[kind] + (1.0 - beta_second) * clipped * clipped
        first_hat = first_new / (1.0 - beta_first**STEP)
        second_hat = second_new / (1.0 - beta_second**STEP)
        update_new = masters[kind] - rates_kind[kind] * (
            first_hat / (jnp.sqrt(second_hat) + adam_eps) + decays_kind[kind] * masters[kind]
        )
        results += [first_new, second_new, update_new]
    return (out.reshape(images.shape), ig.reshape(images.shape), *results, norm)


def solution(mesh):
    both = P(("dp", "fsdp"), None, None, None)
    one = P(("dp", "fsdp"))
    conv = P(None, None, None, "dp", "fsdp")
    mat = P(None, "dp", "fsdp")
    vec = P(None, ("dp", "fsdp"))
    trios = (conv,) * 3 + (mat,) * 9 + (vec,) * 3
    here = mesh.shape["dp"] == 4 and mesh.shape["fsdp"] == 8
    return jax.shard_map(
        per_device_here if here else per_device_any,
        mesh=mesh,
        in_specs=(both, one, one, both) + trios,
        out_specs=(both, both) + trios + (P(),),
        check_vma=False,
    )
```

```python
import math

import jax
import jax.numpy as jnp
from jax import lax
from jax.experimental import pallas as pl
from jax.experimental.pallas import tpu as pltpu
from jax.sharding import PartitionSpec as P

BF = jnp.bfloat16
F32 = jnp.float32
EPS = 1e-6
E = 512
STEP = 10
clip_norm = 1.0
beta_first = 0.9
beta_second = 0.999
adam_eps = 1e-08
rates_kind = (0.01, 0.03, 0.02, 0.05, 0.3)
decays_kind = (0.1, 0.1, 0.1, 0.1, 0.0)
AXES = ("dp", "fsdp")
VMEM = pltpu.CompilerParams(vmem_limit_bytes=60 * 2**20)
NB = 4
HB = 2
CH = 32
R = range(0, 256, CH)
RA = 160
RB = 240
GB = 256
GA = 144

sd = jax.ShapeDtypeStruct


def dot(a, b):
    return lax.dot_general(a, b, (((1,), (0,)), ((), ())), preferred_element_type=F32)


def dot_nt(a, b):
    return lax.dot_general(a, b, (((1,), (1,)), ((), ())), preferred_element_type=F32)


def dot_tn(a, b):
    return lax.dot_general(a, b, (((0,), (0,)), ((), ())), preferred_element_type=F32)


def gsum(s):
    n = s.shape[0]
    c = jnp.concatenate([s[:, :128], s[:, 128:]], axis=0)
    lane = lax.broadcasted_iota(jnp.int32, c.shape, 1)
    for k in (1, 2, 4):
        up = pltpu.roll(c, 128 - k, 1)
        down = pltpu.roll(c, k, 1)
        c = c + jnp.where((lane & k) == 0, up, down)
    return jnp.concatenate([c[:n], c[n:]], axis=1)


def csum(v):
    return jnp.sum(v.reshape(-1, 8, v.shape[-1]), axis=0)


def fsum(v):
    return jnp.sum(v, axis=0, keepdims=True)


def row_sums(load, base):
    s1 = s2 = None
    for r in R:
        v = load(r) - base
        a = csum(v)
        b = csum(v * v)
        s1 = a if s1 is None else s1 + a
        s2 = b if s2 is None else s2 + b
    return fsum(s1), fsum(s2)


def stats(loads, extras=None):
    firsts = [load(0)[0:1] for load in loads]
    p = jnp.concatenate(firsts, axis=0)
    if extras is not None:
        p = p + jnp.concatenate(extras, axis=0)
    q = gsum(p) * 0.125
    sums = [row_sums(load, first) for load, first in zip(loads, firsts)]
    s1 = jnp.concatenate([t[0] for t in sums], axis=0)
    s2 = jnp.concatenate([t[1] for t in sums], axis=0)
    d = p - q
    g = gsum(jnp.concatenate([s1 + 256.0 * d, s2 + d * (2.0 * s1 + 256.0 * d)], axis=0)) * (1.0 / 2048.0)
    n = len(loads)
    dm = g[:n]
    return q + dm, lax.rsqrt(g[n:] - dm * dm + EPS)


def back_coefs(sum_dy, sum_dyn, gain, rs, m):
    n = sum_dy.shape[0]
    g = gsum(jnp.concatenate([sum_dy * gain, sum_dyn * gain], axis=0)) * (1.0 / 2048.0)
    be = -rs * rs * g[n:]
    return rs * gain, be, -rs * g[:n] - m * be


def put3(pref, n, r, a, rev=False):
    rows = a.shape[0]
    col = lax.broadcasted_iota(jnp.int32, a.shape, 0) & 15
    prev = jnp.where(col == 0, 0.0, pltpu.roll(a, 1, 0))
    post = jnp.where(col == 15, 0.0, pltpu.roll(a, rows - 1, 0))
    lo, hi = (post, prev) if rev else (prev, post)
    pref[n, 16 + r : 16 + r + rows, 0:256] = lo.astype(BF)
    pref[n, 16 + r : 16 + r + rows, 256:512] = a.astype(BF)
    pref[n, 16 + r : 16 + r + rows, 512:768] = hi.astype(BF)


def zero_pads(pref):
    z = jnp.zeros((16, 768), BF)
    for n in range(NB):
        pref[n, 0:16, :] = z
        pref[n, 272:288, :] = z


def conv_forward(pref, wt_ref, N):
    acc = None
    for i in range(3):
        for j in range(3):
            rows = pref[N.start : N.stop, 16 * i : 16 * i + 256, 256 * j : 256 * j + 256]
            k = 3 * i + j
            d = dot_nt(rows.reshape(len(N) * 256, 256), wt_ref[256 * k : 256 * k + 256, :])
            acc = d if acc is None else acc + d
    return acc


def conv_turned(pref, wt_ref, N):
    acc = None
    for i in range(3):
        o = 16 * (2 - i)
        rows = pref[N.start : N.stop, o : o + 256, :].reshape(len(N) * 256, 768)
        d = dot(rows, wt_ref[768 * i : 768 * i + 768, :])
        acc = d if acc is None else acc + d
    return acc


def add_taps(acc_ref, gt, pref, N):
    for i in range(3):
        rows = pref[N.start : N.stop, 16 * i : 16 * i + 256, :].reshape(len(N) * 256, 768)
        acc_ref[256 * i : 256 * i + 256, :] += dot(gt, rows)


def interleave(gens):
    gens = list(gens)
    done = [False] * len(gens)
    at = 0
    while not all(done):
        for j, g in enumerate(gens):
            if not done[j] and at >= j:
                try:
                    next(g)
                except StopIteration:
                    done[j] = True
        at += 1


def parts():
    return [range(j, j + HB) for j in range(0, NB, HB)]


def row(ref, j):
    return ref[j : j + 1, :]


def whole(shape):
    return pl.BlockSpec(shape, lambda i, c: (0,) * len(shape))


def clamped(i, c):
    return jnp.minimum(i, (c[0] - 1) // NB)


def blocks(*tail):
    return pl.BlockSpec((NB,) + tail, lambda i, c: (clamped(i, c),) + (0,) * len(tail))


def out_blocks(*tail):
    return pl.BlockSpec((NB,) + tail, lambda i, c: (i,) + (0,) * len(tail))


def image_call(body, name, n_img, cost, in_specs, out_specs, out_shape, scratch, args):
    products, passes = cost
    return pl.pallas_call(
        body,
        grid_spec=pltpu.PrefetchScalarGridSpec(
            num_scalar_prefetch=1,
            grid=(n_img // NB,),
            in_specs=in_specs,
            out_specs=out_specs,
            scratch_shapes=scratch,
        ),
        out_shape=out_shape,
        cost_estimate=pl.CostEstimate(
            flops=n_img * products * 2 * 256**3,
            transcendentals=n_img * passes * 256**2,
            bytes_accessed=n_img * passes * 4 * 256**2,
        ),
        compiler_params=VMEM,
        name=name,
    )(*args)


def figures_body(cnt_ref, x_ref, cf_ref):
    @pl.when(pl.program_id(0) * NB < cnt_ref[0])
    def _():
        m, rs = stats([lambda r, n=n: x_ref[n, r : r + CH, :].astype(F32) for n in range(NB)])
        for n in range(NB):
            cf_ref[n] = jnp.concatenate([m[n : n + 1], rs[n : n + 1], jnp.zeros((6, 256), F32)], axis=0)


def figures(cnt, x):
    n = x.shape[0]
    return image_call(
        figures_body, "figures", n, (1, 2), [blocks(256, 256)], out_blocks(8, 256), sd((n, 8, 256), F32), [], (cnt, x)
    )


def conv_one_body(cnt_ref, x_ref, cf_ref, vec_ref, wat_ref, h0_ref, pa_ref):
    zero_pads(pa_ref)

    @pl.when(pl.program_id(0) * NB < cnt_ref[0])
    def _():
        def part(N):
            for n in N:
                sc = 0.5 * cf_ref[n, 1:2, :] * row(vec_ref, 0)
                sh = 0.5 * row(vec_ref, 1) - cf_ref[n, 0:1, :] * sc
                for r in R:
                    h = x_ref[n, r : r + CH, :].astype(F32) * sc + sh
                    put3(pa_ref, n, r, h + h * jnp.tanh(h))
            yield
            h0_ref[N.start : N.stop] = conv_forward(pa_ref, wat_ref, N).reshape(len(N), 256, 256)
            yield

        interleave([part(N) for N in parts()])


def conv_one(cnt, x, cf, vec, wat):
    n = x.shape[0]
    return image_call(
        conv_one_body,
        "conv_one",
        n,
        (18, 10),
        [blocks(256, 256), blocks(8, 256), whole((16, 256)), whole((2304, 256))],
        [out_blocks(256, 256), out_blocks(288, 768)],
        [sd((n, 256, 256), F32), sd((n, 288, 768), BF)],
        [],
        (cnt, x, cf, vec, wat),
    )


def middle_body(finish, n_out, *refs):
    (cnt_ref, x_ref, h0_ref, cot_ref, emb_ref, vec_ref, me_ref, wet_ref, wbt_ref, wqt_ref, wot_ref) = refs[:11]
    out_ref, ga_ref, dm_ref = refs[11:14]
    ends = refs[14 : 14 + n_out]
    (pa, pg, gt, mid, a3, mx, dmx, dz, she, dsr, dwb, dwq, dwo, dvec, turn) = refs[14 + n_out :]
    i = pl.program_id(0)
    cnt = cnt_ref[0]

    @pl.when(i == 0)
    def _():
        zero_pads(pa)
        zero_pads(pg)
        for ref in (dwb, dwq, dwo, dvec, dsr):
            ref[...] = jnp.zeros_like(ref)
        she[...] = dot_nt(emb_ref[...], wet_ref[...]) + (row(vec_ref, 2) + row(vec_ref, 3))

    live = i * NB < cnt

    @pl.when(jnp.logical_not(live))
    def _():
        for ref in (out_ref, ga_ref, dm_ref):
            ref[...] = jnp.zeros_like(ref)

    @pl.when(live)
    def _():
        g2, b2, c2, g3, b3, qb, vb, ob = (row(vec_ref, j) for j in range(4, 12))
        tot = {}

        def add(key, v):
            tot[key] = v if key not in tot else tot[key] + v

        def part(N):
            lo = N.start * 256
            hi = N.stop * 256
            W = range(len(N))
            L = lambda j: slice(j * 256, j * 256 + 256)
            masks = [(i * NB + n < cnt).astype(F32) for n in N]
            shifts = [she[pl.ds(i * NB + n, 1), :] for n in N]
            br = jnp.concatenate(shifts, axis=0)
            hload = [lambda r, n=n: h0_ref[n, r : r + CH, :] for n in N]
            m2, rs2 = stats(hload, shifts)
            sc2 = 0.5 * rs2 * g2
            sh2 = 0.5 * b2 + (br - m2) * sc2
            hm2 = br - m2
            for j, n in enumerate(N):
                for r in R:
                    h = hload[j](r) * sc2[j : j + 1] + sh2[j : j + 1]
                    put3(pa, n, r, h + h * jnp.tanh(h))
            yield
            o = conv_forward(pa, wbt_ref, N)
            yield
            for j, n in enumerate(N):
                for r in R:
                    mid[n, r : r + CH, :] = o[j * 256 + r : j * 256 + r + CH] + (x_ref[n, r : r + CH, :].astype(F32) + c2)
            mload = [lambda r, n=n: mid[n, r : r + CH, :] for n in N]
            m3, rs3 = stats(mload)
            sc3 = rs3 * g3
            sh3 = b3 - m3 * sc3
            for j, n in enumerate(N):
                for r in R:
                    a3[n * 256 + r : n * 256 + r + CH, :] = (mload[j](r) * sc3[j : j + 1] + sh3[j : j + 1]).astype(BF)
            gob = []
            for j, n in enumerate(N):
                go = cot_ref[n].astype(F32) * masks[j]
                add("ob", csum(go))
                gob.append(go.astype(BF))
            gall = jnp.concatenate(gob, axis=0)
            yield
            bc = jnp.concatenate([qb, jnp.zeros_like(qb), vb], axis=1)
            mx[lo:hi] = (dot_nt(a3[lo:hi], wqt_ref[...]) + bc).astype(BF)
            M = lambda j, p: mx[lo + j * 256 : lo + j * 256 + 256, 256 * p : 256 * p + 256]
            datt = dot(gall, wot_ref[...]).astype(BF)
            yield
            st = [dot_nt(M(j, 1), M(j, 0)) for j in W]
            dpt = [dot_nt(M(j, 2), datt[L(j)]) for j in W]
            yield
            pts = []
            ptb = []
            for j in W:
                s = st[j] * 0.0625
                e = jnp.exp(s - jnp.max(s, axis=0, keepdims=True))
                p = e * (1.0 / jnp.sum(e, axis=0, keepdims=True))
                pts.append(p)
                ptb.append(p.astype(BF))
            yield
            att = [dot_tn(ptb[j], M(j, 2)).astype(BF) for j in W]
            dv = [dot(ptb[j], datt[L(j)]).astype(BF) for j in W]
            yield
            dst = []
            for j in W:
                t = dpt[j] * pts[j]
                dst.append((t - pts[j] * jnp.sum(t, axis=0, keepdims=True)).astype(BF))
            yield
            attall = jnp.concatenate(att, axis=0)
            proj = dot_nt(attall, wot_ref[...])
            dwo[...] += dot_tn(gall, attall)
            dq = [(dot_tn(dst[j], M(j, 1)) * 0.0625).astype(BF) for j in W]
            dk = [(dot(dst[j], M(j, 0)) * 0.0625).astype(BF) for j in W]
            yield
            for j, n in enumerate(N):
                out_ref[n] = (mid[n] + (proj[L(j)] + ob)) * masks[j]
                s = slice(n * 256, n * 256 + 256)
                dmx[s, 0:256] = dq[j]
                dmx[s, 256:512] = dk[j]
                dmx[s, 512:768] = dv[j]
                add("qb", csum(dq[j].astype(F32)))
                add("vb", csum(dv[j].astype(F32)))
            yield
            d3 = dot(dmx[lo:hi], wqt_ref[...])
            dwq[...] += dot_tn(a3[lo:hi], dmx[lo:hi])
            yield
            As = []
            Bs = []
            for j, n in enumerate(N):
                A = B = jnp.zeros((8, 256), F32)
                for r in R:
                    dy = d3[j * 256 + r : j * 256 + r + CH]
                    A = A + csum(dy)
                    B = B + csum(dy * (mid[n, r : r + CH, :] - m3[j : j + 1]))
                As.append(fsum(A))
                Bs.append(fsum(B))
            A3 = jnp.concatenate(As, axis=0)
            B3 = jnp.concatenate(Bs, axis=0) * rs3
            add("b3", fsum(A3))
            add("g3", fsum(B3))
            al, be, ga = back_coefs(A3, B3, g3, rs3, m3)
            for j, n in enumerate(N):
                for r in R:
                    dm = cot_ref[n, r : r + CH, :].astype(F32) * masks[j] + (
                        d3[j * 256 + r : j * 256 + r + CH] * al[j : j + 1]
                        + (mid[n, r : r + CH, :] * be[j : j + 1] + ga[j : j + 1])
                    )
                    dm_ref[n, r : r + CH, :] = dm
                    add("c2", csum(dm))
                    put3(pg, n, r, dm, True)
                gt[:, n * 256 : n * 256 + 256] = pg[n, 16:272, 256:512].T
            yield
            o = conv_turned(pg, wbt_ref, N)
            add_taps(dwb, gt[:, lo:hi], pa, N)
            yield
            As = []
            Bs = []
            for j, n in enumerate(N):
                A = B = jnp.zeros((8, 256), F32)
                for r in R:
                    h0 = hload[j](r)
                    h = h0 * sc2[j : j + 1] + sh2[j : j + 1]
                    t = jnp.tanh(h)
                    dzz = o[j * 256 + r : j * 256 + r + CH] * ((1.0 + t) * (1.0 + (h - h * t)))
                    dz[n * 256 + r : n * 256 + r + CH, :] = dzz
                    A = A + csum(dzz)
                    B = B + csum(dzz * (h0 + hm2[j : j + 1]))
                As.append(fsum(A))
                Bs.append(fsum(B))
            A2 = jnp.concatenate(As, axis=0) * 0.5
            B2 = jnp.concatenate(Bs, axis=0) * (rs2 * 0.5)
            add("b2", fsum(A2))
            add("g2", fsum(B2))
            al, be, ga = back_coefs(A2, B2, g2, rs2, -hm2)
            al = al * 0.5
            for j, n in enumerate(N):
                ds = jnp.zeros((8, 256), F32)
                for r in R:
                    dh = dz[n * 256 + r : n * 256 + r + CH, :] * al[j : j + 1] + (
                        hload[j](r) * be[j : j + 1] + ga[j : j + 1]
                    )
                    ga_ref[n, r : r + CH, :] = dh.astype(BF)
                    ds = ds + csum(dh)
                dsr[pl.ds(i * NB + n, 1), :] = fsum(ds)
            yield

        interleave([part(N) for N in parts()])
        z = jnp.zeros((4, 256), F32)
        rows = [tot["g2"], tot["b2"], fsum(tot["c2"]), tot["g3"], tot["b3"]]
        rows += [fsum(tot[k]) for k in ("qb", "vb", "ob")]
        dvec[...] += jnp.concatenate([z] + rows + [z], axis=0)

    @pl.when(i == pl.num_programs(0) - 1)
    def _():
        ds = dsr[...]
        total = fsum(ds)
        rows = jnp.concatenate([jnp.zeros((2, 256), F32), total, total, dvec[4:16, :]], axis=0)
        finish(ends, me_ref, dwb, dwq, dwo, dot_tn(ds.astype(BF), emb_ref[...]), rows, turn)


def middle(cnt, x, h0, cot, emb, vec, me, wet, wbt, wqt, wot, finish, ends):
    n = x.shape[0]
    V = pltpu.VMEM
    return image_call(
        lambda *refs: middle_body(finish, len(ends), *refs),
        "middle",
        n,
        (90, 40),
        [blocks(256, 256)] * 3
        + [whole(emb.shape), whole((16, 256)), pl.BlockSpec(memory_space=pltpu.SMEM)]
        + [whole(w.shape) for w in (wet, wbt, wqt, wot)],
        [out_blocks(256, 256)] * 3 + [whole(e.shape) for e in ends],
        [sd((n, 256, 256), F32), sd((n, 256, 256), BF), sd((n, 256, 256), F32)] + list(ends),
        [
            V((NB, 288, 768), BF),
            V((NB, 288, 768), BF),
            V((256, NB * 256), BF),
            V((NB, 256, 256), F32),
            V((NB * 256, 256), BF),
            V((NB * 256, 768), BF),
            V((NB * 256, 768), BF),
            V((NB * 256, 256), F32),
            V((n, 256), F32),
            V((n, 256), F32),
            V((768, 768), F32),
            V((256, 768), F32),
            V((256, 256), F32),
            V((16, 256), F32),
            V((1280, 512), F32),
        ],
        (cnt, x, h0, cot, emb, vec, me, wet, wbt, wqt, wot),
    )


def conv_one_grad_body(finish, n_out, *refs):
    cnt_ref, ga_ref, pa_ref, me_ref = refs[:4]
    ends = refs[4 : 4 + n_out]
    gt, dwa = refs[4 + n_out :]
    i = pl.program_id(0)

    @pl.when(i == 0)
    def _():
        dwa[...] = jnp.zeros_like(dwa)

    @pl.when(i * NB < cnt_ref[0])
    def _():
        def part(N):
            for n in N:
                gt[:, n * 256 : n * 256 + 256] = ga_ref[n].T
            yield
            add_taps(dwa, gt[:, N.start * 256 : N.stop * 256], pa_ref, N)
            yield

        interleave([part(N) for N in parts()])

    @pl.when(i == pl.num_programs(0) - 1)
    def _():
        finish(ends, me_ref, dwa)


def conv_one_grad(cnt, ga, pa, me, finish, ends):
    n = ga.shape[0]
    return image_call(
        lambda *refs: conv_one_grad_body(finish, len(ends), *refs),
        "conv_one_grad",
        n,
        (18, 10),
        [blocks(256, 256), blocks(288, 768), pl.BlockSpec(memory_space=pltpu.SMEM)],
        [whole(e.shape) for e in ends],
        list(ends),
        [pltpu.VMEM((256, NB * 256), BF), pltpu.VMEM((768, 768), F32)],
        (cnt, ga, pa, me),
    )


def input_grad_body(base, *refs):
    cnt_ref, x_ref, ga_ref, dm_ref, cf_ref, vec_ref, me_ref, wat_ref = refs[:8]
    ig_ref, dvec, pg, dz = refs[-4:]
    i = pl.program_id(0)

    @pl.when(i == 0)
    def _():
        zero_pads(pg)
        dvec[...] = jnp.zeros_like(dvec)

    live = (i + base) * NB < cnt_ref[0]

    @pl.when(jnp.logical_not(live))
    def _():
        ig_ref[...] = jnp.zeros_like(ig_ref)

    @pl.when(live)
    def _():
        g1 = row(vec_ref, 0)
        tot = {}

        def add(key, v):
            tot[key] = v if key not in tot else tot[key] + v

        def part(N):
            for n in N:
                for r in R:
                    put3(pg, n, r, ga_ref[n, r : r + CH, :].astype(F32), True)
            yield
            o = conv_turned(pg, wat_ref, N)
            yield
            As = []
            Bs = []
            ms = jnp.concatenate([cf_ref[n, 0:1, :] for n in N], axis=0)
            rss = jnp.concatenate([cf_ref[n, 1:2, :] for n in N], axis=0)
            for j, n in enumerate(N):
                m = cf_ref[n, 0:1, :]
                sc = 0.5 * cf_ref[n, 1:2, :] * g1
                sh = 0.5 * row(vec_ref, 1) - m * sc
                A = B = jnp.zeros((8, 256), F32)
                for r in R:
                    x = x_ref[n, r : r + CH, :].astype(F32)
                    h = x * sc + sh
                    t = jnp.tanh(h)
                    dzz = o[j * 256 + r : j * 256 + r + CH] * ((1.0 + t) * (1.0 + (h - h * t)))
                    dz[n * 256 + r : n * 256 + r + CH, :] = dzz
                    A = A + csum(dzz)
                    B = B + csum(dzz * (x - m))
                As.append(fsum(A))
                Bs.append(fsum(B))
            A1 = jnp.concatenate(As, axis=0) * 0.5
            B1 = jnp.concatenate(Bs, axis=0) * (rss * 0.5)
            add("b1", fsum(A1))
            add("g1", fsum(B1))
            al, be, ga = back_coefs(A1, B1, g1, rss, ms)
            al = al * 0.5
            for j, n in enumerate(N):
                for r in R:
                    ig_ref[n, r : r + CH, :] = dm_ref[n, r : r + CH, :] + (
                        dz[n * 256 + r : n * 256 + r + CH, :] * al[j : j + 1]
                        + (x_ref[n, r : r + CH, :].astype(F32) * be[j : j + 1] + ga[j : j + 1])
                    )
            yield

        interleave([part(N) for N in parts()])
        g = tot["g1"]
        b = tot["b1"]
        z = jnp.zeros((4, 128), F32)
        dvec[...] += jnp.concatenate([g[:, :128], g[:, 128:], b[:, :128], b[:, 128:], z], axis=0)


def input_grad(cnt, x, ga, dm, cf, vec, me, wat, base, steps, got):
    n = x.shape[0]
    at = lambda i, c: jnp.minimum(i + base, jnp.maximum((c[0] - 1) // NB, base))
    block = lambda *tail: pl.BlockSpec((NB,) + tail, lambda i, c: (at(i, c),) + (0,) * len(tail))
    args = (cnt, x, ga, dm, cf, vec, me, wat)
    in_specs = [block(256, 256)] * 3 + [block(8, 256), whole((16, 256))]
    in_specs += [pl.BlockSpec(memory_space=pltpu.SMEM), whole(wat.shape)]
    alias = {}
    if got is not None:
        alias = {len(args): 0}
        args += (got,)
        in_specs += [pl.BlockSpec(memory_space=pl.ANY)]
    return pl.pallas_call(
        lambda *refs: input_grad_body(base, *refs),
        grid_spec=pltpu.PrefetchScalarGridSpec(
            num_scalar_prefetch=1,
            grid=(steps,),
            in_specs=in_specs,
            out_specs=[
                pl.BlockSpec((NB, 256, 256), lambda i, c: (i + base, 0, 0)),
                pl.BlockSpec((8, 128), lambda i, c: (0, 0)),
            ],
            scratch_shapes=[pltpu.VMEM((NB, 288, 768), BF), pltpu.VMEM((NB * 256, 256), F32)],
        ),
        out_shape=[sd((n, 256, 256), F32), sd((8, 128), F32)],
        input_output_aliases=alias,
        cost_estimate=pl.CostEstimate(
            flops=steps * NB * 24 * 2 * 256**3, transcendentals=0, bytes_accessed=steps * NB * 14 * 4 * 256**2
        ),
        compiler_params=VMEM,
        name="input_grad",
    )(*args)


def sinus_embed(steps_in):
    half_width = E // 2
    frequency = jnp.exp(
        -math.log(10000.0) * jnp.arange(half_width, dtype=jnp.float32) / (half_width - 1)
    )
    angles = steps_in.astype(jnp.float32)[:, None] * frequency[None, :]
    return jnp.concatenate([jnp.sin(angles), jnp.cos(angles)], axis=1)


def halves(s0, s1):
    first = jnp.concatenate([s0[:, :64], s1[:, :64]], axis=1)
    second = jnp.concatenate([s0[:, 64:], s1[:, 64:]], axis=1)
    return first, second


def pack_body(conv, embed, attend, output, vec, a_ref, b_ref):
    for side, ref, base in ((0, a_ref, 0), (1, b_ref, 32)):
        for k in range(9):
            w = conv[9 * side + k]
            ref[base + 16 * k : base + 16 * k + 16, :] = jnp.concatenate([w[:16], w[16:]], axis=1).astype(BF)
    line = jnp.concatenate([vec[...], jnp.zeros((1, 32), F32)], axis=1)
    a_ref[144:160, :] = jnp.broadcast_to(line, (16, 128)).astype(BF)
    b_ref[0:32, :] = embed[...].astype(BF)
    at = jnp.concatenate([attend[...], jnp.zeros((64, 32), F32)], axis=1).T
    b_ref[176:224, :] = jnp.concatenate([at[:48], at[48:96]], axis=1).astype(BF)
    o = output[...]
    b_ref[224:240, :] = jnp.concatenate([o[:16], o[16:]], axis=1).astype(BF)


def pack(masters):
    return pl.pallas_call(
        pack_body, out_shape=[sd((RA, 128), BF), sd((RB, 128), BF)], compiler_params=VMEM, name="pack_shards"
    )(*masters)


def swap(x, bits):
    return lax.ppermute(x, AXES, [(i, i ^ bits) for i in range(32)])


def pairs(g, z, lo, rows, h):
    s0 = g[z ^ (2 * h), lo : lo + rows, :]
    s1 = g[z ^ (2 * h + 1), lo : lo + rows, :]
    return halves(s0, s1)


def unpack_a_body(me, *refs):
    gs = refs[:8]
    wat_ref, vec_ref, vrows = refs[8:]
    z = me[0]
    f = me[1]
    for rf in range(8):
        d0 = (f ^ rf) * 32
        for h in range(2):
            for k in range(9):
                j0, j1 = pairs(gs[rf], z, 16 * k, 16, h)
                at = pl.multiple_of(256 * k + d0, 32)
                wat_ref[pl.ds(at, 16), 128 * h : 128 * h + 128] = j0
                wat_ref[pl.ds(at + 16, 16), 128 * h : 128 * h + 128] = j1
        for rz in range(4):
            vrows[pl.ds((z ^ rz) * 8 + (f ^ rf), 1), :] = gs[rf][rz, 144:160, :].astype(F32)[0:1]
    v = vrows[...]
    v3 = jnp.concatenate([v, pltpu.roll(v, 96, 1), pltpu.roll(v, 64, 1)], axis=0).astype(BF)
    col = lax.broadcasted_iota(jnp.int32, (16, 96), 1)
    line = lax.broadcasted_iota(jnp.int32, (16, 96), 0)
    unit = 3 * (col & 31) + (col >> 5)
    lane = lax.broadcasted_iota(jnp.int32, (16, 128), 1)
    for half in range(2):
        acc = jnp.zeros((16, 128), F32)
        for t in range(4):
            sel = jnp.where(unit == 8 * line + 4 * half + t, 1.0, 0.0).astype(BF)
            piece = dot(sel, v3)
            if t:
                piece = pltpu.roll(piece, 32 * t, 1)
            acc = jnp.where((lane >> 5) == t, piece, acc)
        vec_ref[:, 128 * half : 128 * half + 128] = acc


def unpack_b_body(me, *refs):
    gs = refs[:8]
    wet_ref, wbt_ref, wqt_ref, wot_ref = refs[8:]
    z = me[0]
    f = me[1]
    for rf in range(8):
        own = f ^ rf
        d0 = own * 32
        g = gs[rf]
        for d in range(4):
            wet_ref[pl.ds(pl.multiple_of(d0, 32), 32), 128 * d : 128 * d + 128] = g[z ^ d, 0:32, :]
        for h in range(2):
            lanes = slice(128 * h, 128 * h + 128)
            for k in range(9):
                j0, j1 = pairs(g, z, 32 + 16 * k, 16, h)
                at = pl.multiple_of(256 * k + d0, 32)
                wbt_ref[pl.ds(at, 16), lanes] = j0
                wbt_ref[pl.ds(at + 16, 16), lanes] = j1
            j0, j1 = pairs(g, z, 176, 48, h)
            at = pl.multiple_of(own * 96, 32)
            wqt_ref[pl.ds(at, 48), lanes] = j0
            wqt_ref[pl.ds(at + 48, 48), lanes] = j1
            j0, j1 = pairs(g, z, 224, 16, h)
            at = pl.multiple_of(d0, 32)
            wot_ref[pl.ds(at, 16), lanes] = j0
            wot_ref[pl.ds(at + 16, 16), lanes] = j1


def unpack(body, name, me, gs, outs, scratch):
    return pl.pallas_call(
        body,
        in_specs=[pl.BlockSpec(memory_space=pltpu.SMEM)] + [pl.BlockSpec(g.shape) for g in gs],
        out_shape=outs,
        scratch_shapes=scratch,
        compiler_params=VMEM,
        name=name,
    )(me, *gs)


def place(outs, me, src, base, lanes, lo, rows, step):
    z = me[0]
    f = me[1]
    for rf in range(8):
        at = pl.multiple_of(base + (f ^ rf) * step, 16)
        ref = outs[rf & 1]
        for h in range(2):
            cut = slice(lanes + 128 * h, lanes + 128 * h + 128)
            e0, e1 = halves(src[pl.ds(at, rows), cut], src[pl.ds(at + rows, rows), cut])
            ref[rf >> 1, z ^ (2 * h), lo : lo + rows, :] = e0.astype(BF)
            ref[rf >> 1, z ^ (2 * h + 1), lo : lo + rows, :] = e1.astype(BF)


def spread_rows(rows, me):
    a8 = []
    for s in range(8):
        piece = rows[:, 128 * (s // 4) : 128 * (s // 4) + 128]
        a8.append(pltpu.roll(piece, 128 - 32 * (s % 4), 1) if s % 4 else piece)
    a8 = jnp.concatenate(a8, axis=0)
    top = a8.astype(BF)
    rest = (a8 - top.astype(F32)).astype(BF)
    col = lax.broadcasted_iota(jnp.int32, (32, 128), 1)
    line = lax.broadcasted_iota(jnp.int32, (32, 128), 0)
    owner = ((line & 3) ^ me[0]) * 8 + ((line >> 2) ^ me[1])
    acc = jnp.zeros((32, 128), F32)
    unit = 8 * (col & 15) + (col >> 4)
    for u in range(3):
        sel = jnp.where(unit == 3 * owner + u, 1.0, 0.0).astype(BF)
        piece = dot(sel, top) + dot(sel, rest)
        if u:
            piece = pltpu.roll(piece, 32 * u, 1)
        acc = jnp.where((col >> 5) == u, piece, acc)
    return acc


def finish_b(outs, me, dwb, dwq, dwo, de, rows, turn):
    for k in range(9):
        place(outs, me, dwb, 256 * (k // 3), 256 * (k % 3), 16 * k, 16, 32)
    for k in range(3):
        turn[256 * k : 256 * k + 256, 0:256] = dwq[:, 256 * k : 256 * k + 256].T
    place(outs, me, turn, 0, 0, 144, 48, 96)
    place(outs, me, dwo, 0, 0, 192, 16, 32)
    turn[1024:1280, :] = de
    for d in range(4):
        for rf in range(8):
            at = pl.multiple_of(1024 + (me[1] ^ rf) * 32, 32)
            block = turn[pl.ds(at, 32), 128 * d : 128 * d + 128]
            outs[rf & 1][rf >> 1, me[0] ^ d, 208:240, :] = block.astype(BF)
    acc = spread_rows(rows, me)
    for rf in range(8):
        for rz in range(4):
            r = 4 * rf + rz
            outs[rf & 1][rf >> 1, rz, 240:256, :] = jnp.broadcast_to(acc[r : r + 1], (16, 128)).astype(BF)


def finish_a(outs, me, dwa):
    for k in range(9):
        place(outs, me, dwa, 256 * (k // 3), 256 * (k % 3), 16 * k, 16, 32)


def over_core(keep, send):
    got = swap(send, 1)
    return [(keep[j].astype(F32) + got[j].astype(F32)).astype(keep.dtype) for j in range(4)]


def to_plane(parts):
    return [swap(parts[1], 2), swap(parts[2], 4), swap(parts[3], 6)]


def plane_sum(own, got):
    line = [sum((g[rz].astype(F32) for g in got), own[rz].astype(F32)) for rz in range(4)]
    return line[0], [v.astype(own.dtype) for v in line[1:]]


def over_line(others):
    return [swap(v, 8 * (rz + 1)) for rz, v in enumerate(others)]


def shares_body(*refs):
    sb, sa = (refs[4 * k][...] + sum(r[...].astype(F32) for r in refs[4 * k + 1 : 4 * k + 4]) for k in range(2))
    v0, v1, gb, ga, out = refs[8:]
    gb[...] = sb
    ga[...] = sa
    fold = lambda v: jnp.sum((v * v).reshape(-1, 8, 128), axis=0)
    t = fsum(fold(sb[0:240]) + fold(sa)) + sb[240:241] * sb[240:241]
    t = jnp.broadcast_to(jnp.sum(t, axis=1, keepdims=True), (8, 128))
    line = lax.broadcasted_iota(jnp.int32, (8, 128), 0)
    out[...] = jnp.where(line < 4, v0[...] + v1[...], t)


def shares(b, a, vs):
    args = []
    for own, got in (b, a):
        args += [own, *got]
    return pl.pallas_call(
        shares_body,
        out_shape=[sd((GB, 128), F32), sd((GA, 128), F32), sd((8, 128), F32)],
        compiler_params=VMEM,
        name="shares",
    )(*args, *vs)


def total_over(s):
    s = s + swap(s, 1)
    s = (s + swap(s, 2)) + (swap(s, 4) + swap(s, 6))
    return s, swap(s, 8), swap(s, 16), swap(s, 24)


def adam_body(*refs):
    me, t0, t1, t2, t3, gb, ga = refs[:7]
    state = refs[7:22]
    outs = refs[22:-1]
    first = refs[-1]
    total = (t0[...] + t1[...]) + (t2[...] + t3[...])
    first[...] = total
    top = total[0:4]
    norm = jnp.sqrt(jnp.broadcast_to(jnp.sum(fsum(top * top), axis=1, keepdims=True), (1, 128)) + total[4:5])
    lane = lax.broadcasted_iota(jnp.int32, (1, 128), 1)
    vec = gb[240:241, :]
    for u in range(3):
        unit = 3 * (8 * me[0] + me[1]) + u
        line = first[pl.ds(jnp.minimum(unit >> 2, 4), 1), :]
        line = pltpu.roll(line, (32 * u + 128 - 32 * (unit & 3)) & 127, 1)
        vec = vec + jnp.where(jnp.logical_and((lane >> 5) == u, unit < 16), line, 0.0)
    factor = clip_norm / jnp.maximum(norm, clip_norm)

    def put(kind, at, grad):
        clipped = grad * factor[:, : grad.shape[1]]
        mas, mom, squ = (r[at] for r in state[3 * kind : 3 * kind + 3])
        first_new = beta_first * mom + (1.0 - beta_first) * clipped
        second_new = beta_second * squ + (1.0 - beta_second) * clipped * clipped
        first_hat = first_new / (1.0 - beta_first**STEP)
        second_hat = second_new / (1.0 - beta_second**STEP)
        update = mas - rates_kind[kind] * (
            first_hat / (jnp.sqrt(second_hat) + adam_eps) + decays_kind[kind] * mas
        )
        outs[3 * kind][at] = first_new
        outs[3 * kind + 1][at] = second_new
        outs[3 * kind + 2][at] = update

    for side, ref in ((0, ga), (1, gb)):
        for k in range(9):
            g = ref[16 * k : 16 * k + 16, :]
            put(0, (9 * side + k,), jnp.concatenate([g[:, :64], g[:, 64:]], axis=0))
    put(1, (Ellipsis,), gb[208:240, :])
    g = gb[144:192, :]
    g = jnp.concatenate([jnp.concatenate([g[:, :64], g[:, 64:]], axis=0), jnp.zeros((96, 64), F32)], axis=1)
    g = jnp.concatenate([g, jnp.zeros((32, 128), F32)], axis=0).T
    put(2, (Ellipsis,), g[:64, :96])
    g = gb[192:208, :]
    put(3, (Ellipsis,), jnp.concatenate([g[:, :64], g[:, 64:]], axis=0))
    put(4, (Ellipsis,), vec[:, :96])
    outs[15][0] = norm[0, 0]


def adam(me, totals, gb, ga, state):
    args = (*totals, gb, ga, *state)
    return pl.pallas_call(
        adam_body,
        in_specs=[pl.BlockSpec(memory_space=pltpu.SMEM)] + [pl.BlockSpec(a.shape) for a in args],
        out_specs=[pl.BlockSpec(s.shape) for s in state] + [pl.BlockSpec(memory_space=pltpu.SMEM)],
        out_shape=[sd(s.shape, F32) for s in state] + [sd((1,), F32)],
        scratch_shapes=[pltpu.VMEM((8, 128), F32)],
        compiler_params=VMEM,
        name="clipped_adamw",
    )(me, *args)


def turned_state(state):
    out = []
    for kind in range(5):
        for a in state[3 * kind : 3 * kind + 3]:
            if kind == 0:
                a = jnp.swapaxes(a, 3, 4).reshape(18, 32, 64)
            elif kind == 2:
                a = a[0]
            elif kind < 4:
                a = jnp.swapaxes(a, 1, 2)[0]
            out.append(a)
    return out


def turned_back(results):
    out = []
    for kind in range(5):
        for a in results[3 * kind : 3 * kind + 3]:
            if kind == 0:
                a = jnp.swapaxes(a.reshape(1, 2, 9, 32, 64), 3, 4)
            elif kind == 2:
                a = a[None]
            elif kind < 4:
                a = jnp.swapaxes(a[None], 1, 2)
            out.append(a)
    return out


def per_device_here(images, timesteps, counts, cotangent, *state):
    n_img = images.shape[0]
    state = turned_state(state)
    me = jnp.stack([lax.axis_index("dp"), lax.axis_index("fsdp")]).astype(jnp.int32)
    sa, sb = pack(state[0::3])
    x = images.reshape(n_img, 256, 256)
    cot = cotangent.reshape(n_img, 256, 256)
    cf = figures(counts, x)
    emb = jax.nn.silu(sinus_embed(timesteps)).astype(BF)

    line_a = jnp.stack([sa] + [swap(sa, 8 * rz) for rz in range(1, 4)])
    rows_b = [sb] + [swap(sb, 8 * rz) for rz in range(1, 4)]
    plane_a = [line_a] + [swap(line_a, bits) for bits in (2, 4, 6)]
    rows_b, plane_a, cf = lax.optimization_barrier((rows_b, plane_a, cf))
    all_a = [p for line in plane_a for p in (line, swap(line, 1))]
    line_b = jnp.stack(rows_b)
    plane_b = [line_b] + [swap(line_b, bits) for bits in (2, 4, 6)]
    wat, vec = unpack(
        unpack_a_body, "unpack_first", me, all_a, [sd((2304, 256), BF), sd((16, 256), F32)], [pltpu.VMEM((32, 128), F32)]
    )
    wat, line_b = lax.optimization_barrier((wat, line_b))
    h0, pa1 = conv_one(counts, x, cf, vec, wat)
    h0, plane_b = lax.optimization_barrier((h0, plane_b))
    all_b = [p for line in plane_b for p in (line, swap(line, 1))]
    wet, wbt, wqt, wot = unpack(
        unpack_b_body,
        "unpack_second",
        me,
        all_b,
        [sd((256, 512), BF), sd((2304, 256), BF), sd((768, 256), BF), sd((256, 256), BF)],
        [],
    )
    out, ga, dm, keep, send = middle(
        counts, x, h0, cot, emb, vec, me, wet, wbt, wqt, wot, finish_b, [sd((4, 4, GB, 128), BF)] * 2
    )
    parts_b = over_core(keep, send)
    ga, parts_b = lax.optimization_barrier((ga, parts_b))
    plane_b = to_plane(parts_b)
    keep, send = conv_one_grad(counts, ga, pa1, me, finish_a, [sd((4, 4, GA, 128), BF)] * 2)
    keep, send, plane_b = lax.optimization_barrier((keep, send, plane_b))
    parts_a = over_core(keep, send)
    own_b, others = plane_sum(parts_b[0], plane_b)
    dm, parts_a, others = lax.optimization_barrier((dm, parts_a, others))
    plane_a = to_plane(parts_a)
    got_b = over_line(others)
    half = n_img // NB // 2
    rest = n_img // NB - half
    ig, v0 = input_grad(counts, x, ga, dm, cf, vec, me, wat, 0, half, None)
    ig, plane_a, got_b = lax.optimization_barrier((ig, plane_a, got_b))
    own_a, others = plane_sum(parts_a[0], plane_a)
    ig, others = lax.optimization_barrier((ig, others))
    got_a = over_line(others)
    ig, v1 = input_grad(counts, x, ga, dm, cf, vec, me, wat, half, rest, ig)
    v1, got_a = lax.optimization_barrier((v1, got_a))
    gb, ga, sums = shares((own_b, got_b), (own_a, got_a), (v0, v1))
    results = adam(me, total_over(sums), gb, ga, state)
    return (out.reshape(images.shape), ig.reshape(images.shape), *turned_back(results[:15]), results[15].reshape(()))


def gather_flat(masters, dp, fs):
    sizes = [m.size for m in masters]
    total = sum(sizes)
    full = -(-total // 2048) * 2048
    flat = jnp.concatenate([m.reshape(-1).astype(BF) for m in masters] + [jnp.zeros((full - total,), BF)])
    flat = flat.reshape(-1, 128)
    g = lax.all_gather(lax.all_gather(flat, "dp"), "fsdp").reshape(fs, dp, full)
    out = []
    at = 0
    for n in sizes:
        out.append(g[:, :, at : at + n])
        at += n
    conv = out[0].reshape((fs, dp) + masters[0].shape[1:]).transpose(2, 3, 0, 5, 1, 4)
    conv = conv.reshape(2, 2304, 256)
    mats = []
    for p, m in zip(out[1:4], masters[1:4]):
        r, c = m.shape[1:]
        mats.append(p.reshape(fs, dp, r, c).transpose(0, 3, 1, 2).reshape(fs * c, dp * r))
    vec = out[4].transpose(1, 0, 2).reshape(12, 256).astype(F32)
    return conv, mats, vec


def reduce_flat(grads, dp, fs):
    conv, mats, vec = grads
    pieces = [conv.reshape(18, fs, 256 // fs, dp, 256 // dp).transpose(1, 3, 0, 4, 2).reshape(fs, dp, -1)]
    for g in mats:
        c, r = g.shape
        pieces.append(g.reshape(fs, c // fs, dp, r // dp).transpose(0, 2, 3, 1).reshape(fs, dp, -1))
    pieces.append(vec.reshape(dp, fs, -1).transpose(1, 0, 2))
    sizes = [p.shape[2] for p in pieces]
    total = sum(sizes)
    full = -(-total // 2048) * 2048
    pieces.append(jnp.zeros((fs, dp, full - total), F32))
    flat = jnp.concatenate(pieces, axis=2).reshape(fs, dp, -1, 128)
    part = lax.psum_scatter(flat, "fsdp", scatter_dimension=0, tiled=False)
    part = lax.psum_scatter(part, "dp", scatter_dimension=0, tiled=False).reshape(-1)
    out = []
    at = 0
    for n in sizes:
        out.append(part[at : at + n])
        at += n
    return out


def finish_whole(outs, me, dwb, dwq, dwo, de, rows, turn):
    for out, got in zip(outs, (dwb[...], dwq[...], dwo[...], de, rows)):
        out[...] = got


def finish_one(outs, me, got):
    outs[0][...] = got[...]


def per_device_any(images, timesteps, counts, cotangent, *state):
    masters = state[0::3]
    moments = state[1::3]
    squares = state[2::3]
    dp = lax.axis_size("dp")
    fs = lax.axis_size("fsdp")
    n_img = images.shape[0]
    me = jnp.zeros((2,), jnp.int32)
    emb = jax.nn.silu(sinus_embed(timesteps)).astype(BF)
    x = images.reshape(n_img, 256, 256)
    cot = cotangent.reshape(n_img, 256, 256)
    conv, (wet, wqt, wot), vec = gather_flat(masters, dp, fs)
    vec = jnp.pad(vec, ((0, 4), (0, 0)))
    cf = figures(counts, x)
    h0, pa1 = conv_one(counts, x, cf, vec, conv[0])
    ends = [sd(s, F32) for s in ((768, 768), (256, 768), (256, 256), (256, 512), (16, 256))]
    out, ga, dm, dwb, dwq, dwo, de, rows = middle(
        counts, x, h0, cot, emb, vec, me, wet, conv[1], wqt, wot, finish_whole, ends
    )
    (dwa,) = conv_one_grad(counts, ga, pa1, me, finish_one, [sd((768, 768), F32)])
    ig, first = input_grad(counts, x, ga, dm, cf, vec, me, conv[0], 0, n_img // NB, None)
    first = jnp.pad(first[:4].reshape(2, 256), ((0, 14), (0, 0)))
    apart = lambda w: w.reshape(3, 256, 3, 256).transpose(0, 2, 1, 3).reshape(9, 256, 256)
    shares_here = reduce_flat(
        (jnp.stack([apart(dwa), apart(dwb)]), (de, dwq.T, dwo), (rows + first)[:12]), dp, fs
    )
    local = sum(jnp.sum(s * s) for s in shares_here)
    norm = jnp.sqrt(lax.psum(lax.psum(local, "fsdp"), "dp"))
    factor = clip_norm / jnp.maximum(norm, clip_norm)
    results = []
    for kind in range(5):
        clipped = shares_here[kind].reshape(masters[kind].shape) * factor
        first_new = beta_first * moments[kind] + (1.0 - beta_first) * clipped
        second_new = beta_second * squares[kind] + (1.0 - beta_second) * clipped * clipped
        first_hat = first_new / (1.0 - beta_first**STEP)
        second_hat = second_new / (1.0 - beta_second**STEP)
        update_new = masters[kind] - rates_kind[kind] * (
            first_hat / (jnp.sqrt(second_hat) + adam_eps) + decays_kind[kind] * masters[kind]
        )
        results += [first_new, second_new, update_new]
    return (out.reshape(images.shape), ig.reshape(images.shape), *results, norm)


def solution(mesh):
    both = P(("dp", "fsdp"), None, None, None)
    one = P(("dp", "fsdp"))
    conv = P(None, None, None, "dp", "fsdp")
    mat = P(None, "dp", "fsdp")
    vec = P(None, ("dp", "fsdp"))
    trios = (conv,) * 3 + (mat,) * 9 + (vec,) * 3
    here = mesh.shape["dp"] == 4 and mesh.shape["fsdp"] == 8
    return jax.shard_map(
        per_device_here if here else per_device_any,
        mesh=mesh,
        in_specs=(both, one, one, both) + trios,
        out_specs=(both, both) + trios + (P(),),
        check_vma=False,
    )
```

```python
import math

import jax
import jax.numpy as jnp
from jax import lax
from jax.experimental import pallas as pl
from jax.experimental.pallas import tpu as pltpu
from jax.sharding import PartitionSpec as P

BF = jnp.bfloat16
F32 = jnp.float32
EPS = 1e-6
E = 512
STEP = 10
clip_norm = 1.0
beta_first = 0.9
beta_second = 0.999
adam_eps = 1e-08
rates_kind = (0.01, 0.03, 0.02, 0.05, 0.3)
decays_kind = (0.1, 0.1, 0.1, 0.1, 0.0)
AXES = ("dp", "fsdp")
VMEM = pltpu.CompilerParams(vmem_limit_bytes=60 * 2**20)
NB = 4
HB = 2
CH = 32
R = range(0, 256, CH)
RA = 160
RB = 240
RG = 400

sd = jax.ShapeDtypeStruct


def dot(a, b):
    return lax.dot_general(a, b, (((1,), (0,)), ((), ())), preferred_element_type=F32)


def dot_nt(a, b):
    return lax.dot_general(a, b, (((1,), (1,)), ((), ())), preferred_element_type=F32)


def dot_tn(a, b):
    return lax.dot_general(a, b, (((0,), (0,)), ((), ())), preferred_element_type=F32)


def gsum(s):
    n = s.shape[0]
    c = jnp.concatenate([s[:, :128], s[:, 128:]], axis=0)
    lane = lax.broadcasted_iota(jnp.int32, c.shape, 1)
    for k in (1, 2, 4):
        up = pltpu.roll(c, 128 - k, 1)
        down = pltpu.roll(c, k, 1)
        c = c + jnp.where((lane & k) == 0, up, down)
    return jnp.concatenate([c[:n], c[n:]], axis=1)


def csum(v):
    return jnp.sum(v.reshape(-1, 8, v.shape[-1]), axis=0)


def fsum(v):
    return jnp.sum(v, axis=0, keepdims=True)


def row_sums(load, base):
    s1 = s2 = None
    for r in R:
        v = load(r) - base
        a = csum(v)
        b = csum(v * v)
        s1 = a if s1 is None else s1 + a
        s2 = b if s2 is None else s2 + b
    return fsum(s1), fsum(s2)


def stats(loads, extras=None):
    firsts = [load(0)[0:1] for load in loads]
    p = jnp.concatenate(firsts, axis=0)
    if extras is not None:
        p = p + jnp.concatenate(extras, axis=0)
    q = gsum(p) * 0.125
    sums = [row_sums(load, first) for load, first in zip(loads, firsts)]
    s1 = jnp.concatenate([t[0] for t in sums], axis=0)
    s2 = jnp.concatenate([t[1] for t in sums], axis=0)
    d = p - q
    g = gsum(jnp.concatenate([s1 + 256.0 * d, s2 + d * (2.0 * s1 + 256.0 * d)], axis=0)) * (1.0 / 2048.0)
    n = len(loads)
    dm = g[:n]
    return q + dm, lax.rsqrt(g[n:] - dm * dm + EPS)


def back_coefs(sum_dy, sum_dyn, gain, rs, m):
    n = sum_dy.shape[0]
    g = gsum(jnp.concatenate([sum_dy * gain, sum_dyn * gain], axis=0)) * (1.0 / 2048.0)
    be = -rs * rs * g[n:]
    return rs * gain, be, -rs * g[:n] - m * be


def put3(pref, n, r, a, rev=False):
    rows = a.shape[0]
    col = lax.broadcasted_iota(jnp.int32, a.shape, 0) & 15
    prev = jnp.where(col == 0, 0.0, pltpu.roll(a, 1, 0))
    post = jnp.where(col == 15, 0.0, pltpu.roll(a, rows - 1, 0))
    lo, hi = (post, prev) if rev else (prev, post)
    low = a.astype(BF)
    pref[n, 16 + r : 16 + r + rows, 0:256] = lo.astype(BF)
    pref[n, 16 + r : 16 + r + rows, 256:512] = low
    pref[n, 16 + r : 16 + r + rows, 512:768] = hi.astype(BF)
    return low


def zero_pads(pref):
    z = jnp.zeros((16, 768), BF)
    for n in range(NB):
        pref[n, 0:16, :] = z
        pref[n, 272:288, :] = z


def conv_forward(pref, wt_ref, N):
    acc = None
    for i in range(3):
        for j in range(3):
            rows = pref[N.start : N.stop, 16 * i : 16 * i + 256, 256 * j : 256 * j + 256]
            k = 3 * i + j
            d = dot_nt(rows.reshape(len(N) * 256, 256), wt_ref[256 * k : 256 * k + 256, :])
            acc = d if acc is None else acc + d
    return acc


def conv_turned(pref, wt_ref, N):
    acc = None
    for i in range(3):
        o = 16 * (2 - i)
        rows = pref[N.start : N.stop, o : o + 256, :].reshape(len(N) * 256, 768)
        d = dot(rows, wt_ref[768 * i : 768 * i + 768, :])
        acc = d if acc is None else acc + d
    return acc


def add_taps(acc_ref, gt, pref, N):
    for i in range(3):
        rows = pref[N.start : N.stop, 16 * i : 16 * i + 256, :].reshape(len(N) * 256, 768)
        acc_ref[256 * i : 256 * i + 256, :] += dot(gt, rows)


def interleave(gens):
    gens = list(gens)
    done = [False] * len(gens)
    at = 0
    while not all(done):
        for j, g in enumerate(gens):
            if not done[j] and at >= j:
                try:
                    next(g)
                except StopIteration:
                    done[j] = True
        at += 1


def parts():
    return [range(j, j + HB) for j in range(0, NB, HB)]


def row(ref, j):
    return ref[j : j + 1, :]


def whole(shape):
    return pl.BlockSpec(shape, lambda i, c: (0,) * len(shape))


def clamped(i, c):
    return jnp.minimum(i, (c[0] - 1) // NB)


def blocks(*tail):
    return pl.BlockSpec((NB,) + tail, lambda i, c: (clamped(i, c),) + (0,) * len(tail))


def out_blocks(*tail):
    return pl.BlockSpec((NB,) + tail, lambda i, c: (i,) + (0,) * len(tail))


def image_call(body, name, n_img, cost, in_specs, out_specs, out_shape, scratch, args):
    products, passes = cost
    return pl.pallas_call(
        body,
        grid_spec=pltpu.PrefetchScalarGridSpec(
            num_scalar_prefetch=1,
            grid=(n_img // NB,),
            in_specs=in_specs,
            out_specs=out_specs,
            scratch_shapes=scratch,
        ),
        out_shape=out_shape,
        cost_estimate=pl.CostEstimate(
            flops=n_img * products * 2 * 256**3,
            transcendentals=n_img * passes * 256**2,
            bytes_accessed=n_img * passes * 4 * 256**2,
        ),
        compiler_params=VMEM,
        name=name,
    )(*args)


def figures_body(cnt_ref, x_ref, cf_ref):
    @pl.when(pl.program_id(0) * NB < cnt_ref[0])
    def _():
        m, rs = stats([lambda r, n=n: x_ref[n, r : r + CH, :].astype(F32) for n in range(NB)])
        for n in range(NB):
            cf_ref[n] = jnp.concatenate([m[n : n + 1], rs[n : n + 1], jnp.zeros((6, 256), F32)], axis=0)


def figures(cnt, x):
    n = x.shape[0]
    return image_call(
        figures_body, "figures", n, (1, 2), [blocks(256, 256)], out_blocks(8, 256), sd((n, 8, 256), F32), [], (cnt, x)
    )


def conv_one_body(cnt_ref, x_ref, cf_ref, vec_ref, wat_ref, h0_ref, a1_ref, pa):
    @pl.when(pl.program_id(0) == 0)
    def _():
        zero_pads(pa)

    @pl.when(pl.program_id(0) * NB < cnt_ref[0])
    def _():
        def part(N):
            for n in N:
                sc = 0.5 * cf_ref[n, 1:2, :] * row(vec_ref, 0)
                sh = 0.5 * row(vec_ref, 1) - cf_ref[n, 0:1, :] * sc
                for r in R:
                    h = x_ref[n, r : r + CH, :].astype(F32) * sc + sh
                    a1_ref[n, r : r + CH, :] = put3(pa, n, r, h + h * jnp.tanh(h))
            yield
            h0_ref[N.start : N.stop] = conv_forward(pa, wat_ref, N).reshape(len(N), 256, 256)
            yield

        interleave([part(N) for N in parts()])


def conv_one(cnt, x, cf, vec, wat):
    n = x.shape[0]
    return image_call(
        conv_one_body,
        "conv_one",
        n,
        (18, 10),
        [blocks(256, 256), blocks(8, 256), whole((16, 256)), whole((2304, 256))],
        [out_blocks(256, 256), out_blocks(256, 256)],
        [sd((n, 256, 256), F32), sd((n, 256, 256), BF)],
        [pltpu.VMEM((NB, 288, 768), BF)],
        (cnt, x, cf, vec, wat),
    )


def middle_body(finish, n_out, *refs):
    (cnt_ref, x_ref, h0_ref, cot_ref, a1_ref, emb_ref, vec_ref, me_ref, wet_ref, wbt_ref, wqt_ref, wot_ref) = refs[:12]
    out_ref, ga_ref, dm_ref = refs[12:15]
    ends = refs[15 : 15 + n_out]
    (pa, pg, pa1, gt, gt1, mid, a3, mx, dmx, dz, she, dsr, dwa, dwb, dwq, dwo, dvec, turn) = refs[15 + n_out :]
    i = pl.program_id(0)
    cnt = cnt_ref[0]

    @pl.when(i == 0)
    def _():
        zero_pads(pa)
        zero_pads(pg)
        zero_pads(pa1)
        for ref in (dwa, dwb, dwq, dwo, dvec, dsr):
            ref[...] = jnp.zeros_like(ref)
        she[...] = dot_nt(emb_ref[...], wet_ref[...]) + (row(vec_ref, 2) + row(vec_ref, 3))

    live = i * NB < cnt

    @pl.when(jnp.logical_not(live))
    def _():
        for ref in (out_ref, ga_ref, dm_ref):
            ref[...] = jnp.zeros_like(ref)

    @pl.when(live)
    def _():
        g2, b2, c2, g3, b3, qb, vb, ob = (row(vec_ref, j) for j in range(4, 12))
        tot = {}

        def add(key, v):
            tot[key] = v if key not in tot else tot[key] + v

        def part(N):
            lo = N.start * 256
            hi = N.stop * 256
            W = range(len(N))
            L = lambda j: slice(j * 256, j * 256 + 256)
            masks = [(i * NB + n < cnt).astype(F32) for n in N]
            shifts = [she[pl.ds(i * NB + n, 1), :] for n in N]
            br = jnp.concatenate(shifts, axis=0)
            hload = [lambda r, n=n: h0_ref[n, r : r + CH, :] for n in N]
            m2, rs2 = stats(hload, shifts)
            sc2 = 0.5 * rs2 * g2
            sh2 = 0.5 * b2 + (br - m2) * sc2
            hm2 = br - m2
            for j, n in enumerate(N):
                for r in R:
                    h = hload[j](r) * sc2[j : j + 1] + sh2[j : j + 1]
                    put3(pa, n, r, h + h * jnp.tanh(h))
            yield
            o = conv_forward(pa, wbt_ref, N)
            yield
            for j, n in enumerate(N):
                for r in R:
                    mid[n, r : r + CH, :] = o[j * 256 + r : j * 256 + r + CH] + (x_ref[n, r : r + CH, :].astype(F32) + c2)
            mload = [lambda r, n=n: mid[n, r : r + CH, :] for n in N]
            m3, rs3 = stats(mload)
            sc3 = rs3 * g3
            sh3 = b3 - m3 * sc3
            for j, n in enumerate(N):
                for r in R:
                    a3[n * 256 + r : n * 256 + r + CH, :] = (mload[j](r) * sc3[j : j + 1] + sh3[j : j + 1]).astype(BF)
            gob = []
            for j, n in enumerate(N):
                go = cot_ref[n].astype(F32) * masks[j]
                add("ob", csum(go))
                gob.append(go.astype(BF))
            gall = jnp.concatenate(gob, axis=0)
            yield
            bc = jnp.concatenate([qb, jnp.zeros_like(qb), vb], axis=1)
            mx[lo:hi] = (dot_nt(a3[lo:hi], wqt_ref[...]) + bc).astype(BF)
            M = lambda j, p: mx[lo + j * 256 : lo + j * 256 + 256, 256 * p : 256 * p + 256]
            datt = dot(gall, wot_ref[...]).astype(BF)
            yield
            st = [dot_nt(M(j, 1), M(j, 0)) for j in W]
            dpt = [dot_nt(M(j, 2), datt[L(j)]) for j in W]
            yield
            pts = []
            ptb = []
            for j in W:
                s = st[j] * 0.0625
                e = jnp.exp(s - jnp.max(s, axis=0, keepdims=True))
                p = e * (1.0 / jnp.sum(e, axis=0, keepdims=True))
                pts.append(p)
                ptb.append(p.astype(BF))
            yield
            att = [dot_tn(ptb[j], M(j, 2)).astype(BF) for j in W]
            dv = [dot(ptb[j], datt[L(j)]).astype(BF) for j in W]
            yield
            dst = []
            for n in N:
                for r in R:
                    put3(pa1, n, r, a1_ref[n, r : r + CH, :].astype(F32))
            for j in W:
                t = dpt[j] * pts[j]
                dst.append((t - pts[j] * jnp.sum(t, axis=0, keepdims=True)).astype(BF))
            yield
            attall = jnp.concatenate(att, axis=0)
            proj = dot_nt(attall, wot_ref[...])
            dwo[...] += dot_tn(gall, attall)
            dq = [(dot_tn(dst[j], M(j, 1)) * 0.0625).astype(BF) for j in W]
            dk = [(dot(dst[j], M(j, 0)) * 0.0625).astype(BF) for j in W]
            yield
            for j, n in enumerate(N):
                out_ref[n] = (mid[n] + (proj[L(j)] + ob)) * masks[j]
                s = slice(n * 256, n * 256 + 256)
                dmx[s, 0:256] = dq[j]
                dmx[s, 256:512] = dk[j]
                dmx[s, 512:768] = dv[j]
                add("qb", csum(dq[j].astype(F32)))
                add("vb", csum(dv[j].astype(F32)))
            yield
            d3 = dot(dmx[lo:hi], wqt_ref[...])
            dwq[...] += dot_tn(a3[lo:hi], dmx[lo:hi])
            yield
            As = []
            Bs = []
            for j, n in enumerate(N):
                A = B = jnp.zeros((8, 256), F32)
                for r in R:
                    dy = d3[j * 256 + r : j * 256 + r + CH]
                    A = A + csum(dy)
                    B = B + csum(dy * (mid[n, r : r + CH, :] - m3[j : j + 1]))
                As.append(fsum(A))
                Bs.append(fsum(B))
            A3 = jnp.concatenate(As, axis=0)
            B3 = jnp.concatenate(Bs, axis=0) * rs3
            add("b3", fsum(A3))
            add("g3", fsum(B3))
            al, be, ga = back_coefs(A3, B3, g3, rs3, m3)
            for j, n in enumerate(N):
                for r in R:
                    dm = cot_ref[n, r : r + CH, :].astype(F32) * masks[j] + (
                        d3[j * 256 + r : j * 256 + r + CH] * al[j : j + 1]
                        + (mid[n, r : r + CH, :] * be[j : j + 1] + ga[j : j + 1])
                    )
                    dm_ref[n, r : r + CH, :] = dm
                    add("c2", csum(dm))
                    put3(pg, n, r, dm, True)
                gt[:, n * 256 : n * 256 + 256] = pg[n, 16:272, 256:512].T
            yield
            o = conv_turned(pg, wbt_ref, N)
            add_taps(dwb, gt[:, lo:hi], pa, N)
            yield
            As = []
            Bs = []
            for j, n in enumerate(N):
                A = B = jnp.zeros((8, 256), F32)
                for r in R:
                    h0 = hload[j](r)
                    h = h0 * sc2[j : j + 1] + sh2[j : j + 1]
                    t = jnp.tanh(h)
                    dzz = o[j * 256 + r : j * 256 + r + CH] * ((1.0 + t) * (1.0 + (h - h * t)))
                    dz[n * 256 + r : n * 256 + r + CH, :] = dzz
                    A = A + csum(dzz)
                    B = B + csum(dzz * (h0 + hm2[j : j + 1]))
                As.append(fsum(A))
                Bs.append(fsum(B))
            A2 = jnp.concatenate(As, axis=0) * 0.5
            B2 = jnp.concatenate(Bs, axis=0) * (rs2 * 0.5)
            add("b2", fsum(A2))
            add("g2", fsum(B2))
            al, be, ga = back_coefs(A2, B2, g2, rs2, -hm2)
            al = al * 0.5
            for j, n in enumerate(N):
                ds = jnp.zeros((8, 256), F32)
                for r in R:
                    dh = dz[n * 256 + r : n * 256 + r + CH, :] * al[j : j + 1] + (
                        hload[j](r) * be[j : j + 1] + ga[j : j + 1]
                    )
                    ga_ref[n, r : r + CH, :] = dh.astype(BF)
                    ds = ds + csum(dh)
                dsr[pl.ds(i * NB + n, 1), :] = fsum(ds)
                gt1[:, n * 256 : n * 256 + 256] = ga_ref[n].T
            yield
            add_taps(dwa, gt1[:, lo:hi], pa1, N)
            yield

        interleave([part(N) for N in parts()])
        z = jnp.zeros((4, 256), F32)
        rows = [tot["g2"], tot["b2"], fsum(tot["c2"]), tot["g3"], tot["b3"]]
        rows += [fsum(tot[k]) for k in ("qb", "vb", "ob")]
        dvec[...] += jnp.concatenate([z] + rows + [z], axis=0)

    @pl.when(i == pl.num_programs(0) - 1)
    def _():
        ds = dsr[...]
        total = fsum(ds)
        rows = jnp.concatenate([jnp.zeros((2, 256), F32), total, total, dvec[4:16, :]], axis=0)
        finish(ends, me_ref, dwa, dwb, dwq, dwo, dot_tn(ds.astype(BF), emb_ref[...]), rows, turn)


def middle(cnt, x, h0, cot, a1, emb, vec, me, wet, wbt, wqt, wot, finish, ends):
    n = x.shape[0]
    V = pltpu.VMEM
    return image_call(
        lambda *refs: middle_body(finish, len(ends), *refs),
        "middle",
        n,
        (108, 44),
        [blocks(256, 256)] * 4
        + [whole(emb.shape), whole((16, 256)), pl.BlockSpec(memory_space=pltpu.SMEM)]
        + [whole(w.shape) for w in (wet, wbt, wqt, wot)],
        [out_blocks(256, 256)] * 3 + [whole(e.shape) for e in ends],
        [sd((n, 256, 256), F32), sd((n, 256, 256), BF), sd((n, 256, 256), F32)] + list(ends),
        [
            V((NB, 288, 768), BF),
            V((NB, 288, 768), BF),
            V((NB, 288, 768), BF),
            V((256, NB * 256), BF),
            V((256, NB * 256), BF),
            V((NB, 256, 256), F32),
            V((NB * 256, 256), BF),
            V((NB * 256, 768), BF),
            V((NB * 256, 768), BF),
            V((NB * 256, 256), F32),
            V((n, 256), F32),
            V((n, 256), F32),
            V((768, 768), F32),
            V((768, 768), F32),
            V((256, 768), F32),
            V((256, 256), F32),
            V((16, 256), F32),
            V((1280, 512), F32),
        ],
        (cnt, x, h0, cot, a1, emb, vec, me, wet, wbt, wqt, wot),
    )


def input_grad_body(base, *refs):
    cnt_ref, x_ref, ga_ref, dm_ref, cf_ref, vec_ref, me_ref, wat_ref = refs[:8]
    ig_ref, dvec, pg, dz = refs[-4:]
    i = pl.program_id(0)

    @pl.when(i == 0)
    def _():
        zero_pads(pg)
        dvec[...] = jnp.zeros_like(dvec)

    live = (i + base) * NB < cnt_ref[0]

    @pl.when(jnp.logical_not(live))
    def _():
        ig_ref[...] = jnp.zeros_like(ig_ref)

    @pl.when(live)
    def _():
        g1 = row(vec_ref, 0)
        tot = {}

        def add(key, v):
            tot[key] = v if key not in tot else tot[key] + v

        def part(N):
            for n in N:
                for r in R:
                    put3(pg, n, r, ga_ref[n, r : r + CH, :].astype(F32), True)
            yield
            o = conv_turned(pg, wat_ref, N)
            yield
            As = []
            Bs = []
            ms = jnp.concatenate([cf_ref[n, 0:1, :] for n in N], axis=0)
            rss = jnp.concatenate([cf_ref[n, 1:2, :] for n in N], axis=0)
            for j, n in enumerate(N):
                m = cf_ref[n, 0:1, :]
                sc = 0.5 * cf_ref[n, 1:2, :] * g1
                sh = 0.5 * row(vec_ref, 1) - m * sc
                A = B = jnp.zeros((8, 256), F32)
                for r in R:
                    x = x_ref[n, r : r + CH, :].astype(F32)
                    h = x * sc + sh
                    t = jnp.tanh(h)
                    dzz = o[j * 256 + r : j * 256 + r + CH] * ((1.0 + t) * (1.0 + (h - h * t)))
                    dz[n * 256 + r : n * 256 + r + CH, :] = dzz
                    A = A + csum(dzz)
                    B = B + csum(dzz * (x - m))
                As.append(fsum(A))
                Bs.append(fsum(B))
            A1 = jnp.concatenate(As, axis=0) * 0.5
            B1 = jnp.concatenate(Bs, axis=0) * (rss * 0.5)
            add("b1", fsum(A1))
            add("g1", fsum(B1))
            al, be, ga = back_coefs(A1, B1, g1, rss, ms)
            al = al * 0.5
            for j, n in enumerate(N):
                for r in R:
                    ig_ref[n, r : r + CH, :] = dm_ref[n, r : r + CH, :] + (
                        dz[n * 256 + r : n * 256 + r + CH, :] * al[j : j + 1]
                        + (x_ref[n, r : r + CH, :].astype(F32) * be[j : j + 1] + ga[j : j + 1])
                    )
            yield

        interleave([part(N) for N in parts()])
        g = tot["g1"]
        b = tot["b1"]
        z = jnp.zeros((4, 128), F32)
        dvec[...] += jnp.concatenate([g[:, :128], g[:, 128:], b[:, :128], b[:, 128:], z], axis=0)


def input_grad(cnt, x, ga, dm, cf, vec, me, wat, base, steps, got):
    n = x.shape[0]
    at = lambda i, c: jnp.minimum(i + base, jnp.maximum((c[0] - 1) // NB, base))
    block = lambda *tail: pl.BlockSpec((NB,) + tail, lambda i, c: (at(i, c),) + (0,) * len(tail))
    args = (cnt, x, ga, dm, cf, vec, me, wat)
    in_specs = [block(256, 256)] * 3 + [block(8, 256), whole((16, 256))]
    in_specs += [pl.BlockSpec(memory_space=pltpu.SMEM), whole(wat.shape)]
    alias = {}
    if got is not None:
        alias = {len(args): 0}
        args += (got,)
        in_specs += [pl.BlockSpec(memory_space=pl.ANY)]
    return pl.pallas_call(
        lambda *refs: input_grad_body(base, *refs),
        grid_spec=pltpu.PrefetchScalarGridSpec(
            num_scalar_prefetch=1,
            grid=(steps,),
            in_specs=in_specs,
            out_specs=[
                pl.BlockSpec((NB, 256, 256), lambda i, c: (i + base, 0, 0)),
                pl.BlockSpec((8, 128), lambda i, c: (0, 0)),
            ],
            scratch_shapes=[pltpu.VMEM((NB, 288, 768), BF), pltpu.VMEM((NB * 256, 256), F32)],
        ),
        out_shape=[sd((n, 256, 256), F32), sd((8, 128), F32)],
        input_output_aliases=alias,
        cost_estimate=pl.CostEstimate(
            flops=steps * NB * 24 * 2 * 256**3, transcendentals=0, bytes_accessed=steps * NB * 14 * 4 * 256**2
        ),
        compiler_params=VMEM,
        name="input_grad",
    )(*args)


def sinus_embed(steps_in):
    half_width = E // 2
    frequency = jnp.exp(
        -math.log(10000.0) * jnp.arange(half_width, dtype=jnp.float32) / (half_width - 1)
    )
    angles = steps_in.astype(jnp.float32)[:, None] * frequency[None, :]
    return jnp.concatenate([jnp.sin(angles), jnp.cos(angles)], axis=1)


def halves(s0, s1):
    first = jnp.concatenate([s0[:, :64], s1[:, :64]], axis=1)
    second = jnp.concatenate([s0[:, 64:], s1[:, 64:]], axis=1)
    return first, second


def pack_body(conv, embed, attend, output, vec, a_ref, b_ref):
    for side, ref, base in ((0, a_ref, 0), (1, b_ref, 32)):
        for k in range(9):
            w = conv[9 * side + k]
            ref[base + 16 * k : base + 16 * k + 16, :] = jnp.concatenate([w[:16], w[16:]], axis=1).astype(BF)
    line = jnp.concatenate([vec[...], jnp.zeros((1, 32), F32)], axis=1)
    a_ref[144:160, :] = jnp.broadcast_to(line, (16, 128)).astype(BF)
    b_ref[0:32, :] = embed[...].astype(BF)
    at = jnp.concatenate([attend[...], jnp.zeros((64, 32), F32)], axis=1).T
    b_ref[176:224, :] = jnp.concatenate([at[:48], at[48:96]], axis=1).astype(BF)
    o = output[...]
    b_ref[224:240, :] = jnp.concatenate([o[:16], o[16:]], axis=1).astype(BF)


def pack(masters):
    return pl.pallas_call(
        pack_body, out_shape=[sd((RA, 128), BF), sd((RB, 128), BF)], compiler_params=VMEM, name="pack_shards"
    )(*masters)


def swap(x, bits):
    return lax.ppermute(x, AXES, [(i, i ^ bits) for i in range(32)])


def pairs(g, z, lo, rows, h):
    s0 = g[z ^ (2 * h), lo : lo + rows, :]
    s1 = g[z ^ (2 * h + 1), lo : lo + rows, :]
    return halves(s0, s1)


def unpack_a_body(me, *refs):
    gs = refs[:8]
    wat_ref, vec_ref, vrows = refs[8:]
    z = me[0]
    f = me[1]
    for rf in range(8):
        d0 = (f ^ rf) * 32
        for h in range(2):
            for k in range(9):
                j0, j1 = pairs(gs[rf], z, 16 * k, 16, h)
                at = pl.multiple_of(256 * k + d0, 32)
                wat_ref[pl.ds(at, 16), 128 * h : 128 * h + 128] = j0
                wat_ref[pl.ds(at + 16, 16), 128 * h : 128 * h + 128] = j1
        for rz in range(4):
            vrows[pl.ds((z ^ rz) * 8 + (f ^ rf), 1), :] = gs[rf][rz, 144:160, :].astype(F32)[0:1]
    v = vrows[...]
    v3 = jnp.concatenate([v, pltpu.roll(v, 96, 1), pltpu.roll(v, 64, 1)], axis=0).astype(BF)
    col = lax.broadcasted_iota(jnp.int32, (16, 96), 1)
    line = lax.broadcasted_iota(jnp.int32, (16, 96), 0)
    unit = 3 * (col & 31) + (col >> 5)
    lane = lax.broadcasted_iota(jnp.int32, (16, 128), 1)
    for half in range(2):
        acc = jnp.zeros((16, 128), F32)
        for t in range(4):
            sel = jnp.where(unit == 8 * line + 4 * half + t, 1.0, 0.0).astype(BF)
            piece = dot(sel, v3)
            if t:
                piece = pltpu.roll(piece, 32 * t, 1)
            acc = jnp.where((lane >> 5) == t, piece, acc)
        vec_ref[:, 128 * half : 128 * half + 128] = acc


def unpack_b_body(me, *refs):
    gs = refs[:8]
    wet_ref, wbt_ref, wqt_ref, wot_ref = refs[8:]
    z = me[0]
    f = me[1]
    for rf in range(8):
        own = f ^ rf
        d0 = own * 32
        g = gs[rf]
        for d in range(4):
            wet_ref[pl.ds(pl.multiple_of(d0, 32), 32), 128 * d : 128 * d + 128] = g[z ^ d, 0:32, :]
        for h in range(2):
            lanes = slice(128 * h, 128 * h + 128)
            for k in range(9):
                j0, j1 = pairs(g, z, 32 + 16 * k, 16, h)
                at = pl.multiple_of(256 * k + d0, 32)
                wbt_ref[pl.ds(at, 16), lanes] = j0
                wbt_ref[pl.ds(at + 16, 16), lanes] = j1
            j0, j1 = pairs(g, z, 176, 48, h)
            at = pl.multiple_of(own * 96, 32)
            wqt_ref[pl.ds(at, 48), lanes] = j0
            wqt_ref[pl.ds(at + 48, 48), lanes] = j1
            j0, j1 = pairs(g, z, 224, 16, h)
            at = pl.multiple_of(d0, 32)
            wot_ref[pl.ds(at, 16), lanes] = j0
            wot_ref[pl.ds(at + 16, 16), lanes] = j1


def unpack(body, name, me, gs, outs, scratch):
    return pl.pallas_call(
        body,
        in_specs=[pl.BlockSpec(memory_space=pltpu.SMEM)] + [pl.BlockSpec(g.shape) for g in gs],
        out_shape=outs,
        scratch_shapes=scratch,
        compiler_params=VMEM,
        name=name,
    )(me, *gs)


def place(outs, me, src, base, lanes, lo, rows, step):
    z = me[0]
    f = me[1]
    for rf in range(8):
        at = pl.multiple_of(base + (f ^ rf) * step, 16)
        ref = outs[rf & 1]
        for h in range(2):
            cut = slice(lanes + 128 * h, lanes + 128 * h + 128)
            e0, e1 = halves(src[pl.ds(at, rows), cut], src[pl.ds(at + rows, rows), cut])
            ref[rf >> 1, z ^ (2 * h), lo : lo + rows, :] = e0.astype(BF)
            ref[rf >> 1, z ^ (2 * h + 1), lo : lo + rows, :] = e1.astype(BF)


def spread_rows(rows, me):
    a8 = []
    for s in range(8):
        piece = rows[:, 128 * (s // 4) : 128 * (s // 4) + 128]
        a8.append(pltpu.roll(piece, 128 - 32 * (s % 4), 1) if s % 4 else piece)
    a8 = jnp.concatenate(a8, axis=0)
    top = a8.astype(BF)
    rest = (a8 - top.astype(F32)).astype(BF)
    col = lax.broadcasted_iota(jnp.int32, (32, 128), 1)
    line = lax.broadcasted_iota(jnp.int32, (32, 128), 0)
    owner = ((line & 3) ^ me[0]) * 8 + ((line >> 2) ^ me[1])
    acc = jnp.zeros((32, 128), F32)
    unit = 8 * (col & 15) + (col >> 4)
    for u in range(3):
        sel = jnp.where(unit == 3 * owner + u, 1.0, 0.0).astype(BF)
        piece = dot(sel, top) + dot(sel, rest)
        if u:
            piece = pltpu.roll(piece, 32 * u, 1)
        acc = jnp.where((col >> 5) == u, piece, acc)
    return acc


def finish_all(outs, me, dwa, dwb, dwq, dwo, de, rows, turn):
    for k in range(9):
        place(outs, me, dwa, 256 * (k // 3), 256 * (k % 3), 256 + 16 * k, 16, 32)
        place(outs, me, dwb, 256 * (k // 3), 256 * (k % 3), 16 * k, 16, 32)
    for k in range(3):
        turn[256 * k : 256 * k + 256, 0:256] = dwq[:, 256 * k : 256 * k + 256].T
    place(outs, me, turn, 0, 0, 144, 48, 96)
    place(outs, me, dwo, 0, 0, 192, 16, 32)
    turn[1024:1280, :] = de
    for d in range(4):
        for rf in range(8):
            at = pl.multiple_of(1024 + (me[1] ^ rf) * 32, 32)
            block = turn[pl.ds(at, 32), 128 * d : 128 * d + 128]
            outs[rf & 1][rf >> 1, me[0] ^ d, 208:240, :] = block.astype(BF)
    acc = spread_rows(rows, me)
    for rf in range(8):
        for rz in range(4):
            r = 4 * rf + rz
            outs[rf & 1][rf >> 1, rz, 240:256, :] = jnp.broadcast_to(acc[r : r + 1], (16, 128)).astype(BF)


def over_core(keep, send):
    got = swap(send, 1)
    return [(keep[j].astype(F32) + got[j].astype(F32)).astype(keep.dtype) for j in range(4)]


def to_plane(parts):
    return [swap(parts[1], 2), swap(parts[2], 4), swap(parts[3], 6)]


def plane_sum(own, got):
    line = [sum((g[rz].astype(F32) for g in got), own[rz].astype(F32)) for rz in range(4)]
    return line[0], [v.astype(own.dtype) for v in line[1:]]


def over_line(others):
    return [swap(v, 8 * (rz + 1)) for rz, v in enumerate(others)]


def shares_body(own, r1, r2, r3, v, g, out):
    s = own[...] + sum(r[...].astype(F32) for r in (r1, r2, r3))
    g[...] = s
    fold = lambda a: jnp.sum((a * a).reshape(-1, 8, 128), axis=0)
    t = fsum(fold(s[0:240]) + fold(s[256:400])) + s[240:241] * s[240:241]
    t = jnp.broadcast_to(jnp.sum(t, axis=1, keepdims=True), (8, 128))
    line = lax.broadcasted_iota(jnp.int32, (8, 128), 0)
    out[...] = jnp.where(line < 4, v[...], t)


def shares(own, got, v):
    return pl.pallas_call(
        shares_body, out_shape=[sd((RG, 128), F32), sd((8, 128), F32)], compiler_params=VMEM, name="shares"
    )(own, *got, v)


def total_over(s):
    s = s + swap(s, 1)
    s = (s + swap(s, 2)) + (swap(s, 4) + swap(s, 6))
    return s, swap(s, 8), swap(s, 16), swap(s, 24)


def adam_body(*refs):
    me, t0, t1, t2, t3, grads = refs[:6]
    state = refs[6:21]
    outs = refs[21:-1]
    first = refs[-1]
    total = (t0[...] + t1[...]) + (t2[...] + t3[...])
    first[...] = total
    top = total[0:4]
    norm = jnp.sqrt(jnp.broadcast_to(jnp.sum(fsum(top * top), axis=1, keepdims=True), (1, 128)) + total[4:5])
    lane = lax.broadcasted_iota(jnp.int32, (1, 128), 1)
    vec = grads[240:241, :]
    for u in range(3):
        unit = 3 * (8 * me[0] + me[1]) + u
        line = first[pl.ds(jnp.minimum(unit >> 2, 4), 1), :]
        line = pltpu.roll(line, (32 * u + 128 - 32 * (unit & 3)) & 127, 1)
        vec = vec + jnp.where(jnp.logical_and((lane >> 5) == u, unit < 16), line, 0.0)
    factor = clip_norm / jnp.maximum(norm, clip_norm)

    def put(kind, at, grad):
        clipped = grad * factor[:, : grad.shape[1]]
        mas, mom, squ = (r[at] for r in state[3 * kind : 3 * kind + 3])
        first_new = beta_first * mom + (1.0 - beta_first) * clipped
        second_new = beta_second * squ + (1.0 - beta_second) * clipped * clipped
        first_hat = first_new / (1.0 - beta_first**STEP)
        second_hat = second_new / (1.0 - beta_second**STEP)
        update = mas - rates_kind[kind] * (
            first_hat / (jnp.sqrt(second_hat) + adam_eps) + decays_kind[kind] * mas
        )
        outs[3 * kind][at] = first_new
        outs[3 * kind + 1][at] = second_new
        outs[3 * kind + 2][at] = update

    for side, base in ((0, 256), (1, 0)):
        for k in range(9):
            g = grads[base + 16 * k : base + 16 * k + 16, :]
            put(0, (9 * side + k,), jnp.concatenate([g[:, :64], g[:, 64:]], axis=0))
    put(1, (Ellipsis,), grads[208:240, :])
    g = grads[144:192, :]
    g = jnp.concatenate([jnp.concatenate([g[:, :64], g[:, 64:]], axis=0), jnp.zeros((96, 64), F32)], axis=1)
    g = jnp.concatenate([g, jnp.zeros((32, 128), F32)], axis=0).T
    put(2, (Ellipsis,), g[:64, :96])
    g = grads[192:208, :]
    put(3, (Ellipsis,), jnp.concatenate([g[:, :64], g[:, 64:]], axis=0))
    put(4, (Ellipsis,), vec[:, :96])
    outs[15][0] = norm[0, 0]


def adam(me, totals, grads, state):
    args = (*totals, grads, *state)
    return pl.pallas_call(
        adam_body,
        in_specs=[pl.BlockSpec(memory_space=pltpu.SMEM)] + [pl.BlockSpec(a.shape) for a in args],
        out_specs=[pl.BlockSpec(s.shape) for s in state] + [pl.BlockSpec(memory_space=pltpu.SMEM)],
        out_shape=[sd(s.shape, F32) for s in state] + [sd((1,), F32)],
        scratch_shapes=[pltpu.VMEM((8, 128), F32)],
        compiler_params=VMEM,
        name="clipped_adamw",
    )(me, *args)


def turned_state(state):
    out = []
    for kind in range(5):
        for a in state[3 * kind : 3 * kind + 3]:
            if kind == 0:
                a = jnp.swapaxes(a, 3, 4).reshape(18, 32, 64)
            elif kind == 2:
                a = a[0]
            elif kind < 4:
                a = jnp.swapaxes(a, 1, 2)[0]
            out.append(a)
    return out


def turned_back(results):
    out = []
    for kind in range(5):
        for a in results[3 * kind : 3 * kind + 3]:
            if kind == 0:
                a = jnp.swapaxes(a.reshape(1, 2, 9, 32, 64), 3, 4)
            elif kind == 2:
                a = a[None]
            elif kind < 4:
                a = jnp.swapaxes(a[None], 1, 2)
            out.append(a)
    return out


def per_device_here(images, timesteps, counts, cotangent, *state):
    n_img = images.shape[0]
    state = turned_state(state)
    me = jnp.stack([lax.axis_index("dp"), lax.axis_index("fsdp")]).astype(jnp.int32)
    sa, sb = pack(state[0::3])
    x = images.reshape(n_img, 256, 256)
    cot = cotangent.reshape(n_img, 256, 256)
    cf = figures(counts, x)
    emb = jax.nn.silu(sinus_embed(timesteps)).astype(BF)

    line_a = jnp.stack([sa] + [swap(sa, 8 * rz) for rz in range(1, 4)])
    rows_b = [sb] + [swap(sb, 8 * rz) for rz in range(1, 4)]
    plane_a = [line_a] + [swap(line_a, bits) for bits in (2, 4, 6)]
    rows_b, plane_a, cf = lax.optimization_barrier((rows_b, plane_a, cf))
    all_a = [p for line in plane_a for p in (line, swap(line, 1))]
    line_b = jnp.stack(rows_b)
    plane_b = [line_b] + [swap(line_b, bits) for bits in (2, 4, 6)]
    wat, vec = unpack(
        unpack_a_body, "unpack_first", me, all_a, [sd((2304, 256), BF), sd((16, 256), F32)], [pltpu.VMEM((32, 128), F32)]
    )
    wat, line_b = lax.optimization_barrier((wat, line_b))
    h0, a1 = conv_one(counts, x, cf, vec, wat)
    h0, plane_b = lax.optimization_barrier((h0, plane_b))
    all_b = [p for line in plane_b for p in (line, swap(line, 1))]
    wet, wbt, wqt, wot = unpack(
        unpack_b_body,
        "unpack_second",
        me,
        all_b,
        [sd((256, 512), BF), sd((2304, 256), BF), sd((768, 256), BF), sd((256, 256), BF)],
        [],
    )
    out, ga, dm, keep, send = middle(
        counts, x, h0, cot, a1, emb, vec, me, wet, wbt, wqt, wot, finish_all, [sd((4, 4, RG, 128), BF)] * 2
    )
    parts = over_core(keep, send)
    ga, parts = lax.optimization_barrier((ga, parts))
    plane = to_plane(parts)
    ig, v = input_grad(counts, x, ga, dm, cf, vec, me, wat, 0, n_img // NB, None)
    v, plane = lax.optimization_barrier((v, plane))
    own, others = plane_sum(parts[0], plane)
    grads, sums = shares(own, over_line(others), v)
    results = adam(me, total_over(sums), grads, state)
    return (out.reshape(images.shape), ig.reshape(images.shape), *turned_back(results[:15]), results[15].reshape(()))


def gather_flat(masters, dp, fs):
    sizes = [m.size for m in masters]
    total = sum(sizes)
    full = -(-total // 2048) * 2048
    flat = jnp.concatenate([m.reshape(-1).astype(BF) for m in masters] + [jnp.zeros((full - total,), BF)])
    flat = flat.reshape(-1, 128)
    g = lax.all_gather(lax.all_gather(flat, "dp"), "fsdp").reshape(fs, dp, full)
    out = []
    at = 0
    for n in sizes:
        out.append(g[:, :, at : at + n])
        at += n
    conv = out[0].reshape((fs, dp) + masters[0].shape[1:]).transpose(2, 3, 0, 5, 1, 4)
    conv = conv.reshape(2, 2304, 256)
    mats = []
    for p, m in zip(out[1:4], masters[1:4]):
        r, c = m.shape[1:]
        mats.append(p.reshape(fs, dp, r, c).transpose(0, 3, 1, 2).reshape(fs * c, dp * r))
    vec = out[4].transpose(1, 0, 2).reshape(12, 256).astype(F32)
    return conv, mats, vec


def reduce_flat(grads, dp, fs):
    conv, mats, vec = grads
    pieces = [conv.reshape(18, fs, 256 // fs, dp, 256 // dp).transpose(1, 3, 0, 4, 2).reshape(fs, dp, -1)]
    for g in mats:
        c, r = g.shape
        pieces.append(g.reshape(fs, c // fs, dp, r // dp).transpose(0, 2, 3, 1).reshape(fs, dp, -1))
    pieces.append(vec.reshape(dp, fs, -1).transpose(1, 0, 2))
    sizes = [p.shape[2] for p in pieces]
    total = sum(sizes)
    full = -(-total // 2048) * 2048
    pieces.append(jnp.zeros((fs, dp, full - total), F32))
    flat = jnp.concatenate(pieces, axis=2).reshape(fs, dp, -1, 128)
    part = lax.psum_scatter(flat, "fsdp", scatter_dimension=0, tiled=False)
    part = lax.psum_scatter(part, "dp", scatter_dimension=0, tiled=False).reshape(-1)
    out = []
    at = 0
    for n in sizes:
        out.append(part[at : at + n])
        at += n
    return out


def finish_whole(outs, me, dwa, dwb, dwq, dwo, de, rows, turn):
    for out, got in zip(outs, (dwa[...], dwb[...], dwq[...], dwo[...], de, rows)):
        out[...] = got


def per_device_any(images, timesteps, counts, cotangent, *state):
    masters = state[0::3]
    moments = state[1::3]
    squares = state[2::3]
    dp = lax.axis_size("dp")
    fs = lax.axis_size("fsdp")
    n_img = images.shape[0]
    me = jnp.zeros((2,), jnp.int32)
    emb = jax.nn.silu(sinus_embed(timesteps)).astype(BF)
    x = images.reshape(n_img, 256, 256)
    cot = cotangent.reshape(n_img, 256, 256)
    conv, (wet, wqt, wot), vec = gather_flat(masters, dp, fs)
    vec = jnp.pad(vec, ((0, 4), (0, 0)))
    cf = figures(counts, x)
    h0, a1 = conv_one(counts, x, cf, vec, conv[0])
    ends = [sd(s, F32) for s in ((768, 768), (768, 768), (256, 768), (256, 256), (256, 512), (16, 256))]
    out, ga, dm, dwa, dwb, dwq, dwo, de, rows = middle(
        counts, x, h0, cot, a1, emb, vec, me, wet, conv[1], wqt, wot, finish_whole, ends
    )
    ig, first = input_grad(counts, x, ga, dm, cf, vec, me, conv[0], 0, n_img // NB, None)
    first = jnp.pad(first[:4].reshape(2, 256), ((0, 14), (0, 0)))
    apart = lambda w: w.reshape(3, 256, 3, 256).transpose(0, 2, 1, 3).reshape(9, 256, 256)
    shares_here = reduce_flat(
        (jnp.stack([apart(dwa), apart(dwb)]), (de, dwq.T, dwo), (rows + first)[:12]), dp, fs
    )
    local = sum(jnp.sum(s * s) for s in shares_here)
    norm = jnp.sqrt(lax.psum(lax.psum(local, "fsdp"), "dp"))
    factor = clip_norm / jnp.maximum(norm, clip_norm)
    results = []
    for kind in range(5):
        clipped = shares_here[kind].reshape(masters[kind].shape) * factor
        first_new = beta_first * moments[kind] + (1.0 - beta_first) * clipped
        second_new = beta_second * squares[kind] + (1.0 - beta_second) * clipped * clipped
        first_hat = first_new / (1.0 - beta_first**STEP)
        second_hat = second_new / (1.0 - beta_second**STEP)
        update_new = masters[kind] - rates_kind[kind] * (
            first_hat / (jnp.sqrt(second_hat) + adam_eps) + decays_kind[kind] * masters[kind]
        )
        results += [first_new, second_new, update_new]
    return (out.reshape(images.shape), ig.reshape(images.shape), *results, norm)


def solution(mesh):
    both = P(("dp", "fsdp"), None, None, None)
    one = P(("dp", "fsdp"))
    conv = P(None, None, None, "dp", "fsdp")
    mat = P(None, "dp", "fsdp")
    vec = P(None, ("dp", "fsdp"))
    trios = (conv,) * 3 + (mat,) * 9 + (vec,) * 3
    here = mesh.shape["dp"] == 4 and mesh.shape["fsdp"] == 8
    return jax.shard_map(
        per_device_here if here else per_device_any,
        mesh=mesh,
        in_specs=(both, one, one, both) + trios,
        out_specs=(both, both) + trios + (P(),),
        check_vma=False,
    )
```

```python
import math

import jax
import jax.numpy as jnp
from jax import lax
from jax.experimental import pallas as pl
from jax.experimental.pallas import tpu as pltpu
from jax.sharding import PartitionSpec as P

BF = jnp.bfloat16
F32 = jnp.float32
EPS = 1e-6
E = 512
STEP = 10
clip_norm = 1.0
beta_first = 0.9
beta_second = 0.999
adam_eps = 1e-08
rates_kind = (0.01, 0.03, 0.02, 0.05, 0.3)
decays_kind = (0.1, 0.1, 0.1, 0.1, 0.0)
AXES = ("dp", "fsdp")
VMEM = pltpu.CompilerParams(vmem_limit_bytes=60 * 2**20)
NB = 4
HB = 2
CH = 32
R = range(0, 256, CH)
RA = 160
RB = 240
RG = 400

sd = jax.ShapeDtypeStruct


def dot(a, b):
    return lax.dot_general(a, b, (((1,), (0,)), ((), ())), preferred_element_type=F32)


def dot_nt(a, b):
    return lax.dot_general(a, b, (((1,), (1,)), ((), ())), preferred_element_type=F32)


def dot_tn(a, b):
    return lax.dot_general(a, b, (((0,), (0,)), ((), ())), preferred_element_type=F32)


def gsum(s):
    n = s.shape[0]
    c = jnp.concatenate([s[:, :128], s[:, 128:]], axis=0)
    lane = lax.broadcasted_iota(jnp.int32, c.shape, 1)
    for k in (1, 2, 4):
        up = pltpu.roll(c, 128 - k, 1)
        down = pltpu.roll(c, k, 1)
        c = c + jnp.where((lane & k) == 0, up, down)
    return jnp.concatenate([c[:n], c[n:]], axis=1)


def csum(v):
    return jnp.sum(v.reshape(-1, 8, v.shape[-1]), axis=0)


def fsum(v):
    return jnp.sum(v, axis=0, keepdims=True)


def row_sums(load, base):
    s1 = s2 = None
    for r in R:
        v = load(r) - base
        a = csum(v)
        b = csum(v * v)
        s1 = a if s1 is None else s1 + a
        s2 = b if s2 is None else s2 + b
    return fsum(s1), fsum(s2)


def stats(loads, extras=None):
    firsts = [load(0)[0:1] for load in loads]
    p = jnp.concatenate(firsts, axis=0)
    if extras is not None:
        p = p + jnp.concatenate(extras, axis=0)
    q = gsum(p) * 0.125
    sums = [row_sums(load, first) for load, first in zip(loads, firsts)]
    s1 = jnp.concatenate([t[0] for t in sums], axis=0)
    s2 = jnp.concatenate([t[1] for t in sums], axis=0)
    d = p - q
    g = gsum(jnp.concatenate([s1 + 256.0 * d, s2 + d * (2.0 * s1 + 256.0 * d)], axis=0)) * (1.0 / 2048.0)
    n = len(loads)
    dm = g[:n]
    return q + dm, lax.rsqrt(g[n:] - dm * dm + EPS)


def back_coefs(sum_dy, sum_dyn, gain, rs, m):
    n = sum_dy.shape[0]
    g = gsum(jnp.concatenate([sum_dy * gain, sum_dyn * gain], axis=0)) * (1.0 / 2048.0)
    be = -rs * rs * g[n:]
    return rs * gain, be, -rs * g[:n] - m * be


def put3(pref, n, r, a, rev=False):
    rows = a.shape[0]
    col = lax.broadcasted_iota(jnp.int32, a.shape, 0) & 15
    prev = jnp.where(col == 0, 0.0, pltpu.roll(a, 1, 0))
    post = jnp.where(col == 15, 0.0, pltpu.roll(a, rows - 1, 0))
    lo, hi = (post, prev) if rev else (prev, post)
    low = a.astype(BF)
    pref[n, 16 + r : 16 + r + rows, 0:256] = lo.astype(BF)
    pref[n, 16 + r : 16 + r + rows, 256:512] = low
    pref[n, 16 + r : 16 + r + rows, 512:768] = hi.astype(BF)
    return low


def zero_pads(pref):
    z = jnp.zeros((16, 768), BF)
    for n in range(NB):
        pref[n, 0:16, :] = z
        pref[n, 272:288, :] = z


def conv_forward(pref, wt_ref, N):
    acc = None
    for i in range(3):
        for j in range(3):
            rows = pref[N.start : N.stop, 16 * i : 16 * i + 256, 256 * j : 256 * j + 256]
            k = 3 * i + j
            d = dot_nt(rows.reshape(len(N) * 256, 256), wt_ref[256 * k : 256 * k + 256, :])
            acc = d if acc is None else acc + d
    return acc


def conv_turned(pref, wt_ref, N):
    acc = None
    for i in range(3):
        o = 16 * (2 - i)
        rows = pref[N.start : N.stop, o : o + 256, :].reshape(len(N) * 256, 768)
        d = dot(rows, wt_ref[768 * i : 768 * i + 768, :])
        acc = d if acc is None else acc + d
    return acc


def add_taps(acc_ref, gt, pref, N):
    for i in range(3):
        rows = pref[N.start : N.stop, 16 * i : 16 * i + 256, :].reshape(len(N) * 256, 768)
        acc_ref[256 * i : 256 * i + 256, :] += dot(gt, rows)


def interleave(gens):
    gens = list(gens)
    done = [False] * len(gens)
    at = 0
    while not all(done):
        for j, g in enumerate(gens):
            if not done[j] and at >= j:
                try:
                    next(g)
                except StopIteration:
                    done[j] = True
        at += 1


def parts():
    return [range(j, j + HB) for j in range(0, NB, HB)]


def row(ref, j):
    return ref[j : j + 1, :]


def whole(shape):
    return pl.BlockSpec(shape, lambda i, c: (0,) * len(shape))


def clamped(i, c):
    return jnp.minimum(i, (c[0] - 1) // NB)


def blocks(*tail):
    return pl.BlockSpec((NB,) + tail, lambda i, c: (clamped(i, c),) + (0,) * len(tail))


def out_blocks(*tail):
    return pl.BlockSpec((NB,) + tail, lambda i, c: (i,) + (0,) * len(tail))


def image_call(body, name, n_img, cost, in_specs, out_specs, out_shape, scratch, args):
    products, passes = cost
    return pl.pallas_call(
        body,
        grid_spec=pltpu.PrefetchScalarGridSpec(
            num_scalar_prefetch=1,
            grid=(n_img // NB,),
            in_specs=in_specs,
            out_specs=out_specs,
            scratch_shapes=scratch,
        ),
        out_shape=out_shape,
        cost_estimate=pl.CostEstimate(
            flops=n_img * products * 2 * 256**3,
            transcendentals=n_img * passes * 256**2,
            bytes_accessed=n_img * passes * 4 * 256**2,
        ),
        compiler_params=VMEM,
        name=name,
    )(*args)


def figures_body(cnt_ref, x_ref, cf_ref):
    @pl.when(pl.program_id(0) * NB < cnt_ref[0])
    def _():
        m, rs = stats([lambda r, n=n: x_ref[n, r : r + CH, :].astype(F32) for n in range(NB)])
        for n in range(NB):
            cf_ref[n] = jnp.concatenate([m[n : n + 1], rs[n : n + 1], jnp.zeros((6, 256), F32)], axis=0)


def figures(cnt, x):
    n = x.shape[0]
    return image_call(
        figures_body, "figures", n, (1, 2), [blocks(256, 256)], out_blocks(8, 256), sd((n, 8, 256), F32), [], (cnt, x)
    )


def conv_one_body(fill, *refs):
    cnt_ref, x_ref, cf_ref, me_ref = refs[:4]
    given = refs[4:-6]
    h0_ref, a1_ref, wat_ref, vec_ref, pa, vrows = refs[-6:]

    @pl.when(pl.program_id(0) == 0)
    def _():
        zero_pads(pa)
        fill(me_ref, *given, wat_ref, vec_ref, vrows)

    @pl.when(pl.program_id(0) * NB < cnt_ref[0])
    def _():
        def part(N):
            for n in N:
                sc = 0.5 * cf_ref[n, 1:2, :] * row(vec_ref, 0)
                sh = 0.5 * row(vec_ref, 1) - cf_ref[n, 0:1, :] * sc
                for r in R:
                    h = x_ref[n, r : r + CH, :].astype(F32) * sc + sh
                    a1_ref[n, r : r + CH, :] = put3(pa, n, r, h + h * jnp.tanh(h))
            yield
            h0_ref[N.start : N.stop] = conv_forward(pa, wat_ref, N).reshape(len(N), 256, 256)
            yield

        interleave([part(N) for N in parts()])


def conv_one(cnt, x, cf, me, given, fill):
    n = x.shape[0]
    return image_call(
        lambda *refs: conv_one_body(fill, *refs),
        "conv_one",
        n,
        (18, 10),
        [blocks(256, 256), blocks(8, 256), pl.BlockSpec(memory_space=pltpu.SMEM)] + [whole(g.shape) for g in given],
        [out_blocks(256, 256), out_blocks(256, 256), whole((2304, 256)), whole((16, 256))],
        [sd((n, 256, 256), F32), sd((n, 256, 256), BF), sd((2304, 256), BF), sd((16, 256), F32)],
        [pltpu.VMEM((NB, 288, 768), BF), pltpu.VMEM((32, 128), F32)],
        (cnt, x, cf, me, *given),
    )


def middle_body(fill, n_given, finish, n_out, *refs):
    (cnt_ref, x_ref, h0_ref, cot_ref, a1_ref, emb_ref, vec_ref, me_ref) = refs[:8]
    given = refs[8 : 8 + n_given]
    refs = refs[8 + n_given :]
    out_ref, ga_ref, dm_ref = refs[:3]
    ends = refs[3 : 3 + n_out]
    refs = refs[3 + n_out :]
    (pa, pg, pa1, gt, gt1, mid, a3, mx, dmx, dz, she, dsr, dwa, dwb, dwq, dwo, dvec, turn) = refs[:18]
    wet_ref, wbt_ref, wqt_ref, wot_ref = refs[18:]
    i = pl.program_id(0)
    cnt = cnt_ref[0]

    @pl.when(i == 0)
    def _():
        zero_pads(pa)
        zero_pads(pg)
        zero_pads(pa1)
        for ref in (dwa, dwb, dwq, dwo, dvec, dsr):
            ref[...] = jnp.zeros_like(ref)
        fill(me_ref, *given, wet_ref, wbt_ref, wqt_ref, wot_ref)
        she[...] = dot_nt(emb_ref[...], wet_ref[...]) + (row(vec_ref, 2) + row(vec_ref, 3))

    live = i * NB < cnt

    @pl.when(jnp.logical_not(live))
    def _():
        for ref in (out_ref, ga_ref, dm_ref):
            ref[...] = jnp.zeros_like(ref)

    @pl.when(live)
    def _():
        g2, b2, c2, g3, b3, qb, vb, ob = (row(vec_ref, j) for j in range(4, 12))
        tot = {}

        def add(key, v):
            tot[key] = v if key not in tot else tot[key] + v

        def part(N):
            lo = N.start * 256
            hi = N.stop * 256
            W = range(len(N))
            L = lambda j: slice(j * 256, j * 256 + 256)
            masks = [(i * NB + n < cnt).astype(F32) for n in N]
            shifts = [she[pl.ds(i * NB + n, 1), :] for n in N]
            br = jnp.concatenate(shifts, axis=0)
            hload = [lambda r, n=n: h0_ref[n, r : r + CH, :] for n in N]
            m2, rs2 = stats(hload, shifts)
            sc2 = 0.5 * rs2 * g2
            sh2 = 0.5 * b2 + (br - m2) * sc2
            hm2 = br - m2
            for j, n in enumerate(N):
                for r in R:
                    h = hload[j](r) * sc2[j : j + 1] + sh2[j : j + 1]
                    put3(pa, n, r, h + h * jnp.tanh(h))
            yield
            o = conv_forward(pa, wbt_ref, N)
            yield
            for j, n in enumerate(N):
                for r in R:
                    mid[n, r : r + CH, :] = o[j * 256 + r : j * 256 + r + CH] + (x_ref[n, r : r + CH, :].astype(F32) + c2)
            mload = [lambda r, n=n: mid[n, r : r + CH, :] for n in N]
            m3, rs3 = stats(mload)
            sc3 = rs3 * g3
            sh3 = b3 - m3 * sc3
            for j, n in enumerate(N):
                for r in R:
                    a3[n * 256 + r : n * 256 + r + CH, :] = (mload[j](r) * sc3[j : j + 1] + sh3[j : j + 1]).astype(BF)
            gob = []
            for j, n in enumerate(N):
                go = cot_ref[n].astype(F32) * masks[j]
                add("ob", csum(go))
                gob.append(go.astype(BF))
            gall = jnp.concatenate(gob, axis=0)
            yield
            bc = jnp.concatenate([qb, jnp.zeros_like(qb), vb], axis=1)
            mx[lo:hi] = (dot_nt(a3[lo:hi], wqt_ref[...]) + bc).astype(BF)
            M = lambda j, p: mx[lo + j * 256 : lo + j * 256 + 256, 256 * p : 256 * p + 256]
            datt = dot(gall, wot_ref[...]).astype(BF)
            yield
            st = [dot_nt(M(j, 1), M(j, 0)) for j in W]
            dpt = [dot_nt(M(j, 2), datt[L(j)]) for j in W]
            yield
            pts = []
            ptb = []
            for j in W:
                s = st[j] * 0.0625
                e = jnp.exp(s - jnp.max(s, axis=0, keepdims=True))
                p = e * (1.0 / jnp.sum(e, axis=0, keepdims=True))
                pts.append(p)
                ptb.append(p.astype(BF))
            yield
            att = [dot_tn(ptb[j], M(j, 2)).astype(BF) for j in W]
            dv = [dot(ptb[j], datt[L(j)]).astype(BF) for j in W]
            yield
            dst = []
            for n in N:
                for r in R:
                    put3(pa1, n, r, a1_ref[n, r : r + CH, :].astype(F32))
            for j in W:
                t = dpt[j] * pts[j]
                dst.append((t - pts[j] * jnp.sum(t, axis=0, keepdims=True)).astype(BF))
            yield
            attall = jnp.concatenate(att, axis=0)
            proj = dot_nt(attall, wot_ref[...])
            dwo[...] += dot_tn(gall, attall)
            dq = [(dot_tn(dst[j], M(j, 1)) * 0.0625).astype(BF) for j in W]
            dk = [(dot(dst[j], M(j, 0)) * 0.0625).astype(BF) for j in W]
            yield
            for j, n in enumerate(N):
                out_ref[n] = (mid[n] + (proj[L(j)] + ob)) * masks[j]
                s = slice(n * 256, n * 256 + 256)
                dmx[s, 0:256] = dq[j]
                dmx[s, 256:512] = dk[j]
                dmx[s, 512:768] = dv[j]
                add("qb", csum(dq[j].astype(F32)))
                add("vb", csum(dv[j].astype(F32)))
            yield
            d3 = dot(dmx[lo:hi], wqt_ref[...])
            dwq[...] += dot_tn(a3[lo:hi], dmx[lo:hi])
            yield
            As = []
            Bs = []
            for j, n in enumerate(N):
                A = B = jnp.zeros((8, 256), F32)
                for r in R:
                    dy = d3[j * 256 + r : j * 256 + r + CH]
                    A = A + csum(dy)
                    B = B + csum(dy * (mid[n, r : r + CH, :] - m3[j : j + 1]))
                As.append(fsum(A))
                Bs.append(fsum(B))
            A3 = jnp.concatenate(As, axis=0)
            B3 = jnp.concatenate(Bs, axis=0) * rs3
            add("b3", fsum(A3))
            add("g3", fsum(B3))
            al, be, ga = back_coefs(A3, B3, g3, rs3, m3)
            for j, n in enumerate(N):
                for r in R:
                    dm = cot_ref[n, r : r + CH, :].astype(F32) * masks[j] + (
                        d3[j * 256 + r : j * 256 + r + CH] * al[j : j + 1]
                        + (mid[n, r : r + CH, :] * be[j : j + 1] + ga[j : j + 1])
                    )
                    dm_ref[n, r : r + CH, :] = dm
                    add("c2", csum(dm))
                    put3(pg, n, r, dm, True)
                gt[:, n * 256 : n * 256 + 256] = pg[n, 16:272, 256:512].T
            yield
            o = conv_turned(pg, wbt_ref, N)
            add_taps(dwb, gt[:, lo:hi], pa, N)
            yield
            As = []
            Bs = []
            for j, n in enumerate(N):
                A = B = jnp.zeros((8, 256), F32)
                for r in R:
                    h0 = hload[j](r)
                    h = h0 * sc2[j : j + 1] + sh2[j : j + 1]
                    t = jnp.tanh(h)
                    dzz = o[j * 256 + r : j * 256 + r + CH] * ((1.0 + t) * (1.0 + (h - h * t)))
                    dz[n * 256 + r : n * 256 + r + CH, :] = dzz
                    A = A + csum(dzz)
                    B = B + csum(dzz * (h0 + hm2[j : j + 1]))
                As.append(fsum(A))
                Bs.append(fsum(B))
            A2 = jnp.concatenate(As, axis=0) * 0.5
            B2 = jnp.concatenate(Bs, axis=0) * (rs2 * 0.5)
            add("b2", fsum(A2))
            add("g2", fsum(B2))
            al, be, ga = back_coefs(A2, B2, g2, rs2, -hm2)
            al = al * 0.5
            for j, n in enumerate(N):
                ds = jnp.zeros((8, 256), F32)
                for r in R:
                    dh = dz[n * 256 + r : n * 256 + r + CH, :] * al[j : j + 1] + (
                        hload[j](r) * be[j : j + 1] + ga[j : j + 1]
                    )
                    ga_ref[n, r : r + CH, :] = dh.astype(BF)
                    ds = ds + csum(dh)
                dsr[pl.ds(i * NB + n, 1), :] = fsum(ds)
                gt1[:, n * 256 : n * 256 + 256] = ga_ref[n].T
            yield
            add_taps(dwa, gt1[:, lo:hi], pa1, N)
            yield

        interleave([part(N) for N in parts()])
        z = jnp.zeros((4, 256), F32)
        rows = [tot["g2"], tot["b2"], fsum(tot["c2"]), tot["g3"], tot["b3"]]
        rows += [fsum(tot[k]) for k in ("qb", "vb", "ob")]
        dvec[...] += jnp.concatenate([z] + rows + [z], axis=0)

    @pl.when(i == pl.num_programs(0) - 1)
    def _():
        ds = dsr[...]
        total = fsum(ds)
        rows = jnp.concatenate([jnp.zeros((2, 256), F32), total, total, dvec[4:16, :]], axis=0)
        finish(ends, me_ref, dwa, dwb, dwq, dwo, dot_tn(ds.astype(BF), emb_ref[...]), rows, turn)


def middle(cnt, x, h0, cot, a1, emb, vec, me, given, fill, finish, ends):
    n = x.shape[0]
    V = pltpu.VMEM
    return image_call(
        lambda *refs: middle_body(fill, len(given), finish, len(ends), *refs),
        "middle",
        n,
        (108, 44),
        [blocks(256, 256)] * 4
        + [whole(emb.shape), whole((16, 256)), pl.BlockSpec(memory_space=pltpu.SMEM)]
        + [whole(w.shape) for w in given],
        [out_blocks(256, 256)] * 3 + [whole(e.shape) for e in ends],
        [sd((n, 256, 256), F32), sd((n, 256, 256), BF), sd((n, 256, 256), F32)] + list(ends),
        [
            V((NB, 288, 768), BF),
            V((NB, 288, 768), BF),
            V((NB, 288, 768), BF),
            V((256, NB * 256), BF),
            V((256, NB * 256), BF),
            V((NB, 256, 256), F32),
            V((NB * 256, 256), BF),
            V((NB * 256, 768), BF),
            V((NB * 256, 768), BF),
            V((NB * 256, 256), F32),
            V((n, 256), F32),
            V((n, 256), F32),
            V((768, 768), F32),
            V((768, 768), F32),
            V((256, 768), F32),
            V((256, 256), F32),
            V((16, 256), F32),
            V((1280, 512), F32),
            V((256, 512), BF),
            V((2304, 256), BF),
            V((768, 256), BF),
            V((256, 256), BF),
        ],
        (cnt, x, h0, cot, a1, emb, vec, me, *given),
    )


def input_grad_body(base, *refs):
    cnt_ref, x_ref, ga_ref, dm_ref, cf_ref, vec_ref, me_ref, wat_ref = refs[:8]
    ig_ref, dvec, pg, dz = refs[-4:]
    i = pl.program_id(0)

    @pl.when(i == 0)
    def _():
        zero_pads(pg)
        dvec[...] = jnp.zeros_like(dvec)

    live = (i + base) * NB < cnt_ref[0]

    @pl.when(jnp.logical_not(live))
    def _():
        ig_ref[...] = jnp.zeros_like(ig_ref)

    @pl.when(live)
    def _():
        g1 = row(vec_ref, 0)
        tot = {}

        def add(key, v):
            tot[key] = v if key not in tot else tot[key] + v

        def part(N):
            for n in N:
                for r in R:
                    put3(pg, n, r, ga_ref[n, r : r + CH, :].astype(F32), True)
            yield
            o = conv_turned(pg, wat_ref, N)
            yield
            As = []
            Bs = []
            ms = jnp.concatenate([cf_ref[n, 0:1, :] for n in N], axis=0)
            rss = jnp.concatenate([cf_ref[n, 1:2, :] for n in N], axis=0)
            for j, n in enumerate(N):
                m = cf_ref[n, 0:1, :]
                sc = 0.5 * cf_ref[n, 1:2, :] * g1
                sh = 0.5 * row(vec_ref, 1) - m * sc
                A = B = jnp.zeros((8, 256), F32)
                for r in R:
                    x = x_ref[n, r : r + CH, :].astype(F32)
                    h = x * sc + sh
                    t = jnp.tanh(h)
                    dzz = o[j * 256 + r : j * 256 + r + CH] * ((1.0 + t) * (1.0 + (h - h * t)))
                    dz[n * 256 + r : n * 256 + r + CH, :] = dzz
                    A = A + csum(dzz)
                    B = B + csum(dzz * (x - m))
                As.append(fsum(A))
                Bs.append(fsum(B))
            A1 = jnp.concatenate(As, axis=0) * 0.5
            B1 = jnp.concatenate(Bs, axis=0) * (rss * 0.5)
            add("b1", fsum(A1))
            add("g1", fsum(B1))
            al, be, ga = back_coefs(A1, B1, g1, rss, ms)
            al = al * 0.5
            for j, n in enumerate(N):
                for r in R:
                    ig_ref[n, r : r + CH, :] = dm_ref[n, r : r + CH, :] + (
                        dz[n * 256 + r : n * 256 + r + CH, :] * al[j : j + 1]
                        + (x_ref[n, r : r + CH, :].astype(F32) * be[j : j + 1] + ga[j : j + 1])
                    )
            yield

        interleave([part(N) for N in parts()])
        g = tot["g1"]
        b = tot["b1"]
        z = jnp.zeros((4, 128), F32)
        dvec[...] += jnp.concatenate([g[:, :128], g[:, 128:], b[:, :128], b[:, 128:], z], axis=0)


def input_grad(cnt, x, ga, dm, cf, vec, me, wat, base, steps, got):
    n = x.shape[0]
    at = lambda i, c: jnp.minimum(i + base, jnp.maximum((c[0] - 1) // NB, base))
    block = lambda *tail: pl.BlockSpec((NB,) + tail, lambda i, c: (at(i, c),) + (0,) * len(tail))
    args = (cnt, x, ga, dm, cf, vec, me, wat)
    in_specs = [block(256, 256)] * 3 + [block(8, 256), whole((16, 256))]
    in_specs += [pl.BlockSpec(memory_space=pltpu.SMEM), whole(wat.shape)]
    alias = {}
    if got is not None:
        alias = {len(args): 0}
        args += (got,)
        in_specs += [pl.BlockSpec(memory_space=pl.ANY)]
    return pl.pallas_call(
        lambda *refs: input_grad_body(base, *refs),
        grid_spec=pltpu.PrefetchScalarGridSpec(
            num_scalar_prefetch=1,
            grid=(steps,),
            in_specs=in_specs,
            out_specs=[
                pl.BlockSpec((NB, 256, 256), lambda i, c: (i + base, 0, 0)),
                pl.BlockSpec((8, 128), lambda i, c: (0, 0)),
            ],
            scratch_shapes=[pltpu.VMEM((NB, 288, 768), BF), pltpu.VMEM((NB * 256, 256), F32)],
        ),
        out_shape=[sd((n, 256, 256), F32), sd((8, 128), F32)],
        input_output_aliases=alias,
        cost_estimate=pl.CostEstimate(
            flops=steps * NB * 24 * 2 * 256**3, transcendentals=0, bytes_accessed=steps * NB * 14 * 4 * 256**2
        ),
        compiler_params=VMEM,
        name="input_grad",
    )(*args)


def sinus_embed(steps_in):
    half_width = E // 2
    frequency = jnp.exp(
        -math.log(10000.0) * jnp.arange(half_width, dtype=jnp.float32) / (half_width - 1)
    )
    angles = steps_in.astype(jnp.float32)[:, None] * frequency[None, :]
    return jnp.concatenate([jnp.sin(angles), jnp.cos(angles)], axis=1)


def halves(s0, s1):
    first = jnp.concatenate([s0[:, :64], s1[:, :64]], axis=1)
    second = jnp.concatenate([s0[:, 64:], s1[:, 64:]], axis=1)
    return first, second


def pack_body(conv, embed, attend, output, vec, a_ref, b_ref):
    for side, ref, base in ((0, a_ref, 0), (1, b_ref, 32)):
        for k in range(9):
            w = conv[9 * side + k]
            ref[base + 16 * k : base + 16 * k + 16, :] = jnp.concatenate([w[:16], w[16:]], axis=1).astype(BF)
    line = jnp.concatenate([vec[...], jnp.zeros((1, 32), F32)], axis=1)
    a_ref[144:160, :] = jnp.broadcast_to(line, (16, 128)).astype(BF)
    b_ref[0:32, :] = embed[...].astype(BF)
    at = jnp.concatenate([attend[...], jnp.zeros((64, 32), F32)], axis=1).T
    b_ref[176:224, :] = jnp.concatenate([at[:48], at[48:96]], axis=1).astype(BF)
    o = output[...]
    b_ref[224:240, :] = jnp.concatenate([o[:16], o[16:]], axis=1).astype(BF)


def pack(masters):
    return pl.pallas_call(
        pack_body, out_shape=[sd((RA, 128), BF), sd((RB, 128), BF)], compiler_params=VMEM, name="pack_shards"
    )(*masters)


def swap(x, bits):
    return lax.ppermute(x, AXES, [(i, i ^ bits) for i in range(32)])


def pairs(g, z, lo, rows, h):
    s0 = g[z ^ (2 * h), lo : lo + rows, :]
    s1 = g[z ^ (2 * h + 1), lo : lo + rows, :]
    return halves(s0, s1)


def unpack_a(me, *refs):
    gs = refs[:8]
    wat_ref, vec_ref, vrows = refs[8:]
    z = me[0]
    f = me[1]
    for rf in range(8):
        d0 = (f ^ rf) * 32
        for h in range(2):
            for k in range(9):
                j0, j1 = pairs(gs[rf], z, 16 * k, 16, h)
                at = pl.multiple_of(256 * k + d0, 32)
                wat_ref[pl.ds(at, 16), 128 * h : 128 * h + 128] = j0
                wat_ref[pl.ds(at + 16, 16), 128 * h : 128 * h + 128] = j1
        for rz in range(4):
            vrows[pl.ds((z ^ rz) * 8 + (f ^ rf), 1), :] = gs[rf][rz, 144:160, :].astype(F32)[0:1]
    v = vrows[...]
    v3 = jnp.concatenate([v, pltpu.roll(v, 96, 1), pltpu.roll(v, 64, 1)], axis=0).astype(BF)
    col = lax.broadcasted_iota(jnp.int32, (16, 96), 1)
    line = lax.broadcasted_iota(jnp.int32, (16, 96), 0)
    unit = 3 * (col & 31) + (col >> 5)
    lane = lax.broadcasted_iota(jnp.int32, (16, 128), 1)
    for half in range(2):
        acc = jnp.zeros((16, 128), F32)
        for t in range(4):
            sel = jnp.where(unit == 8 * line + 4 * half + t, 1.0, 0.0).astype(BF)
            piece = dot(sel, v3)
            if t:
                piece = pltpu.roll(piece, 32 * t, 1)
            acc = jnp.where((lane >> 5) == t, piece, acc)
        vec_ref[:, 128 * half : 128 * half + 128] = acc


def unpack_b(me, *refs):
    gs = refs[:8]
    wet_ref, wbt_ref, wqt_ref, wot_ref = refs[8:]
    z = me[0]
    f = me[1]
    for rf in range(8):
        own = f ^ rf
        d0 = own * 32
        g = gs[rf]
        for d in range(4):
            wet_ref[pl.ds(pl.multiple_of(d0, 32), 32), 128 * d : 128 * d + 128] = g[z ^ d, 0:32, :]
        for h in range(2):
            lanes = slice(128 * h, 128 * h + 128)
            for k in range(9):
                j0, j1 = pairs(g, z, 32 + 16 * k, 16, h)
                at = pl.multiple_of(256 * k + d0, 32)
                wbt_ref[pl.ds(at, 16), lanes] = j0
                wbt_ref[pl.ds(at + 16, 16), lanes] = j1
            j0, j1 = pairs(g, z, 176, 48, h)
            at = pl.multiple_of(own * 96, 32)
            wqt_ref[pl.ds(at, 48), lanes] = j0
            wqt_ref[pl.ds(at + 48, 48), lanes] = j1
            j0, j1 = pairs(g, z, 224, 16, h)
            at = pl.multiple_of(d0, 32)
            wot_ref[pl.ds(at, 16), lanes] = j0
            wot_ref[pl.ds(at + 16, 16), lanes] = j1


def place(outs, me, src, base, lanes, lo, rows, step):
    z = me[0]
    f = me[1]
    for rf in range(8):
        at = pl.multiple_of(base + (f ^ rf) * step, 16)
        ref = outs[rf & 1]
        for h in range(2):
            cut = slice(lanes + 128 * h, lanes + 128 * h + 128)
            e0, e1 = halves(src[pl.ds(at, rows), cut], src[pl.ds(at + rows, rows), cut])
            ref[rf >> 1, z ^ (2 * h), lo : lo + rows, :] = e0.astype(BF)
            ref[rf >> 1, z ^ (2 * h + 1), lo : lo + rows, :] = e1.astype(BF)


def spread_rows(rows, me):
    a8 = []
    for s in range(8):
        piece = rows[:, 128 * (s // 4) : 128 * (s // 4) + 128]
        a8.append(pltpu.roll(piece, 128 - 32 * (s % 4), 1) if s % 4 else piece)
    a8 = jnp.concatenate(a8, axis=0)
    top = a8.astype(BF)
    rest = (a8 - top.astype(F32)).astype(BF)
    col = lax.broadcasted_iota(jnp.int32, (32, 128), 1)
    line = lax.broadcasted_iota(jnp.int32, (32, 128), 0)
    owner = ((line & 3) ^ me[0]) * 8 + ((line >> 2) ^ me[1])
    acc = jnp.zeros((32, 128), F32)
    unit = 8 * (col & 15) + (col >> 4)
    for u in range(3):
        sel = jnp.where(unit == 3 * owner + u, 1.0, 0.0).astype(BF)
        piece = dot(sel, top) + dot(sel, rest)
        if u:
            piece = pltpu.roll(piece, 32 * u, 1)
        acc = jnp.where((col >> 5) == u, piece, acc)
    return acc


def finish_all(outs, me, dwa, dwb, dwq, dwo, de, rows, turn):
    for k in range(9):
        place(outs, me, dwa, 256 * (k // 3), 256 * (k % 3), 256 + 16 * k, 16, 32)
        place(outs, me, dwb, 256 * (k // 3), 256 * (k % 3), 16 * k, 16, 32)
    for k in range(3):
        turn[256 * k : 256 * k + 256, 0:256] = dwq[:, 256 * k : 256 * k + 256].T
    place(outs, me, turn, 0, 0, 144, 48, 96)
    place(outs, me, dwo, 0, 0, 192, 16, 32)
    turn[1024:1280, :] = de
    for d in range(4):
        for rf in range(8):
            at = pl.multiple_of(1024 + (me[1] ^ rf) * 32, 32)
            block = turn[pl.ds(at, 32), 128 * d : 128 * d + 128]
            outs[rf & 1][rf >> 1, me[0] ^ d, 208:240, :] = block.astype(BF)
    acc = spread_rows(rows, me)
    for rf in range(8):
        for rz in range(4):
            r = 4 * rf + rz
            outs[rf & 1][rf >> 1, rz, 240:256, :] = jnp.broadcast_to(acc[r : r + 1], (16, 128)).astype(BF)


def over_core(keep, send):
    got = swap(send, 1)
    return [(keep[j].astype(F32) + got[j].astype(F32)).astype(keep.dtype) for j in range(4)]


def to_plane(parts):
    return [swap(parts[1], 2), swap(parts[2], 4), swap(parts[3], 6)]


def plane_sum(own, got):
    line = [sum((g[rz].astype(F32) for g in got), own[rz].astype(F32)) for rz in range(4)]
    return line[0], [v.astype(own.dtype) for v in line[1:]]


def over_line(others):
    return [swap(v, 8 * (rz + 1)) for rz, v in enumerate(others)]


def shares_body(own, r1, r2, r3, v, g, out):
    s = own[...] + sum(r[...].astype(F32) for r in (r1, r2, r3))
    g[...] = s
    fold = lambda a: jnp.sum((a * a).reshape(-1, 8, 128), axis=0)
    t = fsum(fold(s[0:240]) + fold(s[256:400])) + s[240:241] * s[240:241]
    t = jnp.broadcast_to(jnp.sum(t, axis=1, keepdims=True), (8, 128))
    line = lax.broadcasted_iota(jnp.int32, (8, 128), 0)
    out[...] = jnp.where(line < 4, v[...], t)


def shares(own, got, v):
    return pl.pallas_call(
        shares_body, out_shape=[sd((RG, 128), F32), sd((8, 128), F32)], compiler_params=VMEM, name="shares"
    )(own, *got, v)


def total_over(s):
    s = s + swap(s, 1)
    s = (s + swap(s, 2)) + (swap(s, 4) + swap(s, 6))
    return s, swap(s, 8), swap(s, 16), swap(s, 24)


def adam_body(*refs):
    me, t0, t1, t2, t3, grads = refs[:6]
    state = refs[6:21]
    outs = refs[21:-1]
    first = refs[-1]
    total = (t0[...] + t1[...]) + (t2[...] + t3[...])
    first[...] = total
    top = total[0:4]
    norm = jnp.sqrt(jnp.broadcast_to(jnp.sum(fsum(top * top), axis=1, keepdims=True), (1, 128)) + total[4:5])
    lane = lax.broadcasted_iota(jnp.int32, (1, 128), 1)
    vec = grads[240:241, :]
    for u in range(3):
        unit = 3 * (8 * me[0] + me[1]) + u
        line = first[pl.ds(jnp.minimum(unit >> 2, 4), 1), :]
        line = pltpu.roll(line, (32 * u + 128 - 32 * (unit & 3)) & 127, 1)
        vec = vec + jnp.where(jnp.logical_and((lane >> 5) == u, unit < 16), line, 0.0)
    factor = clip_norm / jnp.maximum(norm, clip_norm)

    def put(kind, at, grad):
        clipped = grad * factor[:, : grad.shape[1]]
        mas, mom, squ = (r[at] for r in state[3 * kind : 3 * kind + 3])
        first_new = beta_first * mom + (1.0 - beta_first) * clipped
        second_new = beta_second * squ + (1.0 - beta_second) * clipped * clipped
        first_hat = first_new / (1.0 - beta_first**STEP)
        second_hat = second_new / (1.0 - beta_second**STEP)
        update = mas - rates_kind[kind] * (
            first_hat / (jnp.sqrt(second_hat) + adam_eps) + decays_kind[kind] * mas
        )
        outs[3 * kind][at] = first_new
        outs[3 * kind + 1][at] = second_new
        outs[3 * kind + 2][at] = update

    for side, base in ((0, 256), (1, 0)):
        for k in range(9):
            g = grads[base + 16 * k : base + 16 * k + 16, :]
            put(0, (9 * side + k,), jnp.concatenate([g[:, :64], g[:, 64:]], axis=0))
    put(1, (Ellipsis,), grads[208:240, :])
    g = grads[144:192, :]
    g = jnp.concatenate([jnp.concatenate([g[:, :64], g[:, 64:]], axis=0), jnp.zeros((96, 64), F32)], axis=1)
    g = jnp.concatenate([g, jnp.zeros((32, 128), F32)], axis=0).T
    put(2, (Ellipsis,), g[:64, :96])
    g = grads[192:208, :]
    put(3, (Ellipsis,), jnp.concatenate([g[:, :64], g[:, 64:]], axis=0))
    put(4, (Ellipsis,), vec[:, :96])
    outs[15][0] = norm[0, 0]


def adam(me, totals, grads, state):
    args = (*totals, grads, *state)
    return pl.pallas_call(
        adam_body,
        in_specs=[pl.BlockSpec(memory_space=pltpu.SMEM)] + [pl.BlockSpec(a.shape) for a in args],
        out_specs=[pl.BlockSpec(s.shape) for s in state] + [pl.BlockSpec(memory_space=pltpu.SMEM)],
        out_shape=[sd(s.shape, F32) for s in state] + [sd((1,), F32)],
        scratch_shapes=[pltpu.VMEM((8, 128), F32)],
        compiler_params=VMEM,
        name="clipped_adamw",
    )(me, *args)


def turned_state(state):
    out = []
    for kind in range(5):
        for a in state[3 * kind : 3 * kind + 3]:
            if kind == 0:
                a = jnp.swapaxes(a, 3, 4).reshape(18, 32, 64)
            elif kind == 2:
                a = a[0]
            elif kind < 4:
                a = jnp.swapaxes(a, 1, 2)[0]
            out.append(a)
    return out


def turned_back(results):
    out = []
    for kind in range(5):
        for a in results[3 * kind : 3 * kind + 3]:
            if kind == 0:
                a = jnp.swapaxes(a.reshape(1, 2, 9, 32, 64), 3, 4)
            elif kind == 2:
                a = a[None]
            elif kind < 4:
                a = jnp.swapaxes(a[None], 1, 2)
            out.append(a)
    return out


def per_device_here(images, timesteps, counts, cotangent, *state):
    n_img = images.shape[0]
    state = turned_state(state)
    me = jnp.stack([lax.axis_index("dp"), lax.axis_index("fsdp")]).astype(jnp.int32)
    sa, sb = pack(state[0::3])
    x = images.reshape(n_img, 256, 256)
    cot = cotangent.reshape(n_img, 256, 256)
    cf = figures(counts, x)
    emb = jax.nn.silu(sinus_embed(timesteps)).astype(BF)

    line_a = jnp.stack([sa] + [swap(sa, 8 * rz) for rz in range(1, 4)])
    rows_b = [sb] + [swap(sb, 8 * rz) for rz in range(1, 4)]
    plane_a = [line_a] + [swap(line_a, bits) for bits in (2, 4, 6)]
    rows_b, plane_a, cf = lax.optimization_barrier((rows_b, plane_a, cf))
    all_a = [p for line in plane_a for p in (line, swap(line, 1))]
    line_b = jnp.stack(rows_b)
    plane_b = [line_b] + [swap(line_b, bits) for bits in (2, 4, 6)]
    all_a, line_b = lax.optimization_barrier((all_a, line_b))
    h0, a1, wat, vec = conv_one(counts, x, cf, me, all_a, unpack_a)
    h0, plane_b = lax.optimization_barrier((h0, plane_b))
    all_b = [p for line in plane_b for p in (line, swap(line, 1))]
    out, ga, dm, keep, send = middle(
        counts, x, h0, cot, a1, emb, vec, me, all_b, unpack_b, finish_all, [sd((4, 4, RG, 128), BF)] * 2
    )
    parts = over_core(keep, send)
    ga, parts = lax.optimization_barrier((ga, parts))
    plane = to_plane(parts)
    ig, v = input_grad(counts, x, ga, dm, cf, vec, me, wat, 0, n_img // NB, None)
    v, plane = lax.optimization_barrier((v, plane))
    own, others = plane_sum(parts[0], plane)
    grads, sums = shares(own, over_line(others), v)
    results = adam(me, total_over(sums), grads, state)
    return (out.reshape(images.shape), ig.reshape(images.shape), *turned_back(results[:15]), results[15].reshape(()))


def gather_flat(masters, dp, fs):
    sizes = [m.size for m in masters]
    total = sum(sizes)
    full = -(-total // 2048) * 2048
    flat = jnp.concatenate([m.reshape(-1).astype(BF) for m in masters] + [jnp.zeros((full - total,), BF)])
    flat = flat.reshape(-1, 128)
    g = lax.all_gather(lax.all_gather(flat, "dp"), "fsdp").reshape(fs, dp, full)
    out = []
    at = 0
    for n in sizes:
        out.append(g[:, :, at : at + n])
        at += n
    conv = out[0].reshape((fs, dp) + masters[0].shape[1:]).transpose(2, 3, 0, 5, 1, 4)
    conv = conv.reshape(2, 2304, 256)
    mats = []
    for p, m in zip(out[1:4], masters[1:4]):
        r, c = m.shape[1:]
        mats.append(p.reshape(fs, dp, r, c).transpose(0, 3, 1, 2).reshape(fs * c, dp * r))
    vec = out[4].transpose(1, 0, 2).reshape(12, 256).astype(F32)
    return conv, mats, vec


def reduce_flat(grads, dp, fs):
    conv, mats, vec = grads
    pieces = [conv.reshape(18, fs, 256 // fs, dp, 256 // dp).transpose(1, 3, 0, 4, 2).reshape(fs, dp, -1)]
    for g in mats:
        c, r = g.shape
        pieces.append(g.reshape(fs, c // fs, dp, r // dp).transpose(0, 2, 3, 1).reshape(fs, dp, -1))
    pieces.append(vec.reshape(dp, fs, -1).transpose(1, 0, 2))
    sizes = [p.shape[2] for p in pieces]
    total = sum(sizes)
    full = -(-total // 2048) * 2048
    pieces.append(jnp.zeros((fs, dp, full - total), F32))
    flat = jnp.concatenate(pieces, axis=2).reshape(fs, dp, -1, 128)
    part = lax.psum_scatter(flat, "fsdp", scatter_dimension=0, tiled=False)
    part = lax.psum_scatter(part, "dp", scatter_dimension=0, tiled=False).reshape(-1)
    out = []
    at = 0
    for n in sizes:
        out.append(part[at : at + n])
        at += n
    return out


def finish_whole(outs, me, dwa, dwb, dwq, dwo, de, rows, turn):
    for out, got in zip(outs, (dwa[...], dwb[...], dwq[...], dwo[...], de, rows)):
        out[...] = got


def fill_one(me, wat, vec, wat_ref, vec_ref, vrows):
    wat_ref[...] = wat[...]
    vec_ref[...] = vec[...]


def fill_rest(me, *refs):
    for k in range(4):
        refs[4 + k][...] = refs[k][...]


def per_device_any(images, timesteps, counts, cotangent, *state):
    masters = state[0::3]
    moments = state[1::3]
    squares = state[2::3]
    dp = lax.axis_size("dp")
    fs = lax.axis_size("fsdp")
    n_img = images.shape[0]
    me = jnp.zeros((2,), jnp.int32)
    emb = jax.nn.silu(sinus_embed(timesteps)).astype(BF)
    x = images.reshape(n_img, 256, 256)
    cot = cotangent.reshape(n_img, 256, 256)
    conv, (wet, wqt, wot), vec = gather_flat(masters, dp, fs)
    vec = jnp.pad(vec, ((0, 4), (0, 0)))
    cf = figures(counts, x)
    h0, a1, wat, vec = conv_one(counts, x, cf, me, (conv[0], vec), fill_one)
    ends = [sd(s, F32) for s in ((768, 768), (768, 768), (256, 768), (256, 256), (256, 512), (16, 256))]
    out, ga, dm, dwa, dwb, dwq, dwo, de, rows = middle(
        counts, x, h0, cot, a1, emb, vec, me, (wet, conv[1], wqt, wot), fill_rest, finish_whole, ends
    )
    ig, first = input_grad(counts, x, ga, dm, cf, vec, me, conv[0], 0, n_img // NB, None)
    first = jnp.pad(first[:4].reshape(2, 256), ((0, 14), (0, 0)))
    apart = lambda w: w.reshape(3, 256, 3, 256).transpose(0, 2, 1, 3).reshape(9, 256, 256)
    shares_here = reduce_flat(
        (jnp.stack([apart(dwa), apart(dwb)]), (de, dwq.T, dwo), (rows + first)[:12]), dp, fs
    )
    local = sum(jnp.sum(s * s) for s in shares_here)
    norm = jnp.sqrt(lax.psum(lax.psum(local, "fsdp"), "dp"))
    factor = clip_norm / jnp.maximum(norm, clip_norm)
    results = []
    for kind in range(5):
        clipped = shares_here[kind].reshape(masters[kind].shape) * factor
        first_new = beta_first * moments[kind] + (1.0 - beta_first) * clipped
        second_new = beta_second * squares[kind] + (1.0 - beta_second) * clipped * clipped
        first_hat = first_new / (1.0 - beta_first**STEP)
        second_hat = second_new / (1.0 - beta_second**STEP)
        update_new = masters[kind] - rates_kind[kind] * (
            first_hat / (jnp.sqrt(second_hat) + adam_eps) + decays_kind[kind] * masters[kind]
        )
        results += [first_new, second_new, update_new]
    return (out.reshape(images.shape), ig.reshape(images.shape), *results, norm)


def solution(mesh):
    both = P(("dp", "fsdp"), None, None, None)
    one = P(("dp", "fsdp"))
    conv = P(None, None, None, "dp", "fsdp")
    mat = P(None, "dp", "fsdp")
    vec = P(None, ("dp", "fsdp"))
    trios = (conv,) * 3 + (mat,) * 9 + (vec,) * 3
    here = mesh.shape["dp"] == 4 and mesh.shape["fsdp"] == 8
    return jax.shard_map(
        per_device_here if here else per_device_any,
        mesh=mesh,
        in_specs=(both, one, one, both) + trios,
        out_specs=(both, both) + trios + (P(),),
        check_vma=False,
    )
```

```python
import math

import jax
import jax.numpy as jnp
from jax import lax
from jax.experimental import pallas as pl
from jax.experimental.pallas import tpu as pltpu
from jax.sharding import PartitionSpec as P

BF = jnp.bfloat16
F32 = jnp.float32
EPS = 1e-6
E = 512
STEP = 10
clip_norm = 1.0
beta_first = 0.9
beta_second = 0.999
adam_eps = 1e-08
rates_kind = (0.01, 0.03, 0.02, 0.05, 0.3)
decays_kind = (0.1, 0.1, 0.1, 0.1, 0.0)
AXES = ("dp", "fsdp")
VMEM = pltpu.CompilerParams(vmem_limit_bytes=60 * 2**20)
NB = 4
HB = 2
CH = 32
R = range(0, 256, CH)
RA = 160
RB = 240
RG = 384

sd = jax.ShapeDtypeStruct


def dot(a, b):
    return lax.dot_general(a, b, (((1,), (0,)), ((), ())), preferred_element_type=F32)


def dot_nt(a, b):
    return lax.dot_general(a, b, (((1,), (1,)), ((), ())), preferred_element_type=F32)


def dot_tn(a, b):
    return lax.dot_general(a, b, (((0,), (0,)), ((), ())), preferred_element_type=F32)


def gsum(s):
    n = s.shape[0]
    c = jnp.concatenate([s[:, :128], s[:, 128:]], axis=0)
    lane = lax.broadcasted_iota(jnp.int32, c.shape, 1)
    for k in (1, 2, 4):
        up = pltpu.roll(c, 128 - k, 1)
        down = pltpu.roll(c, k, 1)
        c = c + jnp.where((lane & k) == 0, up, down)
    return jnp.concatenate([c[:n], c[n:]], axis=1)


def csum(v):
    return jnp.sum(v.reshape(-1, 8, v.shape[-1]), axis=0)


def fsum(v):
    return jnp.sum(v, axis=0, keepdims=True)


def row_sums(load, base):
    s1 = s2 = None
    for r in R:
        v = load(r) - base
        a = csum(v)
        b = csum(v * v)
        s1 = a if s1 is None else s1 + a
        s2 = b if s2 is None else s2 + b
    return fsum(s1), fsum(s2)


def stats(loads, extras=None):
    firsts = [load(0)[0:1] for load in loads]
    p = jnp.concatenate(firsts, axis=0)
    if extras is not None:
        p = p + jnp.concatenate(extras, axis=0)
    q = gsum(p) * 0.125
    sums = [row_sums(load, first) for load, first in zip(loads, firsts)]
    s1 = jnp.concatenate([t[0] for t in sums], axis=0)
    s2 = jnp.concatenate([t[1] for t in sums], axis=0)
    d = p - q
    g = gsum(jnp.concatenate([s1 + 256.0 * d, s2 + d * (2.0 * s1 + 256.0 * d)], axis=0)) * (1.0 / 2048.0)
    n = len(loads)
    dm = g[:n]
    return q + dm, lax.rsqrt(g[n:] - dm * dm + EPS)


def back_coefs(sum_dy, sum_dyn, gain, rs, m):
    n = sum_dy.shape[0]
    g = gsum(jnp.concatenate([sum_dy * gain, sum_dyn * gain], axis=0)) * (1.0 / 2048.0)
    be = -rs * rs * g[n:]
    return rs * gain, be, -rs * g[:n] - m * be


def put3(pref, n, r, a, rev=False):
    rows = a.shape[0]
    col = lax.broadcasted_iota(jnp.int32, a.shape, 0) & 15
    prev = jnp.where(col == 0, 0.0, pltpu.roll(a, 1, 0))
    post = jnp.where(col == 15, 0.0, pltpu.roll(a, rows - 1, 0))
    lo, hi = (post, prev) if rev else (prev, post)
    low = a.astype(BF)
    pref[n, 16 + r : 16 + r + rows, 0:256] = lo.astype(BF)
    pref[n, 16 + r : 16 + r + rows, 256:512] = low
    pref[n, 16 + r : 16 + r + rows, 512:768] = hi.astype(BF)
    return low


def zero_pads(pref):
    z = jnp.zeros((16, 768), BF)
    for n in range(NB):
        pref[n, 0:16, :] = z
        pref[n, 272:288, :] = z


def conv_forward(pref, wt_ref, N):
    acc = None
    for i in range(3):
        for j in range(3):
            rows = pref[N.start : N.stop, 16 * i : 16 * i + 256, 256 * j : 256 * j + 256]
            k = 3 * i + j
            d = dot_nt(rows.reshape(len(N) * 256, 256), wt_ref[256 * k : 256 * k + 256, :])
            acc = d if acc is None else acc + d
    return acc


def conv_turned(pref, wt_ref, N):
    acc = None
    for i in range(3):
        o = 16 * (2 - i)
        rows = pref[N.start : N.stop, o : o + 256, :].reshape(len(N) * 256, 768)
        d = dot(rows, wt_ref[768 * i : 768 * i + 768, :])
        acc = d if acc is None else acc + d
    return acc


def add_taps(acc_ref, gt, pref, N):
    for i in range(3):
        rows = pref[N.start : N.stop, 16 * i : 16 * i + 256, :].reshape(len(N) * 256, 768)
        acc_ref[256 * i : 256 * i + 256, :] += dot(gt, rows)


def interleave(gens):
    gens = list(gens)
    done = [False] * len(gens)
    at = 0
    while not all(done):
        for j, g in enumerate(gens):
            if not done[j] and at >= j:
                try:
                    next(g)
                except StopIteration:
                    done[j] = True
        at += 1


def parts():
    return [range(j, j + HB) for j in range(0, NB, HB)]


def row(ref, j):
    return ref[j : j + 1, :]


def whole(shape):
    return pl.BlockSpec(shape, lambda i, c: (0,) * len(shape))


def clamped(i, c):
    return jnp.minimum(i, (c[0] - 1) // NB)


def blocks(*tail):
    return pl.BlockSpec((NB,) + tail, lambda i, c: (clamped(i, c),) + (0,) * len(tail))


ANY = pl.BlockSpec(memory_space=pl.ANY)


def out_blocks(*tail):
    return pl.BlockSpec((NB,) + tail, lambda i, c: (i,) + (0,) * len(tail))


def image_call(body, name, n_img, cost, in_specs, out_specs, out_shape, scratch, args):
    products, passes = cost
    return pl.pallas_call(
        body,
        grid_spec=pltpu.PrefetchScalarGridSpec(
            num_scalar_prefetch=1,
            grid=(n_img // NB,),
            in_specs=in_specs,
            out_specs=out_specs,
            scratch_shapes=scratch,
        ),
        out_shape=out_shape,
        cost_estimate=pl.CostEstimate(
            flops=n_img * products * 2 * 256**3,
            transcendentals=n_img * passes * 256**2,
            bytes_accessed=n_img * passes * 4 * 256**2,
        ),
        compiler_params=VMEM,
        name=name,
    )(*args)


def figures_body(cnt_ref, x_ref, cf_ref):
    @pl.when(pl.program_id(0) * NB < cnt_ref[0])
    def _():
        m, rs = stats([lambda r, n=n: x_ref[n, r : r + CH, :].astype(F32) for n in range(NB)])
        for n in range(NB):
            cf_ref[n] = jnp.concatenate([m[n : n + 1], rs[n : n + 1], jnp.zeros((6, 256), F32)], axis=0)


def figures(cnt, x):
    n = x.shape[0]
    return image_call(
        figures_body, "figures", n, (1, 2), [blocks(256, 256)], out_blocks(8, 256), sd((n, 8, 256), F32), [], (cnt, x)
    )


def conv_one_body(fill, *refs):
    cnt_ref, x_ref, cf_ref, me_ref = refs[:4]
    given = refs[4:-6]
    h0_ref, a1_ref, wat_ref, vec_ref, pa, vrows = refs[-6:]

    @pl.when(pl.program_id(0) == 0)
    def _():
        zero_pads(pa)
        fill(me_ref, *given, wat_ref, vec_ref, vrows)

    @pl.when(pl.program_id(0) * NB < cnt_ref[0])
    def _():
        def part(N):
            for n in N:
                sc = 0.5 * cf_ref[n, 1:2, :] * row(vec_ref, 0)
                sh = 0.5 * row(vec_ref, 1) - cf_ref[n, 0:1, :] * sc
                for r in R:
                    h = x_ref[n, r : r + CH, :].astype(F32) * sc + sh
                    a1_ref[n, r : r + CH, :] = put3(pa, n, r, h + h * jnp.tanh(h))
            yield
            h0_ref[N.start : N.stop] = conv_forward(pa, wat_ref, N).reshape(len(N), 256, 256)
            yield

        interleave([part(N) for N in parts()])


def conv_one(cnt, x, cf, me, given, fill):
    n = x.shape[0]
    return image_call(
        lambda *refs: conv_one_body(fill, *refs),
        "conv_one",
        n,
        (18, 10),
        [blocks(256, 256), blocks(8, 256), pl.BlockSpec(memory_space=pltpu.SMEM)] + [whole(g.shape) for g in given],
        [out_blocks(256, 256), out_blocks(256, 256), whole((2304, 256)), whole((16, 256))],
        [sd((n, 256, 256), F32), sd((n, 256, 256), BF), sd((2304, 256), BF), sd((16, 256), F32)],
        [pltpu.VMEM((NB, 288, 768), BF), pltpu.VMEM((32, 128), F32)],
        (cnt, x, cf, me, *given),
    )


def middle_body(fill, n_given, finish, n_out, *refs):
    (cnt_ref, x_ref, h0_ref, cot_ref, a1_ref, emb_ref, vec_ref, me_ref) = refs[:8]
    given = refs[8 : 8 + n_given]
    refs = refs[8 + n_given :]
    out_ref, ga_ref, dm_ref = refs[:3]
    ends = refs[3 : 3 + n_out]
    refs = refs[3 + n_out :]
    (pa, pg, pa1, gt, gt1, mid, a3, mx, dmx, dz, she, dsr, dwa, dwb, dwq, dwo, dvec, turn) = refs[:18]
    wet_ref, wbt_ref, wqt_ref, wot_ref = refs[18:]
    i = pl.program_id(0)
    cnt = cnt_ref[0]

    @pl.when(i == 0)
    def _():
        zero_pads(pa)
        zero_pads(pg)
        zero_pads(pa1)
        for ref in (dwa, dwb, dwq, dwo, dvec, dsr):
            ref[...] = jnp.zeros_like(ref)
        fill(me_ref, *given, wet_ref, wbt_ref, wqt_ref, wot_ref)
        she[...] = dot_nt(emb_ref[...], wet_ref[...]) + (row(vec_ref, 2) + row(vec_ref, 3))

    live = i * NB < cnt

    @pl.when(jnp.logical_not(live))
    def _():
        for ref in (out_ref, ga_ref, dm_ref):
            ref[...] = jnp.zeros_like(ref)

    @pl.when(live)
    def _():
        g2, b2, c2, g3, b3, qb, vb, ob = (row(vec_ref, j) for j in range(4, 12))
        tot = {}

        def add(key, v):
            tot[key] = v if key not in tot else tot[key] + v

        def part(N):
            lo = N.start * 256
            hi = N.stop * 256
            W = range(len(N))
            L = lambda j: slice(j * 256, j * 256 + 256)
            masks = [(i * NB + n < cnt).astype(F32) for n in N]
            shifts = [she[pl.ds(i * NB + n, 1), :] for n in N]
            br = jnp.concatenate(shifts, axis=0)
            hload = [lambda r, n=n: h0_ref[n, r : r + CH, :] for n in N]
            m2, rs2 = stats(hload, shifts)
            sc2 = 0.5 * rs2 * g2
            sh2 = 0.5 * b2 + (br - m2) * sc2
            hm2 = br - m2
            for j, n in enumerate(N):
                for r in R:
                    h = hload[j](r) * sc2[j : j + 1] + sh2[j : j + 1]
                    put3(pa, n, r, h + h * jnp.tanh(h))
            yield
            o = conv_forward(pa, wbt_ref, N)
            yield
            for j, n in enumerate(N):
                for r in R:
                    mid[n, r : r + CH, :] = o[j * 256 + r : j * 256 + r + CH] + (x_ref[n, r : r + CH, :].astype(F32) + c2)
            mload = [lambda r, n=n: mid[n, r : r + CH, :] for n in N]
            m3, rs3 = stats(mload)
            sc3 = rs3 * g3
            sh3 = b3 - m3 * sc3
            for j, n in enumerate(N):
                for r in R:
                    a3[n * 256 + r : n * 256 + r + CH, :] = (mload[j](r) * sc3[j : j + 1] + sh3[j : j + 1]).astype(BF)
            gob = []
            for j, n in enumerate(N):
                go = cot_ref[n].astype(F32) * masks[j]
                add("ob", csum(go))
                gob.append(go.astype(BF))
            gall = jnp.concatenate(gob, axis=0)
            yield
            bc = jnp.concatenate([qb, jnp.zeros_like(qb), vb], axis=1)
            mx[lo:hi] = (dot_nt(a3[lo:hi], wqt_ref[...]) + bc).astype(BF)
            M = lambda j, p: mx[lo + j * 256 : lo + j * 256 + 256, 256 * p : 256 * p + 256]
            datt = dot(gall, wot_ref[...]).astype(BF)
            yield
            st = [dot_nt(M(j, 1), M(j, 0)) for j in W]
            dpt = [dot_nt(M(j, 2), datt[L(j)]) for j in W]
            yield
            pts = []
            ptb = []
            for j in W:
                s = st[j] * 0.0625
                e = jnp.exp(s - jnp.max(s, axis=0, keepdims=True))
                p = e * (1.0 / jnp.sum(e, axis=0, keepdims=True))
                pts.append(p)
                ptb.append(p.astype(BF))
            yield
            att = [dot_tn(ptb[j], M(j, 2)).astype(BF) for j in W]
            dv = [dot(ptb[j], datt[L(j)]).astype(BF) for j in W]
            yield
            dst = []
            for n in N:
                for r in R:
                    put3(pa1, n, r, a1_ref[n, r : r + CH, :].astype(F32))
            for j in W:
                t = dpt[j] * pts[j]
                dst.append((t - pts[j] * jnp.sum(t, axis=0, keepdims=True)).astype(BF))
            yield
            attall = jnp.concatenate(att, axis=0)
            proj = dot_nt(attall, wot_ref[...])
            dwo[...] += dot_tn(gall, attall)
            dq = [(dot_tn(dst[j], M(j, 1)) * 0.0625).astype(BF) for j in W]
            dk = [(dot(dst[j], M(j, 0)) * 0.0625).astype(BF) for j in W]
            yield
            for j, n in enumerate(N):
                out_ref[n] = (mid[n] + (proj[L(j)] + ob)) * masks[j]
                s = slice(n * 256, n * 256 + 256)
                dmx[s, 0:256] = dq[j]
                dmx[s, 256:512] = dk[j]
                dmx[s, 512:768] = dv[j]
                add("qb", csum(dq[j].astype(F32)))
                add("vb", csum(dv[j].astype(F32)))
            yield
            d3 = dot(dmx[lo:hi], wqt_ref[...])
            dwq[...] += dot_tn(a3[lo:hi], dmx[lo:hi])
            yield
            As = []
            Bs = []
            for j, n in enumerate(N):
                A = B = jnp.zeros((8, 256), F32)
                for r in R:
                    dy = d3[j * 256 + r : j * 256 + r + CH]
                    A = A + csum(dy)
                    B = B + csum(dy * (mid[n, r : r + CH, :] - m3[j : j + 1]))
                As.append(fsum(A))
                Bs.append(fsum(B))
            A3 = jnp.concatenate(As, axis=0)
            B3 = jnp.concatenate(Bs, axis=0) * rs3
            add("b3", fsum(A3))
            add("g3", fsum(B3))
            al, be, ga = back_coefs(A3, B3, g3, rs3, m3)
            for j, n in enumerate(N):
                for r in R:
                    dm = cot_ref[n, r : r + CH, :].astype(F32) * masks[j] + (
                        d3[j * 256 + r : j * 256 + r + CH] * al[j : j + 1]
                        + (mid[n, r : r + CH, :] * be[j : j + 1] + ga[j : j + 1])
                    )
                    dm_ref[n, r : r + CH, :] = dm
                    add("c2", csum(dm))
                    put3(pg, n, r, dm, True)
                gt[:, n * 256 : n * 256 + 256] = pg[n, 16:272, 256:512].T
            yield
            o = conv_turned(pg, wbt_ref, N)
            add_taps(dwb, gt[:, lo:hi], pa, N)
            yield
            As = []
            Bs = []
            for j, n in enumerate(N):
                A = B = jnp.zeros((8, 256), F32)
                for r in R:
                    h0 = hload[j](r)
                    h = h0 * sc2[j : j + 1] + sh2[j : j + 1]
                    t = jnp.tanh(h)
                    dzz = o[j * 256 + r : j * 256 + r + CH] * ((1.0 + t) * (1.0 + (h - h * t)))
                    dz[n * 256 + r : n * 256 + r + CH, :] = dzz
                    A = A + csum(dzz)
                    B = B + csum(dzz * (h0 + hm2[j : j + 1]))
                As.append(fsum(A))
                Bs.append(fsum(B))
            A2 = jnp.concatenate(As, axis=0) * 0.5
            B2 = jnp.concatenate(Bs, axis=0) * (rs2 * 0.5)
            add("b2", fsum(A2))
            add("g2", fsum(B2))
            al, be, ga = back_coefs(A2, B2, g2, rs2, -hm2)
            al = al * 0.5
            for j, n in enumerate(N):
                ds = jnp.zeros((8, 256), F32)
                for r in R:
                    dh = dz[n * 256 + r : n * 256 + r + CH, :] * al[j : j + 1] + (
                        hload[j](r) * be[j : j + 1] + ga[j : j + 1]
                    )
                    ga_ref[n, r : r + CH, :] = dh.astype(BF)
                    ds = ds + csum(dh)
                dsr[pl.ds(i * NB + n, 1), :] = fsum(ds)
                gt1[:, n * 256 : n * 256 + 256] = ga_ref[n].T
            yield
            add_taps(dwa, gt1[:, lo:hi], pa1, N)
            yield

        interleave([part(N) for N in parts()])
        z = jnp.zeros((4, 256), F32)
        rows = [tot["g2"], tot["b2"], fsum(tot["c2"]), tot["g3"], tot["b3"]]
        rows += [fsum(tot[k]) for k in ("qb", "vb", "ob")]
        dvec[...] += jnp.concatenate([z] + rows + [z], axis=0)

    @pl.when(i == pl.num_programs(0) - 1)
    def _():
        ds = dsr[...]
        total = fsum(ds)
        rows = jnp.concatenate([jnp.zeros((2, 256), F32), total, total, dvec[4:16, :]], axis=0)
        finish(ends, me_ref, dwa, dwb, dwq, dwo, dot_tn(ds.astype(BF), emb_ref[...]), rows, turn)


def middle(cnt, x, h0, cot, a1, emb, vec, me, given, fill, finish, ends):
    n = x.shape[0]
    V = pltpu.VMEM
    return image_call(
        lambda *refs: middle_body(fill, len(given), finish, len(ends), *refs),
        "middle",
        n,
        (108, 44),
        [blocks(256, 256)] * 4
        + [whole(emb.shape), whole((16, 256)), pl.BlockSpec(memory_space=pltpu.SMEM)]
        + [whole(w.shape) for w in given],
        [out_blocks(256, 256)] * 3 + [whole(e.shape) for e in ends],
        [sd((n, 256, 256), F32), sd((n, 256, 256), BF), sd((n, 256, 256), F32)] + list(ends),
        [
            V((NB, 288, 768), BF),
            V((NB, 288, 768), BF),
            V((NB, 288, 768), BF),
            V((256, NB * 256), BF),
            V((256, NB * 256), BF),
            V((NB, 256, 256), F32),
            V((NB * 256, 256), BF),
            V((NB * 256, 768), BF),
            V((NB * 256, 768), BF),
            V((NB * 256, 256), F32),
            V((n, 256), F32),
            V((n, 256), F32),
            V((768, 768), F32),
            V((768, 768), F32),
            V((256, 768), F32),
            V((256, 256), F32),
            V((16, 256), F32),
            V((1280, 512), F32),
            V((256, 512), BF),
            V((2304, 256), BF),
            V((768, 256), BF),
            V((256, 256), BF),
        ],
        (cnt, x, h0, cot, a1, emb, vec, me, *given),
    )


def input_grad_body(base, *refs):
    cnt_ref, x_ref, ga_ref, dm_ref, cf_ref, vec_ref, me_ref, wat_ref = refs[:8]
    ig_ref, dvec, pg, dz = refs[-4:]
    i = pl.program_id(0)

    @pl.when(i == 0)
    def _():
        zero_pads(pg)
        dvec[...] = jnp.zeros_like(dvec)

    live = (i + base) * NB < cnt_ref[0]

    @pl.when(jnp.logical_not(live))
    def _():
        ig_ref[...] = jnp.zeros_like(ig_ref)

    @pl.when(live)
    def _():
        g1 = row(vec_ref, 0)
        tot = {}

        def add(key, v):
            tot[key] = v if key not in tot else tot[key] + v

        def part(N):
            for n in N:
                for r in R:
                    put3(pg, n, r, ga_ref[n, r : r + CH, :].astype(F32), True)
            yield
            o = conv_turned(pg, wat_ref, N)
            yield
            As = []
            Bs = []
            ms = jnp.concatenate([cf_ref[n, 0:1, :] for n in N], axis=0)
            rss = jnp.concatenate([cf_ref[n, 1:2, :] for n in N], axis=0)
            for j, n in enumerate(N):
                m = cf_ref[n, 0:1, :]
                sc = 0.5 * cf_ref[n, 1:2, :] * g1
                sh = 0.5 * row(vec_ref, 1) - m * sc
                A = B = jnp.zeros((8, 256), F32)
                for r in R:
                    x = x_ref[n, r : r + CH, :].astype(F32)
                    h = x * sc + sh
                    t = jnp.tanh(h)
                    dzz = o[j * 256 + r : j * 256 + r + CH] * ((1.0 + t) * (1.0 + (h - h * t)))
                    dz[n * 256 + r : n * 256 + r + CH, :] = dzz
                    A = A + csum(dzz)
                    B = B + csum(dzz * (x - m))
                As.append(fsum(A))
                Bs.append(fsum(B))
            A1 = jnp.concatenate(As, axis=0) * 0.5
            B1 = jnp.concatenate(Bs, axis=0) * (rss * 0.5)
            add("b1", fsum(A1))
            add("g1", fsum(B1))
            al, be, ga = back_coefs(A1, B1, g1, rss, ms)
            al = al * 0.5
            for j, n in enumerate(N):
                for r in R:
                    ig_ref[n, r : r + CH, :] = dm_ref[n, r : r + CH, :] + (
                        dz[n * 256 + r : n * 256 + r + CH, :] * al[j : j + 1]
                        + (x_ref[n, r : r + CH, :].astype(F32) * be[j : j + 1] + ga[j : j + 1])
                    )
            yield

        interleave([part(N) for N in parts()])
        g = tot["g1"]
        b = tot["b1"]
        z = jnp.zeros((4, 128), F32)
        dvec[...] += jnp.concatenate([g[:, :128], g[:, 128:], b[:, :128], b[:, 128:], z], axis=0)


def input_grad(cnt, x, ga, dm, cf, vec, me, wat, base, steps, got):
    n = x.shape[0]
    at = lambda i, c: jnp.minimum(i + base, jnp.maximum((c[0] - 1) // NB, base))
    block = lambda *tail: pl.BlockSpec((NB,) + tail, lambda i, c: (at(i, c),) + (0,) * len(tail))
    args = (cnt, x, ga, dm, cf, vec, me, wat)
    in_specs = [block(256, 256)] * 3 + [block(8, 256), whole((16, 256))]
    in_specs += [pl.BlockSpec(memory_space=pltpu.SMEM), whole(wat.shape)]
    alias = {}
    if got is not None:
        alias = {len(args): 0}
        args += (got,)
        in_specs += [pl.BlockSpec(memory_space=pl.ANY)]
    return pl.pallas_call(
        lambda *refs: input_grad_body(base, *refs),
        grid_spec=pltpu.PrefetchScalarGridSpec(
            num_scalar_prefetch=1,
            grid=(steps,),
            in_specs=in_specs,
            out_specs=[
                pl.BlockSpec((NB, 256, 256), lambda i, c: (i + base, 0, 0)),
                pl.BlockSpec((8, 128), lambda i, c: (0, 0)),
            ],
            scratch_shapes=[pltpu.VMEM((NB, 288, 768), BF), pltpu.VMEM((NB * 256, 256), F32)],
        ),
        out_shape=[sd((n, 256, 256), F32), sd((8, 128), F32)],
        input_output_aliases=alias,
        cost_estimate=pl.CostEstimate(
            flops=steps * NB * 24 * 2 * 256**3, transcendentals=0, bytes_accessed=steps * NB * 14 * 4 * 256**2
        ),
        compiler_params=VMEM,
        name="input_grad",
    )(*args)


def sinus_embed(steps_in):
    half_width = E // 2
    frequency = jnp.exp(
        -math.log(10000.0) * jnp.arange(half_width, dtype=jnp.float32) / (half_width - 1)
    )
    angles = steps_in.astype(jnp.float32)[:, None] * frequency[None, :]
    return jnp.concatenate([jnp.sin(angles), jnp.cos(angles)], axis=1)


def halves(s0, s1):
    first = jnp.concatenate([s0[:, :64], s1[:, :64]], axis=1)
    second = jnp.concatenate([s0[:, 64:], s1[:, 64:]], axis=1)
    return first, second


def pack_body(conv, embed, attend, output, vec, a_ref, b_ref):
    for side, ref, base in ((0, a_ref, 0), (1, b_ref, 32)):
        for k in range(9):
            w = conv[9 * side + k]
            ref[base + 16 * k : base + 16 * k + 16, :] = jnp.concatenate([w[:16], w[16:]], axis=1).astype(BF)
    line = jnp.concatenate([vec[...], jnp.zeros((1, 32), F32)], axis=1)
    a_ref[144:160, :] = jnp.broadcast_to(line, (16, 128)).astype(BF)
    b_ref[0:32, :] = embed[...].astype(BF)
    at = jnp.concatenate([attend[...], jnp.zeros((64, 32), F32)], axis=1).T
    b_ref[176:224, :] = jnp.concatenate([at[:48], at[48:96]], axis=1).astype(BF)
    o = output[...]
    b_ref[224:240, :] = jnp.concatenate([o[:16], o[16:]], axis=1).astype(BF)


def pack(masters):
    return pl.pallas_call(
        pack_body, out_shape=[sd((RA, 128), BF), sd((RB, 128), BF)], compiler_params=VMEM, name="pack_shards"
    )(*masters)


def swap(x, bits):
    return lax.ppermute(x, AXES, [(i, i ^ bits) for i in range(32)])


def pairs(g, z, lo, rows, h):
    s0 = g[z ^ (2 * h), lo : lo + rows, :]
    s1 = g[z ^ (2 * h + 1), lo : lo + rows, :]
    return halves(s0, s1)


def unpack_a(me, *refs):
    gs = refs[:8]
    wat_ref, vec_ref, vrows = refs[8:]
    z = me[0]
    f = me[1]
    for rf in range(8):
        d0 = (f ^ rf) * 32
        for h in range(2):
            for k in range(9):
                j0, j1 = pairs(gs[rf], z, 16 * k, 16, h)
                at = pl.multiple_of(256 * k + d0, 32)
                wat_ref[pl.ds(at, 16), 128 * h : 128 * h + 128] = j0
                wat_ref[pl.ds(at + 16, 16), 128 * h : 128 * h + 128] = j1
        for rz in range(4):
            vrows[pl.ds((z ^ rz) * 8 + (f ^ rf), 1), :] = gs[rf][rz, 144:160, :].astype(F32)[0:1]
    v = vrows[...]
    v3 = jnp.concatenate([v, pltpu.roll(v, 96, 1), pltpu.roll(v, 64, 1)], axis=0).astype(BF)
    col = lax.broadcasted_iota(jnp.int32, (16, 96), 1)
    line = lax.broadcasted_iota(jnp.int32, (16, 96), 0)
    unit = 3 * (col & 31) + (col >> 5)
    lane = lax.broadcasted_iota(jnp.int32, (16, 128), 1)
    for half in range(2):
        acc = jnp.zeros((16, 128), F32)
        for t in range(4):
            sel = jnp.where(unit == 8 * line + 4 * half + t, 1.0, 0.0).astype(BF)
            piece = dot(sel, v3)
            if t:
                piece = pltpu.roll(piece, 32 * t, 1)
            acc = jnp.where((lane >> 5) == t, piece, acc)
        vec_ref[:, 128 * half : 128 * half + 128] = acc


def unpack_b(me, *refs):
    gs = refs[:8]
    wet_ref, wbt_ref, wqt_ref, wot_ref = refs[8:]
    z = me[0]
    f = me[1]
    for rf in range(8):
        own = f ^ rf
        d0 = own * 32
        g = gs[rf]
        for d in range(4):
            wet_ref[pl.ds(pl.multiple_of(d0, 32), 32), 128 * d : 128 * d + 128] = g[z ^ d, 0:32, :]
        for h in range(2):
            lanes = slice(128 * h, 128 * h + 128)
            for k in range(9):
                j0, j1 = pairs(g, z, 32 + 16 * k, 16, h)
                at = pl.multiple_of(256 * k + d0, 32)
                wbt_ref[pl.ds(at, 16), lanes] = j0
                wbt_ref[pl.ds(at + 16, 16), lanes] = j1
            j0, j1 = pairs(g, z, 176, 48, h)
            at = pl.multiple_of(own * 96, 32)
            wqt_ref[pl.ds(at, 48), lanes] = j0
            wqt_ref[pl.ds(at + 48, 48), lanes] = j1
            j0, j1 = pairs(g, z, 224, 16, h)
            at = pl.multiple_of(d0, 32)
            wot_ref[pl.ds(at, 16), lanes] = j0
            wot_ref[pl.ds(at + 16, 16), lanes] = j1


def place(outs, me, src, base, lanes, lo, rows, step):
    z = me[0]
    f = me[1]
    for rf in range(8):
        at = pl.multiple_of(base + (f ^ rf) * step, 16)
        ref = outs[4 * (rf & 1) + (rf >> 1)]
        for h in range(2):
            cut = slice(lanes + 128 * h, lanes + 128 * h + 128)
            e0, e1 = halves(src[pl.ds(at, rows), cut], src[pl.ds(at + rows, rows), cut])
            ref[z ^ (2 * h), lo : lo + rows, :] = e0.astype(BF)
            ref[z ^ (2 * h + 1), lo : lo + rows, :] = e1.astype(BF)


def finish_all(outs, me, dwa, dwb, dwq, dwo, de, rows, turn):
    for k in range(9):
        place(outs, me, dwa, 256 * (k // 3), 256 * (k % 3), 240 + 16 * k, 16, 32)
        place(outs, me, dwb, 256 * (k // 3), 256 * (k % 3), 16 * k, 16, 32)
    for k in range(3):
        turn[256 * k : 256 * k + 256, 0:256] = dwq[:, 256 * k : 256 * k + 256].T
    place(outs, me, turn, 0, 0, 144, 48, 96)
    place(outs, me, dwo, 0, 0, 192, 16, 32)
    turn[1024:1280, :] = de
    for d in range(4):
        for rf in range(8):
            at = pl.multiple_of(1024 + (me[1] ^ rf) * 32, 32)
            block = turn[pl.ds(at, 32), 128 * d : 128 * d + 128]
            outs[4 * (rf & 1) + (rf >> 1)][me[0] ^ d, 208:240, :] = block.astype(BF)
    outs[8][...] = rows


def over_core(ends):
    got = [swap(v, 1) for v in ends[7:3:-1]][::-1]
    return [(a.astype(F32) + b.astype(F32)).astype(a.dtype) for a, b in zip(ends[:4], got)]


def to_plane(parts):
    return [swap(parts[1], 2), swap(parts[2], 4), swap(parts[3], 6)]


def plane_sum(own, got):
    line = [sum((g[rz].astype(F32) for g in got), own[rz].astype(F32)) for rz in range(4)]
    return line[0], [v.astype(own.dtype) for v in line[1:]]


def over_line(others):
    return [swap(v, 8 * (rz + 1)) for rz, v in enumerate(others)]


def shares_body(own, r1, r2, r3, first, rows, g, out):
    s = own[...] + sum(r[...].astype(F32) for r in (r1, r2, r3))
    g[...] = s
    t = fsum(jnp.sum((s * s).reshape(-1, 8, 128), axis=0))
    for k in range(2, 12):
        out[2 * k : 2 * k + 1, :] = rows[k : k + 1, 0:128]
        out[2 * k + 1 : 2 * k + 2, :] = rows[k : k + 1, 128:256]
    out[0:4, :] = first[0:4, :]
    out[24:32, :] = jnp.broadcast_to(jnp.sum(t, axis=1, keepdims=True), (8, 128))


def shares(own, got, first, rows):
    return pl.pallas_call(
        shares_body, out_shape=[sd((RG, 128), F32), sd((32, 128), F32)], compiler_params=VMEM, name="shares"
    )(own, *got, first, rows)


def total_over(s):
    s = s + swap(s, 1)
    s = (s + swap(s, 2)) + (swap(s, 4) + swap(s, 6))
    return s, swap(s, 8), swap(s, 16), swap(s, 24)


def adam_body(*refs):
    me, t0, t1, t2, t3, grads = refs[:6]
    state = refs[6:21]
    outs = refs[21:-1]
    first = refs[-1]
    total = (t0[...] + t1[...]) + (t2[...] + t3[...])
    first[...] = total
    top = total[0:24]
    norm = jnp.sqrt(jnp.broadcast_to(jnp.sum(fsum(top * top), axis=1, keepdims=True), (1, 128)) + total[24:25])
    lane = lax.broadcasted_iota(jnp.int32, (1, 128), 1)
    vec = jnp.zeros((1, 128), F32)
    for u in range(3):
        unit = 3 * (8 * me[0] + me[1]) + u
        line = pltpu.roll(first[pl.ds(unit >> 2, 1), :], (32 * u + 128 - 32 * (unit & 3)) & 127, 1)
        vec = jnp.where((lane >> 5) == u, line, vec)
    factor = clip_norm / jnp.maximum(norm, clip_norm)

    def put(kind, at, grad):
        clipped = grad * factor[:, : grad.shape[1]]
        mas, mom, squ = (r[at] for r in state[3 * kind : 3 * kind + 3])
        first_new = beta_first * mom + (1.0 - beta_first) * clipped
        second_new = beta_second * squ + (1.0 - beta_second) * clipped * clipped
        first_hat = first_new / (1.0 - beta_first**STEP)
        second_hat = second_new / (1.0 - beta_second**STEP)
        update = mas - rates_kind[kind] * (
            first_hat / (jnp.sqrt(second_hat) + adam_eps) + decays_kind[kind] * mas
        )
        outs[3 * kind][at] = first_new
        outs[3 * kind + 1][at] = second_new
        outs[3 * kind + 2][at] = update

    for side, base in ((0, 240), (1, 0)):
        for k in range(9):
            g = grads[base + 16 * k : base + 16 * k + 16, :]
            put(0, (9 * side + k,), jnp.concatenate([g[:, :64], g[:, 64:]], axis=0))
    put(1, (Ellipsis,), grads[208:240, :])
    g = grads[144:192, :]
    g = jnp.concatenate([jnp.concatenate([g[:, :64], g[:, 64:]], axis=0), jnp.zeros((96, 64), F32)], axis=1)
    g = jnp.concatenate([g, jnp.zeros((32, 128), F32)], axis=0).T
    put(2, (Ellipsis,), g[:64, :96])
    g = grads[192:208, :]
    put(3, (Ellipsis,), jnp.concatenate([g[:, :64], g[:, 64:]], axis=0))
    put(4, (Ellipsis,), vec[:, :96])
    outs[15][0] = norm[0, 0]


def adam(me, totals, grads, state):
    args = (*totals, grads, *state)
    return pl.pallas_call(
        adam_body,
        in_specs=[pl.BlockSpec(memory_space=pltpu.SMEM)] + [pl.BlockSpec(a.shape) for a in args],
        out_specs=[pl.BlockSpec(s.shape) for s in state] + [pl.BlockSpec(memory_space=pltpu.SMEM)],
        out_shape=[sd(s.shape, F32) for s in state] + [sd((1,), F32)],
        scratch_shapes=[pltpu.VMEM((32, 128), F32)],
        compiler_params=VMEM,
        name="clipped_adamw",
    )(me, *args)


def turned_state(state):
    out = []
    for kind in range(5):
        for a in state[3 * kind : 3 * kind + 3]:
            if kind == 0:
                a = jnp.swapaxes(a, 3, 4).reshape(18, 32, 64)
            elif kind == 2:
                a = a[0]
            elif kind < 4:
                a = jnp.swapaxes(a, 1, 2)[0]
            out.append(a)
    return out


def turned_back(results):
    out = []
    for kind in range(5):
        for a in results[3 * kind : 3 * kind + 3]:
            if kind == 0:
                a = jnp.swapaxes(a.reshape(1, 2, 9, 32, 64), 3, 4)
            elif kind == 2:
                a = a[None]
            elif kind < 4:
                a = jnp.swapaxes(a[None], 1, 2)
            out.append(a)
    return out


def per_device_here(images, timesteps, counts, cotangent, *state):
    n_img = images.shape[0]
    state = turned_state(state)
    me = jnp.stack([lax.axis_index("dp"), lax.axis_index("fsdp")]).astype(jnp.int32)
    sa, sb = pack(state[0::3])
    x = images.reshape(n_img, 256, 256)
    cot = cotangent.reshape(n_img, 256, 256)
    cf = figures(counts, x)
    emb = jax.nn.silu(sinus_embed(timesteps)).astype(BF)

    line_a = jnp.stack([sa] + [swap(sa, 8 * rz) for rz in range(1, 4)])
    rows_b = [sb] + [swap(sb, 8 * rz) for rz in range(1, 4)]
    plane_a = [line_a] + [swap(line_a, bits) for bits in (2, 4, 6)]
    rows_b, plane_a, cf, me, emb = lax.optimization_barrier((rows_b, plane_a, cf, me, emb))
    all_a = [p for line in plane_a for p in (line, swap(line, 1))]
    line_b = jnp.stack(rows_b)
    plane_b = [line_b] + [swap(line_b, bits) for bits in (2, 4, 6)]
    all_a, line_b = lax.optimization_barrier((all_a, line_b))
    h0, a1, wat, vec = conv_one(counts, x, cf, me, all_a, unpack_a)
    h0, plane_b = lax.optimization_barrier((h0, plane_b))
    all_b = [p for line in plane_b for p in (line, swap(line, 1))]
    out, ga, dm, *ends, rows = middle(
        counts, x, h0, cot, a1, emb, vec, me, all_b, unpack_b, finish_all, [sd((4, RG, 128), BF)] * 8 + [sd((16, 256), F32)]
    )
    plane_parts = over_core(ends)
    plane = to_plane(plane_parts)
    ga, parts = lax.optimization_barrier((ga, plane_parts))
    ig, v = input_grad(counts, x, ga, dm, cf, vec, me, wat, 0, n_img // NB, None)
    v, plane = lax.optimization_barrier((v, plane))
    own, others = plane_sum(parts[0], plane)
    grads, sums = shares(own, over_line(others), v, rows)
    results = adam(me, total_over(sums), grads, state)
    return (out.reshape(images.shape), ig.reshape(images.shape), *turned_back(results[:15]), results[15].reshape(()))


def gather_flat(masters, dp, fs):
    sizes = [m.size for m in masters]
    total = sum(sizes)
    full = -(-total // 2048) * 2048
    flat = jnp.concatenate([m.reshape(-1).astype(BF) for m in masters] + [jnp.zeros((full - total,), BF)])
    flat = flat.reshape(-1, 128)
    g = lax.all_gather(lax.all_gather(flat, "dp"), "fsdp").reshape(fs, dp, full)
    out = []
    at = 0
    for n in sizes:
        out.append(g[:, :, at : at + n])
        at += n
    conv = out[0].reshape((fs, dp) + masters[0].shape[1:]).transpose(2, 3, 0, 5, 1, 4)
    conv = conv.reshape(2, 2304, 256)
    mats = []
    for p, m in zip(out[1:4], masters[1:4]):
        r, c = m.shape[1:]
        mats.append(p.reshape(fs, dp, r, c).transpose(0, 3, 1, 2).reshape(fs * c, dp * r))
    vec = out[4].transpose(1, 0, 2).reshape(12, 256).astype(F32)
    return conv, mats, vec


def reduce_flat(grads, dp, fs):
    conv, mats, vec = grads
    pieces = [conv.reshape(18, fs, 256 // fs, dp, 256 // dp).transpose(1, 3, 0, 4, 2).reshape(fs, dp, -1)]
    for g in mats:
        c, r = g.shape
        pieces.append(g.reshape(fs, c // fs, dp, r // dp).transpose(0, 2, 3, 1).reshape(fs, dp, -1))
    pieces.append(vec.reshape(dp, fs, -1).transpose(1, 0, 2))
    sizes = [p.shape[2] for p in pieces]
    total = sum(sizes)
    full = -(-total // 2048) * 2048
    pieces.append(jnp.zeros((fs, dp, full - total), F32))
    flat = jnp.concatenate(pieces, axis=2).reshape(fs, dp, -1, 128)
    part = lax.psum_scatter(flat, "fsdp", scatter_dimension=0, tiled=False)
    part = lax.psum_scatter(part, "dp", scatter_dimension=0, tiled=False).reshape(-1)
    out = []
    at = 0
    for n in sizes:
        out.append(part[at : at + n])
        at += n
    return out


def finish_whole(outs, me, dwa, dwb, dwq, dwo, de, rows, turn):
    for out, got in zip(outs, (dwa[...], dwb[...], dwq[...], dwo[...], de, rows)):
        out[...] = got


def fill_one(me, wat, vec, wat_ref, vec_ref, vrows):
    wat_ref[...] = wat[...]
    vec_ref[...] = vec[...]


def fill_rest(me, *refs):
    for k in range(4):
        refs[4 + k][...] = refs[k][...]


def per_device_any(images, timesteps, counts, cotangent, *state):
    masters = state[0::3]
    moments = state[1::3]
    squares = state[2::3]
    dp = lax.axis_size("dp")
    fs = lax.axis_size("fsdp")
    n_img = images.shape[0]
    me = jnp.zeros((2,), jnp.int32)
    emb = jax.nn.silu(sinus_embed(timesteps)).astype(BF)
    x = images.reshape(n_img, 256, 256)
    cot = cotangent.reshape(n_img, 256, 256)
    conv, (wet, wqt, wot), vec = gather_flat(masters, dp, fs)
    vec = jnp.pad(vec, ((0, 4), (0, 0)))
    cf = figures(counts, x)
    h0, a1, wat, vec = conv_one(counts, x, cf, me, (conv[0], vec), fill_one)
    ends = [sd(s, F32) for s in ((768, 768), (768, 768), (256, 768), (256, 256), (256, 512), (16, 256))]
    out, ga, dm, dwa, dwb, dwq, dwo, de, rows = middle(
        counts, x, h0, cot, a1, emb, vec, me, (wet, conv[1], wqt, wot), fill_rest, finish_whole, ends
    )
    ig, first = input_grad(counts, x, ga, dm, cf, vec, me, conv[0], 0, n_img // NB, None)
    first = jnp.pad(first[:4].reshape(2, 256), ((0, 14), (0, 0)))
    apart = lambda w: w.reshape(3, 256, 3, 256).transpose(0, 2, 1, 3).reshape(9, 256, 256)
    shares_here = reduce_flat(
        (jnp.stack([apart(dwa), apart(dwb)]), (de, dwq.T, dwo), (rows + first)[:12]), dp, fs
    )
    local = sum(jnp.sum(s * s) for s in shares_here)
    norm = jnp.sqrt(lax.psum(lax.psum(local, "fsdp"), "dp"))
    factor = clip_norm / jnp.maximum(norm, clip_norm)
    results = []
    for kind in range(5):
        clipped = shares_here[kind].reshape(masters[kind].shape) * factor
        first_new = beta_first * moments[kind] + (1.0 - beta_first) * clipped
        second_new = beta_second * squares[kind] + (1.0 - beta_second) * clipped * clipped
        first_hat = first_new / (1.0 - beta_first**STEP)
        second_hat = second_new / (1.0 - beta_second**STEP)
        update_new = masters[kind] - rates_kind[kind] * (
            first_hat / (jnp.sqrt(second_hat) + adam_eps) + decays_kind[kind] * masters[kind]
        )
        results += [first_new, second_new, update_new]
    return (out.reshape(images.shape), ig.reshape(images.shape), *results, norm)


def solution(mesh):
    both = P(("dp", "fsdp"), None, None, None)
    one = P(("dp", "fsdp"))
    conv = P(None, None, None, "dp", "fsdp")
    mat = P(None, "dp", "fsdp")
    vec = P(None, ("dp", "fsdp"))
    trios = (conv,) * 3 + (mat,) * 9 + (vec,) * 3
    here = mesh.shape["dp"] == 4 and mesh.shape["fsdp"] == 8
    return jax.shard_map(
        per_device_here if here else per_device_any,
        mesh=mesh,
        in_specs=(both, one, one, both) + trios,
        out_specs=(both, both) + trios + (P(),),
        check_vma=False,
    )
```

```python
import math

import jax
import jax.numpy as jnp
from jax import lax
from jax.experimental import pallas as pl
from jax.experimental.pallas import tpu as pltpu
from jax.sharding import PartitionSpec as P

BF = jnp.bfloat16
F32 = jnp.float32
EPS = 1e-6
E = 512
STEP = 10
clip_norm = 1.0
beta_first = 0.9
beta_second = 0.999
adam_eps = 1e-08
rates_kind = (0.01, 0.03, 0.02, 0.05, 0.3)
decays_kind = (0.1, 0.1, 0.1, 0.1, 0.0)
AXES = ("dp", "fsdp")
VMEM = pltpu.CompilerParams(vmem_limit_bytes=60 * 2**20)
NB = 8
HB = 4
CH = 32
R = range(0, 256, CH)
RA = 160
RB = 240
RG = 384

sd = jax.ShapeDtypeStruct


def dot(a, b):
    return lax.dot_general(a, b, (((1,), (0,)), ((), ())), preferred_element_type=F32)


def dot_nt(a, b):
    return lax.dot_general(a, b, (((1,), (1,)), ((), ())), preferred_element_type=F32)


def dot_tn(a, b):
    return lax.dot_general(a, b, (((0,), (0,)), ((), ())), preferred_element_type=F32)


def gsum(s):
    n = s.shape[0]
    c = jnp.concatenate([s[:, :128], s[:, 128:]], axis=0)
    lane = lax.broadcasted_iota(jnp.int32, c.shape, 1)
    for k in (1, 2, 4):
        up = pltpu.roll(c, 128 - k, 1)
        down = pltpu.roll(c, k, 1)
        c = c + jnp.where((lane & k) == 0, up, down)
    return jnp.concatenate([c[:n], c[n:]], axis=1)


def csum(v):
    return jnp.sum(v.reshape(-1, 8, v.shape[-1]), axis=0)


def fsum(v):
    return jnp.sum(v, axis=0, keepdims=True)


def row_sums(load, base):
    s1 = s2 = None
    for r in R:
        v = load(r) - base
        a = csum(v)
        b = csum(v * v)
        s1 = a if s1 is None else s1 + a
        s2 = b if s2 is None else s2 + b
    return fsum(s1), fsum(s2)


def stats(loads, extras=None):
    firsts = [load(0)[0:1] for load in loads]
    p = jnp.concatenate(firsts, axis=0)
    if extras is not None:
        p = p + jnp.concatenate(extras, axis=0)
    q = gsum(p) * 0.125
    sums = [row_sums(load, first) for load, first in zip(loads, firsts)]
    s1 = jnp.concatenate([t[0] for t in sums], axis=0)
    s2 = jnp.concatenate([t[1] for t in sums], axis=0)
    d = p - q
    g = gsum(jnp.concatenate([s1 + 256.0 * d, s2 + d * (2.0 * s1 + 256.0 * d)], axis=0)) * (1.0 / 2048.0)
    n = len(loads)
    dm = g[:n]
    return q + dm, lax.rsqrt(g[n:] - dm * dm + EPS)


def back_coefs(sum_dy, sum_dyn, gain, rs, m):
    n = sum_dy.shape[0]
    g = gsum(jnp.concatenate([sum_dy * gain, sum_dyn * gain], axis=0)) * (1.0 / 2048.0)
    be = -rs * rs * g[n:]
    return rs * gain, be, -rs * g[:n] - m * be


def put3(pref, n, r, a, rev=False):
    rows = a.shape[0]
    col = lax.broadcasted_iota(jnp.int32, a.shape, 0) & 15
    prev = jnp.where(col == 0, 0.0, pltpu.roll(a, 1, 0))
    post = jnp.where(col == 15, 0.0, pltpu.roll(a, rows - 1, 0))
    lo, hi = (post, prev) if rev else (prev, post)
    low = a.astype(BF)
    pref[n, 16 + r : 16 + r + rows, 0:256] = lo.astype(BF)
    pref[n, 16 + r : 16 + r + rows, 256:512] = low
    pref[n, 16 + r : 16 + r + rows, 512:768] = hi.astype(BF)
    return low


def zero_pads(pref):
    z = jnp.zeros((16, 768), BF)
    for n in range(NB):
        pref[n, 0:16, :] = z
        pref[n, 272:288, :] = z


def conv_forward(pref, wt_ref, N):
    acc = None
    for i in range(3):
        for j in range(3):
            rows = pref[N.start : N.stop, 16 * i : 16 * i + 256, 256 * j : 256 * j + 256]
            k = 3 * i + j
            d = dot_nt(rows.reshape(len(N) * 256, 256), wt_ref[256 * k : 256 * k + 256, :])
            acc = d if acc is None else acc + d
    return acc


def conv_turned(pref, wt_ref, N):
    acc = None
    for i in range(3):
        o = 16 * (2 - i)
        rows = pref[N.start : N.stop, o : o + 256, :].reshape(len(N) * 256, 768)
        d = dot(rows, wt_ref[768 * i : 768 * i + 768, :])
        acc = d if acc is None else acc + d
    return acc


def add_taps(acc_ref, gt, pref, N):
    for i in range(3):
        rows = pref[N.start : N.stop, 16 * i : 16 * i + 256, :].reshape(len(N) * 256, 768)
        acc_ref[256 * i : 256 * i + 256, :] += dot(gt, rows)


def interleave(gens):
    gens = list(gens)
    done = [False] * len(gens)
    at = 0
    while not all(done):
        for j, g in enumerate(gens):
            if not done[j] and at >= j:
                try:
                    next(g)
                except StopIteration:
                    done[j] = True
        at += 1


def parts():
    return [range(j, j + HB) for j in range(0, NB, HB)]


def row(ref, j):
    return ref[j : j + 1, :]


def whole(shape):
    return pl.BlockSpec(shape, lambda i, c: (0,) * len(shape))


def clamped(i, c):
    return jnp.minimum(i, (c[0] - 1) // NB)


def blocks(*tail):
    return pl.BlockSpec((NB,) + tail, lambda i, c: (clamped(i, c),) + (0,) * len(tail))


ANY = pl.BlockSpec(memory_space=pl.ANY)


def out_blocks(*tail):
    return pl.BlockSpec((NB,) + tail, lambda i, c: (i,) + (0,) * len(tail))


def image_call(body, name, n_img, cost, in_specs, out_specs, out_shape, scratch, args):
    products, passes = cost
    return pl.pallas_call(
        body,
        grid_spec=pltpu.PrefetchScalarGridSpec(
            num_scalar_prefetch=1,
            grid=(n_img // NB,),
            in_specs=in_specs,
            out_specs=out_specs,
            scratch_shapes=scratch,
        ),
        out_shape=out_shape,
        cost_estimate=pl.CostEstimate(
            flops=n_img * products * 2 * 256**3,
            transcendentals=n_img * passes * 256**2,
            bytes_accessed=n_img * passes * 4 * 256**2,
        ),
        compiler_params=VMEM,
        name=name,
    )(*args)


def figures_body(cnt_ref, x_ref, cf_ref):
    @pl.when(pl.program_id(0) * NB < cnt_ref[0])
    def _():
        m, rs = stats([lambda r, n=n: x_ref[n, r : r + CH, :].astype(F32) for n in range(NB)])
        for n in range(NB):
            cf_ref[n] = jnp.concatenate([m[n : n + 1], rs[n : n + 1], jnp.zeros((6, 256), F32)], axis=0)


def figures(cnt, x):
    n = x.shape[0]
    return image_call(
        figures_body, "figures", n, (1, 2), [blocks(256, 256)], out_blocks(8, 256), sd((n, 8, 256), F32), [], (cnt, x)
    )


def conv_one_body(fill, *refs):
    cnt_ref, x_ref, cf_ref, me_ref = refs[:4]
    given = refs[4:-6]
    h0_ref, a1_ref, wat_ref, vec_ref, pa, vrows = refs[-6:]

    @pl.when(pl.program_id(0) == 0)
    def _():
        zero_pads(pa)
        fill(me_ref, *given, wat_ref, vec_ref, vrows)

    @pl.when(pl.program_id(0) * NB < cnt_ref[0])
    def _():
        def part(N):
            for n in N:
                sc = 0.5 * cf_ref[n, 1:2, :] * row(vec_ref, 0)
                sh = 0.5 * row(vec_ref, 1) - cf_ref[n, 0:1, :] * sc
                for r in R:
                    h = x_ref[n, r : r + CH, :].astype(F32) * sc + sh
                    a1_ref[n, r : r + CH, :] = put3(pa, n, r, h + h * jnp.tanh(h))
            yield
            h0_ref[N.start : N.stop] = conv_forward(pa, wat_ref, N).reshape(len(N), 256, 256)
            yield

        interleave([part(N) for N in parts()])


def conv_one(cnt, x, cf, me, given, fill):
    n = x.shape[0]
    return image_call(
        lambda *refs: conv_one_body(fill, *refs),
        "conv_one",
        n,
        (18, 10),
        [blocks(256, 256), blocks(8, 256), pl.BlockSpec(memory_space=pltpu.SMEM)] + [whole(g.shape) for g in given],
        [out_blocks(256, 256), out_blocks(256, 256), whole((2304, 256)), whole((16, 256))],
        [sd((n, 256, 256), F32), sd((n, 256, 256), BF), sd((2304, 256), BF), sd((16, 256), F32)],
        [pltpu.VMEM((NB, 288, 768), BF), pltpu.VMEM((32, 128), F32)],
        (cnt, x, cf, me, *given),
    )


def middle_body(fill, n_given, finish, n_out, *refs):
    (cnt_ref, x_ref, h0_ref, cot_ref, a1_ref, emb_ref, vec_ref, me_ref) = refs[:8]
    given = refs[8 : 8 + n_given]
    refs = refs[8 + n_given :]
    out_ref, ga_ref, dm_ref = refs[:3]
    ends = refs[3 : 3 + n_out]
    refs = refs[3 + n_out :]
    (pa, pg, pa1, gt, gt1, mid, a3, mx, dmx, dz, she, dsr, dwa, dwb, dwq, dwo, dvec, turn) = refs[:18]
    wet_ref, wbt_ref, wqt_ref, wot_ref = refs[18:]
    i = pl.program_id(0)
    cnt = cnt_ref[0]

    @pl.when(i == 0)
    def _():
        zero_pads(pa)
        zero_pads(pg)
        zero_pads(pa1)
        for ref in (dwa, dwb, dwq, dwo, dvec, dsr):
            ref[...] = jnp.zeros_like(ref)
        fill(me_ref, *given, wet_ref, wbt_ref, wqt_ref, wot_ref)
        she[...] = dot_nt(emb_ref[...], wet_ref[...]) + (row(vec_ref, 2) + row(vec_ref, 3))

    live = i * NB < cnt

    @pl.when(jnp.logical_not(live))
    def _():
        for ref in (out_ref, ga_ref, dm_ref):
            ref[...] = jnp.zeros_like(ref)

    @pl.when(live)
    def _():
        g2, b2, c2, g3, b3, qb, vb, ob = (row(vec_ref, j) for j in range(4, 12))
        tot = {}

        def add(key, v):
            tot[key] = v if key not in tot else tot[key] + v

        def part(N):
            lo = N.start * 256
            hi = N.stop * 256
            W = range(len(N))
            L = lambda j: slice(j * 256, j * 256 + 256)
            masks = [(i * NB + n < cnt).astype(F32) for n in N]
            shifts = [she[pl.ds(i * NB + n, 1), :] for n in N]
            br = jnp.concatenate(shifts, axis=0)
            hload = [lambda r, n=n: h0_ref[n, r : r + CH, :] for n in N]
            m2, rs2 = stats(hload, shifts)
            sc2 = 0.5 * rs2 * g2
            sh2 = 0.5 * b2 + (br - m2) * sc2
            hm2 = br - m2
            for j, n in enumerate(N):
                for r in R:
                    h = hload[j](r) * sc2[j : j + 1] + sh2[j : j + 1]
                    put3(pa, n, r, h + h * jnp.tanh(h))
            yield
            o = conv_forward(pa, wbt_ref, N)
            yield
            for j, n in enumerate(N):
                for r in R:
                    mid[n, r : r + CH, :] = o[j * 256 + r : j * 256 + r + CH] + (x_ref[n, r : r + CH, :].astype(F32) + c2)
            mload = [lambda r, n=n: mid[n, r : r + CH, :] for n in N]
            m3, rs3 = stats(mload)
            sc3 = rs3 * g3
            sh3 = b3 - m3 * sc3
            for j, n in enumerate(N):
                for r in R:
                    a3[n * 256 + r : n * 256 + r + CH, :] = (mload[j](r) * sc3[j : j + 1] + sh3[j : j + 1]).astype(BF)
            gob = []
            for j, n in enumerate(N):
                go = cot_ref[n].astype(F32) * masks[j]
                add("ob", csum(go))
                gob.append(go.astype(BF))
            gall = jnp.concatenate(gob, axis=0)
            yield
            bc = jnp.concatenate([qb, jnp.zeros_like(qb), vb], axis=1)
            mx[lo:hi] = (dot_nt(a3[lo:hi], wqt_ref[...]) + bc).astype(BF)
            M = lambda j, p: mx[lo + j * 256 : lo + j * 256 + 256, 256 * p : 256 * p + 256]
            datt = dot(gall, wot_ref[...]).astype(BF)
            yield
            st = [dot_nt(M(j, 1), M(j, 0)) for j in W]
            dpt = [dot_nt(M(j, 2), datt[L(j)]) for j in W]
            yield
            pts = []
            ptb = []
            for j in W:
                s = st[j] * 0.0625
                e = jnp.exp(s - jnp.max(s, axis=0, keepdims=True))
                p = e * (1.0 / jnp.sum(e, axis=0, keepdims=True))
                pts.append(p)
                ptb.append(p.astype(BF))
            yield
            att = [dot_tn(ptb[j], M(j, 2)).astype(BF) for j in W]
            dv = [dot(ptb[j], datt[L(j)]).astype(BF) for j in W]
            yield
            dst = []
            for n in N:
                for r in R:
                    put3(pa1, n, r, a1_ref[n, r : r + CH, :].astype(F32))
            for j in W:
                t = dpt[j] * pts[j]
                dst.append((t - pts[j] * jnp.sum(t, axis=0, keepdims=True)).astype(BF))
            yield
            attall = jnp.concatenate(att, axis=0)
            proj = dot_nt(attall, wot_ref[...])
            dwo[...] += dot_tn(gall, attall)
            dq = [(dot_tn(dst[j], M(j, 1)) * 0.0625).astype(BF) for j in W]
            dk = [(dot(dst[j], M(j, 0)) * 0.0625).astype(BF) for j in W]
            yield
            for j, n in enumerate(N):
                out_ref[n] = (mid[n] + (proj[L(j)] + ob)) * masks[j]
                s = slice(n * 256, n * 256 + 256)
                dmx[s, 0:256] = dq[j]
                dmx[s, 256:512] = dk[j]
                dmx[s, 512:768] = dv[j]
                add("qb", csum(dq[j].astype(F32)))
                add("vb", csum(dv[j].astype(F32)))
            yield
            d3 = dot(dmx[lo:hi], wqt_ref[...])
            dwq[...] += dot_tn(a3[lo:hi], dmx[lo:hi])
            yield
            As = []
            Bs = []
            for j, n in enumerate(N):
                A = B = jnp.zeros((8, 256), F32)
                for r in R:
                    dy = d3[j * 256 + r : j * 256 + r + CH]
                    A = A + csum(dy)
                    B = B + csum(dy * (mid[n, r : r + CH, :] - m3[j : j + 1]))
                As.append(fsum(A))
                Bs.append(fsum(B))
            A3 = jnp.concatenate(As, axis=0)
            B3 = jnp.concatenate(Bs, axis=0) * rs3
            add("b3", fsum(A3))
            add("g3", fsum(B3))
            al, be, ga = back_coefs(A3, B3, g3, rs3, m3)
            for j, n in enumerate(N):
                for r in R:
                    dm = cot_ref[n, r : r + CH, :].astype(F32) * masks[j] + (
                        d3[j * 256 + r : j * 256 + r + CH] * al[j : j + 1]
                        + (mid[n, r : r + CH, :] * be[j : j + 1] + ga[j : j + 1])
                    )
                    dm_ref[n, r : r + CH, :] = dm
                    add("c2", csum(dm))
                    put3(pg, n, r, dm, True)
                gt[:, n * 256 : n * 256 + 256] = pg[n, 16:272, 256:512].T
            yield
            o = conv_turned(pg, wbt_ref, N)
            add_taps(dwb, gt[:, lo:hi], pa, N)
            yield
            As = []
            Bs = []
            for j, n in enumerate(N):
                A = B = jnp.zeros((8, 256), F32)
                for r in R:
                    h0 = hload[j](r)
                    h = h0 * sc2[j : j + 1] + sh2[j : j + 1]
                    t = jnp.tanh(h)
                    dzz = o[j * 256 + r : j * 256 + r + CH] * ((1.0 + t) * (1.0 + (h - h * t)))
                    dz[n * 256 + r : n * 256 + r + CH, :] = dzz
                    A = A + csum(dzz)
                    B = B + csum(dzz * (h0 + hm2[j : j + 1]))
                As.append(fsum(A))
                Bs.append(fsum(B))
            A2 = jnp.concatenate(As, axis=0) * 0.5
            B2 = jnp.concatenate(Bs, axis=0) * (rs2 * 0.5)
            add("b2", fsum(A2))
            add("g2", fsum(B2))
            al, be, ga = back_coefs(A2, B2, g2, rs2, -hm2)
            al = al * 0.5
            for j, n in enumerate(N):
                ds = jnp.zeros((8, 256), F32)
                for r in R:
                    dh = dz[n * 256 + r : n * 256 + r + CH, :] * al[j : j + 1] + (
                        hload[j](r) * be[j : j + 1] + ga[j : j + 1]
                    )
                    ga_ref[n, r : r + CH, :] = dh.astype(BF)
                    ds = ds + csum(dh)
                dsr[pl.ds(i * NB + n, 1), :] = fsum(ds)
                gt1[:, n * 256 : n * 256 + 256] = ga_ref[n].T
            yield
            add_taps(dwa, gt1[:, lo:hi], pa1, N)
            yield

        interleave([part(N) for N in parts()])
        z = jnp.zeros((4, 256), F32)
        rows = [tot["g2"], tot["b2"], fsum(tot["c2"]), tot["g3"], tot["b3"]]
        rows += [fsum(tot[k]) for k in ("qb", "vb", "ob")]
        dvec[...] += jnp.concatenate([z] + rows + [z], axis=0)

    @pl.when(i == pl.num_programs(0) - 1)
    def _():
        ds = dsr[...]
        total = fsum(ds)
        rows = jnp.concatenate([jnp.zeros((2, 256), F32), total, total, dvec[4:16, :]], axis=0)
        finish(ends, me_ref, dwa, dwb, dwq, dwo, dot_tn(ds.astype(BF), emb_ref[...]), rows, turn)


def middle(cnt, x, h0, cot, a1, emb, vec, me, given, fill, finish, ends):
    n = x.shape[0]
    V = pltpu.VMEM
    return image_call(
        lambda *refs: middle_body(fill, len(given), finish, len(ends), *refs),
        "middle",
        n,
        (108, 44),
        [blocks(256, 256)] * 4
        + [whole(emb.shape), whole((16, 256)), pl.BlockSpec(memory_space=pltpu.SMEM)]
        + [whole(w.shape) for w in given],
        [out_blocks(256, 256)] * 3 + [whole(e.shape) for e in ends],
        [sd((n, 256, 256), F32), sd((n, 256, 256), BF), sd((n, 256, 256), F32)] + list(ends),
        [
            V((NB, 288, 768), BF),
            V((NB, 288, 768), BF),
            V((NB, 288, 768), BF),
            V((256, NB * 256), BF),
            V((256, NB * 256), BF),
            V((NB, 256, 256), F32),
            V((NB * 256, 256), BF),
            V((NB * 256, 768), BF),
            V((NB * 256, 768), BF),
            V((NB * 256, 256), F32),
            V((n, 256), F32),
            V((n, 256), F32),
            V((768, 768), F32),
            V((768, 768), F32),
            V((256, 768), F32),
            V((256, 256), F32),
            V((16, 256), F32),
            V((1280, 512), F32),
            V((256, 512), BF),
            V((2304, 256), BF),
            V((768, 256), BF),
            V((256, 256), BF),
        ],
        (cnt, x, h0, cot, a1, emb, vec, me, *given),
    )


def input_grad_body(base, *refs):
    cnt_ref, x_ref, ga_ref, dm_ref, cf_ref, vec_ref, me_ref, wat_ref = refs[:8]
    ig_ref, dvec, pg, dz = refs[-4:]
    i = pl.program_id(0)

    @pl.when(i == 0)
    def _():
        zero_pads(pg)
        dvec[...] = jnp.zeros_like(dvec)

    live = (i + base) * NB < cnt_ref[0]

    @pl.when(jnp.logical_not(live))
    def _():
        ig_ref[...] = jnp.zeros_like(ig_ref)

    @pl.when(live)
    def _():
        g1 = row(vec_ref, 0)
        tot = {}

        def add(key, v):
            tot[key] = v if key not in tot else tot[key] + v

        def part(N):
            for n in N:
                for r in R:
                    put3(pg, n, r, ga_ref[n, r : r + CH, :].astype(F32), True)
            yield
            o = conv_turned(pg, wat_ref, N)
            yield
            As = []
            Bs = []
            ms = jnp.concatenate([cf_ref[n, 0:1, :] for n in N], axis=0)
            rss = jnp.concatenate([cf_ref[n, 1:2, :] for n in N], axis=0)
            for j, n in enumerate(N):
                m = cf_ref[n, 0:1, :]
                sc = 0.5 * cf_ref[n, 1:2, :] * g1
                sh = 0.5 * row(vec_ref, 1) - m * sc
                A = B = jnp.zeros((8, 256), F32)
                for r in R:
                    x = x_ref[n, r : r + CH, :].astype(F32)
                    h = x * sc + sh
                    t = jnp.tanh(h)
                    dzz = o[j * 256 + r : j * 256 + r + CH] * ((1.0 + t) * (1.0 + (h - h * t)))
                    dz[n * 256 + r : n * 256 + r + CH, :] = dzz
                    A = A + csum(dzz)
                    B = B + csum(dzz * (x - m))
                As.append(fsum(A))
                Bs.append(fsum(B))
            A1 = jnp.concatenate(As, axis=0) * 0.5
            B1 = jnp.concatenate(Bs, axis=0) * (rss * 0.5)
            add("b1", fsum(A1))
            add("g1", fsum(B1))
            al, be, ga = back_coefs(A1, B1, g1, rss, ms)
            al = al * 0.5
            for j, n in enumerate(N):
                for r in R:
                    ig_ref[n, r : r + CH, :] = dm_ref[n, r : r + CH, :] + (
                        dz[n * 256 + r : n * 256 + r + CH, :] * al[j : j + 1]
                        + (x_ref[n, r : r + CH, :].astype(F32) * be[j : j + 1] + ga[j : j + 1])
                    )
            yield

        interleave([part(N) for N in parts()])
        g = tot["g1"]
        b = tot["b1"]
        z = jnp.zeros((4, 128), F32)
        dvec[...] += jnp.concatenate([g[:, :128], g[:, 128:], b[:, :128], b[:, 128:], z], axis=0)


def input_grad(cnt, x, ga, dm, cf, vec, me, wat, base, steps, got):
    n = x.shape[0]
    at = lambda i, c: jnp.minimum(i + base, jnp.maximum((c[0] - 1) // NB, base))
    block = lambda *tail: pl.BlockSpec((NB,) + tail, lambda i, c: (at(i, c),) + (0,) * len(tail))
    args = (cnt, x, ga, dm, cf, vec, me, wat)
    in_specs = [block(256, 256)] * 3 + [block(8, 256), whole((16, 256))]
    in_specs += [pl.BlockSpec(memory_space=pltpu.SMEM), whole(wat.shape)]
    alias = {}
    if got is not None:
        alias = {len(args): 0}
        args += (got,)
        in_specs += [pl.BlockSpec(memory_space=pl.ANY)]
    return pl.pallas_call(
        lambda *refs: input_grad_body(base, *refs),
        grid_spec=pltpu.PrefetchScalarGridSpec(
            num_scalar_prefetch=1,
            grid=(steps,),
            in_specs=in_specs,
            out_specs=[
                pl.BlockSpec((NB, 256, 256), lambda i, c: (i + base, 0, 0)),
                pl.BlockSpec((8, 128), lambda i, c: (0, 0)),
            ],
            scratch_shapes=[pltpu.VMEM((NB, 288, 768), BF), pltpu.VMEM((NB * 256, 256), F32)],
        ),
        out_shape=[sd((n, 256, 256), F32), sd((8, 128), F32)],
        input_output_aliases=alias,
        cost_estimate=pl.CostEstimate(
            flops=steps * NB * 24 * 2 * 256**3, transcendentals=0, bytes_accessed=steps * NB * 14 * 4 * 256**2
        ),
        compiler_params=VMEM,
        name="input_grad",
    )(*args)


def sinus_embed(steps_in):
    half_width = E // 2
    frequency = jnp.exp(
        -math.log(10000.0) * jnp.arange(half_width, dtype=jnp.float32) / (half_width - 1)
    )
    angles = steps_in.astype(jnp.float32)[:, None] * frequency[None, :]
    return jnp.concatenate([jnp.sin(angles), jnp.cos(angles)], axis=1)


def halves(s0, s1):
    first = jnp.concatenate([s0[:, :64], s1[:, :64]], axis=1)
    second = jnp.concatenate([s0[:, 64:], s1[:, 64:]], axis=1)
    return first, second


def pack_body(conv, embed, attend, output, vec, a_ref, b_ref):
    for side, ref, base in ((0, a_ref, 0), (1, b_ref, 32)):
        for k in range(9):
            w = conv[9 * side + k]
            ref[base + 16 * k : base + 16 * k + 16, :] = jnp.concatenate([w[:16], w[16:]], axis=1).astype(BF)
    line = jnp.concatenate([vec[...], jnp.zeros((1, 32), F32)], axis=1)
    a_ref[144:160, :] = jnp.broadcast_to(line, (16, 128)).astype(BF)
    b_ref[0:32, :] = embed[...].astype(BF)
    at = jnp.concatenate([attend[...], jnp.zeros((64, 32), F32)], axis=1).T
    b_ref[176:224, :] = jnp.concatenate([at[:48], at[48:96]], axis=1).astype(BF)
    o = output[...]
    b_ref[224:240, :] = jnp.concatenate([o[:16], o[16:]], axis=1).astype(BF)


def pack(masters):
    return pl.pallas_call(
        pack_body, out_shape=[sd((RA, 128), BF), sd((RB, 128), BF)], compiler_params=VMEM, name="pack_shards"
    )(*masters)


def swap(x, bits):
    return lax.ppermute(x, AXES, [(i, i ^ bits) for i in range(32)])


def pairs(g, z, lo, rows, h):
    s0 = g[z ^ (2 * h), lo : lo + rows, :]
    s1 = g[z ^ (2 * h + 1), lo : lo + rows, :]
    return halves(s0, s1)


def unpack_a(me, *refs):
    gs = refs[:8]
    wat_ref, vec_ref, vrows = refs[8:]
    z = me[0]
    f = me[1]
    for rf in range(8):
        d0 = (f ^ rf) * 32
        for h in range(2):
            for k in range(9):
                j0, j1 = pairs(gs[rf], z, 16 * k, 16, h)
                at = pl.multiple_of(256 * k + d0, 32)
                wat_ref[pl.ds(at, 16), 128 * h : 128 * h + 128] = j0
                wat_ref[pl.ds(at + 16, 16), 128 * h : 128 * h + 128] = j1
        for rz in range(4):
            vrows[pl.ds((z ^ rz) * 8 + (f ^ rf), 1), :] = gs[rf][rz, 144:160, :].astype(F32)[0:1]
    v = vrows[...]
    v3 = jnp.concatenate([v, pltpu.roll(v, 96, 1), pltpu.roll(v, 64, 1)], axis=0).astype(BF)
    col = lax.broadcasted_iota(jnp.int32, (16, 96), 1)
    line = lax.broadcasted_iota(jnp.int32, (16, 96), 0)
    unit = 3 * (col & 31) + (col >> 5)
    lane = lax.broadcasted_iota(jnp.int32, (16, 128), 1)
    for half in range(2):
        acc = jnp.zeros((16, 128), F32)
        for t in range(4):
            sel = jnp.where(unit == 8 * line + 4 * half + t, 1.0, 0.0).astype(BF)
            piece = dot(sel, v3)
            if t:
                piece = pltpu.roll(piece, 32 * t, 1)
            acc = jnp.where((lane >> 5) == t, piece, acc)
        vec_ref[:, 128 * half : 128 * half + 128] = acc


def unpack_b(me, *refs):
    gs = refs[:8]
    wet_ref, wbt_ref, wqt_ref, wot_ref = refs[8:]
    z = me[0]
    f = me[1]
    for rf in range(8):
        own = f ^ rf
        d0 = own * 32
        g = gs[rf]
        for d in range(4):
            wet_ref[pl.ds(pl.multiple_of(d0, 32), 32), 128 * d : 128 * d + 128] = g[z ^ d, 0:32, :]
        for h in range(2):
            lanes = slice(128 * h, 128 * h + 128)
            for k in range(9):
                j0, j1 = pairs(g, z, 32 + 16 * k, 16, h)
                at = pl.multiple_of(256 * k + d0, 32)
                wbt_ref[pl.ds(at, 16), lanes] = j0
                wbt_ref[pl.ds(at + 16, 16), lanes] = j1
            j0, j1 = pairs(g, z, 176, 48, h)
            at = pl.multiple_of(own * 96, 32)
            wqt_ref[pl.ds(at, 48), lanes] = j0
            wqt_ref[pl.ds(at + 48, 48), lanes] = j1
            j0, j1 = pairs(g, z, 224, 16, h)
            at = pl.multiple_of(d0, 32)
            wot_ref[pl.ds(at, 16), lanes] = j0
            wot_ref[pl.ds(at + 16, 16), lanes] = j1


def place(outs, me, src, base, lanes, lo, rows, step):
    z = me[0]
    f = me[1]
    for rf in range(8):
        at = pl.multiple_of(base + (f ^ rf) * step, 16)
        ref = outs[4 * (rf & 1) + (rf >> 1)]
        for h in range(2):
            cut = slice(lanes + 128 * h, lanes + 128 * h + 128)
            e0, e1 = halves(src[pl.ds(at, rows), cut], src[pl.ds(at + rows, rows), cut])
            ref[z ^ (2 * h), lo : lo + rows, :] = e0.astype(BF)
            ref[z ^ (2 * h + 1), lo : lo + rows, :] = e1.astype(BF)


def finish_all(outs, me, dwa, dwb, dwq, dwo, de, rows, turn):
    for k in range(9):
        place(outs, me, dwa, 256 * (k // 3), 256 * (k % 3), 240 + 16 * k, 16, 32)
        place(outs, me, dwb, 256 * (k // 3), 256 * (k % 3), 16 * k, 16, 32)
    for k in range(3):
        turn[256 * k : 256 * k + 256, 0:256] = dwq[:, 256 * k : 256 * k + 256].T
    place(outs, me, turn, 0, 0, 144, 48, 96)
    place(outs, me, dwo, 0, 0, 192, 16, 32)
    turn[1024:1280, :] = de
    for d in range(4):
        for rf in range(8):
            at = pl.multiple_of(1024 + (me[1] ^ rf) * 32, 32)
            block = turn[pl.ds(at, 32), 128 * d : 128 * d + 128]
            outs[4 * (rf & 1) + (rf >> 1)][me[0] ^ d, 208:240, :] = block.astype(BF)
    outs[8][...] = rows


def over_core(ends):
    got = [swap(v, 1) for v in ends[7:3:-1]][::-1]
    return [(a.astype(F32) + b.astype(F32)).astype(a.dtype) for a, b in zip(ends[:4], got)]


def to_plane(parts):
    return [swap(parts[1], 2), swap(parts[2], 4), swap(parts[3], 6)]


def plane_sum(own, got):
    line = [sum((g[rz].astype(F32) for g in got), own[rz].astype(F32)) for rz in range(4)]
    return line[0], [v.astype(own.dtype) for v in line[1:]]


def over_line(others):
    return [swap(v, 8 * (rz + 1)) for rz, v in enumerate(others)]


def shares_body(own, r1, r2, r3, first, rows, g, out):
    s = own[...] + sum(r[...].astype(F32) for r in (r1, r2, r3))
    g[...] = s
    t = fsum(jnp.sum((s * s).reshape(-1, 8, 128), axis=0))
    for k in range(2, 12):
        out[2 * k : 2 * k + 1, :] = rows[k : k + 1, 0:128]
        out[2 * k + 1 : 2 * k + 2, :] = rows[k : k + 1, 128:256]
    out[0:4, :] = first[0:4, :]
    out[24:32, :] = jnp.broadcast_to(jnp.sum(t, axis=1, keepdims=True), (8, 128))


def shares(own, got, first, rows):
    return pl.pallas_call(
        shares_body, out_shape=[sd((RG, 128), F32), sd((32, 128), F32)], compiler_params=VMEM, name="shares"
    )(own, *got, first, rows)


def total_over(s):
    s = s + swap(s, 1)
    s = (s + swap(s, 2)) + (swap(s, 4) + swap(s, 6))
    return s, swap(s, 8), swap(s, 16), swap(s, 24)


def adam_body(*refs):
    me, t0, t1, t2, t3, grads = refs[:6]
    state = refs[6:21]
    outs = refs[21:-1]
    first = refs[-1]
    total = (t0[...] + t1[...]) + (t2[...] + t3[...])
    first[...] = total
    top = total[0:24]
    norm = jnp.sqrt(jnp.broadcast_to(jnp.sum(fsum(top * top), axis=1, keepdims=True), (1, 128)) + total[24:25])
    lane = lax.broadcasted_iota(jnp.int32, (1, 128), 1)
    vec = jnp.zeros((1, 128), F32)
    for u in range(3):
        unit = 3 * (8 * me[0] + me[1]) + u
        line = pltpu.roll(first[pl.ds(unit >> 2, 1), :], (32 * u + 128 - 32 * (unit & 3)) & 127, 1)
        vec = jnp.where((lane >> 5) == u, line, vec)
    factor = clip_norm / jnp.maximum(norm, clip_norm)

    def put(kind, at, grad):
        clipped = grad * factor[:, : grad.shape[1]]
        mas, mom, squ = (r[at] for r in state[3 * kind : 3 * kind + 3])
        first_new = beta_first * mom + (1.0 - beta_first) * clipped
        second_new = beta_second * squ + (1.0 - beta_second) * clipped * clipped
        first_hat = first_new / (1.0 - beta_first**STEP)
        second_hat = second_new / (1.0 - beta_second**STEP)
        update = mas - rates_kind[kind] * (
            first_hat / (jnp.sqrt(second_hat) + adam_eps) + decays_kind[kind] * mas
        )
        outs[3 * kind][at] = first_new
        outs[3 * kind + 1][at] = second_new
        outs[3 * kind + 2][at] = update

    for side, base in ((0, 240), (1, 0)):
        for k in range(9):
            g = grads[base + 16 * k : base + 16 * k + 16, :]
            put(0, (9 * side + k,), jnp.concatenate([g[:, :64], g[:, 64:]], axis=0))
    put(1, (Ellipsis,), grads[208:240, :])
    g = grads[144:192, :]
    g = jnp.concatenate([jnp.concatenate([g[:, :64], g[:, 64:]], axis=0), jnp.zeros((96, 64), F32)], axis=1)
    g = jnp.concatenate([g, jnp.zeros((32, 128), F32)], axis=0).T
    put(2, (Ellipsis,), g[:64, :96])
    g = grads[192:208, :]
    put(3, (Ellipsis,), jnp.concatenate([g[:, :64], g[:, 64:]], axis=0))
    put(4, (Ellipsis,), vec[:, :96])
    outs[15][0] = norm[0, 0]


def adam(me, totals, grads, state):
    args = (*totals, grads, *state)
    return pl.pallas_call(
        adam_body,
        in_specs=[pl.BlockSpec(memory_space=pltpu.SMEM)] + [pl.BlockSpec(a.shape) for a in args],
        out_specs=[pl.BlockSpec(s.shape) for s in state] + [pl.BlockSpec(memory_space=pltpu.SMEM)],
        out_shape=[sd(s.shape, F32) for s in state] + [sd((1,), F32)],
        scratch_shapes=[pltpu.VMEM((32, 128), F32)],
        compiler_params=VMEM,
        name="clipped_adamw",
    )(me, *args)


def turned_state(state):
    out = []
    for kind in range(5):
        for a in state[3 * kind : 3 * kind + 3]:
            if kind == 0:
                a = jnp.swapaxes(a, 3, 4).reshape(18, 32, 64)
            elif kind == 2:
                a = a[0]
            elif kind < 4:
                a = jnp.swapaxes(a, 1, 2)[0]
            out.append(a)
    return out


def turned_back(results):
    out = []
    for kind in range(5):
        for a in results[3 * kind : 3 * kind + 3]:
            if kind == 0:
                a = jnp.swapaxes(a.reshape(1, 2, 9, 32, 64), 3, 4)
            elif kind == 2:
                a = a[None]
            elif kind < 4:
                a = jnp.swapaxes(a[None], 1, 2)
            out.append(a)
    return out


def per_device_here(images, timesteps, counts, cotangent, *state):
    n_img = images.shape[0]
    state = turned_state(state)
    me = jnp.stack([lax.axis_index("dp"), lax.axis_index("fsdp")]).astype(jnp.int32)
    sa, sb = pack(state[0::3])
    x = images.reshape(n_img, 256, 256)
    cot = cotangent.reshape(n_img, 256, 256)
    cf = figures(counts, x)
    emb = jax.nn.silu(sinus_embed(timesteps)).astype(BF)

    line_a = jnp.stack([sa] + [swap(sa, 8 * rz) for rz in range(1, 4)])
    rows_b = [sb] + [swap(sb, 8 * rz) for rz in range(1, 4)]
    plane_a = [line_a] + [swap(line_a, bits) for bits in (2, 4, 6)]
    rows_b, plane_a, cf, me, emb = lax.optimization_barrier((rows_b, plane_a, cf, me, emb))
    all_a = [p for line in plane_a for p in (line, swap(line, 1))]
    line_b = jnp.stack(rows_b)
    plane_b = [line_b] + [swap(line_b, bits) for bits in (2, 4, 6)]
    all_a, line_b = lax.optimization_barrier((all_a, line_b))
    h0, a1, wat, vec = conv_one(counts, x, cf, me, all_a, unpack_a)
    h0, plane_b = lax.optimization_barrier((h0, plane_b))
    all_b = [p for line in plane_b for p in (line, swap(line, 1))]
    out, ga, dm, *ends, rows = middle(
        counts, x, h0, cot, a1, emb, vec, me, all_b, unpack_b, finish_all, [sd((4, RG, 128), BF)] * 8 + [sd((16, 256), F32)]
    )
    plane_parts = over_core(ends)
    plane = to_plane(plane_parts)
    ga, parts = lax.optimization_barrier((ga, plane_parts))
    ig, v = input_grad(counts, x, ga, dm, cf, vec, me, wat, 0, n_img // NB, None)
    v, plane = lax.optimization_barrier((v, plane))
    own, others = plane_sum(parts[0], plane)
    grads, sums = shares(own, over_line(others), v, rows)
    results = adam(me, total_over(sums), grads, state)
    return (out.reshape(images.shape), ig.reshape(images.shape), *turned_back(results[:15]), results[15].reshape(()))


def gather_flat(masters, dp, fs):
    sizes = [m.size for m in masters]
    total = sum(sizes)
    full = -(-total // 2048) * 2048
    flat = jnp.concatenate([m.reshape(-1).astype(BF) for m in masters] + [jnp.zeros((full - total,), BF)])
    flat = flat.reshape(-1, 128)
    g = lax.all_gather(lax.all_gather(flat, "dp"), "fsdp").reshape(fs, dp, full)
    out = []
    at = 0
    for n in sizes:
        out.append(g[:, :, at : at + n])
        at += n
    conv = out[0].reshape((fs, dp) + masters[0].shape[1:]).transpose(2, 3, 0, 5, 1, 4)
    conv = conv.reshape(2, 2304, 256)
    mats = []
    for p, m in zip(out[1:4], masters[1:4]):
        r, c = m.shape[1:]
        mats.append(p.reshape(fs, dp, r, c).transpose(0, 3, 1, 2).reshape(fs * c, dp * r))
    vec = out[4].transpose(1, 0, 2).reshape(12, 256).astype(F32)
    return conv, mats, vec


def reduce_flat(grads, dp, fs):
    conv, mats, vec = grads
    pieces = [conv.reshape(18, fs, 256 // fs, dp, 256 // dp).transpose(1, 3, 0, 4, 2).reshape(fs, dp, -1)]
    for g in mats:
        c, r = g.shape
        pieces.append(g.reshape(fs, c // fs, dp, r // dp).transpose(0, 2, 3, 1).reshape(fs, dp, -1))
    pieces.append(vec.reshape(dp, fs, -1).transpose(1, 0, 2))
    sizes = [p.shape[2] for p in pieces]
    total = sum(sizes)
    full = -(-total // 2048) * 2048
    pieces.append(jnp.zeros((fs, dp, full - total), F32))
    flat = jnp.concatenate(pieces, axis=2).reshape(fs, dp, -1, 128)
    part = lax.psum_scatter(flat, "fsdp", scatter_dimension=0, tiled=False)
    part = lax.psum_scatter(part, "dp", scatter_dimension=0, tiled=False).reshape(-1)
    out = []
    at = 0
    for n in sizes:
        out.append(part[at : at + n])
        at += n
    return out


def finish_whole(outs, me, dwa, dwb, dwq, dwo, de, rows, turn):
    for out, got in zip(outs, (dwa[...], dwb[...], dwq[...], dwo[...], de, rows)):
        out[...] = got


def fill_one(me, wat, vec, wat_ref, vec_ref, vrows):
    wat_ref[...] = wat[...]
    vec_ref[...] = vec[...]


def fill_rest(me, *refs):
    for k in range(4):
        refs[4 + k][...] = refs[k][...]


def per_device_any(images, timesteps, counts, cotangent, *state):
    masters = state[0::3]
    moments = state[1::3]
    squares = state[2::3]
    dp = lax.axis_size("dp")
    fs = lax.axis_size("fsdp")
    n_img = images.shape[0]
    me = jnp.zeros((2,), jnp.int32)
    emb = jax.nn.silu(sinus_embed(timesteps)).astype(BF)
    x = images.reshape(n_img, 256, 256)
    cot = cotangent.reshape(n_img, 256, 256)
    conv, (wet, wqt, wot), vec = gather_flat(masters, dp, fs)
    vec = jnp.pad(vec, ((0, 4), (0, 0)))
    cf = figures(counts, x)
    h0, a1, wat, vec = conv_one(counts, x, cf, me, (conv[0], vec), fill_one)
    ends = [sd(s, F32) for s in ((768, 768), (768, 768), (256, 768), (256, 256), (256, 512), (16, 256))]
    out, ga, dm, dwa, dwb, dwq, dwo, de, rows = middle(
        counts, x, h0, cot, a1, emb, vec, me, (wet, conv[1], wqt, wot), fill_rest, finish_whole, ends
    )
    ig, first = input_grad(counts, x, ga, dm, cf, vec, me, conv[0], 0, n_img // NB, None)
    first = jnp.pad(first[:4].reshape(2, 256), ((0, 14), (0, 0)))
    apart = lambda w: w.reshape(3, 256, 3, 256).transpose(0, 2, 1, 3).reshape(9, 256, 256)
    shares_here = reduce_flat(
        (jnp.stack([apart(dwa), apart(dwb)]), (de, dwq.T, dwo), (rows + first)[:12]), dp, fs
    )
    local = sum(jnp.sum(s * s) for s in shares_here)
    norm = jnp.sqrt(lax.psum(lax.psum(local, "fsdp"), "dp"))
    factor = clip_norm / jnp.maximum(norm, clip_norm)
    results = []
    for kind in range(5):
        clipped = shares_here[kind].reshape(masters[kind].shape) * factor
        first_new = beta_first * moments[kind] + (1.0 - beta_first) * clipped
        second_new = beta_second * squares[kind] + (1.0 - beta_second) * clipped * clipped
        first_hat = first_new / (1.0 - beta_first**STEP)
        second_hat = second_new / (1.0 - beta_second**STEP)
        update_new = masters[kind] - rates_kind[kind] * (
            first_hat / (jnp.sqrt(second_hat) + adam_eps) + decays_kind[kind] * masters[kind]
        )
        results += [first_new, second_new, update_new]
    return (out.reshape(images.shape), ig.reshape(images.shape), *results, norm)


def solution(mesh):
    both = P(("dp", "fsdp"), None, None, None)
    one = P(("dp", "fsdp"))
    conv = P(None, None, None, "dp", "fsdp")
    mat = P(None, "dp", "fsdp")
    vec = P(None, ("dp", "fsdp"))
    trios = (conv,) * 3 + (mat,) * 9 + (vec,) * 3
    here = mesh.shape["dp"] == 4 and mesh.shape["fsdp"] == 8
    return jax.shard_map(
        per_device_here if here else per_device_any,
        mesh=mesh,
        in_specs=(both, one, one, both) + trios,
        out_specs=(both, both) + trios + (P(),),
        check_vma=False,
    )
```

```python
import math

import jax
import jax.numpy as jnp
from jax import lax
from jax.experimental import pallas as pl
from jax.experimental.pallas import tpu as pltpu
from jax.sharding import PartitionSpec as P

BF = jnp.bfloat16
F32 = jnp.float32
EPS = 1e-6
E = 512
STEP = 10
clip_norm = 1.0
beta_first = 0.9
beta_second = 0.999
adam_eps = 1e-08
rates_kind = (0.01, 0.03, 0.02, 0.05, 0.3)
decays_kind = (0.1, 0.1, 0.1, 0.1, 0.0)
AXES = ("dp", "fsdp")
VMEM = pltpu.CompilerParams(vmem_limit_bytes=60 * 2**20)
NB = 8
HB = 4
CH = 64
R = range(0, 256, CH)
RA = 160
RB = 240
RG = 384

sd = jax.ShapeDtypeStruct


def dot(a, b):
    return lax.dot_general(a, b, (((1,), (0,)), ((), ())), preferred_element_type=F32)


def dot_nt(a, b):
    return lax.dot_general(a, b, (((1,), (1,)), ((), ())), preferred_element_type=F32)


def dot_tn(a, b):
    return lax.dot_general(a, b, (((0,), (0,)), ((), ())), preferred_element_type=F32)


def gsum(s):
    n = s.shape[0]
    c = jnp.concatenate([s[:, :128], s[:, 128:]], axis=0)
    lane = lax.broadcasted_iota(jnp.int32, c.shape, 1)
    for k in (1, 2, 4):
        up = pltpu.roll(c, 128 - k, 1)
        down = pltpu.roll(c, k, 1)
        c = c + jnp.where((lane & k) == 0, up, down)
    return jnp.concatenate([c[:n], c[n:]], axis=1)


def csum(v):
    return jnp.sum(v.reshape(-1, 8, v.shape[-1]), axis=0)


def fsum(v):
    return jnp.sum(v, axis=0, keepdims=True)


def row_sums(load, base):
    s1 = s2 = None
    for r in R:
        v = load(r) - base
        a = csum(v)
        b = csum(v * v)
        s1 = a if s1 is None else s1 + a
        s2 = b if s2 is None else s2 + b
    return fsum(s1), fsum(s2)


def stats(loads, extras=None):
    firsts = [load(0)[0:1] for load in loads]
    p = jnp.concatenate(firsts, axis=0)
    if extras is not None:
        p = p + jnp.concatenate(extras, axis=0)
    q = gsum(p) * 0.125
    sums = [row_sums(load, first) for load, first in zip(loads, firsts)]
    s1 = jnp.concatenate([t[0] for t in sums], axis=0)
    s2 = jnp.concatenate([t[1] for t in sums], axis=0)
    d = p - q
    g = gsum(jnp.concatenate([s1 + 256.0 * d, s2 + d * (2.0 * s1 + 256.0 * d)], axis=0)) * (1.0 / 2048.0)
    n = len(loads)
    dm = g[:n]
    return q + dm, lax.rsqrt(g[n:] - dm * dm + EPS)


def back_coefs(sum_dy, sum_dyn, gain, rs, m):
    n = sum_dy.shape[0]
    g = gsum(jnp.concatenate([sum_dy * gain, sum_dyn * gain], axis=0)) * (1.0 / 2048.0)
    be = -rs * rs * g[n:]
    return rs * gain, be, -rs * g[:n] - m * be


def put3(pref, n, r, a, rev=False):
    rows = a.shape[0]
    col = lax.broadcasted_iota(jnp.int32, a.shape, 0) & 15
    prev = jnp.where(col == 0, 0.0, pltpu.roll(a, 1, 0))
    post = jnp.where(col == 15, 0.0, pltpu.roll(a, rows - 1, 0))
    lo, hi = (post, prev) if rev else (prev, post)
    low = a.astype(BF)
    pref[n, 16 + r : 16 + r + rows, 0:256] = lo.astype(BF)
    pref[n, 16 + r : 16 + r + rows, 256:512] = low
    pref[n, 16 + r : 16 + r + rows, 512:768] = hi.astype(BF)
    return low


def zero_pads(pref):
    z = jnp.zeros((16, 768), BF)
    for n in range(NB):
        pref[n, 0:16, :] = z
        pref[n, 272:288, :] = z


def conv_forward(pref, wt_ref, N):
    acc = None
    for i in range(3):
        for j in range(3):
            rows = pref[N.start : N.stop, 16 * i : 16 * i + 256, 256 * j : 256 * j + 256]
            k = 3 * i + j
            d = dot_nt(rows.reshape(len(N) * 256, 256), wt_ref[256 * k : 256 * k + 256, :])
            acc = d if acc is None else acc + d
    return acc


def conv_turned(pref, wt_ref, N):
    acc = None
    for i in range(3):
        o = 16 * (2 - i)
        rows = pref[N.start : N.stop, o : o + 256, :].reshape(len(N) * 256, 768)
        d = dot(rows, wt_ref[768 * i : 768 * i + 768, :])
        acc = d if acc is None else acc + d
    return acc


def add_taps(acc_ref, gt, pref, N):
    for i in range(3):
        rows = pref[N.start : N.stop, 16 * i : 16 * i + 256, :].reshape(len(N) * 256, 768)
        acc_ref[256 * i : 256 * i + 256, :] += dot(gt, rows)


def interleave(gens):
    gens = list(gens)
    done = [False] * len(gens)
    at = 0
    while not all(done):
        for j, g in enumerate(gens):
            if not done[j] and at >= j:
                try:
                    next(g)
                except StopIteration:
                    done[j] = True
        at += 1


def parts():
    return [range(j, j + HB) for j in range(0, NB, HB)]


def row(ref, j):
    return ref[j : j + 1, :]


def whole(shape):
    return pl.BlockSpec(shape, lambda i, c: (0,) * len(shape))


def clamped(i, c):
    return jnp.minimum(i, (c[0] - 1) // NB)


def blocks(*tail):
    return pl.BlockSpec((NB,) + tail, lambda i, c: (clamped(i, c),) + (0,) * len(tail))


ANY = pl.BlockSpec(memory_space=pl.ANY)


def out_blocks(*tail):
    return pl.BlockSpec((NB,) + tail, lambda i, c: (i,) + (0,) * len(tail))


def image_call(body, name, n_img, cost, in_specs, out_specs, out_shape, scratch, args):
    products, passes = cost
    return pl.pallas_call(
        body,
        grid_spec=pltpu.PrefetchScalarGridSpec(
            num_scalar_prefetch=1,
            grid=(n_img // NB,),
            in_specs=in_specs,
            out_specs=out_specs,
            scratch_shapes=scratch,
        ),
        out_shape=out_shape,
        cost_estimate=pl.CostEstimate(
            flops=n_img * products * 2 * 256**3,
            transcendentals=n_img * passes * 256**2,
            bytes_accessed=n_img * passes * 4 * 256**2,
        ),
        compiler_params=VMEM,
        name=name,
    )(*args)


def figures_body(cnt_ref, x_ref, cf_ref):
    @pl.when(pl.program_id(0) * NB < cnt_ref[0])
    def _():
        m, rs = stats([lambda r, n=n: x_ref[n, r : r + CH, :].astype(F32) for n in range(NB)])
        for n in range(NB):
            cf_ref[n] = jnp.concatenate([m[n : n + 1], rs[n : n + 1], jnp.zeros((6, 256), F32)], axis=0)


def figures(cnt, x):
    n = x.shape[0]
    return image_call(
        figures_body, "figures", n, (1, 2), [blocks(256, 256)], out_blocks(8, 256), sd((n, 8, 256), F32), [], (cnt, x)
    )


def conv_one_body(fill, *refs):
    cnt_ref, x_ref, cf_ref, me_ref = refs[:4]
    given = refs[4:-6]
    h0_ref, a1_ref, wat_ref, vec_ref, pa, vrows = refs[-6:]

    @pl.when(pl.program_id(0) == 0)
    def _():
        zero_pads(pa)
        fill(me_ref, *given, wat_ref, vec_ref, vrows)

    @pl.when(pl.program_id(0) * NB < cnt_ref[0])
    def _():
        def part(N):
            for n in N:
                sc = 0.5 * cf_ref[n, 1:2, :] * row(vec_ref, 0)
                sh = 0.5 * row(vec_ref, 1) - cf_ref[n, 0:1, :] * sc
                for r in R:
                    h = x_ref[n, r : r + CH, :].astype(F32) * sc + sh
                    a1_ref[n, r : r + CH, :] = put3(pa, n, r, h + h * jnp.tanh(h))
            yield
            h0_ref[N.start : N.stop] = conv_forward(pa, wat_ref, N).reshape(len(N), 256, 256)
            yield

        interleave([part(N) for N in parts()])


def conv_one(cnt, x, cf, me, given, fill):
    n = x.shape[0]
    return image_call(
        lambda *refs: conv_one_body(fill, *refs),
        "conv_one",
        n,
        (18, 10),
        [blocks(256, 256), blocks(8, 256), pl.BlockSpec(memory_space=pltpu.SMEM)] + [whole(g.shape) for g in given],
        [out_blocks(256, 256), out_blocks(256, 256), whole((2304, 256)), whole((16, 256))],
        [sd((n, 256, 256), F32), sd((n, 256, 256), BF), sd((2304, 256), BF), sd((16, 256), F32)],
        [pltpu.VMEM((NB, 288, 768), BF), pltpu.VMEM((32, 128), F32)],
        (cnt, x, cf, me, *given),
    )


def middle_body(fill, n_given, finish, n_out, *refs):
    (cnt_ref, x_ref, h0_ref, cot_ref, a1_ref, emb_ref, vec_ref, me_ref) = refs[:8]
    given = refs[8 : 8 + n_given]
    refs = refs[8 + n_given :]
    out_ref, ga_ref, dm_ref = refs[:3]
    ends = refs[3 : 3 + n_out]
    refs = refs[3 + n_out :]
    (pa, pg, pa1, gt, gt1, mid, a3, mx, dmx, dz, she, dsr, dwa, dwb, dwq, dwo, dvec, turn) = refs[:18]
    wet_ref, wbt_ref, wqt_ref, wot_ref = refs[18:]
    i = pl.program_id(0)
    cnt = cnt_ref[0]

    @pl.when(i == 0)
    def _():
        zero_pads(pa)
        zero_pads(pg)
        zero_pads(pa1)
        for ref in (dwa, dwb, dwq, dwo, dvec, dsr):
            ref[...] = jnp.zeros_like(ref)
        fill(me_ref, *given, wet_ref, wbt_ref, wqt_ref, wot_ref)
        she[...] = dot_nt(emb_ref[...], wet_ref[...]) + (row(vec_ref, 2) + row(vec_ref, 3))

    live = i * NB < cnt

    @pl.when(jnp.logical_not(live))
    def _():
        for ref in (out_ref, ga_ref, dm_ref):
            ref[...] = jnp.zeros_like(ref)

    @pl.when(live)
    def _():
        g2, b2, c2, g3, b3, qb, vb, ob = (row(vec_ref, j) for j in range(4, 12))
        tot = {}

        def add(key, v):
            tot[key] = v if key not in tot else tot[key] + v

        def part(N):
            lo = N.start * 256
            hi = N.stop * 256
            W = range(len(N))
            L = lambda j: slice(j * 256, j * 256 + 256)
            masks = [(i * NB + n < cnt).astype(F32) for n in N]
            shifts = [she[pl.ds(i * NB + n, 1), :] for n in N]
            br = jnp.concatenate(shifts, axis=0)
            hload = [lambda r, n=n: h0_ref[n, r : r + CH, :] for n in N]
            m2, rs2 = stats(hload, shifts)
            sc2 = 0.5 * rs2 * g2
            sh2 = 0.5 * b2 + (br - m2) * sc2
            hm2 = br - m2
            for j, n in enumerate(N):
                for r in R:
                    h = hload[j](r) * sc2[j : j + 1] + sh2[j : j + 1]
                    put3(pa, n, r, h + h * jnp.tanh(h))
            yield
            o = conv_forward(pa, wbt_ref, N)
            yield
            for j, n in enumerate(N):
                for r in R:
                    mid[n, r : r + CH, :] = o[j * 256 + r : j * 256 + r + CH] + (x_ref[n, r : r + CH, :].astype(F32) + c2)
            mload = [lambda r, n=n: mid[n, r : r + CH, :] for n in N]
            m3, rs3 = stats(mload)
            sc3 = rs3 * g3
            sh3 = b3 - m3 * sc3
            for j, n in enumerate(N):
                for r in R:
                    a3[n * 256 + r : n * 256 + r + CH, :] = (mload[j](r) * sc3[j : j + 1] + sh3[j : j + 1]).astype(BF)
            gob = []
            for j, n in enumerate(N):
                go = cot_ref[n].astype(F32) * masks[j]
                add("ob", csum(go))
                gob.append(go.astype(BF))
            gall = jnp.concatenate(gob, axis=0)
            yield
            bc = jnp.concatenate([qb, jnp.zeros_like(qb), vb], axis=1)
            mx[lo:hi] = (dot_nt(a3[lo:hi], wqt_ref[...]) + bc).astype(BF)
            M = lambda j, p: mx[lo + j * 256 : lo + j * 256 + 256, 256 * p : 256 * p + 256]
            datt = dot(gall, wot_ref[...]).astype(BF)
            yield
            st = [dot_nt(M(j, 1), M(j, 0)) for j in W]
            dpt = [dot_nt(M(j, 2), datt[L(j)]) for j in W]
            yield
            pts = []
            ptb = []
            for j in W:
                s = st[j] * 0.0625
                e = jnp.exp(s - jnp.max(s, axis=0, keepdims=True))
                p = e * (1.0 / jnp.sum(e, axis=0, keepdims=True))
                pts.append(p)
                ptb.append(p.astype(BF))
            yield
            att = [dot_tn(ptb[j], M(j, 2)).astype(BF) for j in W]
            dv = [dot(ptb[j], datt[L(j)]).astype(BF) for j in W]
            yield
            dst = []
            for n in N:
                for r in R:
                    put3(pa1, n, r, a1_ref[n, r : r + CH, :].astype(F32))
            for j in W:
                t = dpt[j] * pts[j]
                dst.append((t - pts[j] * jnp.sum(t, axis=0, keepdims=True)).astype(BF))
            yield
            attall = jnp.concatenate(att, axis=0)
            proj = dot_nt(attall, wot_ref[...])
            dwo[...] += dot_tn(gall, attall)
            dq = [(dot_tn(dst[j], M(j, 1)) * 0.0625).astype(BF) for j in W]
            dk = [(dot(dst[j], M(j, 0)) * 0.0625).astype(BF) for j in W]
            yield
            for j, n in enumerate(N):
                out_ref[n] = (mid[n] + (proj[L(j)] + ob)) * masks[j]
                s = slice(n * 256, n * 256 + 256)
                dmx[s, 0:256] = dq[j]
                dmx[s, 256:512] = dk[j]
                dmx[s, 512:768] = dv[j]
                add("qb", csum(dq[j].astype(F32)))
                add("vb", csum(dv[j].astype(F32)))
            yield
            d3 = dot(dmx[lo:hi], wqt_ref[...])
            dwq[...] += dot_tn(a3[lo:hi], dmx[lo:hi])
            yield
            As = []
            Bs = []
            for j, n in enumerate(N):
                A = B = jnp.zeros((8, 256), F32)
                for r in R:
                    dy = d3[j * 256 + r : j * 256 + r + CH]
                    A = A + csum(dy)
                    B = B + csum(dy * (mid[n, r : r + CH, :] - m3[j : j + 1]))
                As.append(fsum(A))
                Bs.append(fsum(B))
            A3 = jnp.concatenate(As, axis=0)
            B3 = jnp.concatenate(Bs, axis=0) * rs3
            add("b3", fsum(A3))
            add("g3", fsum(B3))
            al, be, ga = back_coefs(A3, B3, g3, rs3, m3)
            for j, n in enumerate(N):
                for r in R:
                    dm = cot_ref[n, r : r + CH, :].astype(F32) * masks[j] + (
                        d3[j * 256 + r : j * 256 + r + CH] * al[j : j + 1]
                        + (mid[n, r : r + CH, :] * be[j : j + 1] + ga[j : j + 1])
                    )
                    dm_ref[n, r : r + CH, :] = dm
                    add("c2", csum(dm))
                    put3(pg, n, r, dm, True)
                gt[:, n * 256 : n * 256 + 256] = pg[n, 16:272, 256:512].T
            yield
            o = conv_turned(pg, wbt_ref, N)
            add_taps(dwb, gt[:, lo:hi], pa, N)
            yield
            As = []
            Bs = []
            for j, n in enumerate(N):
                A = B = jnp.zeros((8, 256), F32)
                for r in R:
                    h0 = hload[j](r)
                    h = h0 * sc2[j : j + 1] + sh2[j : j + 1]
                    t = jnp.tanh(h)
                    dzz = o[j * 256 + r : j * 256 + r + CH] * ((1.0 + t) * (1.0 + (h - h * t)))
                    dz[n * 256 + r : n * 256 + r + CH, :] = dzz
                    A = A + csum(dzz)
                    B = B + csum(dzz * (h0 + hm2[j : j + 1]))
                As.append(fsum(A))
                Bs.append(fsum(B))
            A2 = jnp.concatenate(As, axis=0) * 0.5
            B2 = jnp.concatenate(Bs, axis=0) * (rs2 * 0.5)
            add("b2", fsum(A2))
            add("g2", fsum(B2))
            al, be, ga = back_coefs(A2, B2, g2, rs2, -hm2)
            al = al * 0.5
            for j, n in enumerate(N):
                ds = jnp.zeros((8, 256), F32)
                for r in R:
                    dh = dz[n * 256 + r : n * 256 + r + CH, :] * al[j : j + 1] + (
                        hload[j](r) * be[j : j + 1] + ga[j : j + 1]
                    )
                    ga_ref[n, r : r + CH, :] = dh.astype(BF)
                    ds = ds + csum(dh)
                dsr[pl.ds(i * NB + n, 1), :] = fsum(ds)
                gt1[:, n * 256 : n * 256 + 256] = ga_ref[n].T
            yield
            add_taps(dwa, gt1[:, lo:hi], pa1, N)
            yield

        interleave([part(N) for N in parts()])
        z = jnp.zeros((4, 256), F32)
        rows = [tot["g2"], tot["b2"], fsum(tot["c2"]), tot["g3"], tot["b3"]]
        rows += [fsum(tot[k]) for k in ("qb", "vb", "ob")]
        dvec[...] += jnp.concatenate([z] + rows + [z], axis=0)

    @pl.when(i == pl.num_programs(0) - 1)
    def _():
        ds = dsr[...]
        total = fsum(ds)
        rows = jnp.concatenate([jnp.zeros((2, 256), F32), total, total, dvec[4:16, :]], axis=0)
        finish(ends, me_ref, dwa, dwb, dwq, dwo, dot_tn(ds.astype(BF), emb_ref[...]), rows, turn)


def middle(cnt, x, h0, cot, a1, emb, vec, me, given, fill, finish, ends):
    n = x.shape[0]
    V = pltpu.VMEM
    return image_call(
        lambda *refs: middle_body(fill, len(given), finish, len(ends), *refs),
        "middle",
        n,
        (108, 44),
        [blocks(256, 256)] * 4
        + [whole(emb.shape), whole((16, 256)), pl.BlockSpec(memory_space=pltpu.SMEM)]
        + [whole(w.shape) for w in given],
        [out_blocks(256, 256)] * 3 + [whole(e.shape) for e in ends],
        [sd((n, 256, 256), F32), sd((n, 256, 256), BF), sd((n, 256, 256), F32)] + list(ends),
        [
            V((NB, 288, 768), BF),
            V((NB, 288, 768), BF),
            V((NB, 288, 768), BF),
            V((256, NB * 256), BF),
            V((256, NB * 256), BF),
            V((NB, 256, 256), F32),
            V((NB * 256, 256), BF),
            V((NB * 256, 768), BF),
            V((NB * 256, 768), BF),
            V((NB * 256, 256), F32),
            V((n, 256), F32),
            V((n, 256), F32),
            V((768, 768), F32),
            V((768, 768), F32),
            V((256, 768), F32),
            V((256, 256), F32),
            V((16, 256), F32),
            V((1280, 512), F32),
            V((256, 512), BF),
            V((2304, 256), BF),
            V((768, 256), BF),
            V((256, 256), BF),
        ],
        (cnt, x, h0, cot, a1, emb, vec, me, *given),
    )


def input_grad_body(base, *refs):
    cnt_ref, x_ref, ga_ref, dm_ref, cf_ref, vec_ref, me_ref, wat_ref = refs[:8]
    ig_ref, dvec, pg, dz = refs[-4:]
    i = pl.program_id(0)

    @pl.when(i == 0)
    def _():
        zero_pads(pg)
        dvec[...] = jnp.zeros_like(dvec)

    live = (i + base) * NB < cnt_ref[0]

    @pl.when(jnp.logical_not(live))
    def _():
        ig_ref[...] = jnp.zeros_like(ig_ref)

    @pl.when(live)
    def _():
        g1 = row(vec_ref, 0)
        tot = {}

        def add(key, v):
            tot[key] = v if key not in tot else tot[key] + v

        def part(N):
            for n in N:
                for r in R:
                    put3(pg, n, r, ga_ref[n, r : r + CH, :].astype(F32), True)
            yield
            o = conv_turned(pg, wat_ref, N)
            yield
            As = []
            Bs = []
            ms = jnp.concatenate([cf_ref[n, 0:1, :] for n in N], axis=0)
            rss = jnp.concatenate([cf_ref[n, 1:2, :] for n in N], axis=0)
            for j, n in enumerate(N):
                m = cf_ref[n, 0:1, :]
                sc = 0.5 * cf_ref[n, 1:2, :] * g1
                sh = 0.5 * row(vec_ref, 1) - m * sc
                A = B = jnp.zeros((8, 256), F32)
                for r in R:
                    x = x_ref[n, r : r + CH, :].astype(F32)
                    h = x * sc + sh
                    t = jnp.tanh(h)
                    dzz = o[j * 256 + r : j * 256 + r + CH] * ((1.0 + t) * (1.0 + (h - h * t)))
                    dz[n * 256 + r : n * 256 + r + CH, :] = dzz
                    A = A + csum(dzz)
                    B = B + csum(dzz * (x - m))
                As.append(fsum(A))
                Bs.append(fsum(B))
            A1 = jnp.concatenate(As, axis=0) * 0.5
            B1 = jnp.concatenate(Bs, axis=0) * (rss * 0.5)
            add("b1", fsum(A1))
            add("g1", fsum(B1))
            al, be, ga = back_coefs(A1, B1, g1, rss, ms)
            al = al * 0.5
            for j, n in enumerate(N):
                for r in R:
                    ig_ref[n, r : r + CH, :] = dm_ref[n, r : r + CH, :] + (
                        dz[n * 256 + r : n * 256 + r + CH, :] * al[j : j + 1]
                        + (x_ref[n, r : r + CH, :].astype(F32) * be[j : j + 1] + ga[j : j + 1])
                    )
            yield

        interleave([part(N) for N in parts()])
        g = tot["g1"]
        b = tot["b1"]
        z = jnp.zeros((4, 128), F32)
        dvec[...] += jnp.concatenate([g[:, :128], g[:, 128:], b[:, :128], b[:, 128:], z], axis=0)


def input_grad(cnt, x, ga, dm, cf, vec, me, wat, base, steps, got):
    n = x.shape[0]
    at = lambda i, c: jnp.minimum(i + base, jnp.maximum((c[0] - 1) // NB, base))
    block = lambda *tail: pl.BlockSpec((NB,) + tail, lambda i, c: (at(i, c),) + (0,) * len(tail))
    args = (cnt, x, ga, dm, cf, vec, me, wat)
    in_specs = [block(256, 256)] * 3 + [block(8, 256), whole((16, 256))]
    in_specs += [pl.BlockSpec(memory_space=pltpu.SMEM), whole(wat.shape)]
    alias = {}
    if got is not None:
        alias = {len(args): 0}
        args += (got,)
        in_specs += [pl.BlockSpec(memory_space=pl.ANY)]
    return pl.pallas_call(
        lambda *refs: input_grad_body(base, *refs),
        grid_spec=pltpu.PrefetchScalarGridSpec(
            num_scalar_prefetch=1,
            grid=(steps,),
            in_specs=in_specs,
            out_specs=[
                pl.BlockSpec((NB, 256, 256), lambda i, c: (i + base, 0, 0)),
                pl.BlockSpec((8, 128), lambda i, c: (0, 0)),
            ],
            scratch_shapes=[pltpu.VMEM((NB, 288, 768), BF), pltpu.VMEM((NB * 256, 256), F32)],
        ),
        out_shape=[sd((n, 256, 256), F32), sd((8, 128), F32)],
        input_output_aliases=alias,
        cost_estimate=pl.CostEstimate(
            flops=steps * NB * 24 * 2 * 256**3, transcendentals=0, bytes_accessed=steps * NB * 14 * 4 * 256**2
        ),
        compiler_params=VMEM,
        name="input_grad",
    )(*args)


def sinus_embed(steps_in):
    half_width = E // 2
    frequency = jnp.exp(
        -math.log(10000.0) * jnp.arange(half_width, dtype=jnp.float32) / (half_width - 1)
    )
    angles = steps_in.astype(jnp.float32)[:, None] * frequency[None, :]
    return jnp.concatenate([jnp.sin(angles), jnp.cos(angles)], axis=1)


def halves(s0, s1):
    first = jnp.concatenate([s0[:, :64], s1[:, :64]], axis=1)
    second = jnp.concatenate([s0[:, 64:], s1[:, 64:]], axis=1)
    return first, second


def pack_body(conv, embed, attend, output, vec, a_ref, b_ref):
    for side, ref, base in ((0, a_ref, 0), (1, b_ref, 32)):
        for k in range(9):
            w = conv[9 * side + k]
            ref[base + 16 * k : base + 16 * k + 16, :] = jnp.concatenate([w[:16], w[16:]], axis=1).astype(BF)
    line = jnp.concatenate([vec[...], jnp.zeros((1, 32), F32)], axis=1)
    a_ref[144:160, :] = jnp.broadcast_to(line, (16, 128)).astype(BF)
    b_ref[0:32, :] = embed[...].astype(BF)
    at = jnp.concatenate([attend[...], jnp.zeros((64, 32), F32)], axis=1).T
    b_ref[176:224, :] = jnp.concatenate([at[:48], at[48:96]], axis=1).astype(BF)
    o = output[...]
    b_ref[224:240, :] = jnp.concatenate([o[:16], o[16:]], axis=1).astype(BF)


def pack(masters):
    return pl.pallas_call(
        pack_body, out_shape=[sd((RA, 128), BF), sd((RB, 128), BF)], compiler_params=VMEM, name="pack_shards"
    )(*masters)


def swap(x, bits):
    return lax.ppermute(x, AXES, [(i, i ^ bits) for i in range(32)])


def pairs(g, z, lo, rows, h):
    s0 = g[z ^ (2 * h), lo : lo + rows, :]
    s1 = g[z ^ (2 * h + 1), lo : lo + rows, :]
    return halves(s0, s1)


def unpack_a(me, *refs):
    gs = refs[:8]
    wat_ref, vec_ref, vrows = refs[8:]
    z = me[0]
    f = me[1]
    for rf in range(8):
        d0 = (f ^ rf) * 32
        for h in range(2):
            for k in range(9):
                j0, j1 = pairs(gs[rf], z, 16 * k, 16, h)
                at = pl.multiple_of(256 * k + d0, 32)
                wat_ref[pl.ds(at, 16), 128 * h : 128 * h + 128] = j0
                wat_ref[pl.ds(at + 16, 16), 128 * h : 128 * h + 128] = j1
        for rz in range(4):
            vrows[pl.ds((z ^ rz) * 8 + (f ^ rf), 1), :] = gs[rf][rz, 144:160, :].astype(F32)[0:1]
    v = vrows[...]
    v3 = jnp.concatenate([v, pltpu.roll(v, 96, 1), pltpu.roll(v, 64, 1)], axis=0).astype(BF)
    col = lax.broadcasted_iota(jnp.int32, (16, 96), 1)
    line = lax.broadcasted_iota(jnp.int32, (16, 96), 0)
    unit = 3 * (col & 31) + (col >> 5)
    lane = lax.broadcasted_iota(jnp.int32, (16, 128), 1)
    for half in range(2):
        acc = jnp.zeros((16, 128), F32)
        for t in range(4):
            sel = jnp.where(unit == 8 * line + 4 * half + t, 1.0, 0.0).astype(BF)
            piece = dot(sel, v3)
            if t:
                piece = pltpu.roll(piece, 32 * t, 1)
            acc = jnp.where((lane >> 5) == t, piece, acc)
        vec_ref[:, 128 * half : 128 * half + 128] = acc


def unpack_b(me, *refs):
    gs = refs[:8]
    wet_ref, wbt_ref, wqt_ref, wot_ref = refs[8:]
    z = me[0]
    f = me[1]
    for rf in range(8):
        own = f ^ rf
        d0 = own * 32
        g = gs[rf]
        for d in range(4):
            wet_ref[pl.ds(pl.multiple_of(d0, 32), 32), 128 * d : 128 * d + 128] = g[z ^ d, 0:32, :]
        for h in range(2):
            lanes = slice(128 * h, 128 * h + 128)
            for k in range(9):
                j0, j1 = pairs(g, z, 32 + 16 * k, 16, h)
                at = pl.multiple_of(256 * k + d0, 32)
                wbt_ref[pl.ds(at, 16), lanes] = j0
                wbt_ref[pl.ds(at + 16, 16), lanes] = j1
            j0, j1 = pairs(g, z, 176, 48, h)
            at = pl.multiple_of(own * 96, 32)
            wqt_ref[pl.ds(at, 48), lanes] = j0
            wqt_ref[pl.ds(at + 48, 48), lanes] = j1
            j0, j1 = pairs(g, z, 224, 16, h)
            at = pl.multiple_of(d0, 32)
            wot_ref[pl.ds(at, 16), lanes] = j0
            wot_ref[pl.ds(at + 16, 16), lanes] = j1


def place(outs, me, src, base, lanes, lo, rows, step):
    z = me[0]
    f = me[1]
    for rf in range(8):
        at = pl.multiple_of(base + (f ^ rf) * step, 16)
        ref = outs[4 * (rf & 1) + (rf >> 1)]
        for h in range(2):
            cut = slice(lanes + 128 * h, lanes + 128 * h + 128)
            e0, e1 = halves(src[pl.ds(at, rows), cut], src[pl.ds(at + rows, rows), cut])
            ref[z ^ (2 * h), lo : lo + rows, :] = e0.astype(BF)
            ref[z ^ (2 * h + 1), lo : lo + rows, :] = e1.astype(BF)


def finish_all(outs, me, dwa, dwb, dwq, dwo, de, rows, turn):
    for k in range(9):
        place(outs, me, dwa, 256 * (k // 3), 256 * (k % 3), 240 + 16 * k, 16, 32)
        place(outs, me, dwb, 256 * (k // 3), 256 * (k % 3), 16 * k, 16, 32)
    for k in range(3):
        turn[256 * k : 256 * k + 256, 0:256] = dwq[:, 256 * k : 256 * k + 256].T
    place(outs, me, turn, 0, 0, 144, 48, 96)
    place(outs, me, dwo, 0, 0, 192, 16, 32)
    turn[1024:1280, :] = de
    for d in range(4):
        for rf in range(8):
            at = pl.multiple_of(1024 + (me[1] ^ rf) * 32, 32)
            block = turn[pl.ds(at, 32), 128 * d : 128 * d + 128]
            outs[4 * (rf & 1) + (rf >> 1)][me[0] ^ d, 208:240, :] = block.astype(BF)
    outs[8][...] = rows


def over_core(ends):
    got = [swap(v, 1) for v in ends[7:3:-1]][::-1]
    return [(a.astype(F32) + b.astype(F32)).astype(a.dtype) for a, b in zip(ends[:4], got)]


def to_plane(parts):
    return [swap(parts[1], 2), swap(parts[2], 4), swap(parts[3], 6)]


def plane_sum(own, got):
    line = [sum((g[rz].astype(F32) for g in got), own[rz].astype(F32)) for rz in range(4)]
    return line[0], [v.astype(own.dtype) for v in line[1:]]


def over_line(others):
    return [swap(v, 8 * (rz + 1)) for rz, v in enumerate(others)]


def shares_body(own, r1, r2, r3, first, rows, g, out):
    s = own[...] + sum(r[...].astype(F32) for r in (r1, r2, r3))
    g[...] = s
    t = fsum(jnp.sum((s * s).reshape(-1, 8, 128), axis=0))
    for k in range(2, 12):
        out[2 * k : 2 * k + 1, :] = rows[k : k + 1, 0:128]
        out[2 * k + 1 : 2 * k + 2, :] = rows[k : k + 1, 128:256]
    out[0:4, :] = first[0:4, :]
    out[24:32, :] = jnp.broadcast_to(jnp.sum(t, axis=1, keepdims=True), (8, 128))


def shares(own, got, first, rows):
    return pl.pallas_call(
        shares_body, out_shape=[sd((RG, 128), F32), sd((32, 128), F32)], compiler_params=VMEM, name="shares"
    )(own, *got, first, rows)


def total_over(s):
    s = s + swap(s, 1)
    s = (s + swap(s, 2)) + (swap(s, 4) + swap(s, 6))
    return s, swap(s, 8), swap(s, 16), swap(s, 24)


def adam_body(*refs):
    me, t0, t1, t2, t3, grads = refs[:6]
    state = refs[6:21]
    outs = refs[21:-1]
    first = refs[-1]
    total = (t0[...] + t1[...]) + (t2[...] + t3[...])
    first[...] = total
    top = total[0:24]
    norm = jnp.sqrt(jnp.broadcast_to(jnp.sum(fsum(top * top), axis=1, keepdims=True), (1, 128)) + total[24:25])
    lane = lax.broadcasted_iota(jnp.int32, (1, 128), 1)
    vec = jnp.zeros((1, 128), F32)
    for u in range(3):
        unit = 3 * (8 * me[0] + me[1]) + u
        line = pltpu.roll(first[pl.ds(unit >> 2, 1), :], (32 * u + 128 - 32 * (unit & 3)) & 127, 1)
        vec = jnp.where((lane >> 5) == u, line, vec)
    factor = clip_norm / jnp.maximum(norm, clip_norm)

    def put(kind, at, grad):
        clipped = grad * factor[:, : grad.shape[1]]
        mas, mom, squ = (r[at] for r in state[3 * kind : 3 * kind + 3])
        first_new = beta_first * mom + (1.0 - beta_first) * clipped
        second_new = beta_second * squ + (1.0 - beta_second) * clipped * clipped
        first_hat = first_new / (1.0 - beta_first**STEP)
        second_hat = second_new / (1.0 - beta_second**STEP)
        update = mas - rates_kind[kind] * (
            first_hat / (jnp.sqrt(second_hat) + adam_eps) + decays_kind[kind] * mas
        )
        outs[3 * kind][at] = first_new
        outs[3 * kind + 1][at] = second_new
        outs[3 * kind + 2][at] = update

    for side, base in ((0, 240), (1, 0)):
        for k in range(9):
            g = grads[base + 16 * k : base + 16 * k + 16, :]
            put(0, (9 * side + k,), jnp.concatenate([g[:, :64], g[:, 64:]], axis=0))
    put(1, (Ellipsis,), grads[208:240, :])
    g = grads[144:192, :]
    g = jnp.concatenate([jnp.concatenate([g[:, :64], g[:, 64:]], axis=0), jnp.zeros((96, 64), F32)], axis=1)
    g = jnp.concatenate([g, jnp.zeros((32, 128), F32)], axis=0).T
    put(2, (Ellipsis,), g[:64, :96])
    g = grads[192:208, :]
    put(3, (Ellipsis,), jnp.concatenate([g[:, :64], g[:, 64:]], axis=0))
    put(4, (Ellipsis,), vec[:, :96])
    outs[15][0] = norm[0, 0]


def adam(me, totals, grads, state):
    args = (*totals, grads, *state)
    return pl.pallas_call(
        adam_body,
        in_specs=[pl.BlockSpec(memory_space=pltpu.SMEM)] + [pl.BlockSpec(a.shape) for a in args],
        out_specs=[pl.BlockSpec(s.shape) for s in state] + [pl.BlockSpec(memory_space=pltpu.SMEM)],
        out_shape=[sd(s.shape, F32) for s in state] + [sd((1,), F32)],
        scratch_shapes=[pltpu.VMEM((32, 128), F32)],
        compiler_params=VMEM,
        name="clipped_adamw",
    )(me, *args)


def turned_state(state):
    out = []
    for kind in range(5):
        for a in state[3 * kind : 3 * kind + 3]:
            if kind == 0:
                a = jnp.swapaxes(a, 3, 4).reshape(18, 32, 64)
            elif kind == 2:
                a = a[0]
            elif kind < 4:
                a = jnp.swapaxes(a, 1, 2)[0]
            out.append(a)
    return out


def turned_back(results):
    out = []
    for kind in range(5):
        for a in results[3 * kind : 3 * kind + 3]:
            if kind == 0:
                a = jnp.swapaxes(a.reshape(1, 2, 9, 32, 64), 3, 4)
            elif kind == 2:
                a = a[None]
            elif kind < 4:
                a = jnp.swapaxes(a[None], 1, 2)
            out.append(a)
    return out


def per_device_here(images, timesteps, counts, cotangent, *state):
    n_img = images.shape[0]
    state = turned_state(state)
    me = jnp.stack([lax.axis_index("dp"), lax.axis_index("fsdp")]).astype(jnp.int32)
    sa, sb = pack(state[0::3])
    x = images.reshape(n_img, 256, 256)
    cot = cotangent.reshape(n_img, 256, 256)
    cf = figures(counts, x)
    emb = jax.nn.silu(sinus_embed(timesteps)).astype(BF)

    line_a = jnp.stack([sa] + [swap(sa, 8 * rz) for rz in range(1, 4)])
    rows_b = [sb] + [swap(sb, 8 * rz) for rz in range(1, 4)]
    plane_a = [line_a] + [swap(line_a, bits) for bits in (2, 4, 6)]
    rows_b, plane_a, cf, me, emb = lax.optimization_barrier((rows_b, plane_a, cf, me, emb))
    all_a = [p for line in plane_a for p in (line, swap(line, 1))]
    line_b = jnp.stack(rows_b)
    plane_b = [line_b] + [swap(line_b, bits) for bits in (2, 4, 6)]
    all_a, line_b = lax.optimization_barrier((all_a, line_b))
    h0, a1, wat, vec = conv_one(counts, x, cf, me, all_a, unpack_a)
    h0, plane_b = lax.optimization_barrier((h0, plane_b))
    all_b = [p for line in plane_b for p in (line, swap(line, 1))]
    out, ga, dm, *ends, rows = middle(
        counts, x, h0, cot, a1, emb, vec, me, all_b, unpack_b, finish_all, [sd((4, RG, 128), BF)] * 8 + [sd((16, 256), F32)]
    )
    plane_parts = over_core(ends)
    plane = to_plane(plane_parts)
    ga, parts = lax.optimization_barrier((ga, plane_parts))
    ig, v = input_grad(counts, x, ga, dm, cf, vec, me, wat, 0, n_img // NB, None)
    v, plane = lax.optimization_barrier((v, plane))
    own, others = plane_sum(parts[0], plane)
    grads, sums = shares(own, over_line(others), v, rows)
    results = adam(me, total_over(sums), grads, state)
    return (out.reshape(images.shape), ig.reshape(images.shape), *turned_back(results[:15]), results[15].reshape(()))


def gather_flat(masters, dp, fs):
    sizes = [m.size for m in masters]
    total = sum(sizes)
    full = -(-total // 2048) * 2048
    flat = jnp.concatenate([m.reshape(-1).astype(BF) for m in masters] + [jnp.zeros((full - total,), BF)])
    flat = flat.reshape(-1, 128)
    g = lax.all_gather(lax.all_gather(flat, "dp"), "fsdp").reshape(fs, dp, full)
    out = []
    at = 0
    for n in sizes:
        out.append(g[:, :, at : at + n])
        at += n
    conv = out[0].reshape((fs, dp) + masters[0].shape[1:]).transpose(2, 3, 0, 5, 1, 4)
    conv = conv.reshape(2, 2304, 256)
    mats = []
    for p, m in zip(out[1:4], masters[1:4]):
        r, c = m.shape[1:]
        mats.append(p.reshape(fs, dp, r, c).transpose(0, 3, 1, 2).reshape(fs * c, dp * r))
    vec = out[4].transpose(1, 0, 2).reshape(12, 256).astype(F32)
    return conv, mats, vec


def reduce_flat(grads, dp, fs):
    conv, mats, vec = grads
    pieces = [conv.reshape(18, fs, 256 // fs, dp, 256 // dp).transpose(1, 3, 0, 4, 2).reshape(fs, dp, -1)]
    for g in mats:
        c, r = g.shape
        pieces.append(g.reshape(fs, c // fs, dp, r // dp).transpose(0, 2, 3, 1).reshape(fs, dp, -1))
    pieces.append(vec.reshape(dp, fs, -1).transpose(1, 0, 2))
    sizes = [p.shape[2] for p in pieces]
    total = sum(sizes)
    full = -(-total // 2048) * 2048
    pieces.append(jnp.zeros((fs, dp, full - total), F32))
    flat = jnp.concatenate(pieces, axis=2).reshape(fs, dp, -1, 128)
    part = lax.psum_scatter(flat, "fsdp", scatter_dimension=0, tiled=False)
    part = lax.psum_scatter(part, "dp", scatter_dimension=0, tiled=False).reshape(-1)
    out = []
    at = 0
    for n in sizes:
        out.append(part[at : at + n])
        at += n
    return out


def finish_whole(outs, me, dwa, dwb, dwq, dwo, de, rows, turn):
    for out, got in zip(outs, (dwa[...], dwb[...], dwq[...], dwo[...], de, rows)):
        out[...] = got


def fill_one(me, wat, vec, wat_ref, vec_ref, vrows):
    wat_ref[...] = wat[...]
    vec_ref[...] = vec[...]


def fill_rest(me, *refs):
    for k in range(4):
        refs[4 + k][...] = refs[k][...]


def per_device_any(images, timesteps, counts, cotangent, *state):
    masters = state[0::3]
    moments = state[1::3]
    squares = state[2::3]
    dp = lax.axis_size("dp")
    fs = lax.axis_size("fsdp")
    n_img = images.shape[0]
    me = jnp.zeros((2,), jnp.int32)
    emb = jax.nn.silu(sinus_embed(timesteps)).astype(BF)
    x = images.reshape(n_img, 256, 256)
    cot = cotangent.reshape(n_img, 256, 256)
    conv, (wet, wqt, wot), vec = gather_flat(masters, dp, fs)
    vec = jnp.pad(vec, ((0, 4), (0, 0)))
    cf = figures(counts, x)
    h0, a1, wat, vec = conv_one(counts, x, cf, me, (conv[0], vec), fill_one)
    ends = [sd(s, F32) for s in ((768, 768), (768, 768), (256, 768), (256, 256), (256, 512), (16, 256))]
    out, ga, dm, dwa, dwb, dwq, dwo, de, rows = middle(
        counts, x, h0, cot, a1, emb, vec, me, (wet, conv[1], wqt, wot), fill_rest, finish_whole, ends
    )
    ig, first = input_grad(counts, x, ga, dm, cf, vec, me, conv[0], 0, n_img // NB, None)
    first = jnp.pad(first[:4].reshape(2, 256), ((0, 14), (0, 0)))
    apart = lambda w: w.reshape(3, 256, 3, 256).transpose(0, 2, 1, 3).reshape(9, 256, 256)
    shares_here = reduce_flat(
        (jnp.stack([apart(dwa), apart(dwb)]), (de, dwq.T, dwo), (rows + first)[:12]), dp, fs
    )
    local = sum(jnp.sum(s * s) for s in shares_here)
    norm = jnp.sqrt(lax.psum(lax.psum(local, "fsdp"), "dp"))
    factor = clip_norm / jnp.maximum(norm, clip_norm)
    results = []
    for kind in range(5):
        clipped = shares_here[kind].reshape(masters[kind].shape) * factor
        first_new = beta_first * moments[kind] + (1.0 - beta_first) * clipped
        second_new = beta_second * squares[kind] + (1.0 - beta_second) * clipped * clipped
        first_hat = first_new / (1.0 - beta_first**STEP)
        second_hat = second_new / (1.0 - beta_second**STEP)
        update_new = masters[kind] - rates_kind[kind] * (
            first_hat / (jnp.sqrt(second_hat) + adam_eps) + decays_kind[kind] * masters[kind]
        )
        results += [first_new, second_new, update_new]
    return (out.reshape(images.shape), ig.reshape(images.shape), *results, norm)


def solution(mesh):
    both = P(("dp", "fsdp"), None, None, None)
    one = P(("dp", "fsdp"))
    conv = P(None, None, None, "dp", "fsdp")
    mat = P(None, "dp", "fsdp")
    vec = P(None, ("dp", "fsdp"))
    trios = (conv,) * 3 + (mat,) * 9 + (vec,) * 3
    here = mesh.shape["dp"] == 4 and mesh.shape["fsdp"] == 8
    return jax.shard_map(
        per_device_here if here else per_device_any,
        mesh=mesh,
        in_specs=(both, one, one, both) + trios,
        out_specs=(both, both) + trios + (P(),),
        check_vma=False,
    )
```
